32 devices in a mesh: blk: 8 (over y, x, core), grp: 4 (over z).
Axes of the slice: x: 2, y: 2, z: 4, core: 2. Of those that a mesh axis runs over, the one named last changes fastest.
Arguments:
- hidden_in: bfloat16 [128, 128, 768], P(('blk', 'grp')), may hold values from -6 to 6
- upstream_grad: bfloat16 [128, 128, 768], P(('blk', 'grp')), may hold values from -6 to 6
- query_vectors: bfloat16 [128, 768], P(('blk', 'grp')), may hold values from -0.5 to 0.5
- loss_weight: float32 [128], P(('blk', 'grp')), may hold values from 4 to 16
- positive_ids: int32 [128, 3], P(('blk', 'grp')), may hold values from 0 to 127, as said below
- positive_count: int32 [128], P(('blk', 'grp')), may hold values from 1 to 3
- query_proj: bfloat16 [768, 768], P(('blk', 'grp')), may hold values from -0.21875 to 0.21875
- key_proj: bfloat16 [768, 768], P(('blk', 'grp')), may hold values from -0.21875 to 0.21875
- value_proj: bfloat16 [768, 768], P(('blk', 'grp')), may hold values from -0.21875 to 0.21875
- attn_proj: bfloat16 [768, 768], P(None, ('blk', 'grp')), may hold values from -1.75 to 1.75
- query_bias: bfloat16 [768], P(('blk', 'grp')), may hold values from -3 to 3
- value_bias: bfloat16 [768], P(('blk', 'grp')), may hold values from -3 to 3
- attn_bias: bfloat16 [768], P(('blk', 'grp')), may hold values from -3 to 3
- first_gain: bfloat16 [768], P(('blk', 'grp')), may hold values from 0.25 to 1.75
- first_shift: bfloat16 [768], P(('blk', 'grp')), may hold values from -2 to 2
- inner_proj: bfloat16 [768, 3072], P(('blk', 'grp')), may hold values from -0.21875 to 0.21875
- inner_bias: bfloat16 [3072], P(('blk', 'grp')), may hold values from -3 to 3
- outer_proj: bfloat16 [3072, 768], P(None, ('blk', 'grp')), may hold values from -0.15625 to 0.15625
- outer_bias: bfloat16 [768], P(('blk', 'grp')), may hold values from -3 to 3
- second_gain: bfloat16 [768], P(('blk', 'grp')), may hold values from 0.25 to 1.75
- second_shift: bfloat16 [768], P(('blk', 'grp')), may hold values from -2 to 2
Outputs:
- layer_output: bfloat16 [128, 128, 768], P(('blk', 'grp'))
- hidden_grad: bfloat16 [128, 128, 768], P(('blk', 'grp'))
- query_grad: float32 [128, 768], P(('blk', 'grp'))
- query_loss: float32 [128], P(('blk', 'grp'))
- grad_query_proj: float32 [768, 768], P(('blk', 'grp'))
- grad_key_proj: float32 [768, 768], P(('blk', 'grp'))
- grad_value_proj: float32 [768, 768], P(('blk', 'grp'))
- grad_attn_proj: float32 [768, 768], P(None, ('blk', 'grp'))
- grad_query_bias: float32 [768], P(('blk', 'grp'))
- grad_value_bias: float32 [768], P(('blk', 'grp'))
- grad_attn_bias: float32 [768], P(('blk', 'grp'))
- grad_first_gain: float32 [768], P(('blk', 'grp'))
- grad_first_shift: float32 [768], P(('blk', 'grp'))
- grad_inner_proj: float32 [768, 3072], P(('blk', 'grp'))
- grad_inner_bias: float32 [3072], P(('blk', 'grp'))
- grad_outer_proj: float32 [3072, 768], P(None, ('blk', 'grp'))
- grad_outer_bias: float32 [768], P(('blk', 'grp'))
- grad_second_gain: float32 [768], P(('blk', 'grp'))
- grad_second_shift: float32 [768], P(('blk', 'grp'))
- cls_grad: float32 [128, 768], P(('blk', 'grp'))
The draws below stay inside these ranges and needn't reach their ends.
Inputs may be any that keep to these rules, and one draw needn't show every extreme that they name: `positive_ids`: each row holds 3 different passage indices; only the first positive_count of them are the query's positives. Every passage index is the first entry of exactly one row.
All inputs are finite; a program needn't handle non-finite values.
Results may differ from the reference program's by a relative error of at most 0.023.
Values may be sent and summed in bfloat16 or wider, within the bound.
A program may use at most 192 MiB of HBM per device.

```python
import math
from functools import partial
import jax
import jax.numpy as jnp
from jax import lax

D = 768
HEADS = 12
HEAD_DIM = 64
FF = 3072
LEN = 128
PASSAGES = 128
QUERIES = 128


def draw_positive_ids(key, part):
    key = jax.random.fold_in(key, 11)
    first_key, second_key, third_key = jax.random.split(key, 3)
    first_ids = jax.random.permutation(first_key, PASSAGES).astype(jnp.int32)
    second_off = jax.random.randint(second_key, (QUERIES,), 1, PASSAGES, dtype=jnp.int32)
    third_step = jax.random.randint(third_key, (QUERIES,), 1, PASSAGES - 1, dtype=jnp.int32)
    third_off = 1 + (second_off - 1 + third_step) % (PASSAGES - 1)
    second_ids = (first_ids + second_off) % PASSAGES
    third_ids = (first_ids + third_off) % PASSAGES
    return jnp.stack([first_ids, second_ids, third_ids], axis=1).astype(jnp.int32)


def draw_positive_count(key, part):
    key = jax.random.fold_in(key, 23)
    counts = jax.random.randint(key, (QUERIES,), 1, 4, dtype=jnp.int32)
    return counts.at[0].set(1).at[1].set(3)


def with_spikes(values, key, source, target, parts, factor):
    def block_of(position):
        return (jnp.arange(values.shape[position]) // (values.shape[position] // parts)).reshape((-1,) + (1,) * (values.ndim - 1 - position))

    near = jax.random.permutation(key, parts)[block_of(target)]
    second = (block_of(target) + parts // 2) % parts
    return jnp.where((block_of(source) == near) | (block_of(source) == second), factor * values, values)


def block_scale(rng, shape, shards, smallest, largest):
    factor_of = 1.0
    for axis_at, shards_of in shards:
        draws = jax.random.uniform(jax.random.fold_in(jax.random.fold_in(rng, 6), axis_at), (shards_of,), jnp.float32, smallest / len(shards), largest / len(shards))
        factor_of = factor_of * jnp.repeat(jnp.exp(draws), shape[axis_at] // shards_of).reshape((-1,) + (1,) * (len(shape) - 1 - axis_at))
    return factor_of


def scatter_about(rng, shape, scale, limit, shards=(), kind=jnp.bfloat16):
    values = jax.random.normal(rng, shape, jnp.float32) * scale
    if len(shards) > 0:
        values = block_scale(rng, shape, shards, -0.22, 0.18) * values
    return jnp.clip(values, min=-limit, max=limit).astype(kind)


def heavy_noise(stream_key, dims, width, most, cuts, heavy, kind=jnp.bfloat16):
    array = width * jax.random.normal(stream_key, dims, jnp.float32)
    if cuts:
        array = array * block_scale(stream_key, dims, cuts, -0.22, 0.18)
    return jnp.clip(with_spikes(array, jax.random.fold_in(stream_key, 3), *heavy), -most, most).astype(kind)


def setup_inputs(seed: int = 0) -> dict:
    splits = jax.random.split(jax.random.key(seed), 22)
    hidden_in = heavy_noise(splits[0], (PASSAGES, LEN, D), 1.0, 6.0, ((0, 32),), (0, 2, 32, 2.75))
    upstream_grad = heavy_noise(splits[1], (PASSAGES, LEN, D), 1.0, 6.0, ((0, 32),), (0, 2, 32, 2.75))
    query_vectors = scatter_about(splits[2], (QUERIES, D), 0.08, 0.5, ((0, 32),))
    loss_weight = jnp.clip(jnp.exp(math.log(16.0) - 1.3862944 * jax.random.uniform(splits[3], (QUERIES,), jnp.float32) ** block_scale(splits[3], (QUERIES,), ((0, 32),), -0.2, 0.2)), 4.0, 16.0)
    positive_ids = draw_positive_ids(jax.random.fold_in(splits[21], 71), 0)
    positive_count = draw_positive_count(jax.random.fold_in(splits[21], 71), 0)
    query_proj = scatter_about(splits[6], (D, D), D ** -0.5, 0.21875, ((0, 32),))
    key_proj = scatter_about(splits[7], (D, D), D ** -0.5, 0.21875, ((0, 32),))
    value_proj = scatter_about(splits[8], (D, D), D ** -0.5, 0.21875, ((0, 32),))
    attn_proj = scatter_about(splits[9], (D, D), (D // 64) ** -0.5, 1.75, ((1, 32),))
    query_bias = scatter_about(splits[10], (D,), 0.5, 3.0, ((0, 32),))
    value_bias = scatter_about(splits[11], (D,), 0.5, 3.0, ((0, 32),))
    attn_bias = scatter_about(splits[12], (D,), 0.5, 3.0, ((0, 32),))
    first_gain = jnp.clip(1.0 + 0.15 * jax.random.normal(splits[13], (D,), jnp.float32), 0.25, 1.75).astype(jnp.bfloat16)
    first_shift = scatter_about(splits[14], (D,), 0.3, 2.0, ((0, 32),))
    inner_proj = scatter_about(splits[15], (D, FF), D ** -0.5, 0.21875, ((0, 32),))
    inner_bias = scatter_about(splits[16], (FF,), 0.5, 3.0, ((0, 32),))
    outer_proj = scatter_about(splits[17], (FF, D), (FF // 2) ** -0.5, 0.15625, ((1, 32),))
    outer_bias = scatter_about(splits[18], (D,), 0.5, 3.0, ((0, 32),))
    second_gain = jnp.clip(1.0 + 0.15 * jax.random.normal(splits[19], (D,), jnp.float32), 0.25, 1.75).astype(jnp.bfloat16)
    second_shift = scatter_about(splits[20], (D,), 0.3, 2.0, ((0, 32),))
    return dict(hidden_in=hidden_in, upstream_grad=upstream_grad, query_vectors=query_vectors, loss_weight=loss_weight, positive_ids=positive_ids, positive_count=positive_count, query_proj=query_proj, key_proj=key_proj, value_proj=value_proj, attn_proj=attn_proj, query_bias=query_bias, value_bias=value_bias, attn_bias=attn_bias, first_gain=first_gain, first_shift=first_shift, inner_proj=inner_proj, inner_bias=inner_bias, outer_proj=outer_proj, outer_bias=outer_bias, second_gain=second_gain, second_shift=second_shift)


@jax.custom_vjp
def low(v):
    return lax.optimization_barrier(v.astype(jnp.bfloat16)).astype(jnp.float32)

@jax.custom_vjp
def low_back(v):
    return v

def low_keep(v):
    return (low(v), None)

def low_pass(kept, grad):
    return (grad,)

def back_keep(v):
    return (v, None)

def back_low(kept, grad):
    return (low(grad),)
low.defvjp(low_keep, low_pass)
low_back.defvjp(back_keep, back_low)
HIGHEST = lax.Precision.HIGHEST
NORM_EPS = 1e-05
NEG_FILL = -1e+30

def matmul_high(left_side, right_side):
    return jnp.dot(left_side, right_side, precision=HIGHEST)

def layer_norm(resid_sum, gain_vec, shift_vec):
    center = resid_sum - lax.optimization_barrier(jnp.mean(resid_sum, axis=-1, keepdims=True))
    spread = lax.optimization_barrier(jnp.mean(center * center, axis=-1, keepdims=True))
    return center * lax.rsqrt(spread + NORM_EPS) * gain_vec + shift_vec

def softmax_rows(scores):
    top_score = lax.optimization_barrier(jnp.max(scores, axis=-1, keepdims=True))
    exp_terms = jnp.exp(scores - top_score)
    return exp_terms / lax.optimization_barrier(jnp.sum(exp_terms, axis=-1, keepdims=True))

def log_total(scores):
    top_score = lax.optimization_barrier(jnp.max(scores, axis=-1))
    return top_score + jnp.log(lax.optimization_barrier(jnp.sum(jnp.exp(scores - top_score[:, None]), axis=-1)))

def positive_table(positive_ids, positive_count):
    slot_live = jnp.arange(positive_ids.shape[1], dtype=jnp.int32)[None, :] < positive_count[:, None]
    passage_index = jnp.arange(PASSAGES, dtype=jnp.int32)
    matches = (positive_ids[:, :, None] == passage_index[None, None, :]) & slot_live[:, :, None]
    return jnp.any(matches, axis=1)

def passage_layer(params, passages):
    query_proj, key_proj, value_proj, attn_proj, query_bias, value_bias, attn_bias, first_gain, first_shift, inner_proj, inner_bias, outer_proj, outer_bias, second_gain, second_shift = params
    pass_count = passages.shape[0]
    head_shape = (pass_count, LEN, HEADS, HEAD_DIM)
    tok_rows = passages.reshape(pass_count * LEN, D)
    queries = low(low_back((matmul_high(tok_rows, query_proj) + query_bias) * 0.125)).reshape(head_shape)
    keys_all = low(low_back(matmul_high(tok_rows, key_proj))).reshape(head_shape)
    values_all = low(low_back(matmul_high(tok_rows, value_proj) + value_bias)).reshape(head_shape)
    scores = low_back(jnp.einsum('bqhd,bkhd->bhqk', queries, keys_all, precision=HIGHEST))
    weights = low(softmax_rows(scores))
    context = jnp.einsum('bhqk,bkhd->bqhd', weights, values_all, precision=HIGHEST)
    context = low(low_back(context.reshape(pass_count * LEN, D)))
    attn_out = low_back(matmul_high(context, attn_proj) + attn_bias)
    normed = layer_norm(tok_rows + attn_out, first_gain, first_shift)
    inner_pre = low_back(matmul_high(low(normed), inner_proj) + inner_bias)
    activated = low(jax.nn.gelu(inner_pre, approximate=False))
    branch = low_back(matmul_high(activated, outer_proj) + outer_bias)
    return layer_norm(normed + branch, second_gain, second_shift).reshape(pass_count, LEN, D)

def reference(hidden_in, upstream_grad, query_vectors, loss_weight, positive_ids, positive_count, query_proj, key_proj, value_proj, attn_proj, query_bias, value_bias, attn_bias, first_gain, first_shift, inner_proj, inner_bias, outer_proj, outer_bias, second_gain, second_shift):
    params = tuple((member.astype(jnp.float32) for member in (query_proj, key_proj, value_proj, attn_proj, query_bias, value_bias, attn_bias, first_gain, first_shift, inner_proj, inner_bias, outer_proj, outer_bias, second_gain, second_shift)))
    positive = positive_table(positive_ids, positive_count)
    group_pass = math.gcd(PASSAGES, max(1, 4096 // LEN))

    def objective(layer_params, hidden_all, query_all, cls_shift):
        grouped = hidden_all.reshape(PASSAGES // group_pass, group_pass, LEN, D)
        layered = jax.checkpoint(partial(passage_layer, layer_params))
        outputs = lax.map(layered, grouped).reshape(PASSAGES, LEN, D)
        cls_vectors = low(outputs[:, 0, :]) + cls_shift
        scores = low_back(matmul_high(query_all, cls_vectors.T))
        losses = log_total(scores) - log_total(jnp.where(positive, scores, NEG_FILL))
        return (outputs, losses)
    cls_zero = jnp.zeros((PASSAGES, D), jnp.float32)
    (outputs, losses), pullback = jax.vjp(objective, params, hidden_in.astype(jnp.float32), query_vectors.astype(jnp.float32), cls_zero)
    param_grads, hidden_grad, query_grad, cls_grad = pullback((upstream_grad.astype(jnp.float32), loss_weight))
    return (outputs.astype(jnp.bfloat16), hidden_grad.astype(jnp.bfloat16), query_grad, losses, param_grads[0], param_grads[1], param_grads[2], param_grads[3], param_grads[4], param_grads[5], param_grads[6], param_grads[7], param_grads[8], param_grads[9], param_grads[10], param_grads[11], param_grads[12], param_grads[13], param_grads[14], cls_grad)
```

```python
import jax
import jax.numpy as jnp
from jax import lax
from jax.experimental import pallas as pl
from jax.experimental.pallas import tpu as pltpu
from jax.sharding import PartitionSpec as P

D = 768
HEADS = 12
HEAD_DIM = 64
LEN = 128


NORM_EPS = 1e-05
NEG_FILL = -1e30


def product(left_side, right_side):
    return jnp.dot(left_side, right_side, preferred_element_type=jnp.float32)


def contract(form_text, first_side, second_side):
    return jnp.einsum(form_text, first_side, second_side, preferred_element_type=jnp.float32)


def norm_forward(resid_sum, gain_vec, shift_vec):
    centered = resid_sum - jnp.mean(resid_sum, axis=-1, keepdims=True)
    inv_dev = lax.rsqrt(jnp.mean(centered * centered, axis=-1, keepdims=True) + NORM_EPS)
    normal_part = centered * inv_dev
    return (normal_part * gain_vec + shift_vec, normal_part, inv_dev)


def norm_backward(out_grad, normal_part, inv_dev, gain_vec):
    scaled_grad = out_grad * gain_vec
    mean_grad = jnp.mean(scaled_grad, axis=-1, keepdims=True)
    mean_cross = jnp.mean(scaled_grad * normal_part, axis=-1, keepdims=True)
    return inv_dev * (scaled_grad - mean_grad - normal_part * mean_cross)


def gelu_exact(pre_act):
    return jax.nn.gelu(pre_act, approximate=False)


def gelu_grad(pre_act, act_grad):
    unused_out, pullback = jax.vjp(gelu_exact, pre_act)
    return pullback(act_grad)[0]


def positive_block(positive_ids, positive_count, span_count):
    slot_live = (
        jnp.arange(positive_ids.shape[1], dtype=jnp.int32)[None, :] < positive_count[:, None]
    )
    passage_index = jnp.arange(span_count, dtype=jnp.int32)
    matches = (positive_ids[:, :, None] == passage_index[None, None, :]) & slot_live[:, :, None]
    return jnp.any(matches, axis=1)


def block_forward(block_in, attn_params, ffn_params):
    (
        query_proj,
        key_proj,
        value_proj,
        attn_proj,
        query_bias,
        value_bias,
        attn_bias,
        first_gain,
        first_shift,
    ) = attn_params
    inner_proj, inner_bias, outer_proj, outer_bias, second_gain, second_shift = ffn_params
    pass_count = block_in.shape[0]
    head_shape = (pass_count, LEN, HEADS, HEAD_DIM)
    tok_rows = block_in.reshape(pass_count * LEN, D)
    queries = ((product(tok_rows, query_proj) + query_bias) * 0.125).astype(jnp.bfloat16)
    keys_low = product(tok_rows, key_proj).astype(jnp.bfloat16)
    values_low = (product(tok_rows, value_proj) + value_bias).astype(jnp.bfloat16)
    scores = contract("bqhd,bkhd->bhqk", queries.reshape(head_shape), keys_low.reshape(head_shape))
    top_score = jnp.max(scores, axis=-1, keepdims=True)
    exp_terms = jnp.exp(scores - top_score)
    totals = jnp.sum(exp_terms, axis=-1, keepdims=True)
    probs_low = (exp_terms / totals).astype(jnp.bfloat16)
    log_norm = top_score + jnp.log(totals)
    context = contract("bhqk,bkhd->bqhd", probs_low, values_low.reshape(head_shape))
    context = context.reshape(pass_count * LEN, D).astype(jnp.bfloat16)
    attn_out = product(context, attn_proj) + attn_bias
    normed, first_normal, first_inv = norm_forward(
        tok_rows.astype(jnp.float32) + attn_out, first_gain, first_shift
    )
    normed_low = normed.astype(jnp.bfloat16)
    inner_pre = product(normed_low, inner_proj) + inner_bias
    activated = gelu_exact(inner_pre).astype(jnp.bfloat16)
    branch = product(activated, outer_proj) + outer_bias
    layer_f32, second_normal, second_inv = norm_forward(normed + branch, second_gain, second_shift)
    kept_state = (
        queries,
        keys_low,
        values_low,
        log_norm,
        context,
        first_normal,
        first_inv,
        normed_low,
        inner_pre,
        activated,
        second_normal,
        second_inv,
    )
    return (layer_f32, kept_state)


def block_backward(block_in, out_grad, kept_state, attn_params, ffn_params):
    (
        query_proj,
        key_proj,
        value_proj,
        attn_proj,
        query_bias,
        value_bias,
        attn_bias,
        first_gain,
        first_shift,
    ) = attn_params
    inner_proj, inner_bias, outer_proj, outer_bias, second_gain, second_shift = ffn_params
    (
        queries,
        keys_low,
        values_low,
        log_norm,
        context,
        first_normal,
        first_inv,
        normed_low,
        inner_pre,
        activated,
        second_normal,
        second_inv,
    ) = kept_state
    pass_count = block_in.shape[0]
    tok_count = pass_count * LEN
    head_shape = (pass_count, LEN, HEADS, HEAD_DIM)
    tok_rows = block_in.reshape(tok_count, D)
    grad_rows = out_grad.reshape(tok_count, D)
    grad_second_gain = jnp.sum(grad_rows * second_normal, axis=0)
    grad_second_shift = jnp.sum(grad_rows, axis=0)
    second_resid = norm_backward(grad_rows, second_normal, second_inv, second_gain)
    branch_grad = second_resid.astype(jnp.bfloat16)
    grad_outer_bias = jnp.sum(branch_grad.astype(jnp.float32), axis=0)
    grad_outer_proj = product(activated.T, branch_grad)
    inner_grad = gelu_grad(inner_pre, product(branch_grad, outer_proj.T)).astype(jnp.bfloat16)
    grad_inner_bias = jnp.sum(inner_grad.astype(jnp.float32), axis=0)
    grad_inner_proj = product(normed_low.T, inner_grad)
    normed_grad = second_resid + product(inner_grad, inner_proj.T)
    grad_first_gain = jnp.sum(normed_grad * first_normal, axis=0)
    grad_first_shift = jnp.sum(normed_grad, axis=0)
    first_resid = norm_backward(normed_grad, first_normal, first_inv, first_gain)
    attn_grad = first_resid.astype(jnp.bfloat16)
    grad_attn_bias = jnp.sum(attn_grad.astype(jnp.float32), axis=0)
    grad_attn_proj = product(context.T, attn_grad)
    context_grad = product(attn_grad, attn_proj.T).astype(jnp.bfloat16).reshape(head_shape)
    query_heads = queries.reshape(head_shape)
    key_heads = keys_low.reshape(head_shape)
    value_heads = values_low.reshape(head_shape)
    scores = contract("bqhd,bkhd->bhqk", query_heads, key_heads)
    prob_full = jnp.exp(scores - log_norm)
    values_grad = contract("bhqk,bqhd->bkhd", prob_full.astype(jnp.bfloat16), context_grad)
    values_grad = values_grad.astype(jnp.bfloat16).reshape(tok_count, D)
    prob_grad = contract("bqhd,bkhd->bhqk", context_grad, value_heads)
    score_grad = (
        prob_full * (prob_grad - jnp.sum(prob_full * prob_grad, axis=-1, keepdims=True))
    ).astype(jnp.bfloat16)
    queries_grad = (
        contract("bhqk,bkhd->bqhd", score_grad, key_heads)
        .astype(jnp.bfloat16)
        .reshape(tok_count, D)
    )
    keys_grad = (
        contract("bhqk,bqhd->bkhd", score_grad, query_heads)
        .astype(jnp.bfloat16)
        .reshape(tok_count, D)
    )
    grad_query_proj = product(tok_rows.T, queries_grad) * 0.125
    grad_query_bias = jnp.sum(queries_grad.astype(jnp.float32), axis=0) * 0.125
    grad_key_proj = product(tok_rows.T, keys_grad)
    grad_value_proj = product(tok_rows.T, values_grad)
    grad_value_bias = jnp.sum(values_grad.astype(jnp.float32), axis=0)
    hidden_grad = (
        first_resid
        + 0.125 * product(queries_grad, query_proj.T)
        + product(keys_grad, key_proj.T)
        + product(values_grad, value_proj.T)
    )
    attn_grads = (
        grad_query_proj,
        grad_key_proj,
        grad_value_proj,
        grad_attn_proj,
        grad_query_bias,
        grad_value_bias,
        grad_attn_bias,
        grad_first_gain,
        grad_first_shift,
    )
    ffn_grads = (
        grad_inner_proj,
        grad_inner_bias,
        grad_outer_proj,
        grad_outer_bias,
        grad_second_gain,
        grad_second_shift,
    )
    return (hidden_grad, attn_grads, ffn_grads)


def plain_local(
    hidden_in,
    upstream_grad,
    query_vectors,
    loss_weight,
    positive_ids,
    positive_count,
    query_proj,
    key_proj,
    value_proj,
    attn_proj,
    query_bias,
    value_bias,
    attn_bias,
    first_gain,
    first_shift,
    inner_proj,
    inner_bias,
    outer_proj,
    outer_bias,
    second_gain,
    second_shift,
):
    attn_params = (
        lax.all_gather(query_proj, ("blk", "grp"), axis=0, tiled=True),
        lax.all_gather(key_proj, ("blk", "grp"), axis=0, tiled=True),
        lax.all_gather(value_proj, ("blk", "grp"), axis=0, tiled=True),
        lax.all_gather(attn_proj, ("blk", "grp"), axis=1, tiled=True),
        lax.all_gather(query_bias, ("blk", "grp"), axis=0, tiled=True),
        lax.all_gather(value_bias, ("blk", "grp"), axis=0, tiled=True),
        lax.all_gather(attn_bias, ("blk", "grp"), axis=0, tiled=True),
        lax.all_gather(first_gain, ("blk", "grp"), axis=0, tiled=True),
        lax.all_gather(first_shift, ("blk", "grp"), axis=0, tiled=True),
    )
    ffn_params = (
        lax.all_gather(inner_proj, ("blk", "grp"), axis=0, tiled=True),
        lax.all_gather(inner_bias, ("blk", "grp"), axis=0, tiled=True),
        lax.all_gather(outer_proj, ("blk", "grp"), axis=1, tiled=True),
        lax.all_gather(outer_bias, ("blk", "grp"), axis=0, tiled=True),
        lax.all_gather(second_gain, ("blk", "grp"), axis=0, tiled=True),
        lax.all_gather(second_shift, ("blk", "grp"), axis=0, tiled=True),
    )
    pass_count = hidden_in.shape[0]
    layer_f32, kept_state = block_forward(hidden_in, attn_params, ffn_params)
    layer_output = layer_f32.astype(jnp.bfloat16).reshape(pass_count, LEN, D)
    cls_local = layer_output[:, 0, :]
    query_count = query_vectors.shape[0]
    lowest = jnp.full((query_count,), NEG_FILL, jnp.float32)
    cls_piece = lax.all_gather(cls_local, ("blk", "grp"), axis=0, tiled=True)
    top_all = lowest
    top_pos = lowest
    scores = contract("qd,pd->qp", query_vectors, cls_piece)
    hit_mask = positive_block(positive_ids, positive_count, cls_piece.shape[0])
    masked = jnp.where(hit_mask, scores, NEG_FILL)
    new_all = jnp.maximum(top_all, jnp.max(scores, axis=1))
    new_pos = jnp.maximum(top_pos, jnp.max(masked, axis=1))
    sum_all = jnp.sum(jnp.exp(scores - new_all[:, None]), axis=1)
    pos_terms = jnp.where(hit_mask, jnp.exp(masked - new_pos[:, None]), 0.0)
    sum_pos = jnp.sum(pos_terms, axis=1)
    top_all, sum_all, top_pos, sum_pos = (new_all, sum_all, new_pos, sum_pos)
    total_all = top_all + jnp.log(sum_all)
    total_pos = top_pos + jnp.log(sum_pos)
    cls_piece = lax.all_gather(cls_local, ("blk", "grp"), axis=0, tiled=True)
    scores = contract("qd,pd->qp", query_vectors, cls_piece)
    hit_mask = positive_block(positive_ids, positive_count, cls_piece.shape[0])
    masked = jnp.where(hit_mask, scores, NEG_FILL)
    weight_rows = loss_weight[:, None] * (
        jnp.exp(scores - total_all[:, None]) - jnp.exp(masked - total_pos[:, None])
    )
    weight_rows = weight_rows.astype(jnp.bfloat16)
    query_acc = product(weight_rows, cls_piece)
    query_loss = total_all - total_pos
    cls_grad = lax.psum_scatter(
        contract("qp,qd->pd", weight_rows, query_vectors),
        ("blk", "grp"),
        scatter_dimension=0,
        tiled=True,
    )
    grad_total = upstream_grad.astype(jnp.float32).at[:, 0, :].add(cls_grad)
    ffn_back = (
        lax.all_gather(inner_proj, ("blk", "grp"), axis=0, tiled=True),
        lax.all_gather(inner_bias, ("blk", "grp"), axis=0, tiled=True),
        lax.all_gather(outer_proj, ("blk", "grp"), axis=1, tiled=True),
        lax.all_gather(outer_bias, ("blk", "grp"), axis=0, tiled=True),
        lax.all_gather(second_gain, ("blk", "grp"), axis=0, tiled=True),
        lax.all_gather(second_shift, ("blk", "grp"), axis=0, tiled=True),
    )
    attn_back = (
        lax.all_gather(query_proj, ("blk", "grp"), axis=0, tiled=True),
        lax.all_gather(key_proj, ("blk", "grp"), axis=0, tiled=True),
        lax.all_gather(value_proj, ("blk", "grp"), axis=0, tiled=True),
        lax.all_gather(attn_proj, ("blk", "grp"), axis=1, tiled=True),
        lax.all_gather(query_bias, ("blk", "grp"), axis=0, tiled=True),
        lax.all_gather(value_bias, ("blk", "grp"), axis=0, tiled=True),
        lax.all_gather(attn_bias, ("blk", "grp"), axis=0, tiled=True),
        lax.all_gather(first_gain, ("blk", "grp"), axis=0, tiled=True),
        lax.all_gather(first_shift, ("blk", "grp"), axis=0, tiled=True),
    )
    hidden_part, attn_grads, ffn_grads = block_backward(
        hidden_in, grad_total, kept_state, attn_back, ffn_back
    )
    attn_shards = (
        lax.psum_scatter(attn_grads[0], ("blk", "grp"), scatter_dimension=0, tiled=True),
        lax.psum_scatter(attn_grads[1], ("blk", "grp"), scatter_dimension=0, tiled=True),
        lax.psum_scatter(attn_grads[2], ("blk", "grp"), scatter_dimension=0, tiled=True),
        lax.psum_scatter(attn_grads[3], ("blk", "grp"), scatter_dimension=1, tiled=True),
        lax.psum_scatter(attn_grads[4], ("blk", "grp"), scatter_dimension=0, tiled=True),
        lax.psum_scatter(attn_grads[5], ("blk", "grp"), scatter_dimension=0, tiled=True),
        lax.psum_scatter(attn_grads[6], ("blk", "grp"), scatter_dimension=0, tiled=True),
        lax.psum_scatter(attn_grads[7], ("blk", "grp"), scatter_dimension=0, tiled=True),
        lax.psum_scatter(attn_grads[8], ("blk", "grp"), scatter_dimension=0, tiled=True),
    )
    ffn_shards = (
        lax.psum_scatter(ffn_grads[0], ("blk", "grp"), scatter_dimension=0, tiled=True),
        lax.psum_scatter(ffn_grads[1], ("blk", "grp"), scatter_dimension=0, tiled=True),
        lax.psum_scatter(ffn_grads[2], ("blk", "grp"), scatter_dimension=1, tiled=True),
        lax.psum_scatter(ffn_grads[3], ("blk", "grp"), scatter_dimension=0, tiled=True),
        lax.psum_scatter(ffn_grads[4], ("blk", "grp"), scatter_dimension=0, tiled=True),
        lax.psum_scatter(ffn_grads[5], ("blk", "grp"), scatter_dimension=0, tiled=True),
    )
    hidden_grad = hidden_part.astype(jnp.bfloat16).reshape(pass_count, LEN, D)
    return (
        layer_output,
        hidden_grad,
        query_acc,
        query_loss,
        attn_shards[0],
        attn_shards[1],
        attn_shards[2],
        attn_shards[3],
        attn_shards[4],
        attn_shards[5],
        attn_shards[6],
        attn_shards[7],
        attn_shards[8],
        ffn_shards[0],
        ffn_shards[1],
        ffn_shards[2],
        ffn_shards[3],
        ffn_shards[4],
        ffn_shards[5],
        cls_grad,
    )


BF = jnp.bfloat16
F32 = jnp.float32
MESH = pl.DeviceIdType.MESH
VM = pl.BlockSpec(memory_space=pltpu.VMEM)
DMA = pltpu.SemaphoreType.DMA
ALL = slice(None)
VMEM_LIMIT = 60 * 2**20
NC = 12
LW = 384
ROWS = 24


class Place:
    def __init__(self):
        self.b = lax.axis_index("blk")
        self.z = lax.axis_index("grp")
        self.y, self.x, self.c = self.b // 4, (self.b // 2) % 2, self.b % 2
        self.zh, self.zl = self.z // 2, self.z % 2
        self.mid = ((self.z + 1) // 2) % 2
        self.xdev = (self.b + 2 - 4 * self.x, self.z)
        self.ydev = (self.b + 4 - 8 * self.y, self.z)
        self.cdev = (self.b + 1 - 2 * self.c, self.z)
        self.zdev = (self.b, self.z + 1 - 2 * self.zl)
        self.fdev = (self.b, 3 - self.z)


def greet(p):
    bar = pltpu.get_barrier_semaphore()
    for k in range(1, 8):
        pl.semaphore_signal(bar, 1, device_id=((p.b + k) % 8, p.z), device_id_type=MESH)
    for k in range(1, 4):
        pl.semaphore_signal(bar, 1, device_id=(p.b, (p.z + k) % 4), device_id_type=MESH)
    pl.semaphore_wait(bar, 10)


def rcopy(src, dst, ss, rs, dev):
    return pltpu.make_async_remote_copy(
        src_ref=src, dst_ref=dst, send_sem=ss, recv_sem=rs, device_id=dev, device_id_type=MESH
    )


class Flow:
    def __init__(self, p, ref, kind, ss, rs):
        self.p, self.ref, self.kind, self.ss, self.rs = p, ref, kind, ss, rs
        self.f, self.s = (p.x, p.y) if kind == 0 else (p.y, p.x)
        self.fdev, self.sdev = (p.xdev, p.ydev) if kind == 0 else (p.ydev, p.xdev)

    def at(self, f, s, zz, c=None):
        c = self.p.c if c is None else c
        return self.ref.at[self.index(f, s, zz, c)]

    def index(self, f, s, zz, c):
        return (s, f, c, zz) if self.kind == 0 else (f, s, c, zz)

    def copy(self, stage, src, dst, dev):
        return rcopy(src, dst, self.ss(stage), self.rs(stage), dev)

    def go(self, stage, view, dev):
        self.copy(stage, view, view, dev).start()

    def got(self, stage, view):
        self.copy(stage, view, view, self.p.cdev).wait_recv()

    def sent(self, stage, view):
        self.copy(stage, view, view, self.p.cdev).wait_send()


class Gather(Flow):
    def s2_send(self):
        self.go(0, self.at(self.f, self.s, self.p.zh), self.fdev)

    def s2_recv(self):
        self.got(0, self.at(1 - self.f, self.s, self.p.zh))

    def s3a_send(self):
        self.go(1, self.at(ALL, self.s, self.p.zh), self.p.fdev)

    def s3a_recv(self):
        self.got(1, self.at(ALL, self.s, 1 - self.p.zh))

    def s3b_send(self):
        self.go(2, self.at(ALL, self.s, 1 - self.p.zh), self.p.zdev)

    def s3b_recv(self):
        self.got(2, self.at(ALL, self.s, 1 - self.p.zh))

    def s4_send(self):
        self.go(3, self.at(ALL, self.s, ALL), self.sdev)

    def s4_recv(self):
        self.got(3, self.at(ALL, 1 - self.s, ALL))

    def c1_send(self):
        self.go(4, self.at(ALL, self.s, ALL), self.p.cdev)

    def c1_recv(self):
        self.got(4, self.at(ALL, self.s, ALL, 1 - self.p.c))

    def c2_send(self):
        self.go(5, self.at(ALL, 1 - self.s, ALL), self.p.cdev)

    def c2_recv(self):
        self.got(5, self.at(ALL, 1 - self.s, ALL, 1 - self.p.c))

    def drain(self):
        self.sent(0, self.at(self.f, self.s, self.p.zh))

        @pl.when(self.p.mid == 1)
        def _():
            self.sent(1, self.at(ALL, self.s, self.p.zh))
            self.sent(2, self.at(ALL, self.s, 1 - self.p.zh))

        self.sent(3, self.at(ALL, self.s, ALL))
        self.sent(4, self.at(ALL, self.s, ALL))
        self.sent(5, self.at(ALL, 1 - self.s, ALL))


def lanes_of(ci):
    return pl.ds(pl.multiple_of((ci % 2) * LW, 128), LW)


def gather_kernel(in_ref, wa, wb, rb, ss, rs, s1s, s1r):
    p = Place()
    greet(p)

    def flows(ci):
        out = []
        for kind, ref in ((0, wa), (1, wb)):
            view = ref.at[ci // 2, :, :, :, :, :, lanes_of(ci)]
            out.append(
                Gather(
                    p,
                    view,
                    kind,
                    lambda st, kind=kind: ss.at[st, kind, ci],
                    lambda st, kind=kind: rs.at[st, kind, ci],
                )
            )
        return out

    def s1(ci):
        src = in_ref.at[ci // 2, :, lanes_of(ci)]
        return rcopy(src, rb.at[ci // 2, :, lanes_of(ci)], s1s.at[ci], s1r.at[ci], p.zdev)

    @pl.loop(0, NC)
    def _(ci):
        s1(ci).start()

    def merge(ci):
        s1(ci).wait_recv()
        i, ln = ci // 2, lanes_of(ci)
        own = in_ref[i, :, ln].astype(F32)
        oth = rb[i, :, ln].astype(F32)
        first = p.zl == 0
        lo = jnp.where(first, own, oth)
        hi = jnp.where(first, oth, own)
        wa[i, p.y, p.x, p.c, p.zh, :, ln] = jnp.concatenate([lo[:ROWS], hi[:ROWS]], 0).astype(BF)
        wb[i, p.y, p.x, p.c, p.zh, :, ln] = jnp.concatenate([lo[ROWS:], hi[ROWS:]], 0).astype(BF)
        for f in flows(ci):
            f.s2_send()

    def s23(ci):
        for f in flows(ci):
            f.s2_recv()

        @pl.when(p.mid == 1)
        def _():
            for f in flows(ci):
                f.s3a_send()

    def s34(ci):
        @pl.when(p.mid == 1)
        def _():
            for f in flows(ci):
                f.s3a_recv()
            for f in flows(ci):
                f.s3b_send()

        @pl.when(p.mid == 0)
        def _():
            for f in flows(ci):
                f.s3b_recv()

        for f in flows(ci):
            f.s4_send()
        for f in flows(ci):
            f.c1_send()

    def s45(ci):
        for f in flows(ci):
            f.s4_recv()
            f.c2_send()

    def core(ci):
        for f in flows(ci):
            f.c1_recv()
            f.c2_recv()

    stages = ((0, merge), (2, s23), (4, s34), (5, s45), (6, core))

    @pl.loop(0, NC + 6)
    def _(t):
        for off, fn in stages:

            @pl.when((t >= off) & (t < NC + off))
            def _(off=off, fn=fn):
                fn(t - off)

    @pl.loop(0, NC)
    def _(ci):
        for f in flows(ci):
            f.drain()
        s1(ci).wait_send()


def gather_weights(pack):
    whole = jax.ShapeDtypeStruct((6, 2, 2, 2, 2, 48, 768), BF)
    return pl.pallas_call(
        gather_kernel,
        out_shape=(whole, whole),
        in_specs=[VM],
        out_specs=(VM, VM),
        scratch_shapes=[pltpu.VMEM((6, 48, 768), BF)] + [DMA((6, 2, NC))] * 2 + [DMA((NC,))] * 2,
        compiler_params=pltpu.CompilerParams(
            collective_id=1, has_side_effects=True, vmem_limit_bytes=VMEM_LIMIT
        ),
    )(pack)


def small_kernel(in_ref, out_ref, zs, zr, bs, br):
    p = Place()
    greet(p)
    out_ref[p.b, p.z] = in_ref[...]

    def zcopy(k):
        view = out_ref.at[p.b, p.z]
        return rcopy(view, view, zs.at[k], zr.at[k], (p.b, (p.z + k) % 4))

    def bcopy(k):
        view = out_ref.at[p.b]
        return rcopy(view, view, bs.at[k], br.at[k], ((p.b + k) % 8, p.z))

    for k in range(1, 4):
        zcopy(k).start()
    for k in range(1, 4):
        view = out_ref.at[p.b, (p.z + 4 - k) % 4]
        rcopy(view, view, zs.at[k], zr.at[k], p.cdev).wait_recv()
    for k in range(1, 8):
        bcopy(k).start()
    for k in range(1, 8):
        view = out_ref.at[(p.b + 8 - k) % 8]
        rcopy(view, view, bs.at[k], br.at[k], p.cdev).wait_recv()
    for k in range(1, 4):
        zcopy(k).wait_send()
    for k in range(1, 8):
        bcopy(k).wait_send()


def gather_small(tile, ident):
    return pl.pallas_call(
        small_kernel,
        out_shape=jax.ShapeDtypeStruct((8, 4) + tile.shape, tile.dtype),
        in_specs=[VM],
        out_specs=VM,
        scratch_shapes=[DMA((4,)), DMA((4,)), DMA((8,)), DMA((8,))],
        compiler_params=pltpu.CompilerParams(collective_id=ident, has_side_effects=True),
    )(tile)


class Scatter(Flow):
    def __init__(self, p, ref, kind, ss, rs, bufs):
        super().__init__(p, ref, kind, ss, rs)
        self.rc, self.r4, self.r3b, self.r3a, self.r2 = bufs

    def add(self, stage, buf, f, s, zz):
        self.copy(stage, buf, buf, self.p.cdev).wait_recv()
        at = self.index(f, s, zz, self.p.c)
        self.ref[at] = (self.ref[at].astype(F32) + buf[...].astype(F32)).astype(BF)

    def t0_send(self):
        self.copy(0, self.at(ALL, ALL, ALL, 1 - self.p.c), self.rc, self.p.cdev).start()

    def t0_add(self):
        self.add(0, self.rc, ALL, ALL, ALL)

    def t1_send(self):
        self.copy(1, self.at(ALL, 1 - self.s, ALL), self.r4, self.sdev).start()

    def t1_add(self):
        self.add(1, self.r4, ALL, self.s, ALL)

    def t2a_send(self):
        self.copy(2, self.at(ALL, self.s, 1 - self.p.zh), self.r3b, self.p.zdev).start()

    def t2a_add(self):
        self.add(2, self.r3b, ALL, self.s, 1 - self.p.zh)

    def t2b_send(self):
        self.copy(3, self.at(ALL, self.s, 1 - self.p.zh), self.r3a, self.p.fdev).start()

    def t2b_add(self):
        self.add(3, self.r3a, ALL, self.s, self.p.zh)

    def t3_send(self):
        self.copy(4, self.at(1 - self.f, self.s, self.p.zh), self.r2, self.fdev).start()

    def t3_sum(self):
        self.copy(4, self.r2, self.r2, self.p.cdev).wait_recv()
        at = self.index(self.f, self.s, self.p.zh, self.p.c)
        return self.ref[at].astype(F32) + self.r2[...].astype(F32)

    def drain(self):
        self.sent(0, self.at(ALL, ALL, ALL, 1 - self.p.c))
        self.sent(1, self.at(ALL, 1 - self.s, ALL))

        @pl.when(self.p.mid == 0)
        def _():
            self.sent(2, self.at(ALL, self.s, 1 - self.p.zh))

        @pl.when(self.p.mid == 1)
        def _():
            self.sent(3, self.at(ALL, self.s, 1 - self.p.zh))

        self.sent(4, self.at(1 - self.f, self.s, self.p.zh))


def scatter_kernel(
    ga_in, gb_in, qg_in, bias, out, q_out, bias_out,
    ga, gb, qg, rc, r4, r3b, r3a, r2, st, r1, qc, q4, q3b, q3a, q2, qst, q1, brecv,
    ss, rs, s1s, s1r, qss, qrs, q1s, q1r, bs, br, ls
):
    p = Place()
    greet(p)
    for k, (src, dst) in enumerate(((ga_in, ga), (gb_in, gb), (qg_in, qg))):
        pltpu.make_async_copy(src, dst, ls.at[k]).start()
    for k, (src, dst) in enumerate(((ga_in, ga), (gb_in, gb), (qg_in, qg))):
        pltpu.make_async_copy(src, dst, ls.at[k]).wait()

    def flows(ci):
        made = []
        for kind, ref in ((0, ga), (1, gb)):
            bufs = (
                rc.at[kind, ci],
                r4.at[kind, ci],
                r3b.at[kind, ci],
                r3a.at[kind, ci],
                r2.at[kind, ci],
            )
            made.append(
                Scatter(
                    p,
                    ref.at[ci // 2, :, :, :, :, :, lanes_of(ci)],
                    kind,
                    lambda s, kind=kind: ss.at[s, kind, ci],
                    lambda s, kind=kind: rs.at[s, kind, ci],
                    bufs,
                )
            )
        return made

    def qflow():
        return Scatter(
            p, qg, 0, lambda s: qss.at[s], lambda s: qrs.at[s], (qc, q4, q3b, q3a, q2)
        )

    def k0(fs):
        for f in fs:
            f.t0_send()

    def k1(fs):
        for f in fs:
            f.t0_add()
            f.t1_send()

    def k2(fs):
        for f in fs:
            f.t1_add()

        @pl.when(p.mid == 0)
        def _():
            for f in fs:
                f.t2a_send()

    def k3(fs):
        @pl.when(p.mid == 1)
        def _():
            for f in fs:
                f.t2a_add()
                f.t2b_send()

    def k4(fs):
        @pl.when(p.mid == 1)
        def _():
            for f in fs:
                f.t2b_add()

        for f in fs:
            f.t3_send()

    first = p.zl == 0

    def halves(total):
        top, low = total[:ROWS], total[ROWS:]
        return jnp.where(first, top, low), jnp.where(first, low, top)

    def s1(ci):
        return rcopy(st.at[ci], r1.at[ci], s1s.at[ci], s1r.at[ci], p.zdev)

    def k5(ci):
        fa, fb = flows(ci)
        keep_a, give_a = halves(fa.t3_sum())
        keep_b, give_b = halves(fb.t3_sum())
        st[ci] = jnp.concatenate([give_a, give_b], 0).astype(BF)
        s1(ci).start()
        out[ci // 2, :, lanes_of(ci)] = jnp.concatenate([keep_a, keep_b], 0)

    def k6(ci):
        s1(ci).wait_recv()
        at = (ci // 2, ALL, lanes_of(ci))
        out[at] = out[at] + r1[ci].astype(F32)

    stages = (
        (0, lambda ci: k0(flows(ci))),
        (1, lambda ci: k1(flows(ci))),
        (2, lambda ci: k2(flows(ci))),
        (4, lambda ci: k3(flows(ci))),
        (6, lambda ci: k4(flows(ci))),
        (8, k5),
        (9, k6),
    )

    @pl.loop(0, NC + 9)
    def _(t):
        for off, fn in stages:

            @pl.when((t >= off) & (t < NC + off))
            def _(off=off, fn=fn):
                fn(t - off)

    q = qflow()
    for fn in (k0, k1, k2, k3, k4):
        fn([q])
    keep, give = halves(q.t3_sum())
    qst[...] = jnp.concatenate([give, jnp.zeros((8, 128), F32)], 0).astype(BF)
    q1copy = rcopy(qst, q1, q1s, q1r, p.zdev)
    q1copy.start()
    q1copy.wait()
    q_out[...] = keep + q1[:ROWS].astype(F32)
    q.drain()

    bias_out[...] = bias[...]
    for k, dev in enumerate((p.cdev, p.xdev, p.ydev, p.zdev, (p.b, (p.z + 2) % 4))):
        brecv[5 + k] = bias_out[...]
        step = rcopy(brecv.at[5 + k], brecv.at[k], bs.at[k], br.at[k], dev)
        step.start()
        step.wait()
        bias_out[...] = bias_out[...] + brecv[k]

    @pl.loop(0, NC)
    def _(ci):
        for f in flows(ci):
            f.drain()
        s1(ci).wait_send()


def scatter_grads(ga, gb, qg, bias):
    def block(*dims):
        return pltpu.VMEM(dims, BF)

    hbm = pl.BlockSpec(memory_space=pl.ANY)
    return pl.pallas_call(
        scatter_kernel,
        out_shape=(
            jax.ShapeDtypeStruct((6, 48, 768), F32),
            jax.ShapeDtypeStruct((ROWS, 128), F32),
            jax.ShapeDtypeStruct((16, 768), F32),
        ),
        in_specs=[hbm, hbm, hbm, VM],
        out_specs=(VM, VM, VM),
        scratch_shapes=[
            block(6, 2, 2, 2, 2, 48, 768),
            block(6, 2, 2, 2, 2, 48, 768),
            block(2, 2, 2, 2, 48, 128),
            block(2, NC, 2, 2, 2, 48, LW),
            block(2, NC, 2, 2, 48, LW),
            block(2, NC, 2, 48, LW),
            block(2, NC, 2, 48, LW),
            block(2, NC, 48, LW),
            block(NC, 48, LW),
            block(NC, 48, LW),
            block(2, 2, 2, 48, 128),
            block(2, 2, 48, 128),
            block(2, 48, 128),
            block(2, 48, 128),
            block(48, 128),
            block(32, 128),
            block(32, 128),
            pltpu.VMEM((10, 16, 768), F32),
            DMA((5, 2, NC)),
            DMA((5, 2, NC)),
            DMA((NC,)),
            DMA((NC,)),
            DMA((5,)),
            DMA((5,)),
            DMA,
            DMA,
            DMA((5,)),
            DMA((5,)),
            DMA((3,)),
        ],
        compiler_params=pltpu.CompilerParams(
            collective_id=2, has_side_effects=True, vmem_limit_bytes=VMEM_LIMIT
        ),
    )(ga, gb, qg, bias)


def fast_local(
    hidden_in,
    upstream_grad,
    query_vectors,
    loss_weight,
    positive_ids,
    positive_count,
    query_proj,
    key_proj,
    value_proj,
    attn_proj,
    query_bias,
    value_bias,
    attn_bias,
    first_gain,
    first_shift,
    inner_proj,
    inner_bias,
    outer_proj,
    outer_bias,
    second_gain,
    second_shift,
):
    outer_t = outer_proj.T
    pairs = [(query_proj, key_proj), (value_proj, attn_proj.T)]
    pairs += [(inner_proj[:, j * D : (j + 1) * D], outer_t[:, j * D : (j + 1) * D]) for j in range(4)]
    pack = jnp.stack([jnp.concatenate(pair, 0) for pair in pairs])
    vecs = jnp.stack(
        [query_bias, value_bias, attn_bias, first_gain, first_shift, outer_bias, second_gain, second_shift]
    ).astype(F32)
    mid = jnp.zeros((8, 96), F32).at[0].set(inner_bias.astype(F32))
    aux = jnp.concatenate(
        [positive_ids.T.astype(F32), positive_count[None].astype(F32), loss_weight[None], jnp.zeros((3, 4), F32)], 0
    )
    tile = jnp.concatenate([vecs, mid, aux, jnp.zeros((8, 4), F32)], 1)
    tile = jnp.concatenate([tile, query_vectors.astype(F32).reshape(ROWS, 128)], 0)
    small = gather_small(tile, 3).reshape(32, 32, 128)
    vec_rows = [small[:, t, :ROWS].reshape(D).astype(BF) for t in range(8)]
    inner_bias = small[:, 0, 24:120].reshape(-1).astype(BF)
    aux = small[:, :5, 120:124].transpose(1, 0, 2).reshape(5, 128)
    queries_all = small[:, 8:].reshape(128, D).astype(BF)
    wa, wb = gather_weights(pack)
    wa = wa.reshape(6, D, D)
    wb = wb.reshape(6, D, D)
    query_bias, value_bias, attn_bias, first_gain, first_shift, outer_bias, second_gain, second_shift = vec_rows
    attn_params = (wa[0], wb[0], wa[1], wb[1].T, query_bias, value_bias, attn_bias, first_gain, first_shift)
    inner_proj = jnp.concatenate([wa[2], wa[3], wa[4], wa[5]], 1)
    outer_proj = jnp.concatenate([wb[2], wb[3], wb[4], wb[5]], 1).T
    ffn_params = (inner_proj, inner_bias, outer_proj, outer_bias, second_gain, second_shift)
    pass_count = hidden_in.shape[0]
    layer_f32, kept_state = block_forward(hidden_in, attn_params, ffn_params)
    layer_output = layer_f32.astype(BF).reshape(pass_count, LEN, D)
    cls_local = layer_output[:, 0, :]
    own_scores = contract("pd,qd->pq", cls_local, queries_all)
    tile = jnp.concatenate([own_scores, jnp.zeros((4, 128), F32)], 0)
    scores = gather_small(tile, 4).reshape(32, 8, 128)[:, :4].reshape(128, 128)
    ids, count, weight = aux[:3], aux[3:4], aux[4:5]
    passage = jnp.arange(128, dtype=F32)[:, None]
    hit = (ids[0:1] == passage) | ((ids[1:2] == passage) & (count > 1)) | ((ids[2:3] == passage) & (count > 2))
    masked = jnp.where(hit, scores, NEG_FILL)
    top_all = jnp.max(scores, axis=0, keepdims=True)
    top_pos = jnp.max(masked, axis=0, keepdims=True)
    total_all = top_all + jnp.log(jnp.sum(jnp.exp(scores - top_all), axis=0, keepdims=True))
    total_pos = top_pos + jnp.log(jnp.sum(jnp.exp(masked - top_pos), axis=0, keepdims=True))
    me = lax.axis_index("blk") * 4 + lax.axis_index("grp")
    own_hit = lax.dynamic_slice(hit, (4 * me, 0), (4, 128))
    own_grad = weight * (
        jnp.exp(own_scores - total_all) - jnp.where(own_hit, jnp.exp(own_scores - total_pos), 0.0)
    )
    own_grad = own_grad.astype(BF)
    cls_grad = product(own_grad, queries_all)
    query_part = contract("pq,pd->qd", own_grad, cls_local).astype(BF).reshape(2, 2, 2, 2, 48, 128)
    query_loss = lax.dynamic_slice((total_all - total_pos)[0], (4 * me,), (4,))
    grad_total = upstream_grad.astype(F32).at[:, 0, :].add(cls_grad)
    hidden_part, attn_grads, ffn_grads = block_backward(
        hidden_in, grad_total, kept_state, attn_params, ffn_params
    )
    inner_g = ffn_grads[0]
    outer_g = ffn_grads[2].T
    ga = [attn_grads[0], attn_grads[2]] + [inner_g[:, j * D : (j + 1) * D] for j in range(4)]
    gb = [attn_grads[1], attn_grads[3].T] + [outer_g[:, j * D : (j + 1) * D] for j in range(4)]
    ga = jnp.stack(ga).astype(BF).reshape(6, 2, 2, 2, 2, 48, D)
    gb = jnp.stack(gb).astype(BF).reshape(6, 2, 2, 2, 2, 48, D)
    rows = list(attn_grads[4:]) + [ffn_grads[3], ffn_grads[4], ffn_grads[5]]
    bias = jnp.concatenate([jnp.stack(rows), ffn_grads[1].reshape(4, D), jnp.zeros((4, D), F32)], 0)
    out, query_acc, bias = scatter_grads(ga, gb, query_part, bias)
    vec = lax.dynamic_slice(bias[:8], (0, ROWS * me), (8, ROWS))
    inner_vec = lax.dynamic_slice(bias[8:12].reshape(-1), (96 * me,), (96,))
    hidden_grad = hidden_part.astype(BF).reshape(pass_count, LEN, D)
    return (
        layer_output,
        hidden_grad,
        query_acc.reshape(4, D),
        query_loss,
        out[0, :ROWS],
        out[0, ROWS:],
        out[1, :ROWS],
        out[1, ROWS:].T,
        vec[0],
        vec[1],
        vec[2],
        vec[3],
        vec[4],
        jnp.concatenate([out[j, :ROWS] for j in range(2, 6)], 1),
        inner_vec,
        jnp.concatenate([out[j, ROWS:] for j in range(2, 6)], 1).T,
        vec[5],
        vec[6],
        vec[7],
        cls_grad,
    )


def solution(mesh):
    in_specs = (
        P(("blk", "grp"), None, None),
        P(("blk", "grp"), None, None),
        P(("blk", "grp"), None),
        P(("blk", "grp")),
        P(("blk", "grp"), None),
        P(("blk", "grp")),
        P(("blk", "grp"), None),
        P(("blk", "grp"), None),
        P(("blk", "grp"), None),
        P(None, ("blk", "grp")),
        P(("blk", "grp")),
        P(("blk", "grp")),
        P(("blk", "grp")),
        P(("blk", "grp")),
        P(("blk", "grp")),
        P(("blk", "grp"), None),
        P(("blk", "grp")),
        P(None, ("blk", "grp")),
        P(("blk", "grp")),
        P(("blk", "grp")),
        P(("blk", "grp")),
    )
    out_specs = (
        P(("blk", "grp"), None, None),
        P(("blk", "grp"), None, None),
        P(("blk", "grp"), None),
        P(("blk", "grp")),
        P(("blk", "grp"), None),
        P(("blk", "grp"), None),
        P(("blk", "grp"), None),
        P(None, ("blk", "grp")),
        P(("blk", "grp")),
        P(("blk", "grp")),
        P(("blk", "grp")),
        P(("blk", "grp")),
        P(("blk", "grp")),
        P(("blk", "grp"), None),
        P(("blk", "grp")),
        P(None, ("blk", "grp")),
        P(("blk", "grp")),
        P(("blk", "grp")),
        P(("blk", "grp")),
        P(("blk", "grp"), None),
    )
    tiled = mesh.shape["blk"] == 8 and mesh.shape["grp"] == 4
    local = fast_local if tiled else plain_local
    return jax.shard_map(local, mesh=mesh, in_specs=in_specs, out_specs=out_specs, check_vma=False)
```

```python
import jax
import jax.numpy as jnp
from jax import lax
from jax.experimental import pallas as pl
from jax.experimental.pallas import tpu as pltpu
from jax.sharding import PartitionSpec as P

D = 768
HEADS = 12
HEAD_DIM = 64
LEN = 128


NORM_EPS = 1e-05
NEG_FILL = -1e30


def product(left_side, right_side):
    return jnp.dot(left_side, right_side, preferred_element_type=jnp.float32)


def contract(form_text, first_side, second_side):
    return jnp.einsum(form_text, first_side, second_side, preferred_element_type=jnp.float32)


def norm_forward(resid_sum, gain_vec, shift_vec):
    centered = resid_sum - jnp.mean(resid_sum, axis=-1, keepdims=True)
    inv_dev = lax.rsqrt(jnp.mean(centered * centered, axis=-1, keepdims=True) + NORM_EPS)
    normal_part = centered * inv_dev
    return (normal_part * gain_vec + shift_vec, normal_part, inv_dev)


def norm_backward(out_grad, normal_part, inv_dev, gain_vec):
    scaled_grad = out_grad * gain_vec
    mean_grad = jnp.mean(scaled_grad, axis=-1, keepdims=True)
    mean_cross = jnp.mean(scaled_grad * normal_part, axis=-1, keepdims=True)
    return inv_dev * (scaled_grad - mean_grad - normal_part * mean_cross)


def gelu_exact(pre_act):
    return jax.nn.gelu(pre_act, approximate=False)


def gelu_grad(pre_act, act_grad):
    unused_out, pullback = jax.vjp(gelu_exact, pre_act)
    return pullback(act_grad)[0]


def positive_block(positive_ids, positive_count, span_count):
    slot_live = (
        jnp.arange(positive_ids.shape[1], dtype=jnp.int32)[None, :] < positive_count[:, None]
    )
    passage_index = jnp.arange(span_count, dtype=jnp.int32)
    matches = (positive_ids[:, :, None] == passage_index[None, None, :]) & slot_live[:, :, None]
    return jnp.any(matches, axis=1)


def block_forward(block_in, attn_params, ffn_params):
    (
        query_proj,
        key_proj,
        value_proj,
        attn_proj,
        query_bias,
        value_bias,
        attn_bias,
        first_gain,
        first_shift,
    ) = attn_params
    inner_proj, inner_bias, outer_proj, outer_bias, second_gain, second_shift = ffn_params
    pass_count = block_in.shape[0]
    head_shape = (pass_count, LEN, HEADS, HEAD_DIM)
    tok_rows = block_in.reshape(pass_count * LEN, D)
    queries = ((product(tok_rows, query_proj) + query_bias) * 0.125).astype(jnp.bfloat16)
    keys_low = product(tok_rows, key_proj).astype(jnp.bfloat16)
    values_low = (product(tok_rows, value_proj) + value_bias).astype(jnp.bfloat16)
    scores = contract("bqhd,bkhd->bhqk", queries.reshape(head_shape), keys_low.reshape(head_shape))
    top_score = jnp.max(scores, axis=-1, keepdims=True)
    exp_terms = jnp.exp(scores - top_score)
    totals = jnp.sum(exp_terms, axis=-1, keepdims=True)
    probs_low = (exp_terms / totals).astype(jnp.bfloat16)
    log_norm = top_score + jnp.log(totals)
    context = contract("bhqk,bkhd->bqhd", probs_low, values_low.reshape(head_shape))
    context = context.reshape(pass_count * LEN, D).astype(jnp.bfloat16)
    attn_out = product(context, attn_proj) + attn_bias
    normed, first_normal, first_inv = norm_forward(
        tok_rows.astype(jnp.float32) + attn_out, first_gain, first_shift
    )
    normed_low = normed.astype(jnp.bfloat16)
    inner_pre = product(normed_low, inner_proj) + inner_bias
    activated = gelu_exact(inner_pre).astype(jnp.bfloat16)
    branch = product(activated, outer_proj) + outer_bias
    layer_f32, second_normal, second_inv = norm_forward(normed + branch, second_gain, second_shift)
    kept_state = (
        queries,
        keys_low,
        values_low,
        log_norm,
        context,
        first_normal,
        first_inv,
        normed_low,
        inner_pre,
        activated,
        second_normal,
        second_inv,
    )
    return (layer_f32, kept_state)


def block_backward(block_in, out_grad, kept_state, attn_params, ffn_params):
    (
        query_proj,
        key_proj,
        value_proj,
        attn_proj,
        query_bias,
        value_bias,
        attn_bias,
        first_gain,
        first_shift,
    ) = attn_params
    inner_proj, inner_bias, outer_proj, outer_bias, second_gain, second_shift = ffn_params
    (
        queries,
        keys_low,
        values_low,
        log_norm,
        context,
        first_normal,
        first_inv,
        normed_low,
        inner_pre,
        activated,
        second_normal,
        second_inv,
    ) = kept_state
    pass_count = block_in.shape[0]
    tok_count = pass_count * LEN
    head_shape = (pass_count, LEN, HEADS, HEAD_DIM)
    tok_rows = block_in.reshape(tok_count, D)
    grad_rows = out_grad.reshape(tok_count, D)
    grad_second_gain = jnp.sum(grad_rows * second_normal, axis=0)
    grad_second_shift = jnp.sum(grad_rows, axis=0)
    second_resid = norm_backward(grad_rows, second_normal, second_inv, second_gain)
    branch_grad = second_resid.astype(jnp.bfloat16)
    grad_outer_bias = jnp.sum(branch_grad.astype(jnp.float32), axis=0)
    grad_outer_proj = product(activated.T, branch_grad)
    inner_grad = gelu_grad(inner_pre, product(branch_grad, outer_proj.T)).astype(jnp.bfloat16)
    grad_inner_bias = jnp.sum(inner_grad.astype(jnp.float32), axis=0)
    grad_inner_proj = product(normed_low.T, inner_grad)
    normed_grad = second_resid + product(inner_grad, inner_proj.T)
    grad_first_gain = jnp.sum(normed_grad * first_normal, axis=0)
    grad_first_shift = jnp.sum(normed_grad, axis=0)
    first_resid = norm_backward(normed_grad, first_normal, first_inv, first_gain)
    attn_grad = first_resid.astype(jnp.bfloat16)
    grad_attn_bias = jnp.sum(attn_grad.astype(jnp.float32), axis=0)
    grad_attn_proj = product(context.T, attn_grad)
    context_grad = product(attn_grad, attn_proj.T).astype(jnp.bfloat16).reshape(head_shape)
    query_heads = queries.reshape(head_shape)
    key_heads = keys_low.reshape(head_shape)
    value_heads = values_low.reshape(head_shape)
    scores = contract("bqhd,bkhd->bhqk", query_heads, key_heads)
    prob_full = jnp.exp(scores - log_norm)
    values_grad = contract("bhqk,bqhd->bkhd", prob_full.astype(jnp.bfloat16), context_grad)
    values_grad = values_grad.astype(jnp.bfloat16).reshape(tok_count, D)
    prob_grad = contract("bqhd,bkhd->bhqk", context_grad, value_heads)
    score_grad = (
        prob_full * (prob_grad - jnp.sum(prob_full * prob_grad, axis=-1, keepdims=True))
    ).astype(jnp.bfloat16)
    queries_grad = (
        contract("bhqk,bkhd->bqhd", score_grad, key_heads)
        .astype(jnp.bfloat16)
        .reshape(tok_count, D)
    )
    keys_grad = (
        contract("bhqk,bqhd->bkhd", score_grad, query_heads)
        .astype(jnp.bfloat16)
        .reshape(tok_count, D)
    )
    grad_query_proj = product(tok_rows.T, queries_grad) * 0.125
    grad_query_bias = jnp.sum(queries_grad.astype(jnp.float32), axis=0) * 0.125
    grad_key_proj = product(tok_rows.T, keys_grad)
    grad_value_proj = product(tok_rows.T, values_grad)
    grad_value_bias = jnp.sum(values_grad.astype(jnp.float32), axis=0)
    hidden_grad = (
        first_resid
        + 0.125 * product(queries_grad, query_proj.T)
        + product(keys_grad, key_proj.T)
        + product(values_grad, value_proj.T)
    )
    attn_grads = (
        grad_query_proj,
        grad_key_proj,
        grad_value_proj,
        grad_attn_proj,
        grad_query_bias,
        grad_value_bias,
        grad_attn_bias,
        grad_first_gain,
        grad_first_shift,
    )
    ffn_grads = (
        grad_inner_proj,
        grad_inner_bias,
        grad_outer_proj,
        grad_outer_bias,
        grad_second_gain,
        grad_second_shift,
    )
    return (hidden_grad, attn_grads, ffn_grads)


def plain_local(
    hidden_in,
    upstream_grad,
    query_vectors,
    loss_weight,
    positive_ids,
    positive_count,
    query_proj,
    key_proj,
    value_proj,
    attn_proj,
    query_bias,
    value_bias,
    attn_bias,
    first_gain,
    first_shift,
    inner_proj,
    inner_bias,
    outer_proj,
    outer_bias,
    second_gain,
    second_shift,
):
    attn_params = (
        lax.all_gather(query_proj, ("blk", "grp"), axis=0, tiled=True),
        lax.all_gather(key_proj, ("blk", "grp"), axis=0, tiled=True),
        lax.all_gather(value_proj, ("blk", "grp"), axis=0, tiled=True),
        lax.all_gather(attn_proj, ("blk", "grp"), axis=1, tiled=True),
        lax.all_gather(query_bias, ("blk", "grp"), axis=0, tiled=True),
        lax.all_gather(value_bias, ("blk", "grp"), axis=0, tiled=True),
        lax.all_gather(attn_bias, ("blk", "grp"), axis=0, tiled=True),
        lax.all_gather(first_gain, ("blk", "grp"), axis=0, tiled=True),
        lax.all_gather(first_shift, ("blk", "grp"), axis=0, tiled=True),
    )
    ffn_params = (
        lax.all_gather(inner_proj, ("blk", "grp"), axis=0, tiled=True),
        lax.all_gather(inner_bias, ("blk", "grp"), axis=0, tiled=True),
        lax.all_gather(outer_proj, ("blk", "grp"), axis=1, tiled=True),
        lax.all_gather(outer_bias, ("blk", "grp"), axis=0, tiled=True),
        lax.all_gather(second_gain, ("blk", "grp"), axis=0, tiled=True),
        lax.all_gather(second_shift, ("blk", "grp"), axis=0, tiled=True),
    )
    pass_count = hidden_in.shape[0]
    layer_f32, kept_state = block_forward(hidden_in, attn_params, ffn_params)
    layer_output = layer_f32.astype(jnp.bfloat16).reshape(pass_count, LEN, D)
    cls_local = layer_output[:, 0, :]
    query_count = query_vectors.shape[0]
    lowest = jnp.full((query_count,), NEG_FILL, jnp.float32)
    cls_piece = lax.all_gather(cls_local, ("blk", "grp"), axis=0, tiled=True)
    top_all = lowest
    top_pos = lowest
    scores = contract("qd,pd->qp", query_vectors, cls_piece)
    hit_mask = positive_block(positive_ids, positive_count, cls_piece.shape[0])
    masked = jnp.where(hit_mask, scores, NEG_FILL)
    new_all = jnp.maximum(top_all, jnp.max(scores, axis=1))
    new_pos = jnp.maximum(top_pos, jnp.max(masked, axis=1))
    sum_all = jnp.sum(jnp.exp(scores - new_all[:, None]), axis=1)
    pos_terms = jnp.where(hit_mask, jnp.exp(masked - new_pos[:, None]), 0.0)
    sum_pos = jnp.sum(pos_terms, axis=1)
    top_all, sum_all, top_pos, sum_pos = (new_all, sum_all, new_pos, sum_pos)
    total_all = top_all + jnp.log(sum_all)
    total_pos = top_pos + jnp.log(sum_pos)
    cls_piece = lax.all_gather(cls_local, ("blk", "grp"), axis=0, tiled=True)
    scores = contract("qd,pd->qp", query_vectors, cls_piece)
    hit_mask = positive_block(positive_ids, positive_count, cls_piece.shape[0])
    masked = jnp.where(hit_mask, scores, NEG_FILL)
    weight_rows = loss_weight[:, None] * (
        jnp.exp(scores - total_all[:, None]) - jnp.exp(masked - total_pos[:, None])
    )
    weight_rows = weight_rows.astype(jnp.bfloat16)
    query_acc = product(weight_rows, cls_piece)
    query_loss = total_all - total_pos
    cls_grad = lax.psum_scatter(
        contract("qp,qd->pd", weight_rows, query_vectors),
        ("blk", "grp"),
        scatter_dimension=0,
        tiled=True,
    )
    grad_total = upstream_grad.astype(jnp.float32).at[:, 0, :].add(cls_grad)
    ffn_back = (
        lax.all_gather(inner_proj, ("blk", "grp"), axis=0, tiled=True),
        lax.all_gather(inner_bias, ("blk", "grp"), axis=0, tiled=True),
        lax.all_gather(outer_proj, ("blk", "grp"), axis=1, tiled=True),
        lax.all_gather(outer_bias, ("blk", "grp"), axis=0, tiled=True),
        lax.all_gather(second_gain, ("blk", "grp"), axis=0, tiled=True),
        lax.all_gather(second_shift, ("blk", "grp"), axis=0, tiled=True),
    )
    attn_back = (
        lax.all_gather(query_proj, ("blk", "grp"), axis=0, tiled=True),
        lax.all_gather(key_proj, ("blk", "grp"), axis=0, tiled=True),
        lax.all_gather(value_proj, ("blk", "grp"), axis=0, tiled=True),
        lax.all_gather(attn_proj, ("blk", "grp"), axis=1, tiled=True),
        lax.all_gather(query_bias, ("blk", "grp"), axis=0, tiled=True),
        lax.all_gather(value_bias, ("blk", "grp"), axis=0, tiled=True),
        lax.all_gather(attn_bias, ("blk", "grp"), axis=0, tiled=True),
        lax.all_gather(first_gain, ("blk", "grp"), axis=0, tiled=True),
        lax.all_gather(first_shift, ("blk", "grp"), axis=0, tiled=True),
    )
    hidden_part, attn_grads, ffn_grads = block_backward(
        hidden_in, grad_total, kept_state, attn_back, ffn_back
    )
    attn_shards = (
        lax.psum_scatter(attn_grads[0], ("blk", "grp"), scatter_dimension=0, tiled=True),
        lax.psum_scatter(attn_grads[1], ("blk", "grp"), scatter_dimension=0, tiled=True),
        lax.psum_scatter(attn_grads[2], ("blk", "grp"), scatter_dimension=0, tiled=True),
        lax.psum_scatter(attn_grads[3], ("blk", "grp"), scatter_dimension=1, tiled=True),
        lax.psum_scatter(attn_grads[4], ("blk", "grp"), scatter_dimension=0, tiled=True),
        lax.psum_scatter(attn_grads[5], ("blk", "grp"), scatter_dimension=0, tiled=True),
        lax.psum_scatter(attn_grads[6], ("blk", "grp"), scatter_dimension=0, tiled=True),
        lax.psum_scatter(attn_grads[7], ("blk", "grp"), scatter_dimension=0, tiled=True),
        lax.psum_scatter(attn_grads[8], ("blk", "grp"), scatter_dimension=0, tiled=True),
    )
    ffn_shards = (
        lax.psum_scatter(ffn_grads[0], ("blk", "grp"), scatter_dimension=0, tiled=True),
        lax.psum_scatter(ffn_grads[1], ("blk", "grp"), scatter_dimension=0, tiled=True),
        lax.psum_scatter(ffn_grads[2], ("blk", "grp"), scatter_dimension=1, tiled=True),
        lax.psum_scatter(ffn_grads[3], ("blk", "grp"), scatter_dimension=0, tiled=True),
        lax.psum_scatter(ffn_grads[4], ("blk", "grp"), scatter_dimension=0, tiled=True),
        lax.psum_scatter(ffn_grads[5], ("blk", "grp"), scatter_dimension=0, tiled=True),
    )
    hidden_grad = hidden_part.astype(jnp.bfloat16).reshape(pass_count, LEN, D)
    return (
        layer_output,
        hidden_grad,
        query_acc,
        query_loss,
        attn_shards[0],
        attn_shards[1],
        attn_shards[2],
        attn_shards[3],
        attn_shards[4],
        attn_shards[5],
        attn_shards[6],
        attn_shards[7],
        attn_shards[8],
        ffn_shards[0],
        ffn_shards[1],
        ffn_shards[2],
        ffn_shards[3],
        ffn_shards[4],
        ffn_shards[5],
        cls_grad,
    )


BF = jnp.bfloat16
F32 = jnp.float32
MESH = pl.DeviceIdType.MESH
VM = pl.BlockSpec(memory_space=pltpu.VMEM)
DMA = pltpu.SemaphoreType.DMA
ALL = slice(None)
VMEM_LIMIT = 60 * 2**20
NC = 12
LW = 384
ROWS = 24
TOK = 512


class Place:
    def __init__(self):
        self.b = lax.axis_index("blk")
        self.z = lax.axis_index("grp")
        self.y, self.x, self.c = self.b // 4, (self.b // 2) % 2, self.b % 2
        self.zh, self.zl = self.z // 2, self.z % 2
        self.mid = ((self.z + 1) // 2) % 2
        self.xdev = (self.b + 2 - 4 * self.x, self.z)
        self.ydev = (self.b + 4 - 8 * self.y, self.z)
        self.cdev = (self.b + 1 - 2 * self.c, self.z)
        self.zdev = (self.b, self.z + 1 - 2 * self.zl)
        self.fdev = (self.b, 3 - self.z)


def greet(p):
    bar = pltpu.get_barrier_semaphore()
    for k in range(1, 8):
        pl.semaphore_signal(bar, 1, device_id=((p.b + k) % 8, p.z), device_id_type=MESH)
    for k in range(1, 4):
        pl.semaphore_signal(bar, 1, device_id=(p.b, (p.z + k) % 4), device_id_type=MESH)
    pl.semaphore_wait(bar, 10)


def rcopy(src, dst, ss, rs, dev):
    return pltpu.make_async_remote_copy(
        src_ref=src, dst_ref=dst, send_sem=ss, recv_sem=rs, device_id=dev, device_id_type=MESH
    )


class Flow:
    def __init__(self, p, ref, kind, ss, rs):
        self.p, self.ref, self.kind, self.ss, self.rs = p, ref, kind, ss, rs
        self.f, self.s = (p.x, p.y) if kind == 0 else (p.y, p.x)
        self.fdev, self.sdev = (p.xdev, p.ydev) if kind == 0 else (p.ydev, p.xdev)

    def at(self, f, s, zz, c=None):
        c = self.p.c if c is None else c
        return self.ref.at[self.index(f, s, zz, c)]

    def index(self, f, s, zz, c):
        return (s, f, c, zz) if self.kind == 0 else (f, s, c, zz)

    def copy(self, stage, src, dst, dev):
        return rcopy(src, dst, self.ss(stage), self.rs(stage), dev)

    def go(self, stage, view, dev):
        self.copy(stage, view, view, dev).start()

    def got(self, stage, view):
        self.copy(stage, view, view, self.p.cdev).wait_recv()

    def sent(self, stage, view):
        self.copy(stage, view, view, self.p.cdev).wait_send()


class Gather(Flow):
    def s2_send(self):
        self.go(0, self.at(self.f, self.s, self.p.zh), self.fdev)

    def s2_recv(self):
        self.got(0, self.at(1 - self.f, self.s, self.p.zh))

    def s3a_send(self):
        self.go(1, self.at(ALL, self.s, self.p.zh), self.p.fdev)

    def s3a_recv(self):
        self.got(1, self.at(ALL, self.s, 1 - self.p.zh))

    def s3b_send(self):
        self.go(2, self.at(ALL, self.s, 1 - self.p.zh), self.p.zdev)

    def s3b_recv(self):
        self.got(2, self.at(ALL, self.s, 1 - self.p.zh))

    def s4_send(self):
        self.go(3, self.at(ALL, self.s, ALL), self.sdev)

    def s4_recv(self):
        self.got(3, self.at(ALL, 1 - self.s, ALL))

    def c1_send(self):
        self.go(4, self.at(ALL, self.s, ALL), self.p.cdev)

    def c1_recv(self):
        self.got(4, self.at(ALL, self.s, ALL, 1 - self.p.c))

    def c2_send(self):
        self.go(5, self.at(ALL, 1 - self.s, ALL), self.p.cdev)

    def c2_recv(self):
        self.got(5, self.at(ALL, 1 - self.s, ALL, 1 - self.p.c))

    def drain(self):
        self.sent(0, self.at(self.f, self.s, self.p.zh))

        @pl.when(self.p.mid == 1)
        def _():
            self.sent(1, self.at(ALL, self.s, self.p.zh))
            self.sent(2, self.at(ALL, self.s, 1 - self.p.zh))

        self.sent(3, self.at(ALL, self.s, ALL))
        self.sent(4, self.at(ALL, self.s, ALL))
        self.sent(5, self.at(ALL, 1 - self.s, ALL))


def lanes_of(ci):
    return pl.ds(pl.multiple_of((ci % 2) * LW, 128), LW)


class Scatter(Flow):
    def __init__(self, p, ref, kind, ss, rs, bufs):
        super().__init__(p, ref, kind, ss, rs)
        self.rc, self.r4, self.r3b, self.r3a, self.r2 = bufs

    def add(self, stage, buf, f, s, zz):
        self.copy(stage, buf, buf, self.p.cdev).wait_recv()
        at = self.index(f, s, zz, self.p.c)
        self.ref[at] = (self.ref[at].astype(F32) + buf[...].astype(F32)).astype(BF)

    def t0_send(self):
        self.copy(0, self.at(ALL, ALL, ALL, 1 - self.p.c), self.rc, self.p.cdev).start()

    def t0_add(self):
        self.add(0, self.rc, ALL, ALL, ALL)

    def t1_send(self):
        self.copy(1, self.at(ALL, 1 - self.s, ALL), self.r4, self.sdev).start()

    def t1_add(self):
        self.add(1, self.r4, ALL, self.s, ALL)

    def t2a_send(self):
        self.copy(2, self.at(ALL, self.s, 1 - self.p.zh), self.r3b, self.p.zdev).start()

    def t2a_add(self):
        self.add(2, self.r3b, ALL, self.s, 1 - self.p.zh)

    def t2b_send(self):
        self.copy(3, self.at(ALL, self.s, 1 - self.p.zh), self.r3a, self.p.fdev).start()

    def t2b_add(self):
        self.add(3, self.r3a, ALL, self.s, self.p.zh)

    def t3_send(self):
        self.copy(4, self.at(1 - self.f, self.s, self.p.zh), self.r2, self.fdev).start()

    def t3_sum(self):
        self.copy(4, self.r2, self.r2, self.p.cdev).wait_recv()
        at = self.index(self.f, self.s, self.p.zh, self.p.c)
        return self.ref[at].astype(F32) + self.r2[...].astype(F32)

    def drain(self):
        self.sent(0, self.at(ALL, ALL, ALL, 1 - self.p.c))
        self.sent(1, self.at(ALL, 1 - self.s, ALL))

        @pl.when(self.p.mid == 0)
        def _():
            self.sent(2, self.at(ALL, self.s, 1 - self.p.zh))

        @pl.when(self.p.mid == 1)
        def _():
            self.sent(3, self.at(ALL, self.s, 1 - self.p.zh))

        self.sent(4, self.at(1 - self.f, self.s, self.p.zh))


def nn(a, b): return lax.dot_general(a, b, (((1,), (0,)), ((), ())), preferred_element_type=F32)
def nt(a, b): return lax.dot_general(a, b, (((1,), (1,)), ((), ())), preferred_element_type=F32)
def tn(a, b): return lax.dot_general(a, b, (((0,), (0,)), ((), ())), preferred_element_type=F32)

def weight(ref, i): return ref[i].reshape(D, D)
def keep(ref, i, val): ref[i] = val.astype(BF).reshape(2, 2, 2, 2, 48, D)

def tiles(n, body, unroll=None):
    def f(r, c):
        body(pl.ds(pl.multiple_of(r * (TOK // n), TOK // n), TOK // n)); return c
    lax.fori_loop(0, n, f, 0, unroll=unroll)

def masks():
    lane = lax.broadcasted_iota(jnp.int32, (1, 128), 1)
    lo = (lane < 64).astype(F32).astype(BF)
    return lo, (1 - lo.astype(F32)).astype(BF)

def qkv(s, MT=2):
    def body(r):
        x = s.x[r, :]
        s.q[r, :] = ((nn(x, weight(s.wa, 1)) + s.vec[0:1, :]) * 0.125).astype(BF)
        s.k[r, :] = nn(x, weight(s.wb, 1)).astype(BF)
        s.v[r, :] = (nn(x, weight(s.wa, 0)) + s.vec[1:2, :]).astype(BF)
    tiles(MT, body)

def split(x, lo, hi): return jnp.concatenate([x * lo, x * hi], 0)

def attn_fwd(s, p):
    lo, hi = masks()
    r = pl.ds(pl.multiple_of(p * 128, 128), 128)
    for h in range(6):
        ln = pl.ds(h * 128, 128)
        sc = nt(s.q[r, ln], split(s.k[r, ln], lo, hi))
        out = []
        for w in (sc[:, :128], sc[:, 128:]):
            e = jnp.exp(w - jnp.max(w, axis=1, keepdims=True))
            out.append((e * (1.0 / jnp.sum(e, axis=1, keepdims=True))).astype(BF))
        pr = jnp.concatenate(out, 1)
        s.p[p, h] = pr
        s.ctx[r, ln] = nn(pr, split(s.v[r, ln], lo, hi)).astype(BF)

def normalize(res):
    c = res - jnp.mean(res, axis=1, keepdims=True)
    inv = lax.rsqrt(jnp.mean(c * c, axis=1, keepdims=True) + NORM_EPS)
    return c * inv, inv

def attn_out(s, n=8):
    def body(r):
        s.acc[r, :] = nt(s.ctx[r, :], weight(s.wb, 0))
    tiles(2, body)
    def body(r):
        n_, inv = normalize(s.x[r, :].astype(F32) + s.acc[r, :] + s.vec[2:3, :])
        s.fn[r, :] = n_
        s.s1[r, :] = inv
        s.nl[r, :] = (n_ * s.vec[3:4, :] + s.vec[4:5, :]).astype(BF)
        s.acc[r, :] = n_ * s.vec[3:4, :] + s.vec[4:5, :] + s.vec[5:6, :]
    tiles(n * 2, body)

def gelu_parts(x):
    ax = jnp.abs(x) * 0.7071067811865476
    t = 1.0 / (1.0 + 0.3275911 * ax)
    e = jnp.exp(x * x * -0.5)
    poly = t * (0.254829592 + t * (-0.284496736 + t * (1.421413741 + t * (-1.453152027 + t * 1.061405429))))
    half = 0.5 * poly * e
    phi = jnp.where(x > 0, 1.0 - half, half)
    return phi, e * 0.3989422804014327

def ffn_fwd(s, j, gelu=True):
    def body(r):
        s.tmp[r, :] = nn(s.nl[r, :], weight(s.wa, 2 + j))
    tiles(2, body)
    def ew(r):
        x = s.tmp[r, :] + s.vec[pl.ds(8 + j, 1), :]
        cdf, pdf = gelu_parts(x)
        s.act[j, r, :] = (x * cdf).astype(BF)
        s.gp[j, r, :] = (cdf + x * pdf).astype(BF)
    tiles(32, ew)
    def body(r):
        s.acc[r, :] += nt(s.act[j, r, :], weight(s.wb, 2 + j))
    tiles(2, body)

def norm2(s):
    def body(r):
        n_, inv = normalize(s.acc[r, :])
        s.acc[r, :] = n_
        s.s2[r, :] = inv
        s.lo[r, :] = (n_ * s.vec[6:7, :] + s.vec[7:8, :]).astype(BF)
    tiles(16, body)

def norm_back(g, n_, inv, gain):
    sg = g * gain
    return inv * (sg - jnp.mean(sg, axis=1, keepdims=True) - n_ * jnp.mean(sg * n_, axis=1, keepdims=True))

def colsum(x): return jnp.sum(x.reshape(-1, 8, x.shape[-1]), axis=0)

def norm2_back(s):
    s.gv[...] = jnp.zeros_like(s.gv)
    def body(r):
        g = s.up[r, :].astype(F32)
        n_ = s.acc[r, :]
        s.gv[6] += colsum(g * n_)
        s.gv[7] += colsum(g)
        res = norm_back(g, n_, s.s2[r, :], s.vec[6:7, :])
        s.acc[r, :] = res
        b = res.astype(BF)
        s.bg[r, :] = b
        s.gv[5] += colsum(b.astype(F32))
    tiles(16, body)

def ffn_back(s, j):
    def body(r):
        s.tmp[r, :] = nn(s.bg[r, :], weight(s.wb, 2 + j))
    tiles(2, body)
    keep(s.wb, 2 + j, tn(s.bg[...], s.act[j]))
    def ew(r):
        ig = (s.tmp[r, :] * s.gp[j, r, :].astype(F32)).astype(BF)
        s.gp[j, r, :] = ig
        s.gv[8 + j] += colsum(ig.astype(F32))
    tiles(16, ew)
    def body(r):
        s.acc[r, :] += nt(s.gp[j, r, :], weight(s.wa, 2 + j))
    tiles(2, body)
    keep(s.wa, 2 + j, tn(s.nl[...], s.gp[j]))

def norm1_back(s):
    def body(r):
        g = s.acc[r, :]
        n_ = s.fn[r, :]
        s.gv[3] += colsum(g * n_)
        s.gv[4] += colsum(g)
        res = norm_back(g, n_, s.s1[r, :], s.vec[3:4, :])
        s.acc[r, :] = res
        b = res.astype(BF)
        s.bg[r, :] = b
        s.gv[2] += colsum(b.astype(F32))
    tiles(16, body)
    def body(r):
        s.nl[r, :] = nn(s.bg[r, :], weight(s.wb, 0)).astype(BF)
    tiles(2, body)
    keep(s.wb, 0, tn(s.bg[...], s.ctx[...]))

def attn_back(s, p):
    lo, hi = masks()
    r = pl.ds(pl.multiple_of(p * 128, 128), 128)
    for h in range(6):
        ln = pl.ds(h * 128, 128)
        qp, kp, vp, cg = s.q[r, ln], s.k[r, ln], s.v[r, ln], s.nl[r, ln]
        dp = nt(cg, split(vp, lo, hi))
        pr = s.p[p, h]
        prf = pr.astype(F32)
        t = prf * dp
        ds = []
        for a, b in ((0, 128), (128, 256)):
            ds.append((t[:, a:b] - prf[:, a:b] * jnp.sum(t[:, a:b], axis=1, keepdims=True)).astype(BF))
        dq = nn(jnp.concatenate(ds, 1), split(kp, lo, hi))
        dk = tn(jnp.concatenate(ds, 0), split(qp, lo, hi))
        dv = tn(jnp.concatenate([pr[:, :128], pr[:, 128:]], 0), split(cg, lo, hi))
        s.q[r, ln] = dq.astype(BF)
        s.k[r, ln] = dk.astype(BF)
        s.v[r, ln] = dv.astype(BF)

def qkv_back(s):
    def body(r):
        h = s.acc[r, :] + 0.125 * nt(s.q[r, :], weight(s.wa, 1))
        h += nt(s.k[r, :], weight(s.wb, 1))
        h += nt(s.v[r, :], weight(s.wa, 0))
        s.hg[r, :] = h.astype(BF)
    tiles(2, body)
    def sums(r):
        s.gv[0] += colsum(s.q[r, :].astype(F32)) * 0.125
        s.gv[1] += colsum(s.v[r, :].astype(F32))
    tiles(8, sums)
    keep(s.wa, 0, tn(s.x[...], s.v[...]))
    keep(s.wa, 1, tn(s.x[...], s.q[...]) * 0.125)
    keep(s.wb, 1, tn(s.x[...], s.k[...]))


class Bag:
    pass


def column_maps(width, offset, first):
    lane = lax.broadcasted_iota(jnp.int32, (128, D), 0).astype(F32)
    col = lax.broadcasted_iota(jnp.int32, (128, D), 1).astype(F32) + first
    owner = jnp.floor((col + 0.5) * (1.0 / width))
    hot = ((lane - offset) == (col - owner * width)).astype(F32)
    return hot, owner[0:1]


def unpack_small(s):
    sm = s.small[...].reshape(32, 32, 128)[:, :8].reshape(256, 128)
    hot, owner = column_maps(24, 0, 0.0)
    dev = jnp.floor((lax.broadcasted_iota(jnp.int32, (256, 1), 0).astype(F32) + 0.5) * 0.125)
    wide = jnp.where(dev == owner, nn(sm.astype(BF), hot.astype(BF)), 0.0)
    s.vec[0:8, :] = jnp.sum(wide.reshape(32, 8, D), axis=0)
    one = s.small[pl.ds(0, 32, stride=32), :].astype(BF)
    dev32 = lax.broadcasted_iota(jnp.int32, (32, 1), 0).astype(F32)
    rows = []
    for j in range(4):
        hot, owner = column_maps(96, 24, float(D * j))
        part = jnp.where(dev32 == owner, nn(one, hot.astype(BF)), 0.0)
        rows.append(jnp.sum(part, axis=0, keepdims=True))
    s.vec[8:16, :] = jnp.concatenate(rows + [jnp.zeros((4, D), F32)], 0)
    hot, owner = column_maps(4, 120, 0.0)
    part = lax.dot_general(
        sm, hot[:, :128], (((1,), (0,)), ((), ())), precision=lax.Precision.HIGHEST, preferred_element_type=F32
    )
    part = jnp.where(dev == owner[:, :128], part, 0.0)
    s.aux[...] = jnp.sum(part.reshape(32, 8, 128), axis=0)
    for q in range(4):
        for k in range(6):
            piece = s.small[pl.ds(8 + 6 * q + k, 32, stride=32), :]
            s.qm[pl.ds(k * 128 + q, 32, stride=4), :] = piece


def all_queries(s):
    return jnp.concatenate([s.qm[k * 128 : (k + 1) * 128, :] for k in range(6)], 1).astype(BF)


def first_rows(s):
    rows = [s.acc[p * LEN : p * LEN + 8, :][0:1] for p in range(4)]
    n_, inv = normalize(jnp.concatenate(rows + [jnp.zeros((4, D), F32)], 0))
    s.cn[...] = n_
    s.ci[...] = inv
    cls = (n_ * s.vec[6:7, :] + s.vec[7:8, :]).astype(BF)
    s.cls[...] = cls.astype(F32)
    return nt(cls, all_queries(s))


def loss_part(s, me):
    scores = s.sc[...]
    row = lax.broadcasted_iota(jnp.int32, (256, 1), 0).astype(F32)
    dev = jnp.floor((row + 0.5) * 0.125)
    slot = row - 8.0 * dev
    real = slot < 4.0
    passage = 4.0 * dev + slot
    ids, count, weight_q = s.aux[0:3, :], s.aux[3:4, :], s.aux[4:5, :]

    def hits(passage):
        return (
            (ids[0:1] == passage)
            | ((ids[1:2] == passage) & (count > 1.5))
            | ((ids[2:3] == passage) & (count > 2.5))
        )

    everyone = jnp.where(real, scores, NEG_FILL)
    masked = jnp.where(hits(passage) & real, scores, NEG_FILL)
    totals = []
    for part in (everyone, masked):
        top = jnp.max(part, axis=0, keepdims=True)
        totals.append(top + jnp.log(jnp.sum(jnp.exp(part - top), axis=0, keepdims=True)))
    total_all, total_pos = totals
    s.loss[...] = jnp.broadcast_to(total_all - total_pos, (8, 128))
    own = s.sc[pl.ds(pl.multiple_of(me * 8, 8), 8), :]
    slot = lax.broadcasted_iota(jnp.int32, (8, 128), 0)
    hit = hits((4 * me + slot).astype(F32))
    pull = jnp.where(hit, jnp.exp(own - total_pos), 0.0)
    grad = weight_q * (jnp.exp(own - total_all) - pull)
    grad = jnp.where(slot < 4, grad, 0.0).astype(BF)
    s.cgrad[...] = nn(grad, all_queries(s))
    part = tn(grad, s.cls[...].astype(BF))
    for k in range(6):
        s.qpart[k * 128 : (k + 1) * 128, :] = part[:, k * 128 : (k + 1) * 128]


def query_rows(s):
    for q in range(4):
        for k in range(6):
            piece = s.qpart[pl.ds(k * 128 + q, 32, stride=4), :]
            s.qrow[pl.ds(6 * q + k, 32, stride=24), :] = piece
    s.qg[...] = s.qrow[...].astype(BF).reshape(2, 2, 2, 2, 48, 128)


def add_cls(s):
    g = jnp.concatenate([s.up[p * LEN : p * LEN + 16, :][0:1].astype(F32) for p in range(4)] + [jnp.zeros((4, D), F32)], 0)
    extra = s.cgrad[...]
    live = (lax.broadcasted_iota(jnp.int32, (8, 1), 0) < 4).astype(F32)
    n_, inv = s.cn[...] * live, s.ci[...]
    s.gv[6] += extra * n_
    s.gv[7] += extra
    res = norm_back(g + extra, n_, inv, s.vec[6:7, :]) * live
    old = norm_back(g, n_, inv, s.vec[6:7, :]) * live
    low = res.astype(BF).astype(F32)
    s.gv[5] += low - old.astype(BF).astype(F32)
    top = (lax.broadcasted_iota(jnp.int32, (16, 1), 0) == 0)
    for p in range(4):
        at = slice(p * LEN, p * LEN + 16)
        s.acc[at, :] = jnp.where(top, res[p : p + 1], s.acc[at, :])
        s.bg[at, :] = jnp.where(top, low[p : p + 1], s.bg[at, :].astype(F32)).astype(BF)


OUTS = dict(
    lo=((TOK, D), BF),
    hg=((TOK, D), BF),
    out=((6, 48, D), F32),
    q_out=((ROWS, 128), F32),
    bias_out=((16, D), F32),
    loss=((8, 128), F32),
    cgrad=((8, D), F32),
)
INS = ("x", "up", "pack", "tile")
SCRATCH = dict(
    wa=((6, 2, 2, 2, 2, 48, D), BF),
    wb=((6, 2, 2, 2, 2, 48, D), BF),
    rb=((6, 48, D), BF),
    q=((TOK, D), BF),
    k=((TOK, D), BF),
    v=((TOK, D), BF),
    ctx=((TOK, D), BF),
    p=((4, 6, 128, 256), BF),
    fn=((TOK, D), F32),
    s1=((TOK, 1), F32),
    s2=((TOK, 1), F32),
    nl=((TOK, D), BF),
    acc=((TOK, D), F32),
    act=((4, TOK, D), BF),
    gp=((4, TOK, D), BF),
    bg=((TOK, D), BF),
    tmp=((TOK, D), F32),
    small=((1024, 128), F32),
    sc=((256, 128), F32),
    vec=((16, D), F32),
    gv=((12, 8, D), F32),
    aux=((8, 128), F32),
    qm=((D, 128), F32),
    cn=((8, D), F32),
    ci=((8, 1), F32),
    cls=((8, D), F32),
    qpart=((D, 128), F32),
    qrow=((D, 128), F32),
    qg=((2, 2, 2, 2, 48, 128), BF),
    rc=((2, NC, 2, 2, 2, 48, LW), BF),
    r4=((2, NC, 2, 2, 48, LW), BF),
    r3b=((2, NC, 2, 48, LW), BF),
    r3a=((2, NC, 2, 48, LW), BF),
    r2=((2, NC, 48, LW), BF),
    st=((NC, 48, LW), BF),
    r1=((NC, 48, LW), BF),
    qc=((2, 2, 2, 48, 128), BF),
    q4=((2, 2, 48, 128), BF),
    q3b=((2, 48, 128), BF),
    q3a=((2, 48, 128), BF),
    q2=((48, 128), BF),
    qst=((32, 128), BF),
    q1=((32, 128), BF),
    bs_buf=((5, 16, D), F32),
    br_buf=((5, 16, D), F32),
)
SEMS = dict(
    gs=(6, 2, NC),
    gr=(6, 2, NC),
    g1s=(NC,),
    g1r=(NC,),
    ss=(5, 2, NC),
    rs=(5, 2, NC),
    s1s=(NC,),
    s1r=(NC,),
    qss=(6,),
    qrs=(6,),
    bss=(5,),
    brs=(5,),
    zs=(2, 4),
    zr=(2, 4),
    bs=(2, 8),
    br=(2, 8),
)


class Spread:
    def __init__(self, p, s, ref, which, rows):
        self.p, self.s, self.ref, self.which, self.rows = p, s, ref, which, rows

    def zview(self, z):
        r = self.rows
        return self.ref.at[pl.ds(pl.multiple_of((self.p.b * 4 + z) * r, r), r), :]

    def bview(self, b):
        r = self.rows * 4
        return self.ref.at[pl.ds(pl.multiple_of(b * r, r), r), :]

    def zcopy(self, k, view):
        p, s, w = self.p, self.s, self.which
        return rcopy(view, view, s.zs.at[w, k], s.zr.at[w, k], (p.b, (p.z + k) % 4))

    def bcopy(self, k, view):
        p, s, w = self.p, self.s, self.which
        return rcopy(view, view, s.bs.at[w, k], s.br.at[w, k], ((p.b + k) % 8, p.z))

    def first(self):
        for k in range(1, 4):
            self.zcopy(k, self.zview(self.p.z)).start()

    def second(self):
        for k in range(1, 4):
            self.zcopy(k, self.zview((self.p.z + 4 - k) % 4)).wait_recv()
        for k in range(1, 8):
            self.bcopy(k, self.bview(self.p.b)).start()

    def finish(self):
        for k in range(1, 8):
            self.bcopy(k, self.bview((self.p.b + 8 - k) % 8)).wait_recv()
        for k in range(1, 4):
            self.zcopy(k, self.zview(self.p.z)).wait_send()
        for k in range(1, 8):
            self.bcopy(k, self.bview(self.p.b)).wait_send()


def gather_steps(p, s):
    def flows(ci):
        out = []
        for kind, ref in ((0, s.wa), (1, s.wb)):
            view = ref.at[ci // 2, :, :, :, :, :, lanes_of(ci)]
            out.append(
                Gather(
                    p,
                    view,
                    kind,
                    lambda st, kind=kind: s.gs.at[st, kind, ci],
                    lambda st, kind=kind: s.gr.at[st, kind, ci],
                )
            )
        return out

    def s1(ci):
        at = (ci // 2, ALL, lanes_of(ci))
        return rcopy(s.pack.at[at], s.rb.at[at], s.g1s.at[ci], s.g1r.at[ci], p.zdev)

    def merge(ci):
        s1(ci).wait_recv()
        i, ln = ci // 2, lanes_of(ci)
        own = s.pack[i, :, ln].astype(F32)
        oth = s.rb[i, :, ln].astype(F32)
        first = p.zl == 0
        lo = jnp.where(first, own, oth)
        hi = jnp.where(first, oth, own)
        s.wa[i, p.y, p.x, p.c, p.zh, :, ln] = jnp.concatenate([lo[:ROWS], hi[:ROWS]], 0).astype(BF)
        s.wb[i, p.y, p.x, p.c, p.zh, :, ln] = jnp.concatenate([lo[ROWS:], hi[ROWS:]], 0).astype(BF)
        for f in flows(ci):
            f.s2_send()

    def s23(ci):
        for f in flows(ci):
            f.s2_recv()

        @pl.when(p.mid == 1)
        def _():
            for f in flows(ci):
                f.s3a_send()

    def s34(ci):
        @pl.when(p.mid == 1)
        def _():
            for f in flows(ci):
                f.s3a_recv()
            for f in flows(ci):
                f.s3b_send()

        @pl.when(p.mid == 0)
        def _():
            for f in flows(ci):
                f.s3b_recv()

        for f in flows(ci):
            f.s4_send()
        for f in flows(ci):
            f.c1_send()

    def s45(ci):
        for f in flows(ci):
            f.s4_recv()
            f.c2_send()

    def core(ci):
        for f in flows(ci):
            f.c1_recv()
            f.c2_recv()
            f.drain()
        s1(ci).wait_send()

    @pl.loop(0, NC)
    def _(ci):
        s1(ci).start()

    return ((0, merge), (2, s23), (4, s34), (5, s45), (6, core))


def scatter_steps(p, s):
    def piece(ci):
        return (ci // 2 + 2) % 6

    def flows(ci):
        made = []
        for kind, ref in ((0, s.wa), (1, s.wb)):
            bufs = tuple(buf.at[kind, ci] for buf in (s.rc, s.r4, s.r3b, s.r3a, s.r2))
            made.append(
                Scatter(
                    p,
                    ref.at[piece(ci), :, :, :, :, :, lanes_of(ci)],
                    kind,
                    lambda st, kind=kind: s.ss.at[st, kind, ci],
                    lambda st, kind=kind: s.rs.at[st, kind, ci],
                    bufs,
                )
            )
        return made

    def k0(fs):
        for f in fs:
            f.t0_send()

    def k1(fs):
        for f in fs:
            f.t0_add()
            f.t1_send()

    def k2(fs):
        for f in fs:
            f.t1_add()

        @pl.when(p.mid == 0)
        def _():
            for f in fs:
                f.t2a_send()

    def k3(fs):
        @pl.when(p.mid == 1)
        def _():
            for f in fs:
                f.t2a_add()
                f.t2b_send()

    def k4(fs):
        @pl.when(p.mid == 1)
        def _():
            for f in fs:
                f.t2b_add()

        for f in fs:
            f.t3_send()

    first = p.zl == 0

    def halves(total):
        top, low = total[:ROWS], total[ROWS:]
        return jnp.where(first, top, low), jnp.where(first, low, top)

    def s1(ci):
        return rcopy(s.st.at[ci], s.r1.at[ci], s.s1s.at[ci], s.s1r.at[ci], p.zdev)

    def k5(ci):
        fa, fb = flows(ci)
        keep_a, give_a = halves(fa.t3_sum())
        keep_b, give_b = halves(fb.t3_sum())
        s.st[ci] = jnp.concatenate([give_a, give_b], 0).astype(BF)
        s1(ci).start()
        s.out[piece(ci), :, lanes_of(ci)] = jnp.concatenate([keep_a, keep_b], 0)

    def k6(ci):
        s1(ci).wait_recv()
        at = (piece(ci), ALL, lanes_of(ci))
        s.out[at] = s.out[at] + s.r1[ci].astype(F32)
        for f in flows(ci):
            f.drain()
        s1(ci).wait_send()

    stages = (
        (0, lambda ci: k0(flows(ci))),
        (1, lambda ci: k1(flows(ci))),
        (2, lambda ci: k2(flows(ci))),
        (4, lambda ci: k3(flows(ci))),
        (6, lambda ci: k4(flows(ci))),
        (8, k5),
        (9, k6),
    )
    q = Scatter(
        p, s.qg, 0, lambda st: s.qss.at[st], lambda st: s.qrs.at[st], (s.qc, s.q4, s.q3b, s.q3a, s.q2)
    )
    q1 = rcopy(s.qst, s.q1, s.qss.at[5], s.qrs.at[5], p.zdev)

    def q5():
        keep, give = halves(q.t3_sum())
        s.qst[...] = jnp.concatenate([give, jnp.zeros((8, 128), F32)], 0).astype(BF)
        q1.start()
        s.q_out[...] = keep

    def q6():
        q1.wait()
        s.q_out[...] = s.q_out[...] + s.q1[:ROWS].astype(F32)
        q.drain()

    query_steps = [lambda fn=fn: fn([q]) for fn in (k0, k1, k2, k3, k4)] + [q5, q6]
    devs = (p.cdev, p.xdev, p.ydev, p.zdev, (p.b, (p.z + 2) % 4))

    def bcopy(k):
        return rcopy(s.bs_buf.at[k], s.br_buf.at[k], s.bss.at[k], s.brs.at[k], devs[k])

    def bias_step(k):
        if k == 0:
            total = jnp.concatenate([jnp.sum(s.gv[...], axis=1), jnp.zeros((4, D), F32)], 0)
        else:
            bcopy(k - 1).wait()
            total = s.bs_buf[k - 1] + s.br_buf[k - 1]
        if k < 5:
            s.bs_buf[k] = total
            bcopy(k).start()
        else:
            s.bias_out[...] = total

    return stages, query_steps, [lambda k=k: bias_step(k) for k in range(6)]


def run_stages(stages, t):
    for off, fn in stages:

        @pl.when((t >= off) & (t < NC + off))
        def _(off=off, fn=fn):
            fn(t - off)


def run_at(t, table):
    for when, fn in table:

        @pl.when(t == when)
        def _(fn=fn):
            fn()


def layer_kernel(*refs):
    s = Bag()
    names = list(INS) + list(OUTS) + list(SCRATCH) + list(SEMS)
    for name, ref in zip(names, refs):
        setattr(s, name, ref)
    p = Place()
    greet(p)
    me = p.b * 4 + p.z
    vectors = Spread(p, s, s.small, 0, 32)
    scores = Spread(p, s, s.sc, 1, 8)
    s.small[pl.ds(pl.multiple_of(me * 32, 32), 32), :] = s.tile[...]
    vectors.first()
    stages = gather_steps(p, s)

    def passages(fn, lo):
        def go():
            pl.loop(lo, lo + 2)(lambda i: fn(s, i))

        return go

    def small_done():
        vectors.finish()
        unpack_small(s)

    forward = (
        (3, vectors.second),
        (7, small_done),
        (9, lambda: qkv(s)),
        (10, passages(attn_fwd, 0)),
        (11, passages(attn_fwd, 2)),
        (12, lambda: attn_out(s)),
    )

    @pl.loop(0, NC + 6)
    def _(t):
        run_stages(stages, t)
        run_at(t, forward)

        @pl.when((t >= 13) & (t <= 15))
        def _():
            ffn_fwd(s, t - 13)

        @pl.when(t == 17)
        def _():
            ffn_fwd(s, 3)

    s.sc[pl.ds(pl.multiple_of(me * 8, 8), 8), :] = first_rows(s)
    scores.first()
    s.gv[...] = jnp.zeros_like(s.gv)
    norm2(s)
    scores.second()
    norm2_back(s)
    scores.finish()
    loss_part(s, me)
    add_cls(s)

    stages, query_steps, bias_steps = scatter_steps(p, s)
    ffn_back(s, 0)
    backward = [
        (3, lambda: norm1_back(s)),
        (4, passages(attn_back, 0)),
        (5, passages(attn_back, 2)),
        (6, lambda: qkv_back(s)),
        (7, lambda: query_rows(s)),
    ]
    backward += [(8 + k, fn) for k, fn in enumerate(query_steps)]
    backward += [(9 + 2 * k, fn) for k, fn in enumerate(bias_steps)]

    @pl.loop(0, NC + 9)
    def _(t):
        run_stages(stages, t)

        @pl.when(t < 3)
        def _():
            ffn_back(s, t + 1)

        run_at(t, backward)


def layer(x, up, pack, tile):
    return pl.pallas_call(
        layer_kernel,
        out_shape=tuple(jax.ShapeDtypeStruct(*o) for o in OUTS.values()),
        in_specs=[VM] * 4,
        out_specs=(VM,) * len(OUTS),
        scratch_shapes=[pltpu.VMEM(*b) for b in SCRATCH.values()] + [DMA(n) for n in SEMS.values()],
        compiler_params=pltpu.CompilerParams(
            collective_id=1, has_side_effects=True, vmem_limit_bytes=VMEM_LIMIT
        ),
    )(x, up, pack, tile)


def fast_local(
    hidden_in,
    upstream_grad,
    query_vectors,
    loss_weight,
    positive_ids,
    positive_count,
    query_proj,
    key_proj,
    value_proj,
    attn_proj,
    query_bias,
    value_bias,
    attn_bias,
    first_gain,
    first_shift,
    inner_proj,
    inner_bias,
    outer_proj,
    outer_bias,
    second_gain,
    second_shift,
):
    outer_t = outer_proj.T
    pairs = [(value_proj, attn_proj.T), (query_proj, key_proj)]
    pairs += [(inner_proj[:, j * D : (j + 1) * D], outer_t[:, j * D : (j + 1) * D]) for j in range(4)]
    pack = jnp.stack([jnp.concatenate(pair, 0) for pair in pairs])
    vecs = jnp.stack(
        [query_bias, value_bias, attn_bias, first_gain, first_shift, outer_bias, second_gain, second_shift]
    ).astype(F32)
    mid = jnp.zeros((8, 96), F32).at[0].set(inner_bias.astype(F32))
    aux = jnp.concatenate(
        [positive_ids.T.astype(F32), positive_count[None].astype(F32), loss_weight[None], jnp.zeros((3, 4), F32)], 0
    )
    tile = jnp.concatenate([vecs, mid, aux, jnp.zeros((8, 4), F32)], 1)
    tile = jnp.concatenate([tile, query_vectors.astype(F32).reshape(ROWS, 128)], 0)
    layer_output, hidden_grad, out, query_acc, bias, loss, cls_grad = layer(
        hidden_in.reshape(TOK, D), upstream_grad.reshape(TOK, D), pack, tile
    )
    me = lax.axis_index("blk") * 4 + lax.axis_index("grp")
    vec = lax.dynamic_slice(bias[:8], (0, ROWS * me), (8, ROWS))
    inner_vec = lax.dynamic_slice(bias[8:12].reshape(-1), (96 * me,), (96,))
    return (
        layer_output.reshape(hidden_in.shape),
        hidden_grad.reshape(hidden_in.shape),
        query_acc.reshape(4, D),
        lax.dynamic_slice(loss[0], (4 * me,), (4,)),
        out[1, :ROWS],
        out[1, ROWS:],
        out[0, :ROWS],
        out[0, ROWS:].T,
        vec[0],
        vec[1],
        vec[2],
        vec[3],
        vec[4],
        jnp.concatenate([out[j, :ROWS] for j in range(2, 6)], 1),
        inner_vec,
        jnp.concatenate([out[j, ROWS:] for j in range(2, 6)], 1).T,
        vec[5],
        vec[6],
        vec[7],
        cls_grad[:4],
    )


def solution(mesh):
    in_specs = (
        P(("blk", "grp"), None, None),
        P(("blk", "grp"), None, None),
        P(("blk", "grp"), None),
        P(("blk", "grp")),
        P(("blk", "grp"), None),
        P(("blk", "grp")),
        P(("blk", "grp"), None),
        P(("blk", "grp"), None),
        P(("blk", "grp"), None),
        P(None, ("blk", "grp")),
        P(("blk", "grp")),
        P(("blk", "grp")),
        P(("blk", "grp")),
        P(("blk", "grp")),
        P(("blk", "grp")),
        P(("blk", "grp"), None),
        P(("blk", "grp")),
        P(None, ("blk", "grp")),
        P(("blk", "grp")),
        P(("blk", "grp")),
        P(("blk", "grp")),
    )
    out_specs = (
        P(("blk", "grp"), None, None),
        P(("blk", "grp"), None, None),
        P(("blk", "grp"), None),
        P(("blk", "grp")),
        P(("blk", "grp"), None),
        P(("blk", "grp"), None),
        P(("blk", "grp"), None),
        P(None, ("blk", "grp")),
        P(("blk", "grp")),
        P(("blk", "grp")),
        P(("blk", "grp")),
        P(("blk", "grp")),
        P(("blk", "grp")),
        P(("blk", "grp"), None),
        P(("blk", "grp")),
        P(None, ("blk", "grp")),
        P(("blk", "grp")),
        P(("blk", "grp")),
        P(("blk", "grp")),
        P(("blk", "grp"), None),
    )
    tiled = mesh.shape["blk"] == 8 and mesh.shape["grp"] == 4
    local = fast_local if tiled else plain_local
    return jax.shard_map(local, mesh=mesh, in_specs=in_specs, out_specs=out_specs, check_vma=False)
```

```python
import jax
import jax.numpy as jnp
from jax import lax
from jax.experimental import pallas as pl
from jax.experimental.pallas import tpu as pltpu
from jax.sharding import PartitionSpec as P

D = 768
HEADS = 12
HEAD_DIM = 64
LEN = 128


NORM_EPS = 1e-05
NEG_FILL = -1e30


def product(left_side, right_side):
    return jnp.dot(left_side, right_side, preferred_element_type=jnp.float32)


def contract(form_text, first_side, second_side):
    return jnp.einsum(form_text, first_side, second_side, preferred_element_type=jnp.float32)


def norm_forward(resid_sum, gain_vec, shift_vec):
    centered = resid_sum - jnp.mean(resid_sum, axis=-1, keepdims=True)
    inv_dev = lax.rsqrt(jnp.mean(centered * centered, axis=-1, keepdims=True) + NORM_EPS)
    normal_part = centered * inv_dev
    return (normal_part * gain_vec + shift_vec, normal_part, inv_dev)


def norm_backward(out_grad, normal_part, inv_dev, gain_vec):
    scaled_grad = out_grad * gain_vec
    mean_grad = jnp.mean(scaled_grad, axis=-1, keepdims=True)
    mean_cross = jnp.mean(scaled_grad * normal_part, axis=-1, keepdims=True)
    return inv_dev * (scaled_grad - mean_grad - normal_part * mean_cross)


def gelu_exact(pre_act):
    return jax.nn.gelu(pre_act, approximate=False)


def gelu_grad(pre_act, act_grad):
    unused_out, pullback = jax.vjp(gelu_exact, pre_act)
    return pullback(act_grad)[0]


def positive_block(positive_ids, positive_count, span_count):
    slot_live = (
        jnp.arange(positive_ids.shape[1], dtype=jnp.int32)[None, :] < positive_count[:, None]
    )
    passage_index = jnp.arange(span_count, dtype=jnp.int32)
    matches = (positive_ids[:, :, None] == passage_index[None, None, :]) & slot_live[:, :, None]
    return jnp.any(matches, axis=1)


def block_forward(block_in, attn_params, ffn_params):
    (
        query_proj,
        key_proj,
        value_proj,
        attn_proj,
        query_bias,
        value_bias,
        attn_bias,
        first_gain,
        first_shift,
    ) = attn_params
    inner_proj, inner_bias, outer_proj, outer_bias, second_gain, second_shift = ffn_params
    pass_count = block_in.shape[0]
    head_shape = (pass_count, LEN, HEADS, HEAD_DIM)
    tok_rows = block_in.reshape(pass_count * LEN, D)
    queries = ((product(tok_rows, query_proj) + query_bias) * 0.125).astype(jnp.bfloat16)
    keys_low = product(tok_rows, key_proj).astype(jnp.bfloat16)
    values_low = (product(tok_rows, value_proj) + value_bias).astype(jnp.bfloat16)
    scores = contract("bqhd,bkhd->bhqk", queries.reshape(head_shape), keys_low.reshape(head_shape))
    top_score = jnp.max(scores, axis=-1, keepdims=True)
    exp_terms = jnp.exp(scores - top_score)
    totals = jnp.sum(exp_terms, axis=-1, keepdims=True)
    probs_low = (exp_terms / totals).astype(jnp.bfloat16)
    log_norm = top_score + jnp.log(totals)
    context = contract("bhqk,bkhd->bqhd", probs_low, values_low.reshape(head_shape))
    context = context.reshape(pass_count * LEN, D).astype(jnp.bfloat16)
    attn_out = product(context, attn_proj) + attn_bias
    normed, first_normal, first_inv = norm_forward(
        tok_rows.astype(jnp.float32) + attn_out, first_gain, first_shift
    )
    normed_low = normed.astype(jnp.bfloat16)
    inner_pre = product(normed_low, inner_proj) + inner_bias
    activated = gelu_exact(inner_pre).astype(jnp.bfloat16)
    branch = product(activated, outer_proj) + outer_bias
    layer_f32, second_normal, second_inv = norm_forward(normed + branch, second_gain, second_shift)
    kept_state = (
        queries,
        keys_low,
        values_low,
        log_norm,
        context,
        first_normal,
        first_inv,
        normed_low,
        inner_pre,
        activated,
        second_normal,
        second_inv,
    )
    return (layer_f32, kept_state)


def block_backward(block_in, out_grad, kept_state, attn_params, ffn_params):
    (
        query_proj,
        key_proj,
        value_proj,
        attn_proj,
        query_bias,
        value_bias,
        attn_bias,
        first_gain,
        first_shift,
    ) = attn_params
    inner_proj, inner_bias, outer_proj, outer_bias, second_gain, second_shift = ffn_params
    (
        queries,
        keys_low,
        values_low,
        log_norm,
        context,
        first_normal,
        first_inv,
        normed_low,
        inner_pre,
        activated,
        second_normal,
        second_inv,
    ) = kept_state
    pass_count = block_in.shape[0]
    tok_count = pass_count * LEN
    head_shape = (pass_count, LEN, HEADS, HEAD_DIM)
    tok_rows = block_in.reshape(tok_count, D)
    grad_rows = out_grad.reshape(tok_count, D)
    grad_second_gain = jnp.sum(grad_rows * second_normal, axis=0)
    grad_second_shift = jnp.sum(grad_rows, axis=0)
    second_resid = norm_backward(grad_rows, second_normal, second_inv, second_gain)
    branch_grad = second_resid.astype(jnp.bfloat16)
    grad_outer_bias = jnp.sum(branch_grad.astype(jnp.float32), axis=0)
    grad_outer_proj = product(activated.T, branch_grad)
    inner_grad = gelu_grad(inner_pre, product(branch_grad, outer_proj.T)).astype(jnp.bfloat16)
    grad_inner_bias = jnp.sum(inner_grad.astype(jnp.float32), axis=0)
    grad_inner_proj = product(normed_low.T, inner_grad)
    normed_grad = second_resid + product(inner_grad, inner_proj.T)
    grad_first_gain = jnp.sum(normed_grad * first_normal, axis=0)
    grad_first_shift = jnp.sum(normed_grad, axis=0)
    first_resid = norm_backward(normed_grad, first_normal, first_inv, first_gain)
    attn_grad = first_resid.astype(jnp.bfloat16)
    grad_attn_bias = jnp.sum(attn_grad.astype(jnp.float32), axis=0)
    grad_attn_proj = product(context.T, attn_grad)
    context_grad = product(attn_grad, attn_proj.T).astype(jnp.bfloat16).reshape(head_shape)
    query_heads = queries.reshape(head_shape)
    key_heads = keys_low.reshape(head_shape)
    value_heads = values_low.reshape(head_shape)
    scores = contract("bqhd,bkhd->bhqk", query_heads, key_heads)
    prob_full = jnp.exp(scores - log_norm)
    values_grad = contract("bhqk,bqhd->bkhd", prob_full.astype(jnp.bfloat16), context_grad)
    values_grad = values_grad.astype(jnp.bfloat16).reshape(tok_count, D)
    prob_grad = contract("bqhd,bkhd->bhqk", context_grad, value_heads)
    score_grad = (
        prob_full * (prob_grad - jnp.sum(prob_full * prob_grad, axis=-1, keepdims=True))
    ).astype(jnp.bfloat16)
    queries_grad = (
        contract("bhqk,bkhd->bqhd", score_grad, key_heads)
        .astype(jnp.bfloat16)
        .reshape(tok_count, D)
    )
    keys_grad = (
        contract("bhqk,bqhd->bkhd", score_grad, query_heads)
        .astype(jnp.bfloat16)
        .reshape(tok_count, D)
    )
    grad_query_proj = product(tok_rows.T, queries_grad) * 0.125
    grad_query_bias = jnp.sum(queries_grad.astype(jnp.float32), axis=0) * 0.125
    grad_key_proj = product(tok_rows.T, keys_grad)
    grad_value_proj = product(tok_rows.T, values_grad)
    grad_value_bias = jnp.sum(values_grad.astype(jnp.float32), axis=0)
    hidden_grad = (
        first_resid
        + 0.125 * product(queries_grad, query_proj.T)
        + product(keys_grad, key_proj.T)
        + product(values_grad, value_proj.T)
    )
    attn_grads = (
        grad_query_proj,
        grad_key_proj,
        grad_value_proj,
        grad_attn_proj,
        grad_query_bias,
        grad_value_bias,
        grad_attn_bias,
        grad_first_gain,
        grad_first_shift,
    )
    ffn_grads = (
        grad_inner_proj,
        grad_inner_bias,
        grad_outer_proj,
        grad_outer_bias,
        grad_second_gain,
        grad_second_shift,
    )
    return (hidden_grad, attn_grads, ffn_grads)


def plain_local(
    hidden_in,
    upstream_grad,
    query_vectors,
    loss_weight,
    positive_ids,
    positive_count,
    query_proj,
    key_proj,
    value_proj,
    attn_proj,
    query_bias,
    value_bias,
    attn_bias,
    first_gain,
    first_shift,
    inner_proj,
    inner_bias,
    outer_proj,
    outer_bias,
    second_gain,
    second_shift,
):
    attn_params = (
        lax.all_gather(query_proj, ("blk", "grp"), axis=0, tiled=True),
        lax.all_gather(key_proj, ("blk", "grp"), axis=0, tiled=True),
        lax.all_gather(value_proj, ("blk", "grp"), axis=0, tiled=True),
        lax.all_gather(attn_proj, ("blk", "grp"), axis=1, tiled=True),
        lax.all_gather(query_bias, ("blk", "grp"), axis=0, tiled=True),
        lax.all_gather(value_bias, ("blk", "grp"), axis=0, tiled=True),
        lax.all_gather(attn_bias, ("blk", "grp"), axis=0, tiled=True),
        lax.all_gather(first_gain, ("blk", "grp"), axis=0, tiled=True),
        lax.all_gather(first_shift, ("blk", "grp"), axis=0, tiled=True),
    )
    ffn_params = (
        lax.all_gather(inner_proj, ("blk", "grp"), axis=0, tiled=True),
        lax.all_gather(inner_bias, ("blk", "grp"), axis=0, tiled=True),
        lax.all_gather(outer_proj, ("blk", "grp"), axis=1, tiled=True),
        lax.all_gather(outer_bias, ("blk", "grp"), axis=0, tiled=True),
        lax.all_gather(second_gain, ("blk", "grp"), axis=0, tiled=True),
        lax.all_gather(second_shift, ("blk", "grp"), axis=0, tiled=True),
    )
    pass_count = hidden_in.shape[0]
    layer_f32, kept_state = block_forward(hidden_in, attn_params, ffn_params)
    layer_output = layer_f32.astype(jnp.bfloat16).reshape(pass_count, LEN, D)
    cls_local = layer_output[:, 0, :]
    query_count = query_vectors.shape[0]
    lowest = jnp.full((query_count,), NEG_FILL, jnp.float32)
    cls_piece = lax.all_gather(cls_local, ("blk", "grp"), axis=0, tiled=True)
    top_all = lowest
    top_pos = lowest
    scores = contract("qd,pd->qp", query_vectors, cls_piece)
    hit_mask = positive_block(positive_ids, positive_count, cls_piece.shape[0])
    masked = jnp.where(hit_mask, scores, NEG_FILL)
    new_all = jnp.maximum(top_all, jnp.max(scores, axis=1))
    new_pos = jnp.maximum(top_pos, jnp.max(masked, axis=1))
    sum_all = jnp.sum(jnp.exp(scores - new_all[:, None]), axis=1)
    pos_terms = jnp.where(hit_mask, jnp.exp(masked - new_pos[:, None]), 0.0)
    sum_pos = jnp.sum(pos_terms, axis=1)
    top_all, sum_all, top_pos, sum_pos = (new_all, sum_all, new_pos, sum_pos)
    total_all = top_all + jnp.log(sum_all)
    total_pos = top_pos + jnp.log(sum_pos)
    cls_piece = lax.all_gather(cls_local, ("blk", "grp"), axis=0, tiled=True)
    scores = contract("qd,pd->qp", query_vectors, cls_piece)
    hit_mask = positive_block(positive_ids, positive_count, cls_piece.shape[0])
    masked = jnp.where(hit_mask, scores, NEG_FILL)
    weight_rows = loss_weight[:, None] * (
        jnp.exp(scores - total_all[:, None]) - jnp.exp(masked - total_pos[:, None])
    )
    weight_rows = weight_rows.astype(jnp.bfloat16)
    query_acc = product(weight_rows, cls_piece)
    query_loss = total_all - total_pos
    cls_grad = lax.psum_scatter(
        contract("qp,qd->pd", weight_rows, query_vectors),
        ("blk", "grp"),
        scatter_dimension=0,
        tiled=True,
    )
    grad_total = upstream_grad.astype(jnp.float32).at[:, 0, :].add(cls_grad)
    ffn_back = (
        lax.all_gather(inner_proj, ("blk", "grp"), axis=0, tiled=True),
        lax.all_gather(inner_bias, ("blk", "grp"), axis=0, tiled=True),
        lax.all_gather(outer_proj, ("blk", "grp"), axis=1, tiled=True),
        lax.all_gather(outer_bias, ("blk", "grp"), axis=0, tiled=True),
        lax.all_gather(second_gain, ("blk", "grp"), axis=0, tiled=True),
        lax.all_gather(second_shift, ("blk", "grp"), axis=0, tiled=True),
    )
    attn_back = (
        lax.all_gather(query_proj, ("blk", "grp"), axis=0, tiled=True),
        lax.all_gather(key_proj, ("blk", "grp"), axis=0, tiled=True),
        lax.all_gather(value_proj, ("blk", "grp"), axis=0, tiled=True),
        lax.all_gather(attn_proj, ("blk", "grp"), axis=1, tiled=True),
        lax.all_gather(query_bias, ("blk", "grp"), axis=0, tiled=True),
        lax.all_gather(value_bias, ("blk", "grp"), axis=0, tiled=True),
        lax.all_gather(attn_bias, ("blk", "grp"), axis=0, tiled=True),
        lax.all_gather(first_gain, ("blk", "grp"), axis=0, tiled=True),
        lax.all_gather(first_shift, ("blk", "grp"), axis=0, tiled=True),
    )
    hidden_part, attn_grads, ffn_grads = block_backward(
        hidden_in, grad_total, kept_state, attn_back, ffn_back
    )
    attn_shards = (
        lax.psum_scatter(attn_grads[0], ("blk", "grp"), scatter_dimension=0, tiled=True),
        lax.psum_scatter(attn_grads[1], ("blk", "grp"), scatter_dimension=0, tiled=True),
        lax.psum_scatter(attn_grads[2], ("blk", "grp"), scatter_dimension=0, tiled=True),
        lax.psum_scatter(attn_grads[3], ("blk", "grp"), scatter_dimension=1, tiled=True),
        lax.psum_scatter(attn_grads[4], ("blk", "grp"), scatter_dimension=0, tiled=True),
        lax.psum_scatter(attn_grads[5], ("blk", "grp"), scatter_dimension=0, tiled=True),
        lax.psum_scatter(attn_grads[6], ("blk", "grp"), scatter_dimension=0, tiled=True),
        lax.psum_scatter(attn_grads[7], ("blk", "grp"), scatter_dimension=0, tiled=True),
        lax.psum_scatter(attn_grads[8], ("blk", "grp"), scatter_dimension=0, tiled=True),
    )
    ffn_shards = (
        lax.psum_scatter(ffn_grads[0], ("blk", "grp"), scatter_dimension=0, tiled=True),
        lax.psum_scatter(ffn_grads[1], ("blk", "grp"), scatter_dimension=0, tiled=True),
        lax.psum_scatter(ffn_grads[2], ("blk", "grp"), scatter_dimension=1, tiled=True),
        lax.psum_scatter(ffn_grads[3], ("blk", "grp"), scatter_dimension=0, tiled=True),
        lax.psum_scatter(ffn_grads[4], ("blk", "grp"), scatter_dimension=0, tiled=True),
        lax.psum_scatter(ffn_grads[5], ("blk", "grp"), scatter_dimension=0, tiled=True),
    )
    hidden_grad = hidden_part.astype(jnp.bfloat16).reshape(pass_count, LEN, D)
    return (
        layer_output,
        hidden_grad,
        query_acc,
        query_loss,
        attn_shards[0],
        attn_shards[1],
        attn_shards[2],
        attn_shards[3],
        attn_shards[4],
        attn_shards[5],
        attn_shards[6],
        attn_shards[7],
        attn_shards[8],
        ffn_shards[0],
        ffn_shards[1],
        ffn_shards[2],
        ffn_shards[3],
        ffn_shards[4],
        ffn_shards[5],
        cls_grad,
    )


BF = jnp.bfloat16
F32 = jnp.float32
MESH = pl.DeviceIdType.MESH
VM = pl.BlockSpec(memory_space=pltpu.VMEM)
DMA = pltpu.SemaphoreType.DMA
ALL = slice(None)
VMEM_LIMIT = 60 * 2**20
LW = 384
PARTS = 2
NC = 6 * PARTS
ROWS = 24
TOK = 512


class Place:
    def __init__(self):
        self.b = lax.axis_index("blk")
        self.z = lax.axis_index("grp")
        self.y, self.x, self.c = self.b // 4, (self.b // 2) % 2, self.b % 2
        self.zh, self.zl = self.z // 2, self.z % 2
        self.mid = ((self.z + 1) // 2) % 2
        self.xdev = (self.b + 2 - 4 * self.x, self.z)
        self.ydev = (self.b + 4 - 8 * self.y, self.z)
        self.cdev = (self.b + 1 - 2 * self.c, self.z)
        self.zdev = (self.b, self.z + 1 - 2 * self.zl)
        self.fdev = (self.b, 3 - self.z)


def greet(p):
    bar = pltpu.get_barrier_semaphore()
    for k in range(1, 8):
        pl.semaphore_signal(bar, 1, device_id=((p.b + k) % 8, p.z), device_id_type=MESH)
    for k in range(1, 4):
        pl.semaphore_signal(bar, 1, device_id=(p.b, (p.z + k) % 4), device_id_type=MESH)
    pl.semaphore_wait(bar, 10)


def rcopy(src, dst, ss, rs, dev):
    return pltpu.make_async_remote_copy(
        src_ref=src, dst_ref=dst, send_sem=ss, recv_sem=rs, device_id=dev, device_id_type=MESH
    )


class Flow:
    def __init__(self, p, ref, kind, ss, rs, lead=()):
        self.p, self.ref, self.kind, self.ss, self.rs, self.lead = p, ref, kind, ss, rs, lead
        self.f, self.s = (p.x, p.y) if kind == 0 else (p.y, p.x)
        self.fdev, self.sdev = (p.xdev, p.ydev) if kind == 0 else (p.ydev, p.xdev)

    def at(self, f, s, zz, c=None):
        c = self.p.c if c is None else c
        return self.ref.at[self.lead + self.index(f, s, zz, c)]

    def index(self, f, s, zz, c):
        return (s, f, c, zz) if self.kind == 0 else (f, s, c, zz)

    def copy(self, stage, src, dst, dev):
        return rcopy(src, dst, self.ss(stage), self.rs(stage), dev)

    def go(self, stage, view, dev):
        self.copy(stage, view, view, dev).start()

    def got(self, stage, view):
        self.copy(stage, view, view, self.p.cdev).wait_recv()

    def sent(self, stage, view):
        self.copy(stage, view, view, self.p.cdev).wait_send()


class Gather(Flow):
    def s2_send(self):
        self.go(0, self.at(self.f, self.s, self.p.zh), self.fdev)

    def s2_recv(self):
        self.got(0, self.at(1 - self.f, self.s, self.p.zh))

    def s3a_send(self):
        self.go(1, self.at(ALL, self.s, self.p.zh), self.p.fdev)

    def s3a_recv(self):
        self.got(1, self.at(ALL, self.s, 1 - self.p.zh))

    def s3b_send(self):
        self.go(2, self.at(ALL, self.s, 1 - self.p.zh), self.p.zdev)

    def s3b_recv(self):
        self.got(2, self.at(ALL, self.s, 1 - self.p.zh))

    def s4a_send(self):
        self.go(3, self.at(ALL, self.s, self.p.zh), self.sdev)

    def s4b_send(self):
        self.go(6, self.at(ALL, self.s, 1 - self.p.zh), self.sdev)

    def s4_recv(self):
        self.got(3, self.at(ALL, 1 - self.s, self.p.zh))
        self.got(6, self.at(ALL, 1 - self.s, 1 - self.p.zh))

    def c1_send(self):
        self.go(4, self.at(ALL, self.s, ALL), self.p.cdev)

    def c1_recv(self):
        self.got(4, self.at(ALL, self.s, ALL, 1 - self.p.c))

    def c2_send(self):
        self.go(5, self.at(ALL, 1 - self.s, ALL), self.p.cdev)

    def c2_recv(self):
        self.got(5, self.at(ALL, 1 - self.s, ALL, 1 - self.p.c))

    def drain(self):
        self.sent(0, self.at(self.f, self.s, self.p.zh))

        @pl.when(self.p.mid == 1)
        def _():
            self.sent(1, self.at(ALL, self.s, self.p.zh))
            self.sent(2, self.at(ALL, self.s, 1 - self.p.zh))

        self.sent(3, self.at(ALL, self.s, self.p.zh))
        self.sent(6, self.at(ALL, self.s, 1 - self.p.zh))
        self.sent(4, self.at(ALL, self.s, ALL))
        self.sent(5, self.at(ALL, 1 - self.s, ALL))


def lanes_of(ci):
    return pl.ds(pl.multiple_of((ci % PARTS) * LW, 128), LW)


class Scatter(Flow):
    def __init__(self, p, ref, kind, ss, rs, bufs, lead=()):
        super().__init__(p, ref, kind, ss, rs, lead)
        self.rc, self.r4a, self.r4b, self.r3b, self.r3a, self.r2 = bufs

    def add(self, stage, buf, f, s, zz):
        self.copy(stage, buf, buf, self.p.cdev).wait_recv()
        at = self.index(f, s, zz, self.p.c)
        self.ref[at] = (self.ref[at].astype(F32) + buf[...].astype(F32)).astype(BF)

    def t0_send(self):
        self.copy(0, self.at(ALL, ALL, ALL, 1 - self.p.c), self.rc, self.p.cdev).start()

    def t0_add(self):
        self.add(0, self.rc, ALL, ALL, ALL)

    def t1a_send(self):
        self.copy(1, self.at(ALL, 1 - self.s, 1 - self.p.zh), self.r4a, self.sdev).start()

    def t1a_add(self):
        self.add(1, self.r4a, ALL, self.s, 1 - self.p.zh)

    def t1b_send(self):
        self.copy(5, self.at(ALL, 1 - self.s, self.p.zh), self.r4b, self.sdev).start()

    def t1b_add(self):
        self.add(5, self.r4b, ALL, self.s, self.p.zh)

    def t2a_send(self):
        self.copy(2, self.at(ALL, self.s, 1 - self.p.zh), self.r3b, self.p.zdev).start()

    def t2a_add(self):
        self.add(2, self.r3b, ALL, self.s, 1 - self.p.zh)

    def t2b_send(self):
        self.copy(3, self.at(ALL, self.s, 1 - self.p.zh), self.r3a, self.p.fdev).start()

    def t2b_add(self):
        self.add(3, self.r3a, ALL, self.s, self.p.zh)

    def t3_send(self):
        self.copy(4, self.at(1 - self.f, self.s, self.p.zh), self.r2, self.fdev).start()

    def t3_sum(self):
        self.copy(4, self.r2, self.r2, self.p.cdev).wait_recv()
        at = self.index(self.f, self.s, self.p.zh, self.p.c)
        return self.ref[at].astype(F32) + self.r2[...].astype(F32)

    def drain(self):
        self.sent(0, self.at(ALL, ALL, ALL, 1 - self.p.c))
        self.sent(1, self.at(ALL, 1 - self.s, 1 - self.p.zh))
        self.sent(5, self.at(ALL, 1 - self.s, self.p.zh))

        @pl.when(self.p.mid == 0)
        def _():
            self.sent(2, self.at(ALL, self.s, 1 - self.p.zh))

        @pl.when(self.p.mid == 1)
        def _():
            self.sent(3, self.at(ALL, self.s, 1 - self.p.zh))

        self.sent(4, self.at(1 - self.f, self.s, self.p.zh))


def nn(a, b): return lax.dot_general(a, b, (((1,), (0,)), ((), ())), preferred_element_type=F32)
def nt(a, b): return lax.dot_general(a, b, (((1,), (1,)), ((), ())), preferred_element_type=F32)
def tn(a, b): return lax.dot_general(a, b, (((0,), (0,)), ((), ())), preferred_element_type=F32)

def weight(ref, i): return ref[i].reshape(D, D)
def keep(ref, i, val): ref[i] = val.astype(BF).reshape(2, 2, 2, 2, 48, D)

def tiles(n, body, unroll=None):
    def f(r, c):
        body(pl.ds(pl.multiple_of(r * (TOK // n), TOK // n), TOK // n)); return c
    lax.fori_loop(0, n, f, 0, unroll=unroll)

def masks():
    lane = lax.broadcasted_iota(jnp.int32, (1, 128), 1)
    lo = (lane < 64).astype(F32).astype(BF)
    return lo, (1 - lo.astype(F32)).astype(BF)

def qkv(s):
    x = s.x[...]
    s.q[...] = ((nn(x, weight(s.wa, 0)) + s.vec[0:1, :]) * 0.125).astype(BF)
    s.k[...] = nn(x, weight(s.wb, 0)).astype(BF)
    s.v[...] = (nn(x, weight(s.wa, 1)) + s.vec[1:2, :]).astype(BF)

def split(x, lo, hi): return jnp.concatenate([x * lo, x * hi], 0)

def attn_fwd(s, p):
    lo, hi = masks()
    r = pl.ds(pl.multiple_of(p * 128, 128), 128)
    for h in range(6):
        ln = pl.ds(h * 128, 128)
        sc = nt(s.q[r, ln], split(s.k[r, ln], lo, hi))
        out = []
        for w in (sc[:, :128], sc[:, 128:]):
            e = jnp.exp(w - jnp.max(w, axis=1, keepdims=True))
            out.append((e * (1.0 / jnp.sum(e, axis=1, keepdims=True))).astype(BF))
        pr = jnp.concatenate(out, 1)
        s.p[p, h] = pr
        s.ctx[r, ln] = nn(pr, split(s.v[r, ln], lo, hi)).astype(BF)

def normalize(res):
    c = res - jnp.mean(res, axis=1, keepdims=True)
    inv = lax.rsqrt(jnp.mean(c * c, axis=1, keepdims=True) + NORM_EPS)
    return c * inv, inv

def attn_out(s, n=8):
    s.acc[...] = nt(s.ctx[...], weight(s.wb, 1))
    def body(r):
        n_, inv = normalize(s.x[r, :].astype(F32) + s.acc[r, :] + s.vec[2:3, :])
        s.fn[r, :] = n_
        s.s1[r, :] = inv
        s.nl[r, :] = (n_ * s.vec[3:4, :] + s.vec[4:5, :]).astype(BF)
        s.acc[r, :] = n_ * s.vec[3:4, :] + s.vec[4:5, :] + s.vec[5:6, :]
    tiles(2, body)

def gelu_parts(x):
    ax = jnp.abs(x) * 0.7071067811865476
    t = 1.0 / (1.0 + 0.3275911 * ax)
    e = jnp.exp(x * x * -0.5)
    poly = t * (0.254829592 + t * (-0.284496736 + t * (1.421413741 + t * (-1.453152027 + t * 1.061405429))))
    half = 0.5 * poly * e
    phi = jnp.where(x > 0, 1.0 - half, half)
    return phi, e * 0.3989422804014327

def ffn_fwd(s, h):
    j, ln = h // PARTS, lanes_of(h)
    w_in = s.wa[2 + j, :, :, :, :, :, ln].reshape(D, LW)
    w_out = s.wb[2 + j, :, :, :, :, :, ln].reshape(D, LW)
    for r in (slice(0, 256), slice(256, 512)):
        x = nn(s.nl[r, :], w_in) + s.vec[pl.ds(8 + j, 1), ln]
        cdf, pdf = gelu_parts(x)
        act = (x * cdf).astype(BF)
        s.act[j, r, ln] = act
        s.gp[j, r, ln] = (cdf + x * pdf).astype(BF)
        s.acc[r, :] += nt(act, w_out)

def norm2(s):
    def body(r):
        n_, inv = normalize(s.acc[r, :])
        s.acc[r, :] = n_
        s.s2[r, :] = inv
        s.lo[r, :] = (n_ * s.vec[6:7, :] + s.vec[7:8, :]).astype(BF)
    tiles(2, body)

def norm_back(g, n_, inv, gain):
    sg = g * gain
    return inv * (sg - jnp.mean(sg, axis=1, keepdims=True) - n_ * jnp.mean(sg * n_, axis=1, keepdims=True))

def colsum(x): return jnp.sum(x.reshape(-1, 8, x.shape[-1]), axis=0)

def norm2_back(s):
    def body(r):
        g = s.up[r, :].astype(F32)
        n_ = s.acc[r, :]
        s.gv[6] += colsum(g * n_)
        s.gv[7] += colsum(g)
        res = norm_back(g, n_, s.s2[r, :], s.vec[6:7, :])
        s.acc[r, :] = res
        b = res.astype(BF)
        s.bg[r, :] = b
        s.gv[5] += colsum(b.astype(F32))
    tiles(2, body)

def ffn_back(s, j):
    s.tmp[...] = nn(s.bg[...], weight(s.wb, 2 + j))
    keep(s.wb, 2 + j, tn(s.bg[...], s.act[j]))
    def ew(r):
        ig = (s.tmp[r, :] * s.gp[j, r, :].astype(F32)).astype(BF)
        s.gp[j, r, :] = ig
        s.gv[8 + j] += colsum(ig.astype(F32))
    tiles(2, ew)
    s.acc[...] += nt(s.gp[j], weight(s.wa, 2 + j))
    keep(s.wa, 2 + j, tn(s.nl[...], s.gp[j]))

def norm1_back(s):
    def body(r):
        g = s.acc[r, :]
        n_ = s.fn[r, :]
        s.gv[3] += colsum(g * n_)
        s.gv[4] += colsum(g)
        res = norm_back(g, n_, s.s1[r, :], s.vec[3:4, :])
        s.acc[r, :] = res
        b = res.astype(BF)
        s.bg[r, :] = b
        s.gv[2] += colsum(b.astype(F32))
    tiles(2, body)
    s.nl[...] = nn(s.bg[...], weight(s.wb, 1)).astype(BF)
    keep(s.wb, 1, tn(s.bg[...], s.ctx[...]))

def attn_back(s, p):
    lo, hi = masks()
    r = pl.ds(pl.multiple_of(p * 128, 128), 128)
    for h in range(6):
        ln = pl.ds(h * 128, 128)
        qp, kp, vp, cg = s.q[r, ln], s.k[r, ln], s.v[r, ln], s.nl[r, ln]
        dp = nt(cg, split(vp, lo, hi))
        pr = s.p[p, h]
        prf = pr.astype(F32)
        t = prf * dp
        ds = []
        for a, b in ((0, 128), (128, 256)):
            ds.append((t[:, a:b] - prf[:, a:b] * jnp.sum(t[:, a:b], axis=1, keepdims=True)).astype(BF))
        dq = nn(jnp.concatenate(ds, 1), split(kp, lo, hi))
        dk = tn(jnp.concatenate(ds, 0), split(qp, lo, hi))
        dv = tn(jnp.concatenate([pr[:, :128], pr[:, 128:]], 0), split(cg, lo, hi))
        s.q[r, ln] = dq.astype(BF)
        s.k[r, ln] = dk.astype(BF)
        s.v[r, ln] = dv.astype(BF)

def qkv_back(s):
    s.acc[...] += 0.125 * nt(s.q[...], weight(s.wa, 0))
    s.acc[...] += nt(s.k[...], weight(s.wb, 0))
    s.hg[...] = (s.acc[...] + nt(s.v[...], weight(s.wa, 1))).astype(BF)
    def sums(r):
        s.gv[0] += colsum(s.q[r, :].astype(F32)) * 0.125
        s.gv[1] += colsum(s.v[r, :].astype(F32))
    tiles(2, sums)
    keep(s.wa, 1, tn(s.x[...], s.v[...]))
    keep(s.wa, 0, tn(s.x[...], s.q[...]) * 0.125)
    keep(s.wb, 0, tn(s.x[...], s.k[...]))


class Bag:
    pass


def column_maps(width, offset, first):
    lane = lax.broadcasted_iota(jnp.int32, (128, D), 0).astype(F32)
    col = lax.broadcasted_iota(jnp.int32, (128, D), 1).astype(F32) + first
    owner = jnp.floor((col + 0.5) * (1.0 / width))
    hot = ((lane - offset) == (col - owner * width)).astype(F32)
    return hot, owner[0:1]


def unpack_small(s):
    sm = s.small[...]
    hot, owner = column_maps(24, 0, 0.0)
    dev = jnp.floor((lax.broadcasted_iota(jnp.int32, (256, 1), 0).astype(F32) + 0.5) * 0.125)
    wide = jnp.where(dev == owner, nn(sm.astype(BF), hot.astype(BF)), 0.0)
    s.vec[0:8, :] = jnp.sum(wide.reshape(32, 8, D), axis=0)
    one = s.small[pl.ds(0, 32, stride=8), :].astype(BF)
    dev32 = lax.broadcasted_iota(jnp.int32, (32, 1), 0).astype(F32)
    rows = []
    for j in range(4):
        hot, owner = column_maps(96, 24, float(D * j))
        part = jnp.where(dev32 == owner, nn(one, hot.astype(BF)), 0.0)
        rows.append(jnp.sum(part, axis=0, keepdims=True))
    s.vec[8:16, :] = jnp.concatenate(rows + [jnp.zeros((4, D), F32)], 0)
    hot, owner = column_maps(4, 120, 0.0)
    part = lax.dot_general(
        sm, hot[:, :128], (((1,), (0,)), ((), ())), precision=lax.Precision.HIGHEST, preferred_element_type=F32
    )
    part = jnp.where(dev == owner[:, :128], part, 0.0)
    s.aux[...] = jnp.sum(part.reshape(32, 8, 128), axis=0)


def unpack_queries(s):
    s.qrow[...] = s.qx[...].reshape(D, 128).astype(F32)
    for q in range(4):
        for k in range(6):
            piece = s.qrow[pl.ds(6 * q + k, 32, stride=24), :]
            s.qm[pl.ds(k * 128 + q, 32, stride=4), :] = piece


def all_queries(s):
    return jnp.concatenate([s.qm[k * 128 : (k + 1) * 128, :] for k in range(6)], 1).astype(BF)


def first_rows(s):
    rows = [s.acc[p * LEN : p * LEN + 8, :][0:1] for p in range(4)]
    n_, inv = normalize(jnp.concatenate(rows + [jnp.zeros((4, D), F32)], 0))
    s.cn[...] = n_
    s.ci[...] = inv
    cls = (n_ * s.vec[6:7, :] + s.vec[7:8, :]).astype(BF)
    s.cls[...] = cls.astype(F32)
    return nt(cls, all_queries(s))


def loss_part(s, me):
    scores = s.sc[...]
    row = lax.broadcasted_iota(jnp.int32, (256, 1), 0).astype(F32)
    dev = jnp.floor((row + 0.5) * 0.125)
    slot = row - 8.0 * dev
    real = slot < 4.0
    passage = 4.0 * dev + slot
    ids, count, weight_q = s.aux[0:3, :], s.aux[3:4, :], s.aux[4:5, :]

    def hits(passage):
        return (
            (ids[0:1] == passage)
            | ((ids[1:2] == passage) & (count > 1.5))
            | ((ids[2:3] == passage) & (count > 2.5))
        )

    everyone = jnp.where(real, scores, NEG_FILL)
    masked = jnp.where(hits(passage) & real, scores, NEG_FILL)
    totals = []
    for part in (everyone, masked):
        top = jnp.max(part, axis=0, keepdims=True)
        totals.append(top + jnp.log(jnp.sum(jnp.exp(part - top), axis=0, keepdims=True)))
    total_all, total_pos = totals
    s.loss[...] = jnp.broadcast_to(total_all - total_pos, (8, 128))
    own = s.sc[pl.ds(pl.multiple_of(me * 8, 8), 8), :]
    slot = lax.broadcasted_iota(jnp.int32, (8, 128), 0)
    hit = hits((4 * me + slot).astype(F32))
    pull = jnp.where(hit, jnp.exp(own - total_pos), 0.0)
    grad = weight_q * (jnp.exp(own - total_all) - pull)
    grad = jnp.where(slot < 4, grad, 0.0).astype(BF)
    s.cgrad[...] = nn(grad, all_queries(s))
    part = tn(grad, s.cls[...].astype(BF))
    for k in range(6):
        s.qpart[k * 128 : (k + 1) * 128, :] = part[:, k * 128 : (k + 1) * 128]


def query_rows(s):
    for q in range(4):
        for k in range(6):
            piece = s.qpart[pl.ds(k * 128 + q, 32, stride=4), :]
            s.qrow[pl.ds(6 * q + k, 32, stride=24), :] = piece
    s.qg[...] = s.qrow[...].astype(BF).reshape(2, 2, 2, 2, 48, 128)


def add_cls(s):
    g = jnp.concatenate([s.up[p * LEN : p * LEN + 16, :][0:1].astype(F32) for p in range(4)] + [jnp.zeros((4, D), F32)], 0)
    extra = s.cgrad[...]
    live = (lax.broadcasted_iota(jnp.int32, (8, 1), 0) < 4).astype(F32)
    n_, inv = s.cn[...] * live, s.ci[...]
    s.gv[6] += extra * n_
    s.gv[7] += extra
    res = norm_back(g + extra, n_, inv, s.vec[6:7, :]) * live
    old = norm_back(g, n_, inv, s.vec[6:7, :]) * live
    low = res.astype(BF).astype(F32)
    s.gv[5] += low - old.astype(BF).astype(F32)
    top = (lax.broadcasted_iota(jnp.int32, (16, 1), 0) == 0)
    for p in range(4):
        at = slice(p * LEN, p * LEN + 16)
        s.acc[at, :] = jnp.where(top, res[p : p + 1], s.acc[at, :])
        s.bg[at, :] = jnp.where(top, low[p : p + 1], s.bg[at, :].astype(F32)).astype(BF)


HBM = pl.BlockSpec(memory_space=pl.ANY)
MERGES, G_S23, G_S4A, G_S34, G_S45, G_END = 2, 1, 2, 3, 5, 6
S_K1, S_K1B, S_K2, S_K3, S_K4, S_K5, S_K6 = 1, 3, 2, 3, 10, 11, 12
S_FAST = 2
S_END = S_K6 + NC // S_FAST
OUTS = dict(
    lo_out=((TOK, D), BF),
    hg_out=((TOK, D), BF),
    out=((6, 48, D), F32),
    q_out=((ROWS, 128), F32),
    bias_out=((16, D), F32),
    loss=((8, 128), F32),
    cgrad=((8, D), F32),
)
INS = ("x_in", "up_in", "pack", "tile", "qpack")
SCRATCH = dict(
    wa=((6, 2, 2, 2, 2, 48, D), BF),
    wb=((6, 2, 2, 2, 2, 48, D), BF),
    rb=((6, 48, D), BF),
    x=((TOK, D), BF),
    up=((TOK, D), BF),
    lo=((TOK, D), BF),
    hg=((TOK, D), BF),
    q=((TOK, D), BF),
    k=((TOK, D), BF),
    v=((TOK, D), BF),
    ctx=((TOK, D), BF),
    p=((4, 6, 128, 256), BF),
    fn=((TOK, D), F32),
    s1=((TOK, 1), F32),
    s2=((TOK, 1), F32),
    nl=((TOK, D), BF),
    acc=((TOK, D), F32),
    act=((4, TOK, D), BF),
    gp=((4, TOK, D), BF),
    bg=((TOK, D), BF),
    tmp=((TOK, D), F32),
    small=((256, 128), F32),
    qx=((2, 2, 2, 2, 48, 128), BF),
    qrb=((32, 128), BF),
    sc=((256, 128), F32),
    vec=((16, D), F32),
    gv=((12, 8, D), F32),
    aux=((8, 128), F32),
    qm=((D, 128), F32),
    cn=((8, D), F32),
    ci=((8, 1), F32),
    cls=((8, D), F32),
    qpart=((D, 128), F32),
    qrow=((D, 128), F32),
    qg=((2, 2, 2, 2, 48, 128), BF),
    rc=((2, NC, 2, 2, 2, 48, LW), BF),
    r4a=((2, NC, 2, 48, LW), BF),
    r4b=((2, NC, 2, 48, LW), BF),
    r3b=((2, NC, 2, 48, LW), BF),
    r3a=((2, NC, 2, 48, LW), BF),
    r2=((2, NC, 48, LW), BF),
    st=((NC, 48, LW), BF),
    r1=((NC, 48, LW), BF),
    qc=((2, 2, 2, 48, 128), BF),
    q4a=((2, 48, 128), BF),
    q4b=((2, 48, 128), BF),
    q3b=((2, 48, 128), BF),
    q3a=((2, 48, 128), BF),
    q2=((48, 128), BF),
    qst=((32, 128), BF),
    q1=((32, 128), BF),
    bs_buf=((5, 16, D), F32),
    br_buf=((5, 16, D), F32),
)
SEMS = dict(
    gs=(7, 2),
    gr=(7, 2, NC),
    g1s=(1,),
    g1r=(NC,),
    xs=(8,),
    xr=(8,),
    bss=(5,),
    brs=(5,),
    zs=(2, 4),
    zr=(2, 4),
    bs=(2, 8),
    br=(2, 8),
    io=(4,),
)


class Spread:
    def __init__(self, p, s, ref, which, rows):
        self.p, self.s, self.ref, self.which, self.rows = p, s, ref, which, rows

    def zview(self, z):
        r = self.rows
        return self.ref.at[pl.ds(pl.multiple_of((self.p.b * 4 + z) * r, r), r), :]

    def bview(self, b):
        r = self.rows * 4
        return self.ref.at[pl.ds(pl.multiple_of(b * r, r), r), :]

    def zcopy(self, k, view):
        p, s, w = self.p, self.s, self.which
        return rcopy(view, view, s.zs.at[w, k], s.zr.at[w, k], (p.b, (p.z + k) % 4))

    def bcopy(self, k, view):
        p, s, w = self.p, self.s, self.which
        return rcopy(view, view, s.bs.at[w, k], s.br.at[w, k], ((p.b + k) % 8, p.z))

    def first(self):
        for k in range(1, 4):
            self.zcopy(k, self.zview(self.p.z)).start()

    def second(self):
        for k in range(1, 4):
            self.zcopy(k, self.zview((self.p.z + 4 - k) % 4)).wait_recv()
        for k in range(1, 8):
            self.bcopy(k, self.bview(self.p.b)).start()

    def finish(self):
        for k in range(1, 8):
            self.bcopy(k, self.bview((self.p.b + 8 - k) % 8)).wait_recv()
        for k in range(1, 4):
            self.zcopy(k, self.zview(self.p.z)).wait_send()
        for k in range(1, 8):
            self.bcopy(k, self.bview(self.p.b)).wait_send()


def gather_steps(p, s):
    def flows(ci):
        out = []
        for kind, ref in ((0, s.wa), (1, s.wb)):
            view = ref.at[ci // PARTS, :, :, :, :, :, lanes_of(ci)]
            out.append(
                Gather(
                    p,
                    view,
                    kind,
                    lambda st, kind=kind: s.gs.at[st, kind],
                    lambda st, kind=kind: s.gr.at[st, kind, ci],
                )
            )
        return out

    def s1(ci):
        at = (ci // PARTS, ALL, lanes_of(ci))
        return rcopy(s.pack.at[at], s.rb.at[at], s.g1s.at[0], s.g1r.at[ci], p.zdev)

    first = p.zl == 0

    def order(own, oth):
        return jnp.where(first, own, oth), jnp.where(first, oth, own)

    def merge(ci):
        s1(ci).wait_recv()
        i, ln = ci // PARTS, lanes_of(ci)
        lo, hi = order(s.pack[i, :, ln].astype(F32), s.rb[i, :, ln].astype(F32))
        s.wa[i, p.y, p.x, p.c, p.zh, :, ln] = jnp.concatenate([lo[:ROWS], hi[:ROWS]], 0).astype(BF)
        s.wb[i, p.y, p.x, p.c, p.zh, :, ln] = jnp.concatenate([lo[ROWS:], hi[ROWS:]], 0).astype(BF)
        for f in flows(ci):
            f.s2_send()

    def s23(fs):
        for f in fs:
            f.s2_recv()

        @pl.when(p.mid == 1)
        def _():
            for f in fs:
                f.s3a_send()

    def s4a(fs):
        for f in fs:
            f.s4a_send()

    def s34(fs):
        @pl.when(p.mid == 1)
        def _():
            for f in fs:
                f.s3a_recv()
                f.s3b_send()

        @pl.when(p.mid == 0)
        def _():
            for f in fs:
                f.s3b_recv()

        for f in fs:
            f.s4b_send()
            f.c1_send()

    def s45(fs):
        for f in fs:
            f.s4_recv()
            f.c2_send()

    def core(fs):
        for f in fs:
            f.c1_recv()
            f.c2_recv()

    def drain():
        for kind, ref in ((0, s.wa), (1, s.wb)):
            sems = lambda st, kind=kind: s.gs.at[st, kind]
            Gather(p, ref, kind, sems, sems, (ALL,)).drain()
        rcopy(s.pack, s.rb, s.g1s.at[0], s.g1r.at[0], p.zdev).wait_send()
        q.drain()

    @pl.loop(0, NC)
    def _(ci):
        s1(ci).start()

    q = Gather(p, s.qx, 0, lambda st: s.xs.at[st], lambda st: s.xr.at[st])
    q1 = rcopy(s.qpack, s.qrb, s.xs.at[7], s.xr.at[7], p.zdev)
    q1.start()

    def qmerge():
        q1.wait()
        lo, hi = order(s.qpack[...].astype(F32), s.qrb[...].astype(F32))
        s.qx[p.y, p.x, p.c, p.zh] = jnp.concatenate([lo[:ROWS], hi[:ROWS]], 0).astype(BF)
        q.s2_send()

    def q23():
        s23([q])
        s4a([q])

    query_steps = [qmerge, q23, lambda: s34([q]), lambda: s45([q]), lambda: core([q])]

    def pack_of(fn):
        return lambda ci: fn(flows(ci))

    stages = (
        (0, MERGES, merge),
        (G_S23, 1, pack_of(s23)),
        (G_S4A, 1, pack_of(s4a)),
        (G_S34, 1, pack_of(s34)),
        (G_S45, 1, pack_of(s45)),
        (G_END, 1, pack_of(core)),
    )
    return stages, query_steps, drain


def scatter_steps(p, s):
    def piece(ci):
        return (ci // PARTS + 2) % 6

    def flows(ci):
        made = []
        for kind, ref in ((0, s.wa), (1, s.wb)):
            bufs = tuple(buf.at[kind, ci] for buf in (s.rc, s.r4a, s.r4b, s.r3b, s.r3a, s.r2))
            made.append(
                Scatter(
                    p,
                    ref.at[piece(ci), :, :, :, :, :, lanes_of(ci)],
                    kind,
                    lambda st, kind=kind: s.gs.at[st, kind],
                    lambda st, kind=kind: s.gr.at[st, kind, ci],
                    bufs,
                )
            )
        return made

    def k0(fs):
        for f in fs:
            f.t0_send()

    def k1(fs):
        for f in fs:
            f.t0_add()
            f.t1a_send()

    def k1b(fs):
        for f in fs:
            f.t1b_send()

    def k2(fs):
        for f in fs:
            f.t1a_add()

            @pl.when(p.mid == 0)
            def _(f=f):
                f.t2a_send()

    def k3(fs):
        @pl.when(p.mid == 1)
        def _():
            for f in fs:
                f.t2a_add()
                f.t2b_send()

    def k4(fs):
        for f in fs:
            f.t1b_add()

            @pl.when(p.mid == 1)
            def _(f=f):
                f.t2b_add()

            f.t3_send()

    first = p.zl == 0

    def halves(total):
        top, low = total[:ROWS], total[ROWS:]
        return jnp.where(first, top, low), jnp.where(first, low, top)

    def s1(ci):
        return rcopy(s.st.at[ci], s.r1.at[ci], s.g1s.at[0], s.g1r.at[ci], p.zdev)

    def k5(ci):
        fa, fb = flows(ci)
        keep_a, give_a = halves(fa.t3_sum())
        keep_b, give_b = halves(fb.t3_sum())
        s.st[ci] = jnp.concatenate([give_a, give_b], 0).astype(BF)
        s1(ci).start()
        s.out[piece(ci), :, lanes_of(ci)] = jnp.concatenate([keep_a, keep_b], 0)

    def k6(ci):
        s1(ci).wait_recv()
        at = (piece(ci), ALL, lanes_of(ci))
        s.out[at] = s.out[at] + s.r1[ci].astype(F32)

    def pack_of(fn):
        return lambda ci: fn(flows(ci))

    stages = (
        (0, 1, pack_of(k0)),
        (S_K1, 1, pack_of(k1)),
        (S_K1B, 1, pack_of(k1b)),
        (S_K2, 1, pack_of(k2)),
        (S_K3, 1, pack_of(k3)),
        (S_K4, S_FAST, pack_of(k4)),
        (S_K5, S_FAST, k5),
        (S_K6, S_FAST, k6),
    )
    q = Scatter(
        p, s.qg, 0, lambda st: s.xs.at[st], lambda st: s.xr.at[st], (s.qc, s.q4a, s.q4b, s.q3b, s.q3a, s.q2)
    )
    q1 = rcopy(s.qst, s.q1, s.xs.at[6], s.xr.at[6], p.zdev)

    def q5():
        keep, give = halves(q.t3_sum())
        s.qst[...] = jnp.concatenate([give, jnp.zeros((8, 128), F32)], 0).astype(BF)
        q1.start()
        s.q_out[...] = keep

    def q6():
        q1.wait()
        s.q_out[...] = s.q_out[...] + s.q1[:ROWS].astype(F32)
        q.drain()

    query_steps = [lambda fn=fn: fn([q]) for fn in (k0, k1, k1b, k2, k3, k4)] + [q5, q6]
    devs = (p.cdev, p.xdev, p.ydev, p.zdev, (p.b, (p.z + 2) % 4))

    def bcopy(k):
        return rcopy(s.bs_buf.at[k], s.br_buf.at[k], s.bss.at[k], s.brs.at[k], devs[k])

    def bias_step(k):
        if k == 0:
            total = jnp.concatenate([jnp.sum(s.gv[...], axis=1), jnp.zeros((4, D), F32)], 0)
        else:
            bcopy(k - 1).wait()
            total = s.bs_buf[k - 1] + s.br_buf[k - 1]
        if k < 5:
            s.bs_buf[k] = total
            bcopy(k).start()
        else:
            s.bias_out[...] = total

    def drain():
        for kind, ref in ((0, s.wa), (1, s.wb)):
            sems = lambda st, kind=kind: s.gs.at[st, kind]
            Scatter(p, ref, kind, sems, sems, (None,) * 6, (ALL,)).drain()
        rcopy(s.st, s.r1, s.g1s.at[0], s.g1r.at[0], p.zdev).wait_send()

    return stages, query_steps, [lambda k=k: bias_step(k) for k in range(6)], drain


def run_stages(stages, t):
    for off, many, fn in stages:
        for k in range(many):
            ci = (t - off) * many + k

            @pl.when((ci >= 0) & (ci < NC))
            def _(ci=ci, fn=fn):
                fn(ci)


def run_at(t, table):
    for when, fn in table:

        @pl.when(t == when)
        def _(fn=fn):
            fn()


def layer_kernel(*refs):
    s = Bag()
    names = list(INS) + list(OUTS) + list(SCRATCH) + list(SEMS)
    for name, ref in zip(names, refs):
        setattr(s, name, ref)
    p = Place()
    greet(p)
    me = p.b * 4 + p.z
    vectors = Spread(p, s, s.small, 0, 8)
    scores = Spread(p, s, s.sc, 1, 8)
    s.small[pl.ds(pl.multiple_of(me * 8, 8), 8), :] = s.tile[...]
    vectors.first()
    copies = {
        name: pltpu.make_async_copy(src, dst, s.io.at[k])
        for k, (name, src, dst) in enumerate(
            (
                ("x", s.x_in, s.x),
                ("up", s.up_in, s.up),
                ("lo", s.lo, s.lo_out),
                ("hg", s.hg, s.hg_out),
            )
        )
    }
    copies["x"].start()
    copies["up"].start()
    stages, query_steps, drain = gather_steps(p, s)

    def passages(fn, lo, many):
        def go():
            pl.loop(lo, lo + many)(lambda i: fn(s, i))

        return go

    def small_done():
        vectors.finish()
        unpack_small(s)

    ready = 2 * PARTS - 1 + G_END
    forward = [
        (1, copies["x"].wait),
        (1, copies["up"].wait),
        (2, vectors.second),
        (6, small_done),
        (ready, lambda: qkv(s)),
        (ready + 1, passages(attn_fwd, 0, 2)),
        (ready + 2, passages(attn_fwd, 2, 2)),
        (ready + 3, lambda: attn_out(s)),
    ]
    forward += [(6 + 2 * k, fn) for k, fn in enumerate(query_steps)]
    forward += [(15, lambda: unpack_queries(s))]

    def ffn_until(t):
        return jnp.minimum(jnp.maximum(2 * (t - ready - 3), 0), jnp.maximum(t - ready, 0))

    @pl.loop(0, NC + G_END)
    def _(t):
        run_stages(stages, t)
        run_at(t, forward)
        pl.loop(ffn_until(t - 1), ffn_until(t))(lambda h: ffn_fwd(s, h))

    drain()
    s.sc[pl.ds(pl.multiple_of(me * 8, 8), 8), :] = first_rows(s)
    scores.first()
    s.gv[...] = jnp.zeros_like(s.gv)
    norm2(s)
    copies["lo"].start()
    scores.second()
    norm2_back(s)
    scores.finish()
    loss_part(s, me)
    add_cls(s)

    stages, query_steps, bias_steps, drain = scatter_steps(p, s)
    ffn_back(s, 0)
    def hidden():
        qkv_back(s)
        copies["hg"].start()

    backward = [
        (3, lambda: norm1_back(s)),
        (4, passages(attn_back, 0, 1)),
        (5, passages(attn_back, 1, 1)),
        (6, passages(attn_back, 2, 2)),
        (7, hidden),
        (8, lambda: query_rows(s)),
    ]
    backward += [(9 + k, fn) for k, fn in enumerate(query_steps)]
    backward += [(8 + 2 * k, fn) for k, fn in enumerate(bias_steps)]

    @pl.loop(0, S_END + 1)
    def _(t):
        run_stages(stages, t)

        @pl.when(t < 3)
        def _():
            ffn_back(s, t + 1)

        run_at(t, backward)

    drain()
    copies["lo"].wait()
    copies["hg"].wait()


def layer(x, up, pack, tile, qpack):
    return pl.pallas_call(
        layer_kernel,
        out_shape=tuple(jax.ShapeDtypeStruct(*o) for o in OUTS.values()),
        in_specs=[HBM] * 2 + [VM] * 3,
        out_specs=(HBM,) * 2 + (VM,) * 5,
        scratch_shapes=[pltpu.VMEM(*b) for b in SCRATCH.values()] + [DMA(n) for n in SEMS.values()],
        compiler_params=pltpu.CompilerParams(
            collective_id=1, has_side_effects=True, vmem_limit_bytes=VMEM_LIMIT
        ),
    )(x, up, pack, tile, qpack)


def fast_local(
    hidden_in,
    upstream_grad,
    query_vectors,
    loss_weight,
    positive_ids,
    positive_count,
    query_proj,
    key_proj,
    value_proj,
    attn_proj,
    query_bias,
    value_bias,
    attn_bias,
    first_gain,
    first_shift,
    inner_proj,
    inner_bias,
    outer_proj,
    outer_bias,
    second_gain,
    second_shift,
):
    outer_t = outer_proj.T
    pairs = [(query_proj, key_proj), (value_proj, attn_proj.T)]
    pairs += [(inner_proj[:, j * D : (j + 1) * D], outer_t[:, j * D : (j + 1) * D]) for j in range(4)]
    pack = jnp.stack([jnp.concatenate(pair, 0) for pair in pairs])
    vecs = jnp.stack(
        [query_bias, value_bias, attn_bias, first_gain, first_shift, outer_bias, second_gain, second_shift]
    ).astype(F32)
    mid = jnp.zeros((8, 96), F32).at[0].set(inner_bias.astype(F32))
    aux = jnp.concatenate(
        [positive_ids.T.astype(F32), positive_count[None].astype(F32), loss_weight[None], jnp.zeros((3, 4), F32)], 0
    )
    tile = jnp.concatenate([vecs, mid, aux, jnp.zeros((8, 4), F32)], 1)
    qpack = jnp.concatenate([query_vectors.reshape(ROWS, 128), jnp.zeros((8, 128), BF)], 0)
    layer_output, hidden_grad, out, query_acc, bias, loss, cls_grad = layer(
        hidden_in.reshape(TOK, D), upstream_grad.reshape(TOK, D), pack, tile, qpack
    )
    me = lax.axis_index("blk") * 4 + lax.axis_index("grp")
    vec = lax.dynamic_slice(bias[:8], (0, ROWS * me), (8, ROWS))
    inner_vec = lax.dynamic_slice(bias[8:12].reshape(-1), (96 * me,), (96,))
    return (
        layer_output.reshape(hidden_in.shape),
        hidden_grad.reshape(hidden_in.shape),
        query_acc.reshape(4, D),
        lax.dynamic_slice(loss[0], (4 * me,), (4,)),
        out[0, :ROWS],
        out[0, ROWS:],
        out[1, :ROWS],
        out[1, ROWS:].T,
        vec[0],
        vec[1],
        vec[2],
        vec[3],
        vec[4],
        jnp.concatenate([out[j, :ROWS] for j in range(2, 6)], 1),
        inner_vec,
        jnp.concatenate([out[j, ROWS:] for j in range(2, 6)], 1).T,
        vec[5],
        vec[6],
        vec[7],
        cls_grad[:4],
    )


def solution(mesh):
    in_specs = (
        P(("blk", "grp"), None, None),
        P(("blk", "grp"), None, None),
        P(("blk", "grp"), None),
        P(("blk", "grp")),
        P(("blk", "grp"), None),
        P(("blk", "grp")),
        P(("blk", "grp"), None),
        P(("blk", "grp"), None),
        P(("blk", "grp"), None),
        P(None, ("blk", "grp")),
        P(("blk", "grp")),
        P(("blk", "grp")),
        P(("blk", "grp")),
        P(("blk", "grp")),
        P(("blk", "grp")),
        P(("blk", "grp"), None),
        P(("blk", "grp")),
        P(None, ("blk", "grp")),
        P(("blk", "grp")),
        P(("blk", "grp")),
        P(("blk", "grp")),
    )
    out_specs = (
        P(("blk", "grp"), None, None),
        P(("blk", "grp"), None, None),
        P(("blk", "grp"), None),
        P(("blk", "grp")),
        P(("blk", "grp"), None),
        P(("blk", "grp"), None),
        P(("blk", "grp"), None),
        P(None, ("blk", "grp")),
        P(("blk", "grp")),
        P(("blk", "grp")),
        P(("blk", "grp")),
        P(("blk", "grp")),
        P(("blk", "grp")),
        P(("blk", "grp"), None),
        P(("blk", "grp")),
        P(None, ("blk", "grp")),
        P(("blk", "grp")),
        P(("blk", "grp")),
        P(("blk", "grp")),
        P(("blk", "grp"), None),
    )
    tiled = mesh.shape["blk"] == 8 and mesh.shape["grp"] == 4
    local = fast_local if tiled else plain_local
    return jax.shard_map(local, mesh=mesh, in_specs=in_specs, out_specs=out_specs, check_vma=False)
```

```python
import jax
import jax.numpy as jnp
from jax import lax
from jax.experimental import pallas as pl
from jax.experimental.pallas import tpu as pltpu
from jax.sharding import PartitionSpec as P

D = 768
HEADS = 12
HEAD_DIM = 64
LEN = 128


NORM_EPS = 1e-05
NEG_FILL = -1e30


def product(left_side, right_side):
    return jnp.dot(left_side, right_side, preferred_element_type=jnp.float32)


def contract(form_text, first_side, second_side):
    return jnp.einsum(form_text, first_side, second_side, preferred_element_type=jnp.float32)


def norm_forward(resid_sum, gain_vec, shift_vec):
    centered = resid_sum - jnp.mean(resid_sum, axis=-1, keepdims=True)
    inv_dev = lax.rsqrt(jnp.mean(centered * centered, axis=-1, keepdims=True) + NORM_EPS)
    normal_part = centered * inv_dev
    return (normal_part * gain_vec + shift_vec, normal_part, inv_dev)


def norm_backward(out_grad, normal_part, inv_dev, gain_vec):
    scaled_grad = out_grad * gain_vec
    mean_grad = jnp.mean(scaled_grad, axis=-1, keepdims=True)
    mean_cross = jnp.mean(scaled_grad * normal_part, axis=-1, keepdims=True)
    return inv_dev * (scaled_grad - mean_grad - normal_part * mean_cross)


def gelu_exact(pre_act):
    return jax.nn.gelu(pre_act, approximate=False)


def gelu_grad(pre_act, act_grad):
    unused_out, pullback = jax.vjp(gelu_exact, pre_act)
    return pullback(act_grad)[0]


def positive_block(positive_ids, positive_count, span_count):
    slot_live = (
        jnp.arange(positive_ids.shape[1], dtype=jnp.int32)[None, :] < positive_count[:, None]
    )
    passage_index = jnp.arange(span_count, dtype=jnp.int32)
    matches = (positive_ids[:, :, None] == passage_index[None, None, :]) & slot_live[:, :, None]
    return jnp.any(matches, axis=1)


def block_forward(block_in, attn_params, ffn_params):
    (
        query_proj,
        key_proj,
        value_proj,
        attn_proj,
        query_bias,
        value_bias,
        attn_bias,
        first_gain,
        first_shift,
    ) = attn_params
    inner_proj, inner_bias, outer_proj, outer_bias, second_gain, second_shift = ffn_params
    pass_count = block_in.shape[0]
    head_shape = (pass_count, LEN, HEADS, HEAD_DIM)
    tok_rows = block_in.reshape(pass_count * LEN, D)
    queries = ((product(tok_rows, query_proj) + query_bias) * 0.125).astype(jnp.bfloat16)
    keys_low = product(tok_rows, key_proj).astype(jnp.bfloat16)
    values_low = (product(tok_rows, value_proj) + value_bias).astype(jnp.bfloat16)
    scores = contract("bqhd,bkhd->bhqk", queries.reshape(head_shape), keys_low.reshape(head_shape))
    top_score = jnp.max(scores, axis=-1, keepdims=True)
    exp_terms = jnp.exp(scores - top_score)
    totals = jnp.sum(exp_terms, axis=-1, keepdims=True)
    probs_low = (exp_terms / totals).astype(jnp.bfloat16)
    log_norm = top_score + jnp.log(totals)
    context = contract("bhqk,bkhd->bqhd", probs_low, values_low.reshape(head_shape))
    context = context.reshape(pass_count * LEN, D).astype(jnp.bfloat16)
    attn_out = product(context, attn_proj) + attn_bias
    normed, first_normal, first_inv = norm_forward(
        tok_rows.astype(jnp.float32) + attn_out, first_gain, first_shift
    )
    normed_low = normed.astype(jnp.bfloat16)
    inner_pre = product(normed_low, inner_proj) + inner_bias
    activated = gelu_exact(inner_pre).astype(jnp.bfloat16)
    branch = product(activated, outer_proj) + outer_bias
    layer_f32, second_normal, second_inv = norm_forward(normed + branch, second_gain, second_shift)
    kept_state = (
        queries,
        keys_low,
        values_low,
        log_norm,
        context,
        first_normal,
        first_inv,
        normed_low,
        inner_pre,
        activated,
        second_normal,
        second_inv,
    )
    return (layer_f32, kept_state)


def block_backward(block_in, out_grad, kept_state, attn_params, ffn_params):
    (
        query_proj,
        key_proj,
        value_proj,
        attn_proj,
        query_bias,
        value_bias,
        attn_bias,
        first_gain,
        first_shift,
    ) = attn_params
    inner_proj, inner_bias, outer_proj, outer_bias, second_gain, second_shift = ffn_params
    (
        queries,
        keys_low,
        values_low,
        log_norm,
        context,
        first_normal,
        first_inv,
        normed_low,
        inner_pre,
        activated,
        second_normal,
        second_inv,
    ) = kept_state
    pass_count = block_in.shape[0]
    tok_count = pass_count * LEN
    head_shape = (pass_count, LEN, HEADS, HEAD_DIM)
    tok_rows = block_in.reshape(tok_count, D)
    grad_rows = out_grad.reshape(tok_count, D)
    grad_second_gain = jnp.sum(grad_rows * second_normal, axis=0)
    grad_second_shift = jnp.sum(grad_rows, axis=0)
    second_resid = norm_backward(grad_rows, second_normal, second_inv, second_gain)
    branch_grad = second_resid.astype(jnp.bfloat16)
    grad_outer_bias = jnp.sum(branch_grad.astype(jnp.float32), axis=0)
    grad_outer_proj = product(activated.T, branch_grad)
    inner_grad = gelu_grad(inner_pre, product(branch_grad, outer_proj.T)).astype(jnp.bfloat16)
    grad_inner_bias = jnp.sum(inner_grad.astype(jnp.float32), axis=0)
    grad_inner_proj = product(normed_low.T, inner_grad)
    normed_grad = second_resid + product(inner_grad, inner_proj.T)
    grad_first_gain = jnp.sum(normed_grad * first_normal, axis=0)
    grad_first_shift = jnp.sum(normed_grad, axis=0)
    first_resid = norm_backward(normed_grad, first_normal, first_inv, first_gain)
    attn_grad = first_resid.astype(jnp.bfloat16)
    grad_attn_bias = jnp.sum(attn_grad.astype(jnp.float32), axis=0)
    grad_attn_proj = product(context.T, attn_grad)
    context_grad = product(attn_grad, attn_proj.T).astype(jnp.bfloat16).reshape(head_shape)
    query_heads = queries.reshape(head_shape)
    key_heads = keys_low.reshape(head_shape)
    value_heads = values_low.reshape(head_shape)
    scores = contract("bqhd,bkhd->bhqk", query_heads, key_heads)
    prob_full = jnp.exp(scores - log_norm)
    values_grad = contract("bhqk,bqhd->bkhd", prob_full.astype(jnp.bfloat16), context_grad)
    values_grad = values_grad.astype(jnp.bfloat16).reshape(tok_count, D)
    prob_grad = contract("bqhd,bkhd->bhqk", context_grad, value_heads)
    score_grad = (
        prob_full * (prob_grad - jnp.sum(prob_full * prob_grad, axis=-1, keepdims=True))
    ).astype(jnp.bfloat16)
    queries_grad = (
        contract("bhqk,bkhd->bqhd", score_grad, key_heads)
        .astype(jnp.bfloat16)
        .reshape(tok_count, D)
    )
    keys_grad = (
        contract("bhqk,bqhd->bkhd", score_grad, query_heads)
        .astype(jnp.bfloat16)
        .reshape(tok_count, D)
    )
    grad_query_proj = product(tok_rows.T, queries_grad) * 0.125
    grad_query_bias = jnp.sum(queries_grad.astype(jnp.float32), axis=0) * 0.125
    grad_key_proj = product(tok_rows.T, keys_grad)
    grad_value_proj = product(tok_rows.T, values_grad)
    grad_value_bias = jnp.sum(values_grad.astype(jnp.float32), axis=0)
    hidden_grad = (
        first_resid
        + 0.125 * product(queries_grad, query_proj.T)
        + product(keys_grad, key_proj.T)
        + product(values_grad, value_proj.T)
    )
    attn_grads = (
        grad_query_proj,
        grad_key_proj,
        grad_value_proj,
        grad_attn_proj,
        grad_query_bias,
        grad_value_bias,
        grad_attn_bias,
        grad_first_gain,
        grad_first_shift,
    )
    ffn_grads = (
        grad_inner_proj,
        grad_inner_bias,
        grad_outer_proj,
        grad_outer_bias,
        grad_second_gain,
        grad_second_shift,
    )
    return (hidden_grad, attn_grads, ffn_grads)


def plain_local(
    hidden_in,
    upstream_grad,
    query_vectors,
    loss_weight,
    positive_ids,
    positive_count,
    query_proj,
    key_proj,
    value_proj,
    attn_proj,
    query_bias,
    value_bias,
    attn_bias,
    first_gain,
    first_shift,
    inner_proj,
    inner_bias,
    outer_proj,
    outer_bias,
    second_gain,
    second_shift,
):
    attn_params = (
        lax.all_gather(query_proj, ("blk", "grp"), axis=0, tiled=True),
        lax.all_gather(key_proj, ("blk", "grp"), axis=0, tiled=True),
        lax.all_gather(value_proj, ("blk", "grp"), axis=0, tiled=True),
        lax.all_gather(attn_proj, ("blk", "grp"), axis=1, tiled=True),
        lax.all_gather(query_bias, ("blk", "grp"), axis=0, tiled=True),
        lax.all_gather(value_bias, ("blk", "grp"), axis=0, tiled=True),
        lax.all_gather(attn_bias, ("blk", "grp"), axis=0, tiled=True),
        lax.all_gather(first_gain, ("blk", "grp"), axis=0, tiled=True),
        lax.all_gather(first_shift, ("blk", "grp"), axis=0, tiled=True),
    )
    ffn_params = (
        lax.all_gather(inner_proj, ("blk", "grp"), axis=0, tiled=True),
        lax.all_gather(inner_bias, ("blk", "grp"), axis=0, tiled=True),
        lax.all_gather(outer_proj, ("blk", "grp"), axis=1, tiled=True),
        lax.all_gather(outer_bias, ("blk", "grp"), axis=0, tiled=True),
        lax.all_gather(second_gain, ("blk", "grp"), axis=0, tiled=True),
        lax.all_gather(second_shift, ("blk", "grp"), axis=0, tiled=True),
    )
    pass_count = hidden_in.shape[0]
    layer_f32, kept_state = block_forward(hidden_in, attn_params, ffn_params)
    layer_output = layer_f32.astype(jnp.bfloat16).reshape(pass_count, LEN, D)
    cls_local = layer_output[:, 0, :]
    query_count = query_vectors.shape[0]
    lowest = jnp.full((query_count,), NEG_FILL, jnp.float32)
    cls_piece = lax.all_gather(cls_local, ("blk", "grp"), axis=0, tiled=True)
    top_all = lowest
    top_pos = lowest
    scores = contract("qd,pd->qp", query_vectors, cls_piece)
    hit_mask = positive_block(positive_ids, positive_count, cls_piece.shape[0])
    masked = jnp.where(hit_mask, scores, NEG_FILL)
    new_all = jnp.maximum(top_all, jnp.max(scores, axis=1))
    new_pos = jnp.maximum(top_pos, jnp.max(masked, axis=1))
    sum_all = jnp.sum(jnp.exp(scores - new_all[:, None]), axis=1)
    pos_terms = jnp.where(hit_mask, jnp.exp(masked - new_pos[:, None]), 0.0)
    sum_pos = jnp.sum(pos_terms, axis=1)
    top_all, sum_all, top_pos, sum_pos = (new_all, sum_all, new_pos, sum_pos)
    total_all = top_all + jnp.log(sum_all)
    total_pos = top_pos + jnp.log(sum_pos)
    cls_piece = lax.all_gather(cls_local, ("blk", "grp"), axis=0, tiled=True)
    scores = contract("qd,pd->qp", query_vectors, cls_piece)
    hit_mask = positive_block(positive_ids, positive_count, cls_piece.shape[0])
    masked = jnp.where(hit_mask, scores, NEG_FILL)
    weight_rows = loss_weight[:, None] * (
        jnp.exp(scores - total_all[:, None]) - jnp.exp(masked - total_pos[:, None])
    )
    weight_rows = weight_rows.astype(jnp.bfloat16)
    query_acc = product(weight_rows, cls_piece)
    query_loss = total_all - total_pos
    cls_grad = lax.psum_scatter(
        contract("qp,qd->pd", weight_rows, query_vectors),
        ("blk", "grp"),
        scatter_dimension=0,
        tiled=True,
    )
    grad_total = upstream_grad.astype(jnp.float32).at[:, 0, :].add(cls_grad)
    ffn_back = (
        lax.all_gather(inner_proj, ("blk", "grp"), axis=0, tiled=True),
        lax.all_gather(inner_bias, ("blk", "grp"), axis=0, tiled=True),
        lax.all_gather(outer_proj, ("blk", "grp"), axis=1, tiled=True),
        lax.all_gather(outer_bias, ("blk", "grp"), axis=0, tiled=True),
        lax.all_gather(second_gain, ("blk", "grp"), axis=0, tiled=True),
        lax.all_gather(second_shift, ("blk", "grp"), axis=0, tiled=True),
    )
    attn_back = (
        lax.all_gather(query_proj, ("blk", "grp"), axis=0, tiled=True),
        lax.all_gather(key_proj, ("blk", "grp"), axis=0, tiled=True),
        lax.all_gather(value_proj, ("blk", "grp"), axis=0, tiled=True),
        lax.all_gather(attn_proj, ("blk", "grp"), axis=1, tiled=True),
        lax.all_gather(query_bias, ("blk", "grp"), axis=0, tiled=True),
        lax.all_gather(value_bias, ("blk", "grp"), axis=0, tiled=True),
        lax.all_gather(attn_bias, ("blk", "grp"), axis=0, tiled=True),
        lax.all_gather(first_gain, ("blk", "grp"), axis=0, tiled=True),
        lax.all_gather(first_shift, ("blk", "grp"), axis=0, tiled=True),
    )
    hidden_part, attn_grads, ffn_grads = block_backward(
        hidden_in, grad_total, kept_state, attn_back, ffn_back
    )
    attn_shards = (
        lax.psum_scatter(attn_grads[0], ("blk", "grp"), scatter_dimension=0, tiled=True),
        lax.psum_scatter(attn_grads[1], ("blk", "grp"), scatter_dimension=0, tiled=True),
        lax.psum_scatter(attn_grads[2], ("blk", "grp"), scatter_dimension=0, tiled=True),
        lax.psum_scatter(attn_grads[3], ("blk", "grp"), scatter_dimension=1, tiled=True),
        lax.psum_scatter(attn_grads[4], ("blk", "grp"), scatter_dimension=0, tiled=True),
        lax.psum_scatter(attn_grads[5], ("blk", "grp"), scatter_dimension=0, tiled=True),
        lax.psum_scatter(attn_grads[6], ("blk", "grp"), scatter_dimension=0, tiled=True),
        lax.psum_scatter(attn_grads[7], ("blk", "grp"), scatter_dimension=0, tiled=True),
        lax.psum_scatter(attn_grads[8], ("blk", "grp"), scatter_dimension=0, tiled=True),
    )
    ffn_shards = (
        lax.psum_scatter(ffn_grads[0], ("blk", "grp"), scatter_dimension=0, tiled=True),
        lax.psum_scatter(ffn_grads[1], ("blk", "grp"), scatter_dimension=0, tiled=True),
        lax.psum_scatter(ffn_grads[2], ("blk", "grp"), scatter_dimension=1, tiled=True),
        lax.psum_scatter(ffn_grads[3], ("blk", "grp"), scatter_dimension=0, tiled=True),
        lax.psum_scatter(ffn_grads[4], ("blk", "grp"), scatter_dimension=0, tiled=True),
        lax.psum_scatter(ffn_grads[5], ("blk", "grp"), scatter_dimension=0, tiled=True),
    )
    hidden_grad = hidden_part.astype(jnp.bfloat16).reshape(pass_count, LEN, D)
    return (
        layer_output,
        hidden_grad,
        query_acc,
        query_loss,
        attn_shards[0],
        attn_shards[1],
        attn_shards[2],
        attn_shards[3],
        attn_shards[4],
        attn_shards[5],
        attn_shards[6],
        attn_shards[7],
        attn_shards[8],
        ffn_shards[0],
        ffn_shards[1],
        ffn_shards[2],
        ffn_shards[3],
        ffn_shards[4],
        ffn_shards[5],
        cls_grad,
    )


BF = jnp.bfloat16
F32 = jnp.float32
MESH = pl.DeviceIdType.MESH
VM = pl.BlockSpec(memory_space=pltpu.VMEM)
DMA = pltpu.SemaphoreType.DMA
ALL = slice(None)
VMEM_LIMIT = 60 * 2**20
LW = 384
PARTS = 2
NC = 6 * PARTS
ROWS = 24
TOK = 512


class Place:
    def __init__(self):
        self.b = lax.axis_index("blk")
        self.z = lax.axis_index("grp")
        self.y, self.x, self.c = self.b // 4, (self.b // 2) % 2, self.b % 2
        self.zh, self.zl = self.z // 2, self.z % 2
        self.mid = ((self.z + 1) // 2) % 2
        self.xdev = (self.b + 2 - 4 * self.x, self.z)
        self.ydev = (self.b + 4 - 8 * self.y, self.z)
        self.cdev = (self.b + 1 - 2 * self.c, self.z)
        self.zdev = (self.b, self.z + 1 - 2 * self.zl)
        self.fdev = (self.b, 3 - self.z)


def greet(p):
    bar = pltpu.get_barrier_semaphore()
    for k in range(1, 8):
        pl.semaphore_signal(bar, 1, device_id=((p.b + k) % 8, p.z), device_id_type=MESH)
    for k in range(1, 4):
        pl.semaphore_signal(bar, 1, device_id=(p.b, (p.z + k) % 4), device_id_type=MESH)
    pl.semaphore_wait(bar, 10)


def rcopy(src, dst, ss, rs, dev):
    return pltpu.make_async_remote_copy(
        src_ref=src, dst_ref=dst, send_sem=ss, recv_sem=rs, device_id=dev, device_id_type=MESH
    )


class Flow:
    def __init__(self, p, ref, kind, ss, rs, lead=()):
        self.p, self.ref, self.kind, self.ss, self.rs, self.lead = p, ref, kind, ss, rs, lead
        self.f, self.s = (p.x, p.y) if kind == 0 else (p.y, p.x)
        self.fdev, self.sdev = (p.xdev, p.ydev) if kind == 0 else (p.ydev, p.xdev)

    def at(self, f, s, zz, c=None):
        c = self.p.c if c is None else c
        return self.ref.at[self.lead + self.index(f, s, zz, c)]

    def index(self, f, s, zz, c):
        return (s, f, c, zz) if self.kind == 0 else (f, s, c, zz)

    def copy(self, stage, src, dst, dev):
        return rcopy(src, dst, self.ss(stage), self.rs(stage), dev)

    def go(self, stage, view, dev):
        self.copy(stage, view, view, dev).start()

    def got(self, stage, view):
        self.copy(stage, view, view, self.p.cdev).wait_recv()

    def sent(self, stage, view):
        self.copy(stage, view, view, self.p.cdev).wait_send()


class Gather(Flow):
    def s2_send(self):
        self.go(0, self.at(self.f, self.s, self.p.zh), self.fdev)

    def s2_recv(self):
        self.got(0, self.at(1 - self.f, self.s, self.p.zh))

    def s3a_send(self):
        self.go(1, self.at(ALL, self.s, self.p.zh), self.p.fdev)

    def s3a_recv(self):
        self.got(1, self.at(ALL, self.s, 1 - self.p.zh))

    def s3b_send(self):
        self.go(2, self.at(ALL, self.s, 1 - self.p.zh), self.p.zdev)

    def s3b_recv(self):
        self.got(2, self.at(ALL, self.s, 1 - self.p.zh))

    def s4a_send(self):
        self.go(3, self.at(ALL, self.s, self.p.zh), self.sdev)

    def s4b_send(self):
        self.go(6, self.at(ALL, self.s, 1 - self.p.zh), self.sdev)

    def s4_recv(self):
        self.got(3, self.at(ALL, 1 - self.s, self.p.zh))
        self.got(6, self.at(ALL, 1 - self.s, 1 - self.p.zh))

    def c1_send(self):
        self.go(4, self.at(ALL, self.s, ALL), self.p.cdev)

    def c1_recv(self):
        self.got(4, self.at(ALL, self.s, ALL, 1 - self.p.c))

    def c2_send(self):
        self.go(5, self.at(ALL, 1 - self.s, ALL), self.p.cdev)

    def c2_recv(self):
        self.got(5, self.at(ALL, 1 - self.s, ALL, 1 - self.p.c))

    def drain(self):
        self.sent(0, self.at(self.f, self.s, self.p.zh))

        @pl.when(self.p.mid == 1)
        def _():
            self.sent(1, self.at(ALL, self.s, self.p.zh))
            self.sent(2, self.at(ALL, self.s, 1 - self.p.zh))

        self.sent(3, self.at(ALL, self.s, self.p.zh))
        self.sent(6, self.at(ALL, self.s, 1 - self.p.zh))
        self.sent(4, self.at(ALL, self.s, ALL))
        self.sent(5, self.at(ALL, 1 - self.s, ALL))


def lanes_of(ci):
    return pl.ds(pl.multiple_of((ci % PARTS) * LW, 128), LW)


class Scatter(Flow):
    def __init__(self, p, ref, kind, ss, rs, bufs, lead=()):
        super().__init__(p, ref, kind, ss, rs, lead)
        self.rc, self.r4a, self.r4b, self.r3b, self.r3a, self.r2 = bufs

    def add(self, stage, buf, f, s, zz):
        self.copy(stage, buf, buf, self.p.cdev).wait_recv()
        at = self.index(f, s, zz, self.p.c)
        self.ref[at] = (self.ref[at].astype(F32) + buf[...].astype(F32)).astype(BF)

    def t0_send(self):
        self.copy(0, self.at(ALL, ALL, ALL, 1 - self.p.c), self.rc, self.p.cdev).start()

    def t0_add(self):
        self.add(0, self.rc, ALL, ALL, ALL)

    def t1a_send(self):
        self.copy(1, self.at(ALL, 1 - self.s, 1 - self.p.zh), self.r4a, self.sdev).start()

    def t1a_add(self):
        self.add(1, self.r4a, ALL, self.s, 1 - self.p.zh)

    def t1b_send(self):
        self.copy(5, self.at(ALL, 1 - self.s, self.p.zh), self.r4b, self.sdev).start()

    def t1b_add(self):
        self.add(5, self.r4b, ALL, self.s, self.p.zh)

    def t2a_send(self):
        self.copy(2, self.at(ALL, self.s, 1 - self.p.zh), self.r3b, self.p.zdev).start()

    def t2a_add(self):
        self.add(2, self.r3b, ALL, self.s, 1 - self.p.zh)

    def t2b_send(self):
        self.copy(3, self.at(ALL, self.s, 1 - self.p.zh), self.r3a, self.p.fdev).start()

    def t2b_add(self):
        self.add(3, self.r3a, ALL, self.s, self.p.zh)

    def t3_send(self):
        self.copy(4, self.at(1 - self.f, self.s, self.p.zh), self.r2, self.fdev).start()

    def t3_sum(self):
        self.copy(4, self.r2, self.r2, self.p.cdev).wait_recv()
        at = self.index(self.f, self.s, self.p.zh, self.p.c)
        return self.ref[at].astype(F32) + self.r2[...].astype(F32)

    def drain(self):
        self.sent(0, self.at(ALL, ALL, ALL, 1 - self.p.c))
        self.sent(1, self.at(ALL, 1 - self.s, 1 - self.p.zh))
        self.sent(5, self.at(ALL, 1 - self.s, self.p.zh))

        @pl.when(self.p.mid == 0)
        def _():
            self.sent(2, self.at(ALL, self.s, 1 - self.p.zh))

        @pl.when(self.p.mid == 1)
        def _():
            self.sent(3, self.at(ALL, self.s, 1 - self.p.zh))

        self.sent(4, self.at(1 - self.f, self.s, self.p.zh))


def nn(a, b): return lax.dot_general(a, b, (((1,), (0,)), ((), ())), preferred_element_type=F32)
def nt(a, b): return lax.dot_general(a, b, (((1,), (1,)), ((), ())), preferred_element_type=F32)
def tn(a, b): return lax.dot_general(a, b, (((0,), (0,)), ((), ())), preferred_element_type=F32)

def weight(ref, i): return ref[i].reshape(D, D)
def keep(ref, i, val): ref[i] = val.astype(BF).reshape(2, 2, 2, 2, 48, D)

def tiles(n, body, unroll=None):
    def f(r, c):
        body(pl.ds(pl.multiple_of(r * (TOK // n), TOK // n), TOK // n)); return c
    lax.fori_loop(0, n, f, 0, unroll=unroll)

def masks():
    lane = lax.broadcasted_iota(jnp.int32, (1, 128), 1)
    lo = (lane < 64).astype(F32).astype(BF)
    return lo, (1 - lo.astype(F32)).astype(BF)

def qkv(s):
    x = s.x[...]
    s.q[...] = ((nn(x, weight(s.wa, 0)) + s.vec[0:1, :]) * 0.125).astype(BF)
    s.k[...] = nn(x, weight(s.wb, 0)).astype(BF)
    s.v[...] = (nn(x, weight(s.wa, 1)) + s.vec[1:2, :]).astype(BF)

def split(x, lo, hi): return jnp.concatenate([x * lo, x * hi], 0)

def attn_fwd(s, p):
    lo, hi = masks()
    r = pl.ds(pl.multiple_of(p * 128, 128), 128)
    for h in range(6):
        ln = pl.ds(h * 128, 128)
        sc = nt(s.q[r, ln], split(s.k[r, ln], lo, hi))
        out = []
        for w in (sc[:, :128], sc[:, 128:]):
            e = jnp.exp(w - jnp.max(w, axis=1, keepdims=True))
            out.append((e * (1.0 / jnp.sum(e, axis=1, keepdims=True))).astype(BF))
        pr = jnp.concatenate(out, 1)
        s.p[p, h] = pr
        s.ctx[r, ln] = nn(pr, split(s.v[r, ln], lo, hi)).astype(BF)

def normalize(res):
    c = res - jnp.mean(res, axis=1, keepdims=True)
    inv = lax.rsqrt(jnp.mean(c * c, axis=1, keepdims=True) + NORM_EPS)
    return c * inv, inv

def attn_out(s, n=8):
    s.acc[...] = nt(s.ctx[...], weight(s.wb, 1))
    def body(r):
        n_, inv = normalize(s.x[r, :].astype(F32) + s.acc[r, :] + s.vec[2:3, :])
        s.fn[r, :] = n_
        s.s1[r, :] = inv
        s.nl[r, :] = (n_ * s.vec[3:4, :] + s.vec[4:5, :]).astype(BF)
        s.acc[r, :] = n_ * s.vec[3:4, :] + s.vec[4:5, :] + s.vec[5:6, :]
    tiles(2, body)

def gelu_parts(x):
    ax = jnp.abs(x) * 0.7071067811865476
    t = 1.0 / (1.0 + 0.3275911 * ax)
    e = jnp.exp(x * x * -0.5)
    poly = t * (0.254829592 + t * (-0.284496736 + t * (1.421413741 + t * (-1.453152027 + t * 1.061405429))))
    half = 0.5 * poly * e
    phi = jnp.where(x > 0, 1.0 - half, half)
    return phi, e * 0.3989422804014327

def ffn_fwd(s, h):
    j, ln = h // PARTS, lanes_of(h)
    w_in = s.wa[2 + j, :, :, :, :, :, ln].reshape(D, LW)
    w_out = s.wb[2 + j, :, :, :, :, :, ln].reshape(D, LW)
    for r in (slice(0, 256), slice(256, 512)):
        x = nn(s.nl[r, :], w_in) + s.vec[pl.ds(8 + j, 1), ln]
        cdf, pdf = gelu_parts(x)
        act = (x * cdf).astype(BF)
        s.act[j, r, ln] = act
        s.gp[j, r, ln] = (cdf + x * pdf).astype(BF)
        s.acc[r, :] += nt(act, w_out)

def norm2(s):
    def body(r):
        n_, inv = normalize(s.acc[r, :])
        s.acc[r, :] = n_
        s.s2[r, :] = inv
        s.lo[r, :] = (n_ * s.vec[6:7, :] + s.vec[7:8, :]).astype(BF)
    tiles(2, body)

def norm_back(g, n_, inv, gain):
    sg = g * gain
    return inv * (sg - jnp.mean(sg, axis=1, keepdims=True) - n_ * jnp.mean(sg * n_, axis=1, keepdims=True))

def colsum(x): return jnp.sum(x.reshape(-1, 8, x.shape[-1]), axis=0)

def norm2_back(s):
    def body(r):
        g = s.up[r, :].astype(F32)
        n_ = s.acc[r, :]
        s.gv[6] += colsum(g * n_)
        s.gv[7] += colsum(g)
        res = norm_back(g, n_, s.s2[r, :], s.vec[6:7, :])
        s.acc[r, :] = res
        b = res.astype(BF)
        s.bg[r, :] = b
        s.gv[5] += colsum(b.astype(F32))
    tiles(2, body)

def ffn_back(s, j):
    s.tmp[...] = nn(s.bg[...], weight(s.wb, 2 + j))
    keep(s.wb, 2 + j, tn(s.bg[...], s.act[j]))
    def ew(r):
        ig = (s.tmp[r, :] * s.gp[j, r, :].astype(F32)).astype(BF)
        s.gp[j, r, :] = ig
        s.gv[8 + j] += colsum(ig.astype(F32))
    tiles(2, ew)
    s.acc[...] += nt(s.gp[j], weight(s.wa, 2 + j))
    keep(s.wa, 2 + j, tn(s.nl[...], s.gp[j]))

def norm1_back(s):
    def body(r):
        g = s.acc[r, :]
        n_ = s.fn[r, :]
        s.gv[3] += colsum(g * n_)
        s.gv[4] += colsum(g)
        res = norm_back(g, n_, s.s1[r, :], s.vec[3:4, :])
        s.acc[r, :] = res
        b = res.astype(BF)
        s.bg[r, :] = b
        s.gv[2] += colsum(b.astype(F32))
    tiles(2, body)
    s.nl[...] = nn(s.bg[...], weight(s.wb, 1)).astype(BF)
    keep(s.wb, 1, tn(s.bg[...], s.ctx[...]))

def attn_back(s, p):
    lo, hi = masks()
    r = pl.ds(pl.multiple_of(p * 128, 128), 128)
    for h in range(6):
        ln = pl.ds(h * 128, 128)
        qp, kp, vp, cg = s.q[r, ln], s.k[r, ln], s.v[r, ln], s.nl[r, ln]
        dp = nt(cg, split(vp, lo, hi))
        pr = s.p[p, h]
        prf = pr.astype(F32)
        t = prf * dp
        ds = []
        for a, b in ((0, 128), (128, 256)):
            ds.append((t[:, a:b] - prf[:, a:b] * jnp.sum(t[:, a:b], axis=1, keepdims=True)).astype(BF))
        dq = nn(jnp.concatenate(ds, 1), split(kp, lo, hi))
        dk = tn(jnp.concatenate(ds, 0), split(qp, lo, hi))
        dv = tn(jnp.concatenate([pr[:, :128], pr[:, 128:]], 0), split(cg, lo, hi))
        s.q[r, ln] = dq.astype(BF)
        s.k[r, ln] = dk.astype(BF)
        s.v[r, ln] = dv.astype(BF)

def qkv_back(s):
    s.acc[...] += 0.125 * nt(s.q[...], weight(s.wa, 0))
    s.acc[...] += nt(s.k[...], weight(s.wb, 0))
    s.hg[...] = (s.acc[...] + nt(s.v[...], weight(s.wa, 1))).astype(BF)
    def sums(r):
        s.gv[0] += colsum(s.q[r, :].astype(F32)) * 0.125
        s.gv[1] += colsum(s.v[r, :].astype(F32))
    tiles(2, sums)
    keep(s.wa, 1, tn(s.x[...], s.v[...]))
    keep(s.wa, 0, tn(s.x[...], s.q[...]) * 0.125)
    keep(s.wb, 0, tn(s.x[...], s.k[...]))


class Bag:
    pass


def column_maps(width, offset, first):
    lane = lax.broadcasted_iota(jnp.int32, (128, D), 0).astype(F32)
    col = lax.broadcasted_iota(jnp.int32, (128, D), 1).astype(F32) + first
    owner = jnp.floor((col + 0.5) * (1.0 / width))
    hot = ((lane - offset) == (col - owner * width)).astype(F32)
    return hot, owner[0:1]


def pack_weights(s, i):
    if i == 0:
        top, low = s.w_query[...].astype(F32), s.w_key[...].astype(F32)
    elif i == 1:
        top, low = s.w_value[...].astype(F32), s.w_attn[...].astype(F32)
    else:
        at = slice((i - 2) * D, (i - 1) * D)
        top, low = s.w_inner[:, at].astype(F32), s.w_outer[:, at].astype(F32)
    s.pack[i] = jnp.concatenate([top, low], 0).astype(BF)


def pack_small(s):
    for t, name in enumerate(VECTORS[:8]):
        s.tile[t : t + 1, 0:ROWS] = getattr(s, name)[...].astype(F32).reshape(1, ROWS)
    row = lax.broadcasted_iota(jnp.int32, (8, 128), 0)
    lane = lax.broadcasted_iota(jnp.int32, (8, 128), 1)
    tile = jnp.where(lane < ROWS, s.tile[...], 0.0)
    inner = s.inner_bias[...].astype(F32).reshape(1, 96)
    inner = pltpu.roll(jnp.concatenate([inner, jnp.zeros((1, 32), F32)], 1), ROWS, 1)
    tile = jnp.where((row == 0) & (lane >= ROWS) & (lane < ROWS + 96), inner, tile)
    for q in range(4):
        values = [s.positive_ids[q, k].astype(F32) for k in range(3)]
        values += [s.positive_count[q].astype(F32), s.loss_weight[q]]
        for t, value in enumerate(values):
            tile = jnp.where((row == t) & (lane == 120 + q), value, tile)
    queries = s.w_queries[...].astype(F32)
    rows = [queries[q : q + 1, k * 128 : (k + 1) * 128] for q in range(4) for k in range(6)]
    s.qpack[...] = jnp.concatenate(rows + [jnp.zeros((8, 128), F32)], 0).astype(BF)
    return tile


def unpack_small(s):
    sm = s.small[...]
    hot, owner = column_maps(24, 0, 0.0)
    dev = jnp.floor((lax.broadcasted_iota(jnp.int32, (256, 1), 0).astype(F32) + 0.5) * 0.125)
    wide = jnp.where(dev == owner, nn(sm.astype(BF), hot.astype(BF)), 0.0)
    s.vec[0:8, :] = jnp.sum(wide.reshape(32, 8, D), axis=0)
    one = s.small[pl.ds(0, 32, stride=8), :].astype(BF)
    dev32 = lax.broadcasted_iota(jnp.int32, (32, 1), 0).astype(F32)
    rows = []
    for j in range(4):
        hot, owner = column_maps(96, 24, float(D * j))
        part = jnp.where(dev32 == owner, nn(one, hot.astype(BF)), 0.0)
        rows.append(jnp.sum(part, axis=0, keepdims=True))
    s.vec[8:16, :] = jnp.concatenate(rows + [jnp.zeros((4, D), F32)], 0)
    hot, owner = column_maps(4, 120, 0.0)
    part = lax.dot_general(
        sm, hot[:, :128], (((1,), (0,)), ((), ())), precision=lax.Precision.HIGHEST, preferred_element_type=F32
    )
    part = jnp.where(dev == owner[:, :128], part, 0.0)
    s.aux[...] = jnp.sum(part.reshape(32, 8, 128), axis=0)


def unpack_queries(s):
    s.qrow[...] = s.qx[...].reshape(D, 128).astype(F32)
    for q in range(4):
        for k in range(6):
            piece = s.qrow[pl.ds(6 * q + k, 32, stride=24), :]
            s.qm[pl.ds(k * 128 + q, 32, stride=4), :] = piece


def all_queries(s):
    return jnp.concatenate([s.qm[k * 128 : (k + 1) * 128, :] for k in range(6)], 1).astype(BF)


def first_rows(s):
    rows = [s.acc[p * LEN : p * LEN + 8, :][0:1] for p in range(4)]
    n_, inv = normalize(jnp.concatenate(rows + [jnp.zeros((4, D), F32)], 0))
    s.cn[...] = n_
    s.ci[...] = inv
    cls = (n_ * s.vec[6:7, :] + s.vec[7:8, :]).astype(BF)
    s.cls[...] = cls.astype(F32)
    return nt(cls, all_queries(s))


def loss_part(s, me):
    scores = s.sc[...]
    row = lax.broadcasted_iota(jnp.int32, (256, 1), 0).astype(F32)
    dev = jnp.floor((row + 0.5) * 0.125)
    slot = row - 8.0 * dev
    real = slot < 4.0
    passage = 4.0 * dev + slot
    ids, count, weight_q = s.aux[0:3, :], s.aux[3:4, :], s.aux[4:5, :]

    def hits(passage):
        return (
            (ids[0:1] == passage)
            | ((ids[1:2] == passage) & (count > 1.5))
            | ((ids[2:3] == passage) & (count > 2.5))
        )

    everyone = jnp.where(real, scores, NEG_FILL)
    masked = jnp.where(hits(passage) & real, scores, NEG_FILL)
    totals = []
    for part in (everyone, masked):
        top = jnp.max(part, axis=0, keepdims=True)
        totals.append(top + jnp.log(jnp.sum(jnp.exp(part - top), axis=0, keepdims=True)))
    total_all, total_pos = totals
    s.loss[...] = jnp.broadcast_to(total_all - total_pos, (8, 128))
    own = s.sc[pl.ds(pl.multiple_of(me * 8, 8), 8), :]
    slot = lax.broadcasted_iota(jnp.int32, (8, 128), 0)
    hit = hits((4 * me + slot).astype(F32))
    pull = jnp.where(hit, jnp.exp(own - total_pos), 0.0)
    grad = weight_q * (jnp.exp(own - total_all) - pull)
    grad = jnp.where(slot < 4, grad, 0.0).astype(BF)
    s.cgrad[...] = nn(grad, all_queries(s))
    part = tn(grad, s.cls[...].astype(BF))
    for k in range(6):
        s.qpart[k * 128 : (k + 1) * 128, :] = part[:, k * 128 : (k + 1) * 128]


def query_rows(s):
    for q in range(4):
        for k in range(6):
            piece = s.qpart[pl.ds(k * 128 + q, 32, stride=4), :]
            s.qrow[pl.ds(6 * q + k, 32, stride=24), :] = piece
    s.qg[...] = s.qrow[...].astype(BF).reshape(2, 2, 2, 2, 48, 128)


def add_cls(s):
    g = jnp.concatenate([s.up[p * LEN : p * LEN + 16, :][0:1].astype(F32) for p in range(4)] + [jnp.zeros((4, D), F32)], 0)
    extra = s.cgrad[...]
    live = (lax.broadcasted_iota(jnp.int32, (8, 1), 0) < 4).astype(F32)
    n_, inv = s.cn[...] * live, s.ci[...]
    s.gv[6] += extra * n_
    s.gv[7] += extra
    res = norm_back(g + extra, n_, inv, s.vec[6:7, :]) * live
    old = norm_back(g, n_, inv, s.vec[6:7, :]) * live
    low = res.astype(BF).astype(F32)
    s.gv[5] += low - old.astype(BF).astype(F32)
    top = (lax.broadcasted_iota(jnp.int32, (16, 1), 0) == 0)
    for p in range(4):
        at = slice(p * LEN, p * LEN + 16)
        s.acc[at, :] = jnp.where(top, res[p : p + 1], s.acc[at, :])
        s.bg[at, :] = jnp.where(top, low[p : p + 1], s.bg[at, :].astype(F32)).astype(BF)


HBM = pl.BlockSpec(memory_space=pl.ANY)
MERGES, G_S23, G_S4A, G_S34, G_S45, G_END = 2, 1, 2, 3, 5, 6
S_K1, S_K1B, S_K2, S_K3, S_K4, S_K5, S_K6 = 1, 3, 2, 3, 10, 11, 12
S_FAST = 2
S_END = S_K6 + NC // S_FAST
OUTS = dict(
    lo_out=((TOK, D), BF),
    hg_out=((TOK, D), BF),
    out=((6, 48, D), F32),
    q_out=((ROWS, 128), F32),
    bias_out=((16, D), F32),
    loss=((8, 128), F32),
    cgrad=((8, D), F32),
)
VECTORS = (
    "query_bias",
    "value_bias",
    "attn_bias",
    "first_gain",
    "first_shift",
    "outer_bias",
    "second_gain",
    "second_shift",
    "inner_bias",
)
INS = ("x_in", "up_in") + ("w_query", "w_key", "w_value", "w_attn", "w_inner", "w_outer", "w_queries") + VECTORS
INS += ("loss_weight", "positive_ids", "positive_count")
SCRATCH = dict(
    wa=((6, 2, 2, 2, 2, 48, D), BF),
    wb=((6, 2, 2, 2, 2, 48, D), BF),
    rb=((6, 48, D), BF),
    pack=((6, 48, D), BF),
    qpack=((32, 128), BF),
    x=((TOK, D), BF),
    up=((TOK, D), BF),
    lo=((TOK, D), BF),
    hg=((TOK, D), BF),
    q=((TOK, D), BF),
    k=((TOK, D), BF),
    v=((TOK, D), BF),
    ctx=((TOK, D), BF),
    p=((4, 6, 128, 256), BF),
    fn=((TOK, D), F32),
    s1=((TOK, 1), F32),
    s2=((TOK, 1), F32),
    nl=((TOK, D), BF),
    acc=((TOK, D), F32),
    act=((4, TOK, D), BF),
    gp=((4, TOK, D), BF),
    bg=((TOK, D), BF),
    tmp=((TOK, D), F32),
    small=((256, 128), F32),
    tile=((8, 128), F32),
    qx=((2, 2, 2, 2, 48, 128), BF),
    qrb=((32, 128), BF),
    sc=((256, 128), F32),
    vec=((16, D), F32),
    gv=((12, 8, D), F32),
    aux=((8, 128), F32),
    qm=((D, 128), F32),
    cn=((8, D), F32),
    ci=((8, 1), F32),
    cls=((8, D), F32),
    qpart=((D, 128), F32),
    qrow=((D, 128), F32),
    qg=((2, 2, 2, 2, 48, 128), BF),
    rc=((2, NC, 2, 2, 2, 48, LW), BF),
    r4a=((2, NC, 2, 48, LW), BF),
    r4b=((2, NC, 2, 48, LW), BF),
    r3b=((2, NC, 2, 48, LW), BF),
    r3a=((2, NC, 2, 48, LW), BF),
    r2=((2, NC, 48, LW), BF),
    st=((NC, 48, LW), BF),
    r1=((NC, 48, LW), BF),
    qc=((2, 2, 2, 48, 128), BF),
    q4a=((2, 48, 128), BF),
    q4b=((2, 48, 128), BF),
    q3b=((2, 48, 128), BF),
    q3a=((2, 48, 128), BF),
    q2=((48, 128), BF),
    qst=((32, 128), BF),
    q1=((32, 128), BF),
    bs_buf=((5, 16, D), F32),
    br_buf=((5, 16, D), F32),
)
SEMS = dict(
    gs=(7, 2),
    gr=(7, 2, NC),
    g1s=(1,),
    g1r=(NC,),
    xs=(8,),
    xr=(8,),
    bss=(5,),
    brs=(5,),
    zs=(2, 4),
    zr=(2, 4),
    bs=(2, 8),
    br=(2, 8),
    io=(4,),
)


class Spread:
    def __init__(self, p, s, ref, which, rows):
        self.p, self.s, self.ref, self.which, self.rows = p, s, ref, which, rows

    def zview(self, z):
        r = self.rows
        return self.ref.at[pl.ds(pl.multiple_of((self.p.b * 4 + z) * r, r), r), :]

    def bview(self, b):
        r = self.rows * 4
        return self.ref.at[pl.ds(pl.multiple_of(b * r, r), r), :]

    def zcopy(self, k, view):
        p, s, w = self.p, self.s, self.which
        return rcopy(view, view, s.zs.at[w, k], s.zr.at[w, k], (p.b, (p.z + k) % 4))

    def bcopy(self, k, view):
        p, s, w = self.p, self.s, self.which
        return rcopy(view, view, s.bs.at[w, k], s.br.at[w, k], ((p.b + k) % 8, p.z))

    def first(self):
        for k in range(1, 4):
            self.zcopy(k, self.zview(self.p.z)).start()

    def second(self):
        for k in range(1, 4):
            self.zcopy(k, self.zview((self.p.z + 4 - k) % 4)).wait_recv()
        for k in range(1, 8):
            self.bcopy(k, self.bview(self.p.b)).start()

    def finish(self):
        for k in range(1, 8):
            self.bcopy(k, self.bview((self.p.b + 8 - k) % 8)).wait_recv()
        for k in range(1, 4):
            self.zcopy(k, self.zview(self.p.z)).wait_send()
        for k in range(1, 8):
            self.bcopy(k, self.bview(self.p.b)).wait_send()


def gather_steps(p, s, me, vectors):
    def flows(ci):
        out = []
        for kind, ref in ((0, s.wa), (1, s.wb)):
            view = ref.at[ci // PARTS, :, :, :, :, :, lanes_of(ci)]
            out.append(
                Gather(
                    p,
                    view,
                    kind,
                    lambda st, kind=kind: s.gs.at[st, kind],
                    lambda st, kind=kind: s.gr.at[st, kind, ci],
                )
            )
        return out

    def s1(ci):
        at = (ci // PARTS, ALL, lanes_of(ci))
        return rcopy(s.pack.at[at], s.rb.at[at], s.g1s.at[0], s.g1r.at[ci], p.zdev)

    first = p.zl == 0

    def order(own, oth):
        return jnp.where(first, own, oth), jnp.where(first, oth, own)

    def merge(ci):
        s1(ci).wait_recv()
        i, ln = ci // PARTS, lanes_of(ci)
        lo, hi = order(s.pack[i, :, ln].astype(F32), s.rb[i, :, ln].astype(F32))
        s.wa[i, p.y, p.x, p.c, p.zh, :, ln] = jnp.concatenate([lo[:ROWS], hi[:ROWS]], 0).astype(BF)
        s.wb[i, p.y, p.x, p.c, p.zh, :, ln] = jnp.concatenate([lo[ROWS:], hi[ROWS:]], 0).astype(BF)
        for f in flows(ci):
            f.s2_send()

    def s23(fs):
        for f in fs:
            f.s2_recv()

        @pl.when(p.mid == 1)
        def _():
            for f in fs:
                f.s3a_send()

    def s4a(fs):
        for f in fs:
            f.s4a_send()

    def s34(fs):
        @pl.when(p.mid == 1)
        def _():
            for f in fs:
                f.s3a_recv()
                f.s3b_send()

        @pl.when(p.mid == 0)
        def _():
            for f in fs:
                f.s3b_recv()

        for f in fs:
            f.s4b_send()
            f.c1_send()

    def s45(fs):
        for f in fs:
            f.s4_recv()
            f.c2_send()

    def core(fs):
        for f in fs:
            f.c1_recv()
            f.c2_recv()

    def drain():
        for kind, ref in ((0, s.wa), (1, s.wb)):
            sems = lambda st, kind=kind: s.gs.at[st, kind]
            Gather(p, ref, kind, sems, sems, (ALL,)).drain()
        rcopy(s.pack, s.rb, s.g1s.at[0], s.g1r.at[0], p.zdev).wait_send()
        q.drain()

    for i in range(6):
        pack_weights(s, i)
        for h in range(PARTS):
            s1(PARTS * i + h).start()

    s.small[pl.ds(pl.multiple_of(me * 8, 8), 8), :] = pack_small(s)
    vectors.first()
    q = Gather(p, s.qx, 0, lambda st: s.xs.at[st], lambda st: s.xr.at[st])
    q1 = rcopy(s.qpack, s.qrb, s.xs.at[7], s.xr.at[7], p.zdev)
    q1.start()

    def qmerge():
        q1.wait()
        lo, hi = order(s.qpack[...].astype(F32), s.qrb[...].astype(F32))
        s.qx[p.y, p.x, p.c, p.zh] = jnp.concatenate([lo[:ROWS], hi[:ROWS]], 0).astype(BF)
        q.s2_send()

    def q23():
        s23([q])
        s4a([q])

    query_steps = [qmerge, q23, lambda: s34([q]), lambda: s45([q]), lambda: core([q])]

    def pack_of(fn):
        return lambda ci: fn(flows(ci))

    stages = (
        (0, MERGES, merge),
        (G_S23, 1, pack_of(s23)),
        (G_S4A, 1, pack_of(s4a)),
        (G_S34, 1, pack_of(s34)),
        (G_S45, 1, pack_of(s45)),
        (G_END, 1, pack_of(core)),
    )
    return stages, query_steps, drain


def scatter_steps(p, s):
    def piece(ci):
        return (ci // PARTS + 2) % 6

    def flows(ci):
        made = []
        for kind, ref in ((0, s.wa), (1, s.wb)):
            bufs = tuple(buf.at[kind, ci] for buf in (s.rc, s.r4a, s.r4b, s.r3b, s.r3a, s.r2))
            made.append(
                Scatter(
                    p,
                    ref.at[piece(ci), :, :, :, :, :, lanes_of(ci)],
                    kind,
                    lambda st, kind=kind: s.gs.at[st, kind],
                    lambda st, kind=kind: s.gr.at[st, kind, ci],
                    bufs,
                )
            )
        return made

    def k0(fs):
        for f in fs:
            f.t0_send()

    def k1(fs):
        for f in fs:
            f.t0_add()
            f.t1a_send()

    def k1b(fs):
        for f in fs:
            f.t1b_send()

    def k2(fs):
        for f in fs:
            f.t1a_add()

            @pl.when(p.mid == 0)
            def _(f=f):
                f.t2a_send()

    def k3(fs):
        @pl.when(p.mid == 1)
        def _():
            for f in fs:
                f.t2a_add()
                f.t2b_send()

    def k4(fs):
        for f in fs:
            f.t1b_add()

            @pl.when(p.mid == 1)
            def _(f=f):
                f.t2b_add()

            f.t3_send()

    first = p.zl == 0

    def halves(total):
        top, low = total[:ROWS], total[ROWS:]
        return jnp.where(first, top, low), jnp.where(first, low, top)

    def s1(ci):
        return rcopy(s.st.at[ci], s.r1.at[ci], s.g1s.at[0], s.g1r.at[ci], p.zdev)

    def k5(ci):
        fa, fb = flows(ci)
        keep_a, give_a = halves(fa.t3_sum())
        keep_b, give_b = halves(fb.t3_sum())
        s.st[ci] = jnp.concatenate([give_a, give_b], 0).astype(BF)
        s1(ci).start()
        s.out[piece(ci), :, lanes_of(ci)] = jnp.concatenate([keep_a, keep_b], 0)

    def k6(ci):
        s1(ci).wait_recv()
        at = (piece(ci), ALL, lanes_of(ci))
        s.out[at] = s.out[at] + s.r1[ci].astype(F32)

    def pack_of(fn):
        return lambda ci: fn(flows(ci))

    stages = (
        (0, 1, pack_of(k0)),
        (S_K1, 1, pack_of(k1)),
        (S_K1B, 1, pack_of(k1b)),
        (S_K2, 1, pack_of(k2)),
        (S_K3, 1, pack_of(k3)),
        (S_K4, S_FAST, pack_of(k4)),
        (S_K5, S_FAST, k5),
        (S_K6, S_FAST, k6),
    )
    q = Scatter(
        p, s.qg, 0, lambda st: s.xs.at[st], lambda st: s.xr.at[st], (s.qc, s.q4a, s.q4b, s.q3b, s.q3a, s.q2)
    )
    q1 = rcopy(s.qst, s.q1, s.xs.at[6], s.xr.at[6], p.zdev)

    def q5():
        keep, give = halves(q.t3_sum())
        s.qst[...] = jnp.concatenate([give, jnp.zeros((8, 128), F32)], 0).astype(BF)
        q1.start()
        s.q_out[...] = keep

    def q6():
        q1.wait()
        s.q_out[...] = s.q_out[...] + s.q1[:ROWS].astype(F32)
        q.drain()

    query_steps = [lambda fn=fn: fn([q]) for fn in (k0, k1, k1b, k2, k3, k4)] + [q5, q6]
    devs = (p.cdev, p.xdev, p.ydev, p.zdev, (p.b, (p.z + 2) % 4))

    def bcopy(k):
        return rcopy(s.bs_buf.at[k], s.br_buf.at[k], s.bss.at[k], s.brs.at[k], devs[k])

    def bias_step(k):
        if k == 0:
            total = jnp.concatenate([jnp.sum(s.gv[...], axis=1), jnp.zeros((4, D), F32)], 0)
        else:
            bcopy(k - 1).wait()
            total = s.bs_buf[k - 1] + s.br_buf[k - 1]
        if k < 5:
            s.bs_buf[k] = total
            bcopy(k).start()
        else:
            s.bias_out[...] = total

    def drain():
        for kind, ref in ((0, s.wa), (1, s.wb)):
            sems = lambda st, kind=kind: s.gs.at[st, kind]
            Scatter(p, ref, kind, sems, sems, (None,) * 6, (ALL,)).drain()
        rcopy(s.st, s.r1, s.g1s.at[0], s.g1r.at[0], p.zdev).wait_send()

    return stages, query_steps, [lambda k=k: bias_step(k) for k in range(6)], drain


def run_stages(stages, t):
    for off, many, fn in stages:
        for k in range(many):
            ci = (t - off) * many + k

            @pl.when((ci >= 0) & (ci < NC))
            def _(ci=ci, fn=fn):
                fn(ci)


def run_at(t, table):
    for when, fn in table:

        @pl.when(t == when)
        def _(fn=fn):
            fn()


def layer_kernel(*refs):
    s = Bag()
    names = list(INS) + list(OUTS) + list(SCRATCH) + list(SEMS)
    for name, ref in zip(names, refs):
        setattr(s, name, ref)
    p = Place()
    greet(p)
    me = p.b * 4 + p.z
    vectors = Spread(p, s, s.small, 0, 8)
    scores = Spread(p, s, s.sc, 1, 8)
    copies = {
        name: pltpu.make_async_copy(src, dst, s.io.at[k])
        for k, (name, src, dst) in enumerate(
            (
                ("x", s.x_in, s.x),
                ("up", s.up_in, s.up),
                ("lo", s.lo, s.lo_out),
                ("hg", s.hg, s.hg_out),
            )
        )
    }
    copies["x"].start()
    copies["up"].start()
    stages, query_steps, drain = gather_steps(p, s, me, vectors)

    def passages(fn, lo, many):
        def go():
            pl.loop(lo, lo + many)(lambda i: fn(s, i))

        return go

    def small_done():
        vectors.finish()
        unpack_small(s)

    ready = 2 * PARTS - 1 + G_END
    forward = [
        (1, copies["x"].wait),
        (1, copies["up"].wait),
        (2, vectors.second),
        (6, small_done),
        (ready, lambda: qkv(s)),
        (ready + 1, passages(attn_fwd, 0, 2)),
        (ready + 2, passages(attn_fwd, 2, 2)),
        (ready + 3, lambda: attn_out(s)),
    ]
    forward += [(6 + 2 * k, fn) for k, fn in enumerate(query_steps)]
    forward += [(15, lambda: unpack_queries(s))]

    def ffn_until(t):
        return jnp.minimum(jnp.maximum(2 * (t - ready - 3), 0), jnp.maximum(t - ready, 0))

    @pl.loop(0, NC + G_END)
    def _(t):
        run_stages(stages, t)
        run_at(t, forward)
        pl.loop(ffn_until(t - 1), ffn_until(t))(lambda h: ffn_fwd(s, h))

    drain()
    s.sc[pl.ds(pl.multiple_of(me * 8, 8), 8), :] = first_rows(s)
    scores.first()
    s.gv[...] = jnp.zeros_like(s.gv)
    norm2(s)
    copies["lo"].start()
    scores.second()
    norm2_back(s)
    scores.finish()
    loss_part(s, me)
    add_cls(s)

    stages, query_steps, bias_steps, drain = scatter_steps(p, s)
    ffn_back(s, 0)
    def hidden():
        qkv_back(s)
        copies["hg"].start()

    backward = [
        (3, lambda: norm1_back(s)),
        (4, passages(attn_back, 0, 1)),
        (5, passages(attn_back, 1, 1)),
        (6, passages(attn_back, 2, 2)),
        (7, hidden),
        (8, lambda: query_rows(s)),
    ]
    backward += [(9 + k, fn) for k, fn in enumerate(query_steps)]
    backward += [(8 + 2 * k, fn) for k, fn in enumerate(bias_steps)]

    @pl.loop(0, max(S_END, 18) + 1)
    def _(t):
        run_stages(stages, t)

        @pl.when(t < 3)
        def _():
            ffn_back(s, t + 1)

        run_at(t, backward)

    drain()
    copies["lo"].wait()
    copies["hg"].wait()


SMEM = pl.BlockSpec(memory_space=pltpu.SMEM)


def layer(*args):
    return pl.pallas_call(
        layer_kernel,
        out_shape=tuple(jax.ShapeDtypeStruct(*o) for o in OUTS.values()),
        in_specs=[HBM] * 2 + [VM] * (len(INS) - 5) + [SMEM] * 3,
        out_specs=(HBM,) * 2 + (VM,) * 5,
        scratch_shapes=[pltpu.VMEM(*b) for b in SCRATCH.values()] + [DMA(n) for n in SEMS.values()],
        compiler_params=pltpu.CompilerParams(
            collective_id=1, has_side_effects=True, vmem_limit_bytes=VMEM_LIMIT
        ),
    )(*args)


def finish_kernel(
    out, q_out, bias, loss, cgrad,
    query_grad, query_loss, g_query, g_key, g_value, g_attn,
    g_qb, g_vb, g_ab, g_fg, g_fs, g_inner, g_ib, g_outer, g_ob, g_sg, g_ss, cls_grad
):
    me = lax.axis_index("blk") * 4 + lax.axis_index("grp")
    for q in range(4):
        for k in range(6):
            query_grad[q : q + 1, k * 128 : (k + 1) * 128] = q_out[6 * q + k : 6 * q + k + 1, :]
    cls_grad[...] = cgrad[0:4, :]
    g_query[...] = out[0, :ROWS]
    g_key[...] = out[0, ROWS:]
    g_value[...] = out[1, :ROWS]
    g_attn[...] = out[1, ROWS:]
    for j in range(4):
        at = slice(j * D, (j + 1) * D)
        g_inner[:, at] = out[2 + j, :ROWS]
        g_outer[:, at] = out[2 + j, ROWS:]
    wide = pltpu.roll(bias[0:8, :], lax.rem(D - ROWS * me, D), 1)
    for t, ref in enumerate((g_qb, g_vb, g_ab, g_fg, g_fs, g_ob, g_sg, g_ss)):
        ref[...] = wide[t, :ROWS]
    group = me // 8
    inner = jnp.sum(jnp.where(lax.broadcasted_iota(jnp.int32, (8, D), 0) == group, bias[8:16, :], 0.0), axis=0, keepdims=True)
    inner = jnp.broadcast_to(inner, (8, D))
    inner = pltpu.roll(inner, lax.rem(D - 96 * lax.rem(me, 8), D), 1)
    g_ib[...] = inner[0, :96]
    query_loss[...] = pltpu.roll(loss[...], lax.rem(128 - 4 * me, 128), 1)[0, :4]


def finish(*args):
    f32 = lambda *dims: jax.ShapeDtypeStruct(dims, F32)
    square = f32(ROWS, D)
    vec = f32(ROWS)
    outs = [f32(4, D), f32(4)] + [square] * 4 + [vec] * 5
    outs += [f32(ROWS, 4 * D), f32(96), f32(ROWS, 4 * D), vec, vec, vec, f32(4, D)]
    return pl.pallas_call(
        finish_kernel,
        out_shape=outs,
        in_specs=[VM] * 5,
        out_specs=[VM] * 18,
        compiler_params=pltpu.CompilerParams(vmem_limit_bytes=VMEM_LIMIT),
    )(*args)


def fast_local(
    hidden_in,
    upstream_grad,
    query_vectors,
    loss_weight,
    positive_ids,
    positive_count,
    query_proj,
    key_proj,
    value_proj,
    attn_proj,
    query_bias,
    value_bias,
    attn_bias,
    first_gain,
    first_shift,
    inner_proj,
    inner_bias,
    outer_proj,
    outer_bias,
    second_gain,
    second_shift,
):
    results = layer(
        hidden_in.reshape(TOK, D),
        upstream_grad.reshape(TOK, D),
        query_proj,
        key_proj,
        value_proj,
        attn_proj.T,
        inner_proj,
        outer_proj.T,
        query_vectors,
        query_bias,
        value_bias,
        attn_bias,
        first_gain,
        first_shift,
        outer_bias,
        second_gain,
        second_shift,
        inner_bias,
        loss_weight,
        positive_ids,
        positive_count,
    )
    layer_output, hidden_grad = (part.reshape(hidden_in.shape) for part in results[:2])
    rest = list(finish(*results[2:]))
    rest[5] = rest[5].T
    rest[13] = rest[13].T
    return (layer_output, hidden_grad, *rest)


def solution(mesh):
    in_specs = (
        P(("blk", "grp"), None, None),
        P(("blk", "grp"), None, None),
        P(("blk", "grp"), None),
        P(("blk", "grp")),
        P(("blk", "grp"), None),
        P(("blk", "grp")),
        P(("blk", "grp"), None),
        P(("blk", "grp"), None),
        P(("blk", "grp"), None),
        P(None, ("blk", "grp")),
        P(("blk", "grp")),
        P(("blk", "grp")),
        P(("blk", "grp")),
        P(("blk", "grp")),
        P(("blk", "grp")),
        P(("blk", "grp"), None),
        P(("blk", "grp")),
        P(None, ("blk", "grp")),
        P(("blk", "grp")),
        P(("blk", "grp")),
        P(("blk", "grp")),
    )
    out_specs = (
        P(("blk", "grp"), None, None),
        P(("blk", "grp"), None, None),
        P(("blk", "grp"), None),
        P(("blk", "grp")),
        P(("blk", "grp"), None),
        P(("blk", "grp"), None),
        P(("blk", "grp"), None),
        P(None, ("blk", "grp")),
        P(("blk", "grp")),
        P(("blk", "grp")),
        P(("blk", "grp")),
        P(("blk", "grp")),
        P(("blk", "grp")),
        P(("blk", "grp"), None),
        P(("blk", "grp")),
        P(None, ("blk", "grp")),
        P(("blk", "grp")),
        P(("blk", "grp")),
        P(("blk", "grp")),
        P(("blk", "grp"), None),
    )
    tiled = mesh.shape["blk"] == 8 and mesh.shape["grp"] == 4
    local = fast_local if tiled else plain_local
    return jax.shard_map(local, mesh=mesh, in_specs=in_specs, out_specs=out_specs, check_vma=False)
```

```python
import jax
import jax.numpy as jnp
from jax import lax
from jax.experimental import pallas as pl
from jax.experimental.pallas import tpu as pltpu
from jax.sharding import PartitionSpec as P

D = 768
HEADS = 12
HEAD_DIM = 64
LEN = 128


NORM_EPS = 1e-05
NEG_FILL = -1e30


def product(left_side, right_side):
    return jnp.dot(left_side, right_side, preferred_element_type=jnp.float32)


def contract(form_text, first_side, second_side):
    return jnp.einsum(form_text, first_side, second_side, preferred_element_type=jnp.float32)


def norm_forward(resid_sum, gain_vec, shift_vec):
    centered = resid_sum - jnp.mean(resid_sum, axis=-1, keepdims=True)
    inv_dev = lax.rsqrt(jnp.mean(centered * centered, axis=-1, keepdims=True) + NORM_EPS)
    normal_part = centered * inv_dev
    return (normal_part * gain_vec + shift_vec, normal_part, inv_dev)


def norm_backward(out_grad, normal_part, inv_dev, gain_vec):
    scaled_grad = out_grad * gain_vec
    mean_grad = jnp.mean(scaled_grad, axis=-1, keepdims=True)
    mean_cross = jnp.mean(scaled_grad * normal_part, axis=-1, keepdims=True)
    return inv_dev * (scaled_grad - mean_grad - normal_part * mean_cross)


def gelu_exact(pre_act):
    return jax.nn.gelu(pre_act, approximate=False)


def gelu_grad(pre_act, act_grad):
    unused_out, pullback = jax.vjp(gelu_exact, pre_act)
    return pullback(act_grad)[0]


def positive_block(positive_ids, positive_count, span_count):
    slot_live = (
        jnp.arange(positive_ids.shape[1], dtype=jnp.int32)[None, :] < positive_count[:, None]
    )
    passage_index = jnp.arange(span_count, dtype=jnp.int32)
    matches = (positive_ids[:, :, None] == passage_index[None, None, :]) & slot_live[:, :, None]
    return jnp.any(matches, axis=1)


def block_forward(block_in, attn_params, ffn_params):
    (
        query_proj,
        key_proj,
        value_proj,
        attn_proj,
        query_bias,
        value_bias,
        attn_bias,
        first_gain,
        first_shift,
    ) = attn_params
    inner_proj, inner_bias, outer_proj, outer_bias, second_gain, second_shift = ffn_params
    pass_count = block_in.shape[0]
    head_shape = (pass_count, LEN, HEADS, HEAD_DIM)
    tok_rows = block_in.reshape(pass_count * LEN, D)
    queries = ((product(tok_rows, query_proj) + query_bias) * 0.125).astype(jnp.bfloat16)
    keys_low = product(tok_rows, key_proj).astype(jnp.bfloat16)
    values_low = (product(tok_rows, value_proj) + value_bias).astype(jnp.bfloat16)
    scores = contract("bqhd,bkhd->bhqk", queries.reshape(head_shape), keys_low.reshape(head_shape))
    top_score = jnp.max(scores, axis=-1, keepdims=True)
    exp_terms = jnp.exp(scores - top_score)
    totals = jnp.sum(exp_terms, axis=-1, keepdims=True)
    probs_low = (exp_terms / totals).astype(jnp.bfloat16)
    log_norm = top_score + jnp.log(totals)
    context = contract("bhqk,bkhd->bqhd", probs_low, values_low.reshape(head_shape))
    context = context.reshape(pass_count * LEN, D).astype(jnp.bfloat16)
    attn_out = product(context, attn_proj) + attn_bias
    normed, first_normal, first_inv = norm_forward(
        tok_rows.astype(jnp.float32) + attn_out, first_gain, first_shift
    )
    normed_low = normed.astype(jnp.bfloat16)
    inner_pre = product(normed_low, inner_proj) + inner_bias
    activated = gelu_exact(inner_pre).astype(jnp.bfloat16)
    branch = product(activated, outer_proj) + outer_bias
    layer_f32, second_normal, second_inv = norm_forward(normed + branch, second_gain, second_shift)
    kept_state = (
        queries,
        keys_low,
        values_low,
        log_norm,
        context,
        first_normal,
        first_inv,
        normed_low,
        inner_pre,
        activated,
        second_normal,
        second_inv,
    )
    return (layer_f32, kept_state)


def block_backward(block_in, out_grad, kept_state, attn_params, ffn_params):
    (
        query_proj,
        key_proj,
        value_proj,
        attn_proj,
        query_bias,
        value_bias,
        attn_bias,
        first_gain,
        first_shift,
    ) = attn_params
    inner_proj, inner_bias, outer_proj, outer_bias, second_gain, second_shift = ffn_params
    (
        queries,
        keys_low,
        values_low,
        log_norm,
        context,
        first_normal,
        first_inv,
        normed_low,
        inner_pre,
        activated,
        second_normal,
        second_inv,
    ) = kept_state
    pass_count = block_in.shape[0]
    tok_count = pass_count * LEN
    head_shape = (pass_count, LEN, HEADS, HEAD_DIM)
    tok_rows = block_in.reshape(tok_count, D)
    grad_rows = out_grad.reshape(tok_count, D)
    grad_second_gain = jnp.sum(grad_rows * second_normal, axis=0)
    grad_second_shift = jnp.sum(grad_rows, axis=0)
    second_resid = norm_backward(grad_rows, second_normal, second_inv, second_gain)
    branch_grad = second_resid.astype(jnp.bfloat16)
    grad_outer_bias = jnp.sum(branch_grad.astype(jnp.float32), axis=0)
    grad_outer_proj = product(activated.T, branch_grad)
    inner_grad = gelu_grad(inner_pre, product(branch_grad, outer_proj.T)).astype(jnp.bfloat16)
    grad_inner_bias = jnp.sum(inner_grad.astype(jnp.float32), axis=0)
    grad_inner_proj = product(normed_low.T, inner_grad)
    normed_grad = second_resid + product(inner_grad, inner_proj.T)
    grad_first_gain = jnp.sum(normed_grad * first_normal, axis=0)
    grad_first_shift = jnp.sum(normed_grad, axis=0)
    first_resid = norm_backward(normed_grad, first_normal, first_inv, first_gain)
    attn_grad = first_resid.astype(jnp.bfloat16)
    grad_attn_bias = jnp.sum(attn_grad.astype(jnp.float32), axis=0)
    grad_attn_proj = product(context.T, attn_grad)
    context_grad = product(attn_grad, attn_proj.T).astype(jnp.bfloat16).reshape(head_shape)
    query_heads = queries.reshape(head_shape)
    key_heads = keys_low.reshape(head_shape)
    value_heads = values_low.reshape(head_shape)
    scores = contract("bqhd,bkhd->bhqk", query_heads, key_heads)
    prob_full = jnp.exp(scores - log_norm)
    values_grad = contract("bhqk,bqhd->bkhd", prob_full.astype(jnp.bfloat16), context_grad)
    values_grad = values_grad.astype(jnp.bfloat16).reshape(tok_count, D)
    prob_grad = contract("bqhd,bkhd->bhqk", context_grad, value_heads)
    score_grad = (
        prob_full * (prob_grad - jnp.sum(prob_full * prob_grad, axis=-1, keepdims=True))
    ).astype(jnp.bfloat16)
    queries_grad = (
        contract("bhqk,bkhd->bqhd", score_grad, key_heads)
        .astype(jnp.bfloat16)
        .reshape(tok_count, D)
    )
    keys_grad = (
        contract("bhqk,bqhd->bkhd", score_grad, query_heads)
        .astype(jnp.bfloat16)
        .reshape(tok_count, D)
    )
    grad_query_proj = product(tok_rows.T, queries_grad) * 0.125
    grad_query_bias = jnp.sum(queries_grad.astype(jnp.float32), axis=0) * 0.125
    grad_key_proj = product(tok_rows.T, keys_grad)
    grad_value_proj = product(tok_rows.T, values_grad)
    grad_value_bias = jnp.sum(values_grad.astype(jnp.float32), axis=0)
    hidden_grad = (
        first_resid
        + 0.125 * product(queries_grad, query_proj.T)
        + product(keys_grad, key_proj.T)
        + product(values_grad, value_proj.T)
    )
    attn_grads = (
        grad_query_proj,
        grad_key_proj,
        grad_value_proj,
        grad_attn_proj,
        grad_query_bias,
        grad_value_bias,
        grad_attn_bias,
        grad_first_gain,
        grad_first_shift,
    )
    ffn_grads = (
        grad_inner_proj,
        grad_inner_bias,
        grad_outer_proj,
        grad_outer_bias,
        grad_second_gain,
        grad_second_shift,
    )
    return (hidden_grad, attn_grads, ffn_grads)


def plain_local(
    hidden_in,
    upstream_grad,
    query_vectors,
    loss_weight,
    positive_ids,
    positive_count,
    query_proj,
    key_proj,
    value_proj,
    attn_proj,
    query_bias,
    value_bias,
    attn_bias,
    first_gain,
    first_shift,
    inner_proj,
    inner_bias,
    outer_proj,
    outer_bias,
    second_gain,
    second_shift,
):
    attn_params = (
        lax.all_gather(query_proj, ("blk", "grp"), axis=0, tiled=True),
        lax.all_gather(key_proj, ("blk", "grp"), axis=0, tiled=True),
        lax.all_gather(value_proj, ("blk", "grp"), axis=0, tiled=True),
        lax.all_gather(attn_proj, ("blk", "grp"), axis=1, tiled=True),
        lax.all_gather(query_bias, ("blk", "grp"), axis=0, tiled=True),
        lax.all_gather(value_bias, ("blk", "grp"), axis=0, tiled=True),
        lax.all_gather(attn_bias, ("blk", "grp"), axis=0, tiled=True),
        lax.all_gather(first_gain, ("blk", "grp"), axis=0, tiled=True),
        lax.all_gather(first_shift, ("blk", "grp"), axis=0, tiled=True),
    )
    ffn_params = (
        lax.all_gather(inner_proj, ("blk", "grp"), axis=0, tiled=True),
        lax.all_gather(inner_bias, ("blk", "grp"), axis=0, tiled=True),
        lax.all_gather(outer_proj, ("blk", "grp"), axis=1, tiled=True),
        lax.all_gather(outer_bias, ("blk", "grp"), axis=0, tiled=True),
        lax.all_gather(second_gain, ("blk", "grp"), axis=0, tiled=True),
        lax.all_gather(second_shift, ("blk", "grp"), axis=0, tiled=True),
    )
    pass_count = hidden_in.shape[0]
    layer_f32, kept_state = block_forward(hidden_in, attn_params, ffn_params)
    layer_output = layer_f32.astype(jnp.bfloat16).reshape(pass_count, LEN, D)
    cls_local = layer_output[:, 0, :]
    query_count = query_vectors.shape[0]
    lowest = jnp.full((query_count,), NEG_FILL, jnp.float32)
    cls_piece = lax.all_gather(cls_local, ("blk", "grp"), axis=0, tiled=True)
    top_all = lowest
    top_pos = lowest
    scores = contract("qd,pd->qp", query_vectors, cls_piece)
    hit_mask = positive_block(positive_ids, positive_count, cls_piece.shape[0])
    masked = jnp.where(hit_mask, scores, NEG_FILL)
    new_all = jnp.maximum(top_all, jnp.max(scores, axis=1))
    new_pos = jnp.maximum(top_pos, jnp.max(masked, axis=1))
    sum_all = jnp.sum(jnp.exp(scores - new_all[:, None]), axis=1)
    pos_terms = jnp.where(hit_mask, jnp.exp(masked - new_pos[:, None]), 0.0)
    sum_pos = jnp.sum(pos_terms, axis=1)
    top_all, sum_all, top_pos, sum_pos = (new_all, sum_all, new_pos, sum_pos)
    total_all = top_all + jnp.log(sum_all)
    total_pos = top_pos + jnp.log(sum_pos)
    cls_piece = lax.all_gather(cls_local, ("blk", "grp"), axis=0, tiled=True)
    scores = contract("qd,pd->qp", query_vectors, cls_piece)
    hit_mask = positive_block(positive_ids, positive_count, cls_piece.shape[0])
    masked = jnp.where(hit_mask, scores, NEG_FILL)
    weight_rows = loss_weight[:, None] * (
        jnp.exp(scores - total_all[:, None]) - jnp.exp(masked - total_pos[:, None])
    )
    weight_rows = weight_rows.astype(jnp.bfloat16)
    query_acc = product(weight_rows, cls_piece)
    query_loss = total_all - total_pos
    cls_grad = lax.psum_scatter(
        contract("qp,qd->pd", weight_rows, query_vectors),
        ("blk", "grp"),
        scatter_dimension=0,
        tiled=True,
    )
    grad_total = upstream_grad.astype(jnp.float32).at[:, 0, :].add(cls_grad)
    ffn_back = (
        lax.all_gather(inner_proj, ("blk", "grp"), axis=0, tiled=True),
        lax.all_gather(inner_bias, ("blk", "grp"), axis=0, tiled=True),
        lax.all_gather(outer_proj, ("blk", "grp"), axis=1, tiled=True),
        lax.all_gather(outer_bias, ("blk", "grp"), axis=0, tiled=True),
        lax.all_gather(second_gain, ("blk", "grp"), axis=0, tiled=True),
        lax.all_gather(second_shift, ("blk", "grp"), axis=0, tiled=True),
    )
    attn_back = (
        lax.all_gather(query_proj, ("blk", "grp"), axis=0, tiled=True),
        lax.all_gather(key_proj, ("blk", "grp"), axis=0, tiled=True),
        lax.all_gather(value_proj, ("blk", "grp"), axis=0, tiled=True),
        lax.all_gather(attn_proj, ("blk", "grp"), axis=1, tiled=True),
        lax.all_gather(query_bias, ("blk", "grp"), axis=0, tiled=True),
        lax.all_gather(value_bias, ("blk", "grp"), axis=0, tiled=True),
        lax.all_gather(attn_bias, ("blk", "grp"), axis=0, tiled=True),
        lax.all_gather(first_gain, ("blk", "grp"), axis=0, tiled=True),
        lax.all_gather(first_shift, ("blk", "grp"), axis=0, tiled=True),
    )
    hidden_part, attn_grads, ffn_grads = block_backward(
        hidden_in, grad_total, kept_state, attn_back, ffn_back
    )
    attn_shards = (
        lax.psum_scatter(attn_grads[0], ("blk", "grp"), scatter_dimension=0, tiled=True),
        lax.psum_scatter(attn_grads[1], ("blk", "grp"), scatter_dimension=0, tiled=True),
        lax.psum_scatter(attn_grads[2], ("blk", "grp"), scatter_dimension=0, tiled=True),
        lax.psum_scatter(attn_grads[3], ("blk", "grp"), scatter_dimension=1, tiled=True),
        lax.psum_scatter(attn_grads[4], ("blk", "grp"), scatter_dimension=0, tiled=True),
        lax.psum_scatter(attn_grads[5], ("blk", "grp"), scatter_dimension=0, tiled=True),
        lax.psum_scatter(attn_grads[6], ("blk", "grp"), scatter_dimension=0, tiled=True),
        lax.psum_scatter(attn_grads[7], ("blk", "grp"), scatter_dimension=0, tiled=True),
        lax.psum_scatter(attn_grads[8], ("blk", "grp"), scatter_dimension=0, tiled=True),
    )
    ffn_shards = (
        lax.psum_scatter(ffn_grads[0], ("blk", "grp"), scatter_dimension=0, tiled=True),
        lax.psum_scatter(ffn_grads[1], ("blk", "grp"), scatter_dimension=0, tiled=True),
        lax.psum_scatter(ffn_grads[2], ("blk", "grp"), scatter_dimension=1, tiled=True),
        lax.psum_scatter(ffn_grads[3], ("blk", "grp"), scatter_dimension=0, tiled=True),
        lax.psum_scatter(ffn_grads[4], ("blk", "grp"), scatter_dimension=0, tiled=True),
        lax.psum_scatter(ffn_grads[5], ("blk", "grp"), scatter_dimension=0, tiled=True),
    )
    hidden_grad = hidden_part.astype(jnp.bfloat16).reshape(pass_count, LEN, D)
    return (
        layer_output,
        hidden_grad,
        query_acc,
        query_loss,
        attn_shards[0],
        attn_shards[1],
        attn_shards[2],
        attn_shards[3],
        attn_shards[4],
        attn_shards[5],
        attn_shards[6],
        attn_shards[7],
        attn_shards[8],
        ffn_shards[0],
        ffn_shards[1],
        ffn_shards[2],
        ffn_shards[3],
        ffn_shards[4],
        ffn_shards[5],
        cls_grad,
    )


BF = jnp.bfloat16
F32 = jnp.float32
MESH = pl.DeviceIdType.MESH
VM = pl.BlockSpec(memory_space=pltpu.VMEM)
DMA = pltpu.SemaphoreType.DMA
ALL = slice(None)
VMEM_LIMIT = 60 * 2**20
LW = 384
PARTS = 2
NC = 6 * PARTS
ROWS = 24
TOK = 512


class Place:
    def __init__(self):
        self.b = lax.axis_index("blk")
        self.z = lax.axis_index("grp")
        self.y, self.x, self.c = self.b // 4, (self.b // 2) % 2, self.b % 2
        self.zh, self.zl = self.z // 2, self.z % 2
        self.mid = ((self.z + 1) // 2) % 2
        self.xdev = (self.b + 2 - 4 * self.x, self.z)
        self.ydev = (self.b + 4 - 8 * self.y, self.z)
        self.cdev = (self.b + 1 - 2 * self.c, self.z)
        self.zdev = (self.b, self.z + 1 - 2 * self.zl)
        self.fdev = (self.b, 3 - self.z)


def greet(p):
    bar = pltpu.get_barrier_semaphore()
    for k in range(1, 8):
        pl.semaphore_signal(bar, 1, device_id=((p.b + k) % 8, p.z), device_id_type=MESH)
    for k in range(1, 4):
        pl.semaphore_signal(bar, 1, device_id=(p.b, (p.z + k) % 4), device_id_type=MESH)
    pl.semaphore_wait(bar, 10)


def rcopy(src, dst, ss, rs, dev):
    return pltpu.make_async_remote_copy(
        src_ref=src, dst_ref=dst, send_sem=ss, recv_sem=rs, device_id=dev, device_id_type=MESH
    )


class Flow:
    def __init__(self, p, ref, kind, ss, rs, lead=()):
        self.p, self.ref, self.kind, self.ss, self.rs, self.lead = p, ref, kind, ss, rs, lead
        self.f, self.s = (p.x, p.y) if kind == 0 else (p.y, p.x)
        self.fdev, self.sdev = (p.xdev, p.ydev) if kind == 0 else (p.ydev, p.xdev)

    def at(self, f, s, zz, c=None):
        c = self.p.c if c is None else c
        return self.ref.at[self.lead + self.index(f, s, zz, c)]

    def index(self, f, s, zz, c):
        return (s, f, c, zz) if self.kind == 0 else (f, s, c, zz)

    def copy(self, stage, src, dst, dev):
        return rcopy(src, dst, self.ss(stage), self.rs(stage), dev)

    def go(self, stage, view, dev):
        self.copy(stage, view, view, dev).start()

    def got(self, stage, view):
        self.copy(stage, view, view, self.p.cdev).wait_recv()

    def sent(self, stage, view):
        self.copy(stage, view, view, self.p.cdev).wait_send()


class Gather(Flow):
    def s2_send(self):
        self.go(0, self.at(self.f, self.s, self.p.zh), self.fdev)

    def s2_recv(self):
        self.got(0, self.at(1 - self.f, self.s, self.p.zh))

    def s3a_send(self):
        self.go(1, self.at(ALL, self.s, self.p.zh), self.p.fdev)

    def s3a_recv(self):
        self.got(1, self.at(ALL, self.s, 1 - self.p.zh))

    def s3b_send(self):
        self.go(2, self.at(ALL, self.s, 1 - self.p.zh), self.p.zdev)

    def s3b_recv(self):
        self.got(2, self.at(ALL, self.s, 1 - self.p.zh))

    def s4a_send(self):
        self.go(3, self.at(ALL, self.s, self.p.zh), self.sdev)

    def s4b_send(self):
        self.go(6, self.at(ALL, self.s, 1 - self.p.zh), self.sdev)

    def s4_recv(self):
        self.got(3, self.at(ALL, 1 - self.s, self.p.zh))
        self.got(6, self.at(ALL, 1 - self.s, 1 - self.p.zh))

    def c1_send(self):
        self.go(4, self.at(ALL, self.s, ALL), self.p.cdev)

    def c1_recv(self):
        self.got(4, self.at(ALL, self.s, ALL, 1 - self.p.c))

    def c2_send(self):
        self.go(5, self.at(ALL, 1 - self.s, ALL), self.p.cdev)

    def c2_recv(self):
        self.got(5, self.at(ALL, 1 - self.s, ALL, 1 - self.p.c))

    def drain(self):
        self.sent(0, self.at(self.f, self.s, self.p.zh))

        @pl.when(self.p.mid == 1)
        def _():
            self.sent(1, self.at(ALL, self.s, self.p.zh))
            self.sent(2, self.at(ALL, self.s, 1 - self.p.zh))

        self.sent(3, self.at(ALL, self.s, self.p.zh))
        self.sent(6, self.at(ALL, self.s, 1 - self.p.zh))
        self.sent(4, self.at(ALL, self.s, ALL))
        self.sent(5, self.at(ALL, 1 - self.s, ALL))


def lanes_of(ci):
    return pl.ds(pl.multiple_of((ci % PARTS) * LW, 128), LW)


class Scatter(Flow):
    def __init__(self, p, ref, kind, ss, rs, bufs, lead=()):
        super().__init__(p, ref, kind, ss, rs, lead)
        self.rc, self.r4a, self.r4b, self.r3b, self.r3a, self.r2 = bufs

    def add(self, stage, buf, f, s, zz):
        self.copy(stage, buf, buf, self.p.cdev).wait_recv()
        at = self.index(f, s, zz, self.p.c)
        self.ref[at] = self.ref[at] + buf[...]

    def t0_send(self):
        self.copy(0, self.at(ALL, ALL, ALL, 1 - self.p.c), self.rc, self.p.cdev).start()

    def t0_add(self):
        self.add(0, self.rc, ALL, ALL, ALL)

    def t1a_send(self):
        self.copy(1, self.at(ALL, 1 - self.s, 1 - self.p.zh), self.r4a, self.sdev).start()

    def t1a_add(self):
        self.add(1, self.r4a, ALL, self.s, 1 - self.p.zh)

    def t1b_send(self):
        self.copy(5, self.at(ALL, 1 - self.s, self.p.zh), self.r4b, self.sdev).start()

    def t1b_add(self):
        self.add(5, self.r4b, ALL, self.s, self.p.zh)

    def t2a_send(self):
        self.copy(2, self.at(ALL, self.s, 1 - self.p.zh), self.r3b, self.p.zdev).start()

    def t2a_add(self):
        self.add(2, self.r3b, ALL, self.s, 1 - self.p.zh)

    def t2b_send(self):
        self.copy(3, self.at(ALL, self.s, 1 - self.p.zh), self.r3a, self.p.fdev).start()

    def t2b_add(self):
        self.add(3, self.r3a, ALL, self.s, self.p.zh)

    def t3_send(self):
        self.copy(4, self.at(1 - self.f, self.s, self.p.zh), self.r2, self.fdev).start()

    def t3_sum(self):
        self.copy(4, self.r2, self.r2, self.p.cdev).wait_recv()
        at = self.index(self.f, self.s, self.p.zh, self.p.c)
        return self.ref[at].astype(F32) + self.r2[...].astype(F32)

    def drain(self):
        self.sent(0, self.at(ALL, ALL, ALL, 1 - self.p.c))
        self.sent(1, self.at(ALL, 1 - self.s, 1 - self.p.zh))
        self.sent(5, self.at(ALL, 1 - self.s, self.p.zh))

        @pl.when(self.p.mid == 0)
        def _():
            self.sent(2, self.at(ALL, self.s, 1 - self.p.zh))

        @pl.when(self.p.mid == 1)
        def _():
            self.sent(3, self.at(ALL, self.s, 1 - self.p.zh))

        self.sent(4, self.at(1 - self.f, self.s, self.p.zh))


def nn(a, b): return lax.dot_general(a, b, (((1,), (0,)), ((), ())), preferred_element_type=F32)
def nt(a, b): return lax.dot_general(a, b, (((1,), (1,)), ((), ())), preferred_element_type=F32)
def tn(a, b): return lax.dot_general(a, b, (((0,), (0,)), ((), ())), preferred_element_type=F32)

def weight(ref, i): return ref[i].reshape(D, D)
def keep(ref, i, val): ref[i] = val.astype(BF).reshape(2, 2, 2, 2, 48, D)

def tiles(n, body, unroll=None):
    def f(r, c):
        body(pl.ds(pl.multiple_of(r * (TOK // n), TOK // n), TOK // n)); return c
    lax.fori_loop(0, n, f, 0, unroll=unroll)

def masks():
    lane = lax.broadcasted_iota(jnp.int32, (1, 128), 1)
    lo = (lane < 64).astype(F32).astype(BF)
    return lo, (1 - lo.astype(F32)).astype(BF)

def queries_keys(s):
    x = s.x[...]
    s.q[...] = ((nn(x, weight(s.wa, 0)) + s.vec[0:1, :]) * 0.125).astype(BF)
    s.k[...] = nn(x, weight(s.wb, 0)).astype(BF)


def values(s):
    s.v[...] = (nn(s.x[...], weight(s.wa, 1)) + s.vec[1:2, :]).astype(BF)


def split(x, lo, hi): return jnp.concatenate([x * lo, x * hi], 0)

def attn_fwd(s, p):
    lo, hi = masks()
    r = pl.ds(pl.multiple_of(p * 128, 128), 128)
    for h in range(6):
        ln = pl.ds(h * 128, 128)
        sc = nt(s.q[r, ln], split(s.k[r, ln], lo, hi))
        out = []
        for w in (sc[:, :128], sc[:, 128:]):
            e = jnp.exp(w - jnp.max(w, axis=1, keepdims=True))
            out.append((e * (1.0 / jnp.sum(e, axis=1, keepdims=True))).astype(BF))
        pr = jnp.concatenate(out, 1)
        s.p[p, h] = pr
        s.ctx[r, ln] = nn(pr, split(s.v[r, ln], lo, hi)).astype(BF)

def normalize(res):
    c = res - jnp.mean(res, axis=1, keepdims=True)
    inv = lax.rsqrt(jnp.mean(c * c, axis=1, keepdims=True) + NORM_EPS)
    return c * inv, inv

def attn_out(s, n=8):
    s.acc[...] = nt(s.ctx[...], weight(s.wb, 1))
    def body(r):
        n_, inv = normalize(s.x[r, :].astype(F32) + s.acc[r, :] + s.vec[2:3, :])
        s.fn[r, :] = n_
        s.s1[r, :] = inv
        s.nl[r, :] = (n_ * s.vec[3:4, :] + s.vec[4:5, :]).astype(BF)
        s.acc[r, :] = n_ * s.vec[3:4, :] + s.vec[4:5, :] + s.vec[5:6, :]
    tiles(2, body)

def gelu_parts(x):
    ax = jnp.abs(x) * 0.7071067811865476
    t = 1.0 / (1.0 + 0.3275911 * ax)
    e = jnp.exp(x * x * -0.5)
    poly = t * (0.254829592 + t * (-0.284496736 + t * (1.421413741 + t * (-1.453152027 + t * 1.061405429))))
    half = 0.5 * poly * e
    phi = jnp.where(x > 0, 1.0 - half, half)
    return phi, e * 0.3989422804014327

def ffn_fwd(s, j, h, width):
    ln = pl.ds(pl.multiple_of(h * width, 128), width) if width < D else ALL
    w_in = s.wa[2 + j, :, :, :, :, :, ln].reshape(D, width)
    w_out = s.wb[2 + j, :, :, :, :, :, ln].reshape(D, width)
    for r in (slice(0, 256), slice(256, 512)):
        x = nn(s.nl[r, :], w_in) + s.vec[pl.ds(8 + j, 1), ln]
        cdf, pdf = gelu_parts(x)
        act = (x * cdf).astype(BF)
        s.act[j, r, ln] = act
        s.gp[j, r, ln] = (cdf + x * pdf).astype(BF)
        s.acc[r, :] += nt(act, w_out)

def norm2(s):
    def body(r):
        n_, inv = normalize(s.acc[r, :])
        s.acc[r, :] = n_
        s.s2[r, :] = inv
        s.lo[r, :] = (n_ * s.vec[6:7, :] + s.vec[7:8, :]).astype(BF)
    tiles(2, body)

def norm_back(g, n_, inv, gain):
    sg = g * gain
    return inv * (sg - jnp.mean(sg, axis=1, keepdims=True) - n_ * jnp.mean(sg * n_, axis=1, keepdims=True))

def colsum(x): return jnp.sum(x.reshape(-1, 8, x.shape[-1]), axis=0)

def norm2_back(s):
    def body(r):
        g = s.up[r, :].astype(F32)
        n_ = s.acc[r, :]
        s.gv[6] += colsum(g * n_)
        s.gv[7] += colsum(g)
        res = norm_back(g, n_, s.s2[r, :], s.vec[6:7, :])
        s.acc[r, :] = res
        b = res.astype(BF)
        s.bg[r, :] = b
        s.gv[5] += colsum(b.astype(F32))
    tiles(2, body)

def outer_back(s, j):
    s.tmp[...] = nn(s.bg[...], weight(s.wb, 2 + j))
    keep(s.wb, 2 + j, tn(s.bg[...], s.act[j]))


def inner_back(s, j):
    def ew(r):
        ig = (s.tmp[r, :] * s.gp[j, r, :].astype(F32)).astype(BF)
        s.gp[j, r, :] = ig
        s.gv[8 + j] += colsum(ig.astype(F32))

    tiles(2, ew)
    s.acc[...] += nt(s.gp[j], weight(s.wa, 2 + j))
    keep(s.wa, 2 + j, tn(s.nl[...], s.gp[j]))


def ffn_back(s, j):
    outer_back(s, j)
    inner_back(s, j)


def norm1_back(s):
    def body(r):
        g = s.acc[r, :]
        n_ = s.fn[r, :]
        s.gv[3] += colsum(g * n_)
        s.gv[4] += colsum(g)
        res = norm_back(g, n_, s.s1[r, :], s.vec[3:4, :])
        s.acc[r, :] = res
        b = res.astype(BF)
        s.bg[r, :] = b
        s.gv[2] += colsum(b.astype(F32))
    tiles(2, body)
    s.nl[...] = nn(s.bg[...], weight(s.wb, 1)).astype(BF)
    keep(s.wb, 1, tn(s.bg[...], s.ctx[...]))

def attn_back(s, p):
    lo, hi = masks()
    r = pl.ds(pl.multiple_of(p * 128, 128), 128)
    for h in range(6):
        ln = pl.ds(h * 128, 128)
        qp, kp, vp, cg = s.q[r, ln], s.k[r, ln], s.v[r, ln], s.nl[r, ln]
        dp = nt(cg, split(vp, lo, hi))
        pr = s.p[p, h]
        prf = pr.astype(F32)
        t = prf * dp
        ds = []
        for a, b in ((0, 128), (128, 256)):
            ds.append((t[:, a:b] - prf[:, a:b] * jnp.sum(t[:, a:b], axis=1, keepdims=True)).astype(BF))
        dq = nn(jnp.concatenate(ds, 1), split(kp, lo, hi))
        dk = tn(jnp.concatenate(ds, 0), split(qp, lo, hi))
        dv = tn(jnp.concatenate([pr[:, :128], pr[:, 128:]], 0), split(cg, lo, hi))
        s.q[r, ln] = dq.astype(BF)
        s.k[r, ln] = dk.astype(BF)
        s.v[r, ln] = dv.astype(BF)

def qkv_back(s):
    s.acc[...] += 0.125 * nt(s.q[...], weight(s.wa, 0))
    s.acc[...] += nt(s.k[...], weight(s.wb, 0))
    s.hg[...] = (s.acc[...] + nt(s.v[...], weight(s.wa, 1))).astype(BF)
    def sums(r):
        s.gv[0] += colsum(s.q[r, :].astype(F32)) * 0.125
        s.gv[1] += colsum(s.v[r, :].astype(F32))
    tiles(2, sums)
    keep(s.wa, 1, tn(s.x[...], s.v[...]))
    keep(s.wa, 0, tn(s.x[...], s.q[...]) * 0.125)
    keep(s.wb, 0, tn(s.x[...], s.k[...]))


class Bag:
    pass


def column_maps(width, offset, first):
    lane = lax.broadcasted_iota(jnp.int32, (128, D), 0).astype(F32)
    col = lax.broadcasted_iota(jnp.int32, (128, D), 1).astype(F32) + first
    owner = jnp.floor((col + 0.5) * (1.0 / width))
    hot = ((lane - offset) == (col - owner * width)).astype(F32)
    return hot, owner[0:1]


def pack_weights(s, i):
    if i == 0:
        top, low = s.w_query[...].astype(F32), s.w_key[...].astype(F32)
    elif i == 1:
        top, low = s.w_value[...].astype(F32), s.w_attn[...].astype(F32)
    else:
        at = slice((i - 2) * D, (i - 1) * D)
        top, low = s.w_inner[:, at].astype(F32), s.w_outer[:, at].astype(F32)
    s.pack[i] = jnp.concatenate([top, low], 0).astype(BF)


def pack_small(s):
    for t, name in enumerate(VECTORS[:8]):
        s.tile[t : t + 1, 0:ROWS] = getattr(s, name)[...].astype(F32).reshape(1, ROWS)
    row = lax.broadcasted_iota(jnp.int32, (8, 128), 0)
    lane = lax.broadcasted_iota(jnp.int32, (8, 128), 1)
    tile = jnp.where(lane < ROWS, s.tile[...], 0.0)
    inner = s.inner_bias[...].astype(F32).reshape(1, 96)
    inner = pltpu.roll(jnp.concatenate([inner, jnp.zeros((1, 32), F32)], 1), ROWS, 1)
    tile = jnp.where((row == 0) & (lane >= ROWS) & (lane < ROWS + 96), inner, tile)
    for q in range(4):
        values = [s.positive_ids[q, k].astype(F32) for k in range(3)]
        values += [s.positive_count[q].astype(F32), s.loss_weight[q]]
        for t, value in enumerate(values):
            tile = jnp.where((row == t) & (lane == 120 + q), value, tile)
    queries = s.w_queries[...].astype(F32)
    rows = [queries[q : q + 1, k * 128 : (k + 1) * 128] for q in range(4) for k in range(6)]
    s.qpack[...] = jnp.concatenate(rows + [jnp.zeros((8, 128), F32)], 0).astype(BF)
    return tile


def unpack_small(s):
    sm = s.small[...]
    hot, owner = column_maps(24, 0, 0.0)
    dev = jnp.floor((lax.broadcasted_iota(jnp.int32, (256, 1), 0).astype(F32) + 0.5) * 0.125)
    wide = jnp.where(dev == owner, nn(sm.astype(BF), hot.astype(BF)), 0.0)
    s.vec[0:8, :] = jnp.sum(wide.reshape(32, 8, D), axis=0)
    one = s.small[pl.ds(0, 32, stride=8), :].astype(BF)
    dev32 = lax.broadcasted_iota(jnp.int32, (32, 1), 0).astype(F32)
    rows = []
    for j in range(4):
        hot, owner = column_maps(96, 24, float(D * j))
        part = jnp.where(dev32 == owner, nn(one, hot.astype(BF)), 0.0)
        rows.append(jnp.sum(part, axis=0, keepdims=True))
    s.vec[8:16, :] = jnp.concatenate(rows + [jnp.zeros((4, D), F32)], 0)
    hot, owner = column_maps(4, 120, 0.0)
    part = lax.dot_general(
        sm, hot[:, :128], (((1,), (0,)), ((), ())), precision=lax.Precision.HIGHEST, preferred_element_type=F32
    )
    part = jnp.where(dev == owner[:, :128], part, 0.0)
    s.aux[...] = jnp.sum(part.reshape(32, 8, 128), axis=0)


def unpack_queries(s):
    s.qrow[...] = s.qx[...].reshape(D, 128).astype(F32)
    for q in range(4):
        for k in range(6):
            piece = s.qrow[pl.ds(6 * q + k, 32, stride=24), :]
            s.qm[pl.ds(k * 128 + q, 32, stride=4), :] = piece


def all_queries(s):
    return jnp.concatenate([s.qm[k * 128 : (k + 1) * 128, :] for k in range(6)], 1).astype(BF)


def first_rows(s, me):
    rows = [s.acc[p * LEN : p * LEN + 8, :][0:1] for p in range(4)]
    n_, inv = normalize(jnp.concatenate(rows + [jnp.zeros((4, D), F32)], 0))
    s.cn[...] = n_
    s.ci[...] = inv
    cls = (n_ * s.vec[6:7, :] + s.vec[7:8, :]).astype(BF)
    low = cls.astype(F32)
    s.cls[...] = low
    parts = [low[0:4, k * 256 : (k + 1) * 256] for k in range(3)]
    tile = jnp.concatenate(parts + [jnp.zeros((4, 256), F32)], 0).astype(BF)
    s.call[pl.ds(pl.multiple_of(me * 16, 16), 16), :] = tile
    return nt(cls, all_queries(s))


def loss_part(s, me):
    scores = s.sc[...]
    row = lax.broadcasted_iota(jnp.int32, (256, 1), 0).astype(F32)
    dev = jnp.floor((row + 0.5) * 0.125)
    slot = row - 8.0 * dev
    real = slot < 4.0
    passage = 4.0 * dev + slot
    ids, count, weight_q = s.aux[0:3, :], s.aux[3:4, :], s.aux[4:5, :]

    def hits(passage):
        return (
            (ids[0:1] == passage)
            | ((ids[1:2] == passage) & (count > 1.5))
            | ((ids[2:3] == passage) & (count > 2.5))
        )

    everyone = jnp.where(real, scores, NEG_FILL)
    masked = jnp.where(hits(passage) & real, scores, NEG_FILL)
    totals = []
    for part in (everyone, masked):
        top = jnp.max(part, axis=0, keepdims=True)
        totals.append(top + jnp.log(jnp.sum(jnp.exp(part - top), axis=0, keepdims=True)))
    total_all, total_pos = totals
    s.loss[...] = jnp.broadcast_to(total_all - total_pos, (8, 128))
    pull = jnp.where(hits(passage) & real, jnp.exp(scores - total_pos), 0.0)
    grad = jnp.where(real, weight_q * (jnp.exp(jnp.where(real, scores - total_all, 0.0)) - pull), 0.0)
    s.sg[...] = grad
    own = s.sg[pl.ds(pl.multiple_of(me * 8, 8), 8), :].astype(BF)
    s.cgrad[...] = nn(own, all_queries(s))


def query_gradient(s, me):
    own = pltpu.roll(s.sg[...], lax.rem(128 - 4 * me, 128), 1).reshape(32, 8, 128)[:, :4]
    vectors = s.call[...]
    for k in range(3):
        pieces = [jnp.zeros((32, 4, 128), F32)] * k + [own] + [jnp.zeros((32, 4, 128), F32)] * (3 - k)
        grad = jnp.concatenate(pieces, 1).reshape(512, 128).astype(BF)
        s.q_out[:, k * 256 : (k + 1) * 256] = tn(grad, vectors)[0:8]


def pack_vectors(s):
    vec = jnp.sum(s.gv[...], axis=1)
    first = lax.broadcasted_iota(jnp.int32, (8, 96), 0) == 0
    for dev in range(32):
        b, z = dev // 4, dev % 4
        wide = vec[0:8, ROWS * dev : ROWS * (dev + 1)]
        at = 96 * (dev % 8)
        inner = jnp.where(first, vec[8 + dev // 8 : 9 + dev // 8, at : at + 96], 0.0)
        tile = jnp.concatenate([inner, wide, jnp.zeros((8, 8), F32)], 1)
        s.pb[(z * 8 + b) * 8 : (z * 8 + b + 1) * 8, :] = tile


def add_cls(s):
    g = jnp.concatenate([s.up[p * LEN : p * LEN + 16, :][0:1].astype(F32) for p in range(4)] + [jnp.zeros((4, D), F32)], 0)
    extra = s.cgrad[...]
    live = (lax.broadcasted_iota(jnp.int32, (8, 1), 0) < 4).astype(F32)
    n_, inv = s.cn[...] * live, s.ci[...]
    s.gv[6] += extra * n_
    s.gv[7] += extra
    res = norm_back(g + extra, n_, inv, s.vec[6:7, :]) * live
    old = norm_back(g, n_, inv, s.vec[6:7, :]) * live
    low = res.astype(BF).astype(F32)
    s.gv[5] += low - old.astype(BF).astype(F32)
    top = (lax.broadcasted_iota(jnp.int32, (16, 1), 0) == 0)
    for p in range(4):
        at = slice(p * LEN, p * LEN + 16)
        s.acc[at, :] = jnp.where(top, res[p : p + 1], s.acc[at, :])
        s.bg[at, :] = jnp.where(top, low[p : p + 1], s.bg[at, :].astype(F32)).astype(BF)


HBM = pl.BlockSpec(memory_space=pl.ANY)
G_MERGE = ((0, 2, NC),)
G_S23 = ((1, 1, NC),)
G_S4A = ((3, 1, NC),)
G_S34 = ((3, 1, NC),)
G_S45 = ((5, 1, NC),)
G_CORE = ((6, 1, NC),)
G_FULL = ((12, 1, 2), (15, 1, 1))
G_HALF = ((16, 1, 2),)
G_END = 18
S_K0 = ((0, 2, 8), (9, 2, 4))
S_K1 = ((1, 2, 8), (11, 2, 4))
S_K1B = ((2, 1, 8), (13, 2, 4))
S_K2 = ((2, 1, 8), (12, 2, 4))
S_K3 = ((4, 1, NC),)
S_K4 = ((11, 2, NC),)
S_K5 = ((12, 2, NC),)
S_K6 = ((15, 2, NC),)
S_END = 21
OUTS = dict(
    lo_out=((TOK, D), BF),
    hg_out=((TOK, D), BF),
    out=((6, 48, D), F32),
    q_out=((8, D), F32),
    bias_out=((8, 128), F32),
    loss=((8, 128), F32),
    cgrad=((8, D), F32),
)
VECTORS = (
    "query_bias",
    "value_bias",
    "attn_bias",
    "first_gain",
    "first_shift",
    "outer_bias",
    "second_gain",
    "second_shift",
    "inner_bias",
)
INS = ("x_in", "up_in") + ("w_query", "w_key", "w_value", "w_attn", "w_inner", "w_outer", "w_queries") + VECTORS
INS += ("loss_weight", "positive_ids", "positive_count")
SCRATCH = dict(
    wa=((6, 2, 2, 2, 2, 48, D), BF),
    wb=((6, 2, 2, 2, 2, 48, D), BF),
    rb=((6, 48, D), BF),
    pack=((6, 48, D), BF),
    qpack=((32, 128), BF),
    x=((TOK, D), BF),
    up=((TOK, D), BF),
    lo=((TOK, D), BF),
    hg=((TOK, D), BF),
    q=((TOK, D), BF),
    k=((TOK, D), BF),
    v=((TOK, D), BF),
    ctx=((TOK, D), BF),
    p=((4, 6, 128, 256), BF),
    fn=((TOK, D), F32),
    s1=((TOK, 1), F32),
    s2=((TOK, 1), F32),
    nl=((TOK, D), BF),
    acc=((TOK, D), F32),
    act=((4, TOK, D), BF),
    gp=((4, TOK, D), BF),
    bg=((TOK, D), BF),
    tmp=((TOK, D), F32),
    small=((256, 128), F32),
    tile=((8, 128), F32),
    qx=((2, 2, 2, 2, 48, 128), BF),
    qrb=((32, 128), BF),
    sc=((256, 128), F32),
    vec=((16, D), F32),
    gv=((12, 8, D), F32),
    aux=((8, 128), F32),
    qm=((D, 128), F32),
    cn=((8, D), F32),
    ci=((8, 1), F32),
    cls=((8, D), F32),
    qrow=((D, 128), F32),
    rc=((2, NC, 2, 2, 2, 48, LW), BF),
    r4a=((2, NC, 2, 48, LW), BF),
    r4b=((2, NC, 2, 48, LW), BF),
    r3b=((2, NC, 2, 48, LW), BF),
    r3a=((2, NC, 2, 48, LW), BF),
    r2=((2, NC, 48, LW), BF),
    st=((NC, 48, LW), BF),
    r1=((NC, 48, LW), BF),
    call=((512, 256), BF),
    sg=((256, 128), F32),
    pb=((256, 128), F32),
    zb=((4, 64, 128), F32),
    bb=((8, 8, 128), F32),
    half=((64, 128), F32),
)
SEMS = dict(
    gs=(7, 2),
    gr=(7, 2, NC),
    g1s=(1,),
    g1r=(NC,),
    xs=(8,),
    xr=(8,),
    zs=(4, 4),
    zr=(4, 4),
    bs=(4, 8),
    br=(4, 8),
    io=(4,),
)


class Spread:
    def __init__(self, p, s, ref, which, rows):
        self.p, self.s, self.ref, self.which, self.rows = p, s, ref, which, rows

    def zview(self, z):
        r = self.rows
        return self.ref.at[pl.ds(pl.multiple_of((self.p.b * 4 + z) * r, r), r), :]

    def bview(self, b):
        r = self.rows * 4
        return self.ref.at[pl.ds(pl.multiple_of(b * r, r), r), :]

    def zcopy(self, k, view):
        p, s, w = self.p, self.s, self.which
        return rcopy(view, view, s.zs.at[w, k], s.zr.at[w, k], (p.b, (p.z + k) % 4))

    def bcopy(self, k, view):
        p, s, w = self.p, self.s, self.which
        return rcopy(view, view, s.bs.at[w, k], s.br.at[w, k], ((p.b + k) % 8, p.z))

    def first(self):
        for k in range(1, 4):
            self.zcopy(k, self.zview(self.p.z)).start()

    def second(self):
        for k in range(1, 4):
            self.zcopy(k, self.zview((self.p.z + 4 - k) % 4)).wait_recv()
        for k in range(1, 8):
            self.bcopy(k, self.bview(self.p.b)).start()

    def finish(self):
        for k in range(1, 8):
            self.bcopy(k, self.bview((self.p.b + 8 - k) % 8)).wait_recv()
        for k in range(1, 4):
            self.zcopy(k, self.zview(self.p.z)).wait_send()
        for k in range(1, 8):
            self.bcopy(k, self.bview(self.p.b)).wait_send()


def gather_steps(p, s, me, vectors):
    def flows(ci):
        out = []
        for kind, ref in ((0, s.wa), (1, s.wb)):
            view = ref.at[ci // PARTS, :, :, :, :, :, lanes_of(ci)]
            out.append(
                Gather(
                    p,
                    view,
                    kind,
                    lambda st, kind=kind: s.gs.at[st, kind],
                    lambda st, kind=kind: s.gr.at[st, kind, ci],
                )
            )
        return out

    def s1(ci):
        at = (ci // PARTS, ALL, lanes_of(ci))
        return rcopy(s.pack.at[at], s.rb.at[at], s.g1s.at[0], s.g1r.at[ci], p.zdev)

    first = p.zl == 0

    def order(own, oth):
        return jnp.where(first, own, oth), jnp.where(first, oth, own)

    def merge(ci):
        s1(ci).wait_recv()
        i, ln = ci // PARTS, lanes_of(ci)
        lo, hi = order(s.pack[i, :, ln].astype(F32), s.rb[i, :, ln].astype(F32))
        s.wa[i, p.y, p.x, p.c, p.zh, :, ln] = jnp.concatenate([lo[:ROWS], hi[:ROWS]], 0).astype(BF)
        s.wb[i, p.y, p.x, p.c, p.zh, :, ln] = jnp.concatenate([lo[ROWS:], hi[ROWS:]], 0).astype(BF)
        for f in flows(ci):
            f.s2_send()

    def s23(fs):
        for f in fs:
            f.s2_recv()

        @pl.when(p.mid == 1)
        def _():
            for f in fs:
                f.s3a_send()

    def s4a(fs):
        for f in fs:
            f.s4a_send()

    def s34(fs):
        @pl.when(p.mid == 1)
        def _():
            for f in fs:
                f.s3a_recv()
                f.s3b_send()

        @pl.when(p.mid == 0)
        def _():
            for f in fs:
                f.s3b_recv()

        for f in fs:
            f.s4b_send()
            f.c1_send()

    def s45(fs):
        for f in fs:
            f.s4_recv()
            f.c2_send()

    def core(fs):
        for f in fs:
            f.c1_recv()
            f.c2_recv()

    def drain():
        for kind, ref in ((0, s.wa), (1, s.wb)):
            sems = lambda st, kind=kind: s.gs.at[st, kind]
            Gather(p, ref, kind, sems, sems, (ALL,)).drain()
        rcopy(s.pack, s.rb, s.g1s.at[0], s.g1r.at[0], p.zdev).wait_send()
        q.drain()

    for i in range(6):
        pack_weights(s, i)
        for h in range(PARTS):
            s1(PARTS * i + h).start()

    s.small[pl.ds(pl.multiple_of(me * 8, 8), 8), :] = pack_small(s)
    vectors.first()
    q = Gather(p, s.qx, 0, lambda st: s.xs.at[st], lambda st: s.xr.at[st])
    q1 = rcopy(s.qpack, s.qrb, s.xs.at[7], s.xr.at[7], p.zdev)
    q1.start()

    def qmerge():
        q1.wait()
        lo, hi = order(s.qpack[...].astype(F32), s.qrb[...].astype(F32))
        s.qx[p.y, p.x, p.c, p.zh] = jnp.concatenate([lo[:ROWS], hi[:ROWS]], 0).astype(BF)
        q.s2_send()

    def q23():
        s23([q])
        s4a([q])

    query_steps = [qmerge, q23, lambda: s34([q]), lambda: s45([q]), lambda: core([q])]

    def pack_of(fn):
        return lambda ci: fn(flows(ci))

    stages = (
        (G_MERGE, merge),
        (G_S23, pack_of(s23)),
        (G_S4A, pack_of(s4a)),
        (G_S34, pack_of(s34)),
        (G_S45, pack_of(s45)),
        (G_CORE, pack_of(core)),
    )
    return stages, query_steps, drain


def scatter_steps(p, s):
    def piece(ci):
        return (ci // PARTS + 2) % 6

    def flows(ci):
        made = []
        for kind, ref in ((0, s.wa), (1, s.wb)):
            bufs = tuple(buf.at[kind, ci] for buf in (s.rc, s.r4a, s.r4b, s.r3b, s.r3a, s.r2))
            made.append(
                Scatter(
                    p,
                    ref.at[piece(ci), :, :, :, :, :, lanes_of(ci)],
                    kind,
                    lambda st, kind=kind: s.gs.at[st, kind],
                    lambda st, kind=kind: s.gr.at[st, kind, ci],
                    bufs,
                )
            )
        return made

    def k0(ci):
        @pl.when(ci >= PARTS)
        def _():
            for f in flows(ci):
                f.t0_send()

    def early(kind):
        for ci in range(PARTS):
            flows(ci)[kind].t0_send()

    def k1(fs):
        for f in fs:
            f.t0_add()
            f.t1a_send()

    def k1b(fs):
        for f in fs:
            f.t1b_send()

    def k2(fs):
        for f in fs:
            f.t1a_add()

            @pl.when(p.mid == 0)
            def _(f=f):
                f.t2a_send()

    def k3(fs):
        @pl.when(p.mid == 1)
        def _():
            for f in fs:
                f.t2a_add()
                f.t2b_send()

    def k4(fs):
        for f in fs:
            f.t1b_add()

            @pl.when(p.mid == 1)
            def _(f=f):
                f.t2b_add()

            f.t3_send()

    first = p.zl == 0

    def halves(total):
        top, low = total[:ROWS], total[ROWS:]
        return jnp.where(first, top, low), jnp.where(first, low, top)

    def s1(ci):
        return rcopy(s.st.at[ci], s.r1.at[ci], s.g1s.at[0], s.g1r.at[ci], p.zdev)

    def k5(ci):
        fa, fb = flows(ci)
        keep_a, give_a = halves(fa.t3_sum())
        keep_b, give_b = halves(fb.t3_sum())
        s.st[ci] = jnp.concatenate([give_a, give_b], 0).astype(BF)
        s1(ci).start()
        s.out[piece(ci), :, lanes_of(ci)] = jnp.concatenate([keep_a, keep_b], 0)

    def k6(ci):
        s1(ci).wait_recv()
        at = (piece(ci), ALL, lanes_of(ci))
        s.out[at] = s.out[at] + s.r1[ci].astype(F32)

    def pack_of(fn):
        return lambda ci: fn(flows(ci))

    stages = (
        (S_K0, k0),
        (S_K1, pack_of(k1)),
        (S_K1B, pack_of(k1b)),
        (S_K2, pack_of(k2)),
        (S_K3, pack_of(k3)),
        (S_K4, pack_of(k4)),
        (S_K5, k5),
        (S_K6, k6),
    )
    def zcopy(k):
        dz = (p.z + k) % 4
        src = s.pb.at[pl.ds(pl.multiple_of(dz * 64, 64), 64), :]
        return rcopy(src, s.zb.at[k], s.zs.at[3, k], s.zr.at[3, k], (p.b, dz))

    def bcopy(k):
        db = (p.b + k) % 8
        src = s.half.at[pl.ds(pl.multiple_of(db * 8, 8), 8), :]
        return rcopy(src, s.bb.at[k], s.bs.at[3, k], s.br.at[3, k], (db, p.z))

    def vectors_out():
        pack_vectors(s)
        for k in range(1, 4):
            zcopy(k).start()

    def vectors_half():
        total = s.pb[pl.ds(pl.multiple_of(p.z * 64, 64), 64), :]
        for k in range(1, 4):
            zcopy(k).wait()
            total = total + s.zb[k]
        s.half[...] = total
        for k in range(1, 8):
            bcopy(k).start()

    def vectors_in():
        total = s.half[pl.ds(pl.multiple_of(p.b * 8, 8), 8), :]
        for k in range(1, 8):
            bcopy(k).wait()
            total = total + s.bb[k]
        s.bias_out[...] = total

    def drain():
        for kind, ref in ((0, s.wa), (1, s.wb)):
            sems = lambda st, kind=kind: s.gs.at[st, kind]
            Scatter(p, ref, kind, sems, sems, (None,) * 6, (ALL,)).drain()
        rcopy(s.st, s.r1, s.g1s.at[0], s.g1r.at[0], p.zdev).wait_send()

    return stages, (vectors_out, vectors_half, vectors_in), early, drain


def done_by(spans, t):
    total = 0
    for first, many, chunks in spans:
        total = total + jnp.minimum(jnp.maximum((t - first + 1) * many, 0), chunks)
    return total


def run_span(spans, t, fn):
    pl.loop(done_by(spans, t - 1), done_by(spans, t))(fn)


def run_stages(stages, t):
    for spans, fn in stages:
        run_span(spans, t, fn)


def run_at(t, table):
    for when, fn in table:

        @pl.when(t == when)
        def _(fn=fn):
            fn()


def layer_kernel(*refs):
    s = Bag()
    names = list(INS) + list(OUTS) + list(SCRATCH) + list(SEMS)
    for name, ref in zip(names, refs):
        setattr(s, name, ref)
    p = Place()
    greet(p)
    me = p.b * 4 + p.z
    vectors = Spread(p, s, s.small, 0, 8)
    scores = Spread(p, s, s.sc, 1, 8)
    firsts = Spread(p, s, s.call, 2, 16)
    copies = {
        name: pltpu.make_async_copy(src, dst, s.io.at[k])
        for k, (name, src, dst) in enumerate(
            (
                ("x", s.x_in, s.x),
                ("up", s.up_in, s.up),
                ("lo", s.lo, s.lo_out),
                ("hg", s.hg, s.hg_out),
            )
        )
    }
    copies["x"].start()
    copies["up"].start()
    stages, query_steps, drain = gather_steps(p, s, me, vectors)

    def passages(fn, lo, many):
        def go():
            pl.loop(lo, lo + many)(lambda i: fn(s, i))

        return go

    def small_done():
        vectors.finish()
        unpack_small(s)

    forward = [
        (1, copies["x"].wait),
        (1, copies["up"].wait),
        (2, vectors.second),
        (6, small_done),
        (7, lambda: queries_keys(s)),
        (9, lambda: values(s)),
        (9, passages(attn_fwd, 0, 1)),
        (10, passages(attn_fwd, 1, 2)),
        (11, passages(attn_fwd, 3, 1)),
        (11, lambda: attn_out(s)),
    ]
    forward += [(5 + 2 * k, fn) for k, fn in enumerate(query_steps)]
    forward += [(14, lambda: unpack_queries(s))]

    @pl.loop(0, G_END)
    def _(t):
        run_stages(stages, t)
        run_at(t, forward)
        run_span(G_FULL, t, lambda j: ffn_fwd(s, j, 0, D))
        run_span(G_HALF, t, lambda h: ffn_fwd(s, 3, h, LW))

    s.sc[pl.ds(pl.multiple_of(me * 8, 8), 8), :] = first_rows(s, me)
    scores.first()
    firsts.first()
    norm2(s)
    copies["lo"].start()
    scores.second()
    firsts.second()
    drain()
    s.gv[...] = jnp.zeros_like(s.gv)
    norm2_back(s)
    scores.finish()
    loss_part(s, me)
    add_cls(s)

    stages, vector_steps, early, drain = scatter_steps(p, s)
    outer_back(s, 0)
    early(1)
    inner_back(s, 0)
    early(0)
    def hidden():
        qkv_back(s)
        copies["hg"].start()

    def query():
        firsts.finish()
        query_gradient(s, me)

    backward = [
        (3, lambda: norm1_back(s)),
        (4, passages(attn_back, 0, 1)),
        (5, passages(attn_back, 1, 1)),
        (6, passages(attn_back, 2, 2)),
        (8, hidden),
        (9, query),
        (10, vector_steps[0]),
        (13, vector_steps[1]),
        (17, vector_steps[2]),
    ]

    @pl.loop(0, S_END)
    def _(t):
        run_stages(stages, t)

        @pl.when(t < 3)
        def _():
            ffn_back(s, t + 1)

        run_at(t, backward)

    drain()
    copies["lo"].wait()
    copies["hg"].wait()


SMEM = pl.BlockSpec(memory_space=pltpu.SMEM)


def layer(*args):
    return pl.pallas_call(
        layer_kernel,
        out_shape=tuple(jax.ShapeDtypeStruct(*o) for o in OUTS.values()),
        in_specs=[HBM] * 2 + [VM] * (len(INS) - 5) + [SMEM] * 3,
        out_specs=(HBM,) * 2 + (VM,) * 5,
        scratch_shapes=[pltpu.VMEM(*b) for b in SCRATCH.values()] + [DMA(n) for n in SEMS.values()],
        compiler_params=pltpu.CompilerParams(
            collective_id=1, has_side_effects=True, vmem_limit_bytes=VMEM_LIMIT
        ),
    )(*args)


def finish_kernel(
    lo_in, hg_in, out, q_out, bias, loss, cgrad,
    lo, hg, query_grad, query_loss, g_query, g_key, g_value, g_attn,
    g_qb, g_vb, g_ab, g_fg, g_fs, g_inner, g_ib, g_outer, g_ob, g_sg, g_ss, cls_grad, held, sems
):
    me = lax.axis_index("blk") * 4 + lax.axis_index("grp")
    into = [pltpu.make_async_copy(ref, held.at[k], sems.at[k]) for k, ref in enumerate((lo_in, hg_in))]
    away = [pltpu.make_async_copy(held.at[k], ref, sems.at[2 + k]) for k, ref in enumerate((lo, hg))]
    for move in into:
        move.start()
    for k in range(2):
        into[k].wait()
        away[k].start()
    query_grad[...] = q_out[0:4, :]
    cls_grad[...] = cgrad[0:4, :]
    g_query[...] = out[0, :ROWS]
    g_key[...] = out[0, ROWS:]
    g_value[...] = out[1, :ROWS]
    g_attn[...] = out[1, ROWS:]
    for j in range(4):
        at = slice(j * D, (j + 1) * D)
        g_inner[:, at] = out[2 + j, :ROWS]
        g_outer[:, at] = out[2 + j, ROWS:]
    for t, ref in enumerate((g_qb, g_vb, g_ab, g_fg, g_fs, g_ob, g_sg, g_ss)):
        ref[...] = pltpu.roll(bias[...], 32, 1)[t, :ROWS]
    g_ib[...] = bias[0, :96]
    query_loss[...] = pltpu.roll(loss[...], lax.rem(128 - 4 * me, 128), 1)[0, :4]
    for move in away:
        move.wait()


def finish(*args):
    f32 = lambda *dims: jax.ShapeDtypeStruct(dims, F32)
    square = f32(ROWS, D)
    vec = f32(ROWS)
    tokens = jax.ShapeDtypeStruct((TOK, D), BF)
    outs = [tokens, tokens, f32(4, D), f32(4)] + [square] * 4 + [vec] * 5
    outs += [f32(ROWS, 4 * D), f32(96), f32(ROWS, 4 * D), vec, vec, vec, f32(4, D)]
    return pl.pallas_call(
        finish_kernel,
        out_shape=outs,
        in_specs=[HBM] * 2 + [VM] * 5,
        out_specs=[HBM] * 2 + [VM] * 18,
        scratch_shapes=[pltpu.VMEM((2, TOK, D), BF), DMA((4,))],
        compiler_params=pltpu.CompilerParams(vmem_limit_bytes=VMEM_LIMIT),
    )(*args)


def fast_local(
    hidden_in,
    upstream_grad,
    query_vectors,
    loss_weight,
    positive_ids,
    positive_count,
    query_proj,
    key_proj,
    value_proj,
    attn_proj,
    query_bias,
    value_bias,
    attn_bias,
    first_gain,
    first_shift,
    inner_proj,
    inner_bias,
    outer_proj,
    outer_bias,
    second_gain,
    second_shift,
):
    results = layer(
        hidden_in.reshape(TOK, D),
        upstream_grad.reshape(TOK, D),
        query_proj,
        key_proj,
        value_proj,
        attn_proj.T,
        inner_proj,
        outer_proj.T,
        query_vectors,
        query_bias,
        value_bias,
        attn_bias,
        first_gain,
        first_shift,
        outer_bias,
        second_gain,
        second_shift,
        inner_bias,
        loss_weight,
        positive_ids,
        positive_count,
    )
    layer_output, hidden_grad, *rest = finish(*results)
    rest[5] = rest[5].T
    rest[13] = rest[13].T
    return (layer_output.reshape(hidden_in.shape), hidden_grad.reshape(hidden_in.shape), *rest)


def solution(mesh):
    in_specs = (
        P(("blk", "grp"), None, None),
        P(("blk", "grp"), None, None),
        P(("blk", "grp"), None),
        P(("blk", "grp")),
        P(("blk", "grp"), None),
        P(("blk", "grp")),
        P(("blk", "grp"), None),
        P(("blk", "grp"), None),
        P(("blk", "grp"), None),
        P(None, ("blk", "grp")),
        P(("blk", "grp")),
        P(("blk", "grp")),
        P(("blk", "grp")),
        P(("blk", "grp")),
        P(("blk", "grp")),
        P(("blk", "grp"), None),
        P(("blk", "grp")),
        P(None, ("blk", "grp")),
        P(("blk", "grp")),
        P(("blk", "grp")),
        P(("blk", "grp")),
    )
    out_specs = (
        P(("blk", "grp"), None, None),
        P(("blk", "grp"), None, None),
        P(("blk", "grp"), None),
        P(("blk", "grp")),
        P(("blk", "grp"), None),
        P(("blk", "grp"), None),
        P(("blk", "grp"), None),
        P(None, ("blk", "grp")),
        P(("blk", "grp")),
        P(("blk", "grp")),
        P(("blk", "grp")),
        P(("blk", "grp")),
        P(("blk", "grp")),
        P(("blk", "grp"), None),
        P(("blk", "grp")),
        P(None, ("blk", "grp")),
        P(("blk", "grp")),
        P(("blk", "grp")),
        P(("blk", "grp")),
        P(("blk", "grp"), None),
    )
    tiled = mesh.shape["blk"] == 8 and mesh.shape["grp"] == 4
    local = fast_local if tiled else plain_local
    return jax.shard_map(local, mesh=mesh, in_specs=in_specs, out_specs=out_specs, check_vma=False)
```

```python
import jax
import jax.numpy as jnp
from jax import lax
from jax.experimental import pallas as pl
from jax.experimental.pallas import tpu as pltpu
from jax.sharding import PartitionSpec as P

D = 768
HEADS = 12
HEAD_DIM = 64
LEN = 128


NORM_EPS = 1e-05
NEG_FILL = -1e30


def product(left_side, right_side):
    return jnp.dot(left_side, right_side, preferred_element_type=jnp.float32)


def contract(form_text, first_side, second_side):
    return jnp.einsum(form_text, first_side, second_side, preferred_element_type=jnp.float32)


def norm_forward(resid_sum, gain_vec, shift_vec):
    centered = resid_sum - jnp.mean(resid_sum, axis=-1, keepdims=True)
    inv_dev = lax.rsqrt(jnp.mean(centered * centered, axis=-1, keepdims=True) + NORM_EPS)
    normal_part = centered * inv_dev
    return (normal_part * gain_vec + shift_vec, normal_part, inv_dev)


def norm_backward(out_grad, normal_part, inv_dev, gain_vec):
    scaled_grad = out_grad * gain_vec
    mean_grad = jnp.mean(scaled_grad, axis=-1, keepdims=True)
    mean_cross = jnp.mean(scaled_grad * normal_part, axis=-1, keepdims=True)
    return inv_dev * (scaled_grad - mean_grad - normal_part * mean_cross)


def gelu_exact(pre_act):
    return jax.nn.gelu(pre_act, approximate=False)


def gelu_grad(pre_act, act_grad):
    unused_out, pullback = jax.vjp(gelu_exact, pre_act)
    return pullback(act_grad)[0]


def positive_block(positive_ids, positive_count, span_count):
    slot_live = (
        jnp.arange(positive_ids.shape[1], dtype=jnp.int32)[None, :] < positive_count[:, None]
    )
    passage_index = jnp.arange(span_count, dtype=jnp.int32)
    matches = (positive_ids[:, :, None] == passage_index[None, None, :]) & slot_live[:, :, None]
    return jnp.any(matches, axis=1)


def block_forward(block_in, attn_params, ffn_params):
    (
        query_proj,
        key_proj,
        value_proj,
        attn_proj,
        query_bias,
        value_bias,
        attn_bias,
        first_gain,
        first_shift,
    ) = attn_params
    inner_proj, inner_bias, outer_proj, outer_bias, second_gain, second_shift = ffn_params
    pass_count = block_in.shape[0]
    head_shape = (pass_count, LEN, HEADS, HEAD_DIM)
    tok_rows = block_in.reshape(pass_count * LEN, D)
    queries = ((product(tok_rows, query_proj) + query_bias) * 0.125).astype(jnp.bfloat16)
    keys_low = product(tok_rows, key_proj).astype(jnp.bfloat16)
    values_low = (product(tok_rows, value_proj) + value_bias).astype(jnp.bfloat16)
    scores = contract("bqhd,bkhd->bhqk", queries.reshape(head_shape), keys_low.reshape(head_shape))
    top_score = jnp.max(scores, axis=-1, keepdims=True)
    exp_terms = jnp.exp(scores - top_score)
    totals = jnp.sum(exp_terms, axis=-1, keepdims=True)
    probs_low = (exp_terms / totals).astype(jnp.bfloat16)
    log_norm = top_score + jnp.log(totals)
    context = contract("bhqk,bkhd->bqhd", probs_low, values_low.reshape(head_shape))
    context = context.reshape(pass_count * LEN, D).astype(jnp.bfloat16)
    attn_out = product(context, attn_proj) + attn_bias
    normed, first_normal, first_inv = norm_forward(
        tok_rows.astype(jnp.float32) + attn_out, first_gain, first_shift
    )
    normed_low = normed.astype(jnp.bfloat16)
    inner_pre = product(normed_low, inner_proj) + inner_bias
    activated = gelu_exact(inner_pre).astype(jnp.bfloat16)
    branch = product(activated, outer_proj) + outer_bias
    layer_f32, second_normal, second_inv = norm_forward(normed + branch, second_gain, second_shift)
    kept_state = (
        queries,
        keys_low,
        values_low,
        log_norm,
        context,
        first_normal,
        first_inv,
        normed_low,
        inner_pre,
        activated,
        second_normal,
        second_inv,
    )
    return (layer_f32, kept_state)


def block_backward(block_in, out_grad, kept_state, attn_params, ffn_params):
    (
        query_proj,
        key_proj,
        value_proj,
        attn_proj,
        query_bias,
        value_bias,
        attn_bias,
        first_gain,
        first_shift,
    ) = attn_params
    inner_proj, inner_bias, outer_proj, outer_bias, second_gain, second_shift = ffn_params
    (
        queries,
        keys_low,
        values_low,
        log_norm,
        context,
        first_normal,
        first_inv,
        normed_low,
        inner_pre,
        activated,
        second_normal,
        second_inv,
    ) = kept_state
    pass_count = block_in.shape[0]
    tok_count = pass_count * LEN
    head_shape = (pass_count, LEN, HEADS, HEAD_DIM)
    tok_rows = block_in.reshape(tok_count, D)
    grad_rows = out_grad.reshape(tok_count, D)
    grad_second_gain = jnp.sum(grad_rows * second_normal, axis=0)
    grad_second_shift = jnp.sum(grad_rows, axis=0)
    second_resid = norm_backward(grad_rows, second_normal, second_inv, second_gain)
    branch_grad = second_resid.astype(jnp.bfloat16)
    grad_outer_bias = jnp.sum(branch_grad.astype(jnp.float32), axis=0)
    grad_outer_proj = product(activated.T, branch_grad)
    inner_grad = gelu_grad(inner_pre, product(branch_grad, outer_proj.T)).astype(jnp.bfloat16)
    grad_inner_bias = jnp.sum(inner_grad.astype(jnp.float32), axis=0)
    grad_inner_proj = product(normed_low.T, inner_grad)
    normed_grad = second_resid + product(inner_grad, inner_proj.T)
    grad_first_gain = jnp.sum(normed_grad * first_normal, axis=0)
    grad_first_shift = jnp.sum(normed_grad, axis=0)
    first_resid = norm_backward(normed_grad, first_normal, first_inv, first_gain)
    attn_grad = first_resid.astype(jnp.bfloat16)
    grad_attn_bias = jnp.sum(attn_grad.astype(jnp.float32), axis=0)
    grad_attn_proj = product(context.T, attn_grad)
    context_grad = product(attn_grad, attn_proj.T).astype(jnp.bfloat16).reshape(head_shape)
    query_heads = queries.reshape(head_shape)
    key_heads = keys_low.reshape(head_shape)
    value_heads = values_low.reshape(head_shape)
    scores = contract("bqhd,bkhd->bhqk", query_heads, key_heads)
    prob_full = jnp.exp(scores - log_norm)
    values_grad = contract("bhqk,bqhd->bkhd", prob_full.astype(jnp.bfloat16), context_grad)
    values_grad = values_grad.astype(jnp.bfloat16).reshape(tok_count, D)
    prob_grad = contract("bqhd,bkhd->bhqk", context_grad, value_heads)
    score_grad = (
        prob_full * (prob_grad - jnp.sum(prob_full * prob_grad, axis=-1, keepdims=True))
    ).astype(jnp.bfloat16)
    queries_grad = (
        contract("bhqk,bkhd->bqhd", score_grad, key_heads)
        .astype(jnp.bfloat16)
        .reshape(tok_count, D)
    )
    keys_grad = (
        contract("bhqk,bqhd->bkhd", score_grad, query_heads)
        .astype(jnp.bfloat16)
        .reshape(tok_count, D)
    )
    grad_query_proj = product(tok_rows.T, queries_grad) * 0.125
    grad_query_bias = jnp.sum(queries_grad.astype(jnp.float32), axis=0) * 0.125
    grad_key_proj = product(tok_rows.T, keys_grad)
    grad_value_proj = product(tok_rows.T, values_grad)
    grad_value_bias = jnp.sum(values_grad.astype(jnp.float32), axis=0)
    hidden_grad = (
        first_resid
        + 0.125 * product(queries_grad, query_proj.T)
        + product(keys_grad, key_proj.T)
        + product(values_grad, value_proj.T)
    )
    attn_grads = (
        grad_query_proj,
        grad_key_proj,
        grad_value_proj,
        grad_attn_proj,
        grad_query_bias,
        grad_value_bias,
        grad_attn_bias,
        grad_first_gain,
        grad_first_shift,
    )
    ffn_grads = (
        grad_inner_proj,
        grad_inner_bias,
        grad_outer_proj,
        grad_outer_bias,
        grad_second_gain,
        grad_second_shift,
    )
    return (hidden_grad, attn_grads, ffn_grads)


def plain_local(
    hidden_in,
    upstream_grad,
    query_vectors,
    loss_weight,
    positive_ids,
    positive_count,
    query_proj,
    key_proj,
    value_proj,
    attn_proj,
    query_bias,
    value_bias,
    attn_bias,
    first_gain,
    first_shift,
    inner_proj,
    inner_bias,
    outer_proj,
    outer_bias,
    second_gain,
    second_shift,
):
    attn_params = (
        lax.all_gather(query_proj, ("blk", "grp"), axis=0, tiled=True),
        lax.all_gather(key_proj, ("blk", "grp"), axis=0, tiled=True),
        lax.all_gather(value_proj, ("blk", "grp"), axis=0, tiled=True),
        lax.all_gather(attn_proj, ("blk", "grp"), axis=1, tiled=True),
        lax.all_gather(query_bias, ("blk", "grp"), axis=0, tiled=True),
        lax.all_gather(value_bias, ("blk", "grp"), axis=0, tiled=True),
        lax.all_gather(attn_bias, ("blk", "grp"), axis=0, tiled=True),
        lax.all_gather(first_gain, ("blk", "grp"), axis=0, tiled=True),
        lax.all_gather(first_shift, ("blk", "grp"), axis=0, tiled=True),
    )
    ffn_params = (
        lax.all_gather(inner_proj, ("blk", "grp"), axis=0, tiled=True),
        lax.all_gather(inner_bias, ("blk", "grp"), axis=0, tiled=True),
        lax.all_gather(outer_proj, ("blk", "grp"), axis=1, tiled=True),
        lax.all_gather(outer_bias, ("blk", "grp"), axis=0, tiled=True),
        lax.all_gather(second_gain, ("blk", "grp"), axis=0, tiled=True),
        lax.all_gather(second_shift, ("blk", "grp"), axis=0, tiled=True),
    )
    pass_count = hidden_in.shape[0]
    layer_f32, kept_state = block_forward(hidden_in, attn_params, ffn_params)
    layer_output = layer_f32.astype(jnp.bfloat16).reshape(pass_count, LEN, D)
    cls_local = layer_output[:, 0, :]
    query_count = query_vectors.shape[0]
    lowest = jnp.full((query_count,), NEG_FILL, jnp.float32)
    cls_piece = lax.all_gather(cls_local, ("blk", "grp"), axis=0, tiled=True)
    top_all = lowest
    top_pos = lowest
    scores = contract("qd,pd->qp", query_vectors, cls_piece)
    hit_mask = positive_block(positive_ids, positive_count, cls_piece.shape[0])
    masked = jnp.where(hit_mask, scores, NEG_FILL)
    new_all = jnp.maximum(top_all, jnp.max(scores, axis=1))
    new_pos = jnp.maximum(top_pos, jnp.max(masked, axis=1))
    sum_all = jnp.sum(jnp.exp(scores - new_all[:, None]), axis=1)
    pos_terms = jnp.where(hit_mask, jnp.exp(masked - new_pos[:, None]), 0.0)
    sum_pos = jnp.sum(pos_terms, axis=1)
    top_all, sum_all, top_pos, sum_pos = (new_all, sum_all, new_pos, sum_pos)
    total_all = top_all + jnp.log(sum_all)
    total_pos = top_pos + jnp.log(sum_pos)
    cls_piece = lax.all_gather(cls_local, ("blk", "grp"), axis=0, tiled=True)
    scores = contract("qd,pd->qp", query_vectors, cls_piece)
    hit_mask = positive_block(positive_ids, positive_count, cls_piece.shape[0])
    masked = jnp.where(hit_mask, scores, NEG_FILL)
    weight_rows = loss_weight[:, None] * (
        jnp.exp(scores - total_all[:, None]) - jnp.exp(masked - total_pos[:, None])
    )
    weight_rows = weight_rows.astype(jnp.bfloat16)
    query_acc = product(weight_rows, cls_piece)
    query_loss = total_all - total_pos
    cls_grad = lax.psum_scatter(
        contract("qp,qd->pd", weight_rows, query_vectors),
        ("blk", "grp"),
        scatter_dimension=0,
        tiled=True,
    )
    grad_total = upstream_grad.astype(jnp.float32).at[:, 0, :].add(cls_grad)
    ffn_back = (
        lax.all_gather(inner_proj, ("blk", "grp"), axis=0, tiled=True),
        lax.all_gather(inner_bias, ("blk", "grp"), axis=0, tiled=True),
        lax.all_gather(outer_proj, ("blk", "grp"), axis=1, tiled=True),
        lax.all_gather(outer_bias, ("blk", "grp"), axis=0, tiled=True),
        lax.all_gather(second_gain, ("blk", "grp"), axis=0, tiled=True),
        lax.all_gather(second_shift, ("blk", "grp"), axis=0, tiled=True),
    )
    attn_back = (
        lax.all_gather(query_proj, ("blk", "grp"), axis=0, tiled=True),
        lax.all_gather(key_proj, ("blk", "grp"), axis=0, tiled=True),
        lax.all_gather(value_proj, ("blk", "grp"), axis=0, tiled=True),
        lax.all_gather(attn_proj, ("blk", "grp"), axis=1, tiled=True),
        lax.all_gather(query_bias, ("blk", "grp"), axis=0, tiled=True),
        lax.all_gather(value_bias, ("blk", "grp"), axis=0, tiled=True),
        lax.all_gather(attn_bias, ("blk", "grp"), axis=0, tiled=True),
        lax.all_gather(first_gain, ("blk", "grp"), axis=0, tiled=True),
        lax.all_gather(first_shift, ("blk", "grp"), axis=0, tiled=True),
    )
    hidden_part, attn_grads, ffn_grads = block_backward(
        hidden_in, grad_total, kept_state, attn_back, ffn_back
    )
    attn_shards = (
        lax.psum_scatter(attn_grads[0], ("blk", "grp"), scatter_dimension=0, tiled=True),
        lax.psum_scatter(attn_grads[1], ("blk", "grp"), scatter_dimension=0, tiled=True),
        lax.psum_scatter(attn_grads[2], ("blk", "grp"), scatter_dimension=0, tiled=True),
        lax.psum_scatter(attn_grads[3], ("blk", "grp"), scatter_dimension=1, tiled=True),
        lax.psum_scatter(attn_grads[4], ("blk", "grp"), scatter_dimension=0, tiled=True),
        lax.psum_scatter(attn_grads[5], ("blk", "grp"), scatter_dimension=0, tiled=True),
        lax.psum_scatter(attn_grads[6], ("blk", "grp"), scatter_dimension=0, tiled=True),
        lax.psum_scatter(attn_grads[7], ("blk", "grp"), scatter_dimension=0, tiled=True),
        lax.psum_scatter(attn_grads[8], ("blk", "grp"), scatter_dimension=0, tiled=True),
    )
    ffn_shards = (
        lax.psum_scatter(ffn_grads[0], ("blk", "grp"), scatter_dimension=0, tiled=True),
        lax.psum_scatter(ffn_grads[1], ("blk", "grp"), scatter_dimension=0, tiled=True),
        lax.psum_scatter(ffn_grads[2], ("blk", "grp"), scatter_dimension=1, tiled=True),
        lax.psum_scatter(ffn_grads[3], ("blk", "grp"), scatter_dimension=0, tiled=True),
        lax.psum_scatter(ffn_grads[4], ("blk", "grp"), scatter_dimension=0, tiled=True),
        lax.psum_scatter(ffn_grads[5], ("blk", "grp"), scatter_dimension=0, tiled=True),
    )
    hidden_grad = hidden_part.astype(jnp.bfloat16).reshape(pass_count, LEN, D)
    return (
        layer_output,
        hidden_grad,
        query_acc,
        query_loss,
        attn_shards[0],
        attn_shards[1],
        attn_shards[2],
        attn_shards[3],
        attn_shards[4],
        attn_shards[5],
        attn_shards[6],
        attn_shards[7],
        attn_shards[8],
        ffn_shards[0],
        ffn_shards[1],
        ffn_shards[2],
        ffn_shards[3],
        ffn_shards[4],
        ffn_shards[5],
        cls_grad,
    )


BF = jnp.bfloat16
F32 = jnp.float32
MESH = pl.DeviceIdType.MESH
VM = pl.BlockSpec(memory_space=pltpu.VMEM)
DMA = pltpu.SemaphoreType.DMA
ALL = slice(None)
VMEM_LIMIT = 60 * 2**20
LW = 384
PARTS = 2
NC = 6 * PARTS
ROWS = 24
TOK = 512


class Place:
    def __init__(self):
        self.b = lax.axis_index("blk")
        self.z = lax.axis_index("grp")
        self.y, self.x, self.c = self.b // 4, (self.b // 2) % 2, self.b % 2
        self.zh, self.zl = self.z // 2, self.z % 2
        self.mid = ((self.z + 1) // 2) % 2
        self.xdev = (self.b + 2 - 4 * self.x, self.z)
        self.ydev = (self.b + 4 - 8 * self.y, self.z)
        self.cdev = (self.b + 1 - 2 * self.c, self.z)
        self.zdev = (self.b, self.z + 1 - 2 * self.zl)
        self.fdev = (self.b, 3 - self.z)


def greet(p):
    bar = pltpu.get_barrier_semaphore()
    for k in range(1, 8):
        pl.semaphore_signal(bar, 1, device_id=((p.b + k) % 8, p.z), device_id_type=MESH)
    for k in range(1, 4):
        pl.semaphore_signal(bar, 1, device_id=(p.b, (p.z + k) % 4), device_id_type=MESH)
    pl.semaphore_wait(bar, 10)


def rcopy(src, dst, ss, rs, dev):
    return pltpu.make_async_remote_copy(
        src_ref=src, dst_ref=dst, send_sem=ss, recv_sem=rs, device_id=dev, device_id_type=MESH
    )


class Flow:
    def __init__(self, p, ref, kind, ss, rs, lead=()):
        self.p, self.ref, self.kind, self.ss, self.rs, self.lead = p, ref, kind, ss, rs, lead
        self.f, self.s = (p.x, p.y) if kind == 0 else (p.y, p.x)
        self.fdev, self.sdev = (p.xdev, p.ydev) if kind == 0 else (p.ydev, p.xdev)

    def at(self, f, s, zz, c=None):
        c = self.p.c if c is None else c
        return self.ref.at[self.lead + self.index(f, s, zz, c)]

    def index(self, f, s, zz, c):
        return (s, f, c, zz) if self.kind == 0 else (f, s, c, zz)

    def copy(self, stage, src, dst, dev):
        return rcopy(src, dst, self.ss(stage), self.rs(stage), dev)

    def go(self, stage, view, dev):
        self.copy(stage, view, view, dev).start()

    def got(self, stage, view):
        self.copy(stage, view, view, self.p.cdev).wait_recv()

    def sent(self, stage, view):
        self.copy(stage, view, view, self.p.cdev).wait_send()


class Gather(Flow):
    def s2_send(self):
        self.go(0, self.at(self.f, self.s, self.p.zh), self.fdev)

    def s2_recv(self):
        self.got(0, self.at(1 - self.f, self.s, self.p.zh))

    def s3a_send(self):
        self.go(1, self.at(ALL, self.s, self.p.zh), self.p.fdev)

    def s3a_recv(self):
        self.got(1, self.at(ALL, self.s, 1 - self.p.zh))

    def s3b_send(self):
        self.go(2, self.at(ALL, self.s, 1 - self.p.zh), self.p.zdev)

    def s3b_recv(self):
        self.got(2, self.at(ALL, self.s, 1 - self.p.zh))

    def s4a_send(self):
        self.go(3, self.at(ALL, self.s, self.p.zh), self.sdev)

    def s4b_send(self):
        self.go(4, self.at(ALL, self.s, 1 - self.p.zh), self.sdev)

    def s4_recv(self):
        self.got(3, self.at(ALL, 1 - self.s, self.p.zh))
        self.got(4, self.at(ALL, 1 - self.s, 1 - self.p.zh))

    def core_send(self):
        self.go(5, self.at(ALL, ALL, ALL), self.p.cdev)

    def core_recv(self):
        self.got(5, self.at(ALL, ALL, ALL, 1 - self.p.c))

    def drain(self):
        self.sent(0, self.at(self.f, self.s, self.p.zh))

        @pl.when(self.p.mid == 1)
        def _():
            self.sent(1, self.at(ALL, self.s, self.p.zh))
            self.sent(2, self.at(ALL, self.s, 1 - self.p.zh))

        self.sent(3, self.at(ALL, self.s, self.p.zh))
        self.sent(4, self.at(ALL, self.s, 1 - self.p.zh))
        self.sent(5, self.at(ALL, ALL, ALL))


def lanes_of(ci):
    return pl.ds(pl.multiple_of((ci % PARTS) * LW, 128), LW)


class Scatter(Flow):
    def __init__(self, p, ref, kind, ss, rs, bufs, lead=()):
        super().__init__(p, ref, kind, ss, rs, lead)
        self.rc, self.r4a, self.r4b, self.r3b, self.r3a, self.r2 = bufs

    def add(self, stage, buf, f, s, zz):
        self.copy(stage, buf, buf, self.p.cdev).wait_recv()
        at = self.index(f, s, zz, self.p.c)
        self.ref[at] = self.ref[at] + buf[...]

    def t0_send(self):
        self.copy(0, self.at(ALL, ALL, ALL, 1 - self.p.c), self.rc, self.p.cdev).start()

    def t0_add(self):
        self.add(0, self.rc, ALL, ALL, ALL)

    def t1a_send(self):
        self.copy(1, self.at(ALL, 1 - self.s, 1 - self.p.zh), self.r4a, self.sdev).start()

    def t1a_add(self):
        self.add(1, self.r4a, ALL, self.s, 1 - self.p.zh)

    def t1b_send(self):
        self.copy(5, self.at(ALL, 1 - self.s, self.p.zh), self.r4b, self.sdev).start()

    def t1b_add(self):
        self.add(5, self.r4b, ALL, self.s, self.p.zh)

    def t2a_send(self):
        self.copy(2, self.at(ALL, self.s, 1 - self.p.zh), self.r3b, self.p.zdev).start()

    def t2a_add(self):
        self.add(2, self.r3b, ALL, self.s, 1 - self.p.zh)

    def t2b_send(self):
        self.copy(3, self.at(ALL, self.s, 1 - self.p.zh), self.r3a, self.p.fdev).start()

    def t2b_add(self):
        self.add(3, self.r3a, ALL, self.s, self.p.zh)

    def t3_send(self):
        self.copy(4, self.at(1 - self.f, self.s, self.p.zh), self.r2, self.fdev).start()

    def t3_sum(self):
        self.copy(4, self.r2, self.r2, self.p.cdev).wait_recv()
        at = self.index(self.f, self.s, self.p.zh, self.p.c)
        return self.ref[at].astype(F32) + self.r2[...].astype(F32)

    def drain(self):
        self.sent(0, self.at(ALL, ALL, ALL, 1 - self.p.c))
        self.sent(1, self.at(ALL, 1 - self.s, 1 - self.p.zh))
        self.sent(5, self.at(ALL, 1 - self.s, self.p.zh))

        @pl.when(self.p.mid == 0)
        def _():
            self.sent(2, self.at(ALL, self.s, 1 - self.p.zh))

        @pl.when(self.p.mid == 1)
        def _():
            self.sent(3, self.at(ALL, self.s, 1 - self.p.zh))

        self.sent(4, self.at(1 - self.f, self.s, self.p.zh))


def nn(a, b): return lax.dot_general(a, b, (((1,), (0,)), ((), ())), preferred_element_type=F32)
def nt(a, b): return lax.dot_general(a, b, (((1,), (1,)), ((), ())), preferred_element_type=F32)
def tn(a, b): return lax.dot_general(a, b, (((0,), (0,)), ((), ())), preferred_element_type=F32)

def weight(ref, i): return ref[i].reshape(D, D)
def keep(ref, i, val): ref[i] = val.astype(BF).reshape(2, 2, 2, 2, 48, D)

def tiles(n, body, unroll=None):
    def f(r, c):
        body(pl.ds(pl.multiple_of(r * (TOK // n), TOK // n), TOK // n)); return c
    lax.fori_loop(0, n, f, 0, unroll=unroll)

def masks():
    lane = lax.broadcasted_iota(jnp.int32, (1, 128), 1)
    lo = (lane < 64).astype(F32).astype(BF)
    return lo, (1 - lo.astype(F32)).astype(BF)

def queries_keys(s):
    x = s.x[...]
    s.q[...] = ((nn(x, weight(s.wa, 0)) + s.vec[0:1, :]) * 0.125).astype(BF)
    s.k[...] = nn(x, weight(s.wb, 0)).astype(BF)


def values(s):
    s.v[...] = (nn(s.x[...], weight(s.wa, 1)) + s.vec[1:2, :]).astype(BF)


def split(x, lo, hi): return jnp.concatenate([x * lo, x * hi], 0)

def attn_fwd(s, p):
    lo, hi = masks()
    r = pl.ds(pl.multiple_of(p * 128, 128), 128)
    for h in range(6):
        ln = pl.ds(h * 128, 128)
        sc = nt(s.q[r, ln], split(s.k[r, ln], lo, hi))
        out = []
        for w in (sc[:, :128], sc[:, 128:]):
            e = jnp.exp(w - jnp.max(w, axis=1, keepdims=True))
            out.append((e * (1.0 / jnp.sum(e, axis=1, keepdims=True))).astype(BF))
        pr = jnp.concatenate(out, 1)
        s.p[p, h] = pr
        s.ctx[r, ln] = nn(pr, split(s.v[r, ln], lo, hi)).astype(BF)

def normalize(res):
    c = res - jnp.mean(res, axis=1, keepdims=True)
    inv = lax.rsqrt(jnp.mean(c * c, axis=1, keepdims=True) + NORM_EPS)
    return c * inv, inv

def attn_out(s, n=8):
    s.acc[...] = nt(s.ctx[...], weight(s.wb, 1))
    def body(r):
        n_, inv = normalize(s.x[r, :].astype(F32) + s.acc[r, :] + s.vec[2:3, :])
        s.fn[r, :] = n_
        s.s1[r, :] = inv
        s.nl[r, :] = (n_ * s.vec[3:4, :] + s.vec[4:5, :]).astype(BF)
        s.acc[r, :] = n_ * s.vec[3:4, :] + s.vec[4:5, :] + s.vec[5:6, :]
    tiles(2, body)

def gelu_parts(x):
    ax = jnp.abs(x) * 0.7071067811865476
    t = 1.0 / (1.0 + 0.3275911 * ax)
    e = jnp.exp(x * x * -0.5)
    poly = t * (0.254829592 + t * (-0.284496736 + t * (1.421413741 + t * (-1.453152027 + t * 1.061405429))))
    half = 0.5 * poly * e
    phi = jnp.where(x > 0, 1.0 - half, half)
    return phi, e * 0.3989422804014327

def ffn_fwd(s, j, h, width):
    ln = pl.ds(pl.multiple_of(h * width, 128), width) if width < D else ALL
    w_in = s.wa[2 + j, :, :, :, :, :, ln].reshape(D, width)
    w_out = s.wb[2 + j, :, :, :, :, :, ln].reshape(D, width)
    for r in (slice(0, 256), slice(256, 512)):
        x = nn(s.nl[r, :], w_in) + s.vec[pl.ds(8 + j, 1), ln]
        cdf, pdf = gelu_parts(x)
        act = (x * cdf).astype(BF)
        s.act[j, r, ln] = act
        s.gp[j, r, ln] = (cdf + x * pdf).astype(BF)
        s.acc[r, :] += nt(act, w_out)

def norm2(s):
    def body(r):
        n_, inv = normalize(s.acc[r, :])
        s.acc[r, :] = n_
        s.s2[r, :] = inv
        s.lo[r, :] = (n_ * s.vec[6:7, :] + s.vec[7:8, :]).astype(BF)
    tiles(2, body)

def norm_back(g, n_, inv, gain):
    sg = g * gain
    return inv * (sg - jnp.mean(sg, axis=1, keepdims=True) - n_ * jnp.mean(sg * n_, axis=1, keepdims=True))

def colsum(x): return jnp.sum(x.reshape(-1, 8, x.shape[-1]), axis=0)

def norm2_back(s):
    def body(r):
        g = s.up[r, :].astype(F32)
        n_ = s.acc[r, :]
        s.gv[6] += colsum(g * n_)
        s.gv[7] += colsum(g)
        res = norm_back(g, n_, s.s2[r, :], s.vec[6:7, :])
        s.acc[r, :] = res
        b = res.astype(BF)
        s.bg[r, :] = b
        s.gv[5] += colsum(b.astype(F32))
    tiles(2, body)

def outer_back(s, j):
    s.tmp[...] = nn(s.bg[...], weight(s.wb, 2 + j))
    keep(s.wb, 2 + j, tn(s.bg[...], s.act[j]))


def inner_back(s, j):
    def ew(r):
        ig = (s.tmp[r, :] * s.gp[j, r, :].astype(F32)).astype(BF)
        s.gp[j, r, :] = ig
        s.gv[8 + j] += colsum(ig.astype(F32))

    tiles(2, ew)
    s.acc[...] += nt(s.gp[j], weight(s.wa, 2 + j))
    keep(s.wa, 2 + j, tn(s.nl[...], s.gp[j]))


def ffn_back(s, j):
    outer_back(s, j)
    inner_back(s, j)


def norm1_back(s):
    def body(r):
        g = s.acc[r, :]
        n_ = s.fn[r, :]
        s.gv[3] += colsum(g * n_)
        s.gv[4] += colsum(g)
        res = norm_back(g, n_, s.s1[r, :], s.vec[3:4, :])
        s.acc[r, :] = res
        b = res.astype(BF)
        s.bg[r, :] = b
        s.gv[2] += colsum(b.astype(F32))
    tiles(2, body)
    s.nl[...] = nn(s.bg[...], weight(s.wb, 1)).astype(BF)
    keep(s.wb, 1, tn(s.bg[...], s.ctx[...]))

def attn_back(s, p):
    lo, hi = masks()
    r = pl.ds(pl.multiple_of(p * 128, 128), 128)
    for h in range(6):
        ln = pl.ds(h * 128, 128)
        qp, kp, vp, cg = s.q[r, ln], s.k[r, ln], s.v[r, ln], s.nl[r, ln]
        dp = nt(cg, split(vp, lo, hi))
        pr = s.p[p, h]
        prf = pr.astype(F32)
        t = prf * dp
        ds = []
        for a, b in ((0, 128), (128, 256)):
            ds.append((t[:, a:b] - prf[:, a:b] * jnp.sum(t[:, a:b], axis=1, keepdims=True)).astype(BF))
        dq = nn(jnp.concatenate(ds, 1), split(kp, lo, hi))
        dk = tn(jnp.concatenate(ds, 0), split(qp, lo, hi))
        dv = tn(jnp.concatenate([pr[:, :128], pr[:, 128:]], 0), split(cg, lo, hi))
        s.q[r, ln] = dq.astype(BF)
        s.k[r, ln] = dk.astype(BF)
        s.v[r, ln] = dv.astype(BF)

def qkv_back(s):
    s.acc[...] += 0.125 * nt(s.q[...], weight(s.wa, 0))
    s.acc[...] += nt(s.k[...], weight(s.wb, 0))
    s.hg[...] = (s.acc[...] + nt(s.v[...], weight(s.wa, 1))).astype(BF)
    def sums(r):
        s.gv[0] += colsum(s.q[r, :].astype(F32)) * 0.125
        s.gv[1] += colsum(s.v[r, :].astype(F32))
    tiles(2, sums)
    keep(s.wa, 1, tn(s.x[...], s.v[...]))
    keep(s.wa, 0, tn(s.x[...], s.q[...]) * 0.125)
    keep(s.wb, 0, tn(s.x[...], s.k[...]))


class Bag:
    pass


def column_maps(width, offset, first):
    lane = lax.broadcasted_iota(jnp.int32, (128, D), 0).astype(F32)
    col = lax.broadcasted_iota(jnp.int32, (128, D), 1).astype(F32) + first
    owner = jnp.floor((col + 0.5) * (1.0 / width))
    hot = ((lane - offset) == (col - owner * width)).astype(F32)
    return hot, owner[0:1]


def pack_weights(s, i):
    if i == 0:
        top, low = s.w_query[...].astype(F32), s.w_key[...].astype(F32)
    elif i == 1:
        top, low = s.w_value[...].astype(F32), s.w_attn[...].astype(F32)
    else:
        at = slice((i - 2) * D, (i - 1) * D)
        top, low = s.w_inner[:, at].astype(F32), s.w_outer[:, at].astype(F32)
    s.pack[i] = jnp.concatenate([top, low], 0).astype(BF)


def pack_small(s):
    for t, name in enumerate(VECTORS[:8]):
        s.tile[t : t + 1, 0:ROWS] = getattr(s, name)[...].astype(F32).reshape(1, ROWS)
    row = lax.broadcasted_iota(jnp.int32, (8, 128), 0)
    lane = lax.broadcasted_iota(jnp.int32, (8, 128), 1)
    tile = jnp.where(lane < ROWS, s.tile[...], 0.0)
    inner = s.inner_bias[...].astype(F32).reshape(1, 96)
    inner = pltpu.roll(jnp.concatenate([inner, jnp.zeros((1, 32), F32)], 1), ROWS, 1)
    tile = jnp.where((row == 0) & (lane >= ROWS) & (lane < ROWS + 96), inner, tile)
    for q in range(4):
        values = [s.positive_ids[q, k].astype(F32) for k in range(3)]
        values += [s.positive_count[q].astype(F32), s.loss_weight[q]]
        for t, value in enumerate(values):
            tile = jnp.where((row == t) & (lane == 120 + q), value, tile)
    queries = s.w_queries[...].astype(F32)
    rows = [queries[q : q + 1, k * 128 : (k + 1) * 128] for q in range(4) for k in range(6)]
    s.qpack[...] = jnp.concatenate(rows + [jnp.zeros((8, 128), F32)], 0).astype(BF)
    return tile


def unpack_small(s):
    sm = s.small[...]
    hot, owner = column_maps(24, 0, 0.0)
    dev = jnp.floor((lax.broadcasted_iota(jnp.int32, (256, 1), 0).astype(F32) + 0.5) * 0.125)
    wide = jnp.where(dev == owner, nn(sm.astype(BF), hot.astype(BF)), 0.0)
    s.vec[0:8, :] = jnp.sum(wide.reshape(32, 8, D), axis=0)
    one = s.small[pl.ds(0, 32, stride=8), :].astype(BF)
    dev32 = lax.broadcasted_iota(jnp.int32, (32, 1), 0).astype(F32)
    rows = []
    for j in range(4):
        hot, owner = column_maps(96, 24, float(D * j))
        part = jnp.where(dev32 == owner, nn(one, hot.astype(BF)), 0.0)
        rows.append(jnp.sum(part, axis=0, keepdims=True))
    s.vec[8:16, :] = jnp.concatenate(rows + [jnp.zeros((4, D), F32)], 0)
    hot, owner = column_maps(4, 120, 0.0)
    part = lax.dot_general(
        sm, hot[:, :128], (((1,), (0,)), ((), ())), precision=lax.Precision.HIGHEST, preferred_element_type=F32
    )
    part = jnp.where(dev == owner[:, :128], part, 0.0)
    s.aux[...] = jnp.sum(part.reshape(32, 8, 128), axis=0)


def unpack_queries(s):
    s.qrow[...] = s.qx[...].reshape(D, 128).astype(F32)
    for q in range(4):
        for k in range(6):
            piece = s.qrow[pl.ds(6 * q + k, 32, stride=24), :]
            s.qm[pl.ds(k * 128 + q, 32, stride=4), :] = piece


def all_queries(s):
    return jnp.concatenate([s.qm[k * 128 : (k + 1) * 128, :] for k in range(6)], 1).astype(BF)


def first_rows(s, me):
    rows = [s.acc[p * LEN : p * LEN + 8, :][0:1] for p in range(4)]
    n_, inv = normalize(jnp.concatenate(rows + [jnp.zeros((4, D), F32)], 0))
    s.cn[...] = n_
    s.ci[...] = inv
    cls = (n_ * s.vec[6:7, :] + s.vec[7:8, :]).astype(BF)
    low = cls.astype(F32)
    s.cls[...] = low
    parts = [low[0:4, k * 256 : (k + 1) * 256] for k in range(3)]
    tile = jnp.concatenate(parts + [jnp.zeros((4, 256), F32)], 0).astype(BF)
    s.call[pl.ds(pl.multiple_of(me * 16, 16), 16), :] = tile
    return nt(cls, all_queries(s))


def loss_part(s, me):
    scores = s.sc[...]
    row = lax.broadcasted_iota(jnp.int32, (256, 1), 0).astype(F32)
    dev = jnp.floor((row + 0.5) * 0.125)
    slot = row - 8.0 * dev
    real = slot < 4.0
    passage = 4.0 * dev + slot
    ids, count, weight_q = s.aux[0:3, :], s.aux[3:4, :], s.aux[4:5, :]

    def hits(passage):
        return (
            (ids[0:1] == passage)
            | ((ids[1:2] == passage) & (count > 1.5))
            | ((ids[2:3] == passage) & (count > 2.5))
        )

    everyone = jnp.where(real, scores, NEG_FILL)
    masked = jnp.where(hits(passage) & real, scores, NEG_FILL)
    totals = []
    for part in (everyone, masked):
        top = jnp.max(part, axis=0, keepdims=True)
        totals.append(top + jnp.log(jnp.sum(jnp.exp(part - top), axis=0, keepdims=True)))
    total_all, total_pos = totals
    s.loss[...] = jnp.broadcast_to(total_all - total_pos, (8, 128))
    pull = jnp.where(hits(passage) & real, jnp.exp(scores - total_pos), 0.0)
    grad = jnp.where(real, weight_q * (jnp.exp(jnp.where(real, scores - total_all, 0.0)) - pull), 0.0)
    s.sg[...] = grad
    own = s.sg[pl.ds(pl.multiple_of(me * 8, 8), 8), :].astype(BF)
    s.cgrad[...] = nn(own, all_queries(s))


def query_gradient(s, me):
    own = pltpu.roll(s.sg[...], lax.rem(128 - 4 * me, 128), 1).reshape(32, 8, 128)[:, :4]
    vectors = s.call[...]
    for k in range(3):
        pieces = [jnp.zeros((32, 4, 128), F32)] * k + [own] + [jnp.zeros((32, 4, 128), F32)] * (3 - k)
        grad = jnp.concatenate(pieces, 1).reshape(512, 128).astype(BF)
        s.q_out[:, k * 256 : (k + 1) * 256] = tn(grad, vectors)[0:8]


def pack_vectors(s):
    vec = jnp.sum(s.gv[...], axis=1)
    first = lax.broadcasted_iota(jnp.int32, (8, 96), 0) == 0
    for dev in range(32):
        b, z = dev // 4, dev % 4
        wide = vec[0:8, ROWS * dev : ROWS * (dev + 1)]
        at = 96 * (dev % 8)
        inner = jnp.where(first, vec[8 + dev // 8 : 9 + dev // 8, at : at + 96], 0.0)
        tile = jnp.concatenate([inner, wide, jnp.zeros((8, 8), F32)], 1)
        s.pb[(z * 8 + b) * 8 : (z * 8 + b + 1) * 8, :] = tile


def add_cls(s):
    g = jnp.concatenate([s.up[p * LEN : p * LEN + 16, :][0:1].astype(F32) for p in range(4)] + [jnp.zeros((4, D), F32)], 0)
    extra = s.cgrad[...]
    live = (lax.broadcasted_iota(jnp.int32, (8, 1), 0) < 4).astype(F32)
    n_, inv = s.cn[...] * live, s.ci[...]
    s.gv[6] += extra * n_
    s.gv[7] += extra
    res = norm_back(g + extra, n_, inv, s.vec[6:7, :]) * live
    old = norm_back(g, n_, inv, s.vec[6:7, :]) * live
    low = res.astype(BF).astype(F32)
    s.gv[5] += low - old.astype(BF).astype(F32)
    top = (lax.broadcasted_iota(jnp.int32, (16, 1), 0) == 0)
    for p in range(4):
        at = slice(p * LEN, p * LEN + 16)
        s.acc[at, :] = jnp.where(top, res[p : p + 1], s.acc[at, :])
        s.bg[at, :] = jnp.where(top, low[p : p + 1], s.bg[at, :].astype(F32)).astype(BF)


HBM = pl.BlockSpec(memory_space=pl.ANY)
G_MERGE = ((0, 2, NC),)
G_S23 = ((1, 1, NC),)
G_S4A = ((3, 1, NC),)
G_S34 = ((3, 1, NC),)
G_S45 = ((5, 1, NC),)
G_CORE = ((6, 1, NC),)
G_FULL = ((12, 1, 2), (15, 1, 1))
G_HALF = ((16, 1, 2),)
G_END = 18
S_K0 = ((0, 2, 8), (9, 2, 4))
S_K1 = ((1, 2, 8), (11, 2, 4))
S_K1B = ((2, 1, 8), (13, 2, 4))
S_K2 = ((2, 1, 8), (12, 2, 4))
S_K3 = ((4, 1, NC),)
S_K4 = ((11, 2, NC),)
S_K5 = ((12, 2, NC),)
S_K6 = ((15, 2, NC),)
S_END = 21
OUTS = dict(
    lo_out=((TOK, D), BF),
    hg_out=((TOK, D), BF),
    sums_out=((6, 48, D), F32),
    q_out=((8, D), F32),
    bias_out=((8, 128), F32),
    loss=((8, 128), F32),
    cgrad=((8, D), F32),
)
VECTORS = (
    "query_bias",
    "value_bias",
    "attn_bias",
    "first_gain",
    "first_shift",
    "outer_bias",
    "second_gain",
    "second_shift",
    "inner_bias",
)
INS = ("x_in", "up_in") + ("w_query", "w_key", "w_value", "w_attn", "w_inner", "w_outer", "w_queries") + VECTORS
INS += ("loss_weight", "positive_ids", "positive_count")
SCRATCH = dict(
    wa=((6, 2, 2, 2, 2, 48, D), BF),
    wb=((6, 2, 2, 2, 2, 48, D), BF),
    rb=((6, 48, D), BF),
    pack=((6, 48, D), BF),
    qpack=((32, 128), BF),
    x=((TOK, D), BF),
    up=((TOK, D), BF),
    lo=((TOK, D), BF),
    hg=((TOK, D), BF),
    out=((6, 48, D), F32),
    q=((TOK, D), BF),
    k=((TOK, D), BF),
    v=((TOK, D), BF),
    ctx=((TOK, D), BF),
    p=((4, 6, 128, 256), BF),
    fn=((TOK, D), F32),
    s1=((TOK, 1), F32),
    s2=((TOK, 1), F32),
    nl=((TOK, D), BF),
    acc=((TOK, D), F32),
    act=((4, TOK, D), BF),
    gp=((4, TOK, D), BF),
    bg=((TOK, D), BF),
    tmp=((TOK, D), F32),
    small=((256, 128), F32),
    tile=((8, 128), F32),
    qx=((2, 2, 2, 2, 48, 128), BF),
    qrb=((32, 128), BF),
    sc=((256, 128), F32),
    vec=((16, D), F32),
    gv=((12, 8, D), F32),
    aux=((8, 128), F32),
    qm=((D, 128), F32),
    cn=((8, D), F32),
    ci=((8, 1), F32),
    cls=((8, D), F32),
    qrow=((D, 128), F32),
    rc=((2, NC, 2, 2, 2, 48, LW), BF),
    r4a=((2, NC, 2, 48, LW), BF),
    r4b=((2, NC, 2, 48, LW), BF),
    r3b=((2, NC, 2, 48, LW), BF),
    r3a=((2, NC, 2, 48, LW), BF),
    r2=((2, NC, 48, LW), BF),
    st=((NC, 48, LW), BF),
    r1=((NC, 48, LW), BF),
    call=((512, 256), BF),
    sg=((256, 128), F32),
    pb=((256, 128), F32),
    zb=((4, 64, 128), F32),
    bb=((8, 8, 128), F32),
    half=((64, 128), F32),
)
SEMS = dict(
    gs=(6, 2),
    gr=(6, 2, NC),
    g1s=(1,),
    g1r=(NC,),
    xs=(8,),
    xr=(8,),
    zs=(3, 4),
    zr=(3, 4),
    bs=(3, 8),
    br=(3, 8),
    io=(5,),
)


class Spread:
    def __init__(self, p, s, ref, which, rows):
        self.p, self.s, self.ref, self.which, self.rows = p, s, ref, which, rows

    def zview(self, z):
        r = self.rows
        return self.ref.at[pl.ds(pl.multiple_of((self.p.b * 4 + z) * r, r), r), :]

    def bview(self, b):
        r = self.rows * 4
        return self.ref.at[pl.ds(pl.multiple_of(b * r, r), r), :]

    def zcopy(self, k, view):
        p, s, w = self.p, self.s, self.which
        return rcopy(view, view, s.zs.at[w, k], s.zr.at[w, k], (p.b, (p.z + k) % 4))

    def bcopy(self, k, view):
        p, s, w = self.p, self.s, self.which
        return rcopy(view, view, s.bs.at[w, k], s.br.at[w, k], ((p.b + k) % 8, p.z))

    def first(self):
        for k in range(1, 4):
            self.zcopy(k, self.zview(self.p.z)).start()

    def second(self):
        for k in range(1, 4):
            self.zcopy(k, self.zview((self.p.z + 4 - k) % 4)).wait_recv()
        for k in range(1, 8):
            self.bcopy(k, self.bview(self.p.b)).start()

    def finish(self):
        for k in range(1, 8):
            self.bcopy(k, self.bview((self.p.b + 8 - k) % 8)).wait_recv()
        for k in range(1, 4):
            self.zcopy(k, self.zview(self.p.z)).wait_send()
        for k in range(1, 8):
            self.bcopy(k, self.bview(self.p.b)).wait_send()


def gather_steps(p, s, me, vectors):
    def flows(ci):
        out = []
        for kind, ref in ((0, s.wa), (1, s.wb)):
            view = ref.at[ci // PARTS, :, :, :, :, :, lanes_of(ci)]
            out.append(
                Gather(
                    p,
                    view,
                    kind,
                    lambda st, kind=kind: s.gs.at[st, kind],
                    lambda st, kind=kind: s.gr.at[st, kind, ci],
                )
            )
        return out

    def s1(ci):
        at = (ci // PARTS, ALL, lanes_of(ci))
        return rcopy(s.pack.at[at], s.rb.at[at], s.g1s.at[0], s.g1r.at[ci], p.zdev)

    first = p.zl == 0

    def order(own, oth):
        return jnp.where(first, own, oth), jnp.where(first, oth, own)

    def merge(ci):
        s1(ci).wait_recv()
        i, ln = ci // PARTS, lanes_of(ci)
        lo, hi = order(s.pack[i, :, ln].astype(F32), s.rb[i, :, ln].astype(F32))
        s.wa[i, p.y, p.x, p.c, p.zh, :, ln] = jnp.concatenate([lo[:ROWS], hi[:ROWS]], 0).astype(BF)
        s.wb[i, p.y, p.x, p.c, p.zh, :, ln] = jnp.concatenate([lo[ROWS:], hi[ROWS:]], 0).astype(BF)
        for f in flows(ci):
            f.s2_send()

    def s23(fs):
        for f in fs:
            f.s2_recv()

        @pl.when(p.mid == 1)
        def _():
            for f in fs:
                f.s3a_send()

    def s4a(fs):
        for f in fs:
            f.s4a_send()

    def s34(fs):
        @pl.when(p.mid == 1)
        def _():
            for f in fs:
                f.s3a_recv()
                f.s3b_send()

        @pl.when(p.mid == 0)
        def _():
            for f in fs:
                f.s3b_recv()

        for f in fs:
            f.s4b_send()

    def s45(fs):
        for f in fs:
            f.s4_recv()
            f.core_send()

    def core(fs):
        for f in fs:
            f.core_recv()

    def drain():
        for kind, ref in ((0, s.wa), (1, s.wb)):
            sems = lambda st, kind=kind: s.gs.at[st, kind]
            Gather(p, ref, kind, sems, sems, (ALL,)).drain()
        rcopy(s.pack, s.rb, s.g1s.at[0], s.g1r.at[0], p.zdev).wait_send()
        q.drain()

    q = Gather(p, s.qx, 0, lambda st: s.xs.at[st], lambda st: s.xr.at[st])
    q1 = rcopy(s.qpack, s.qrb, s.xs.at[7], s.xr.at[7], p.zdev)
    for i in range(6):
        pack_weights(s, i)
        for h in range(PARTS):
            s1(PARTS * i + h).start()
        if i == 0:
            s.small[pl.ds(pl.multiple_of(me * 8, 8), 8), :] = pack_small(s)
            vectors.first()
            q1.start()

    def qmerge():
        q1.wait()
        lo, hi = order(s.qpack[...].astype(F32), s.qrb[...].astype(F32))
        s.qx[p.y, p.x, p.c, p.zh] = jnp.concatenate([lo[:ROWS], hi[:ROWS]], 0).astype(BF)
        q.s2_send()

    def q23():
        s23([q])
        s4a([q])

    query_steps = [qmerge, q23, lambda: s34([q]), lambda: s45([q]), lambda: core([q])]

    def pack_of(fn):
        return lambda ci: fn(flows(ci))

    stages = (
        (G_MERGE, merge),
        (G_S23, pack_of(s23)),
        (G_S4A, pack_of(s4a)),
        (G_S34, pack_of(s34)),
        (G_S45, pack_of(s45)),
        (G_CORE, pack_of(core)),
    )
    return stages, query_steps, drain


def scatter_steps(p, s):
    def piece(ci):
        return (ci // PARTS + 2) % 6

    def flows(ci):
        made = []
        for kind, ref in ((0, s.wa), (1, s.wb)):
            bufs = tuple(buf.at[kind, ci] for buf in (s.rc, s.r4a, s.r4b, s.r3b, s.r3a, s.r2))
            made.append(
                Scatter(
                    p,
                    ref.at[piece(ci), :, :, :, :, :, lanes_of(ci)],
                    kind,
                    lambda st, kind=kind: s.gs.at[st, kind],
                    lambda st, kind=kind: s.gr.at[st, kind, ci],
                    bufs,
                )
            )
        return made

    def k0(ci):
        @pl.when(ci >= PARTS)
        def _():
            for f in flows(ci):
                f.t0_send()

    def early(kind):
        for ci in range(PARTS):
            flows(ci)[kind].t0_send()

    def k1(fs):
        for f in fs:
            f.t0_add()
            f.t1a_send()

    def k1b(fs):
        for f in fs:
            f.t1b_send()

    def k2(fs):
        for f in fs:
            f.t1a_add()

            @pl.when(p.mid == 0)
            def _(f=f):
                f.t2a_send()

    def k3(fs):
        @pl.when(p.mid == 1)
        def _():
            for f in fs:
                f.t2a_add()
                f.t2b_send()

    def k4(fs):
        for f in fs:
            f.t1b_add()

            @pl.when(p.mid == 1)
            def _(f=f):
                f.t2b_add()

            f.t3_send()

    first = p.zl == 0

    def halves(total):
        top, low = total[:ROWS], total[ROWS:]
        return jnp.where(first, top, low), jnp.where(first, low, top)

    def s1(ci):
        return rcopy(s.st.at[ci], s.r1.at[ci], s.g1s.at[0], s.g1r.at[ci], p.zdev)

    def k5(ci):
        fa, fb = flows(ci)
        keep_a, give_a = halves(fa.t3_sum())
        keep_b, give_b = halves(fb.t3_sum())
        s.st[ci] = jnp.concatenate([give_a, give_b], 0).astype(BF)
        s1(ci).start()
        s.out[piece(ci), :, lanes_of(ci)] = jnp.concatenate([keep_a, keep_b], 0)

    def k6(ci):
        s1(ci).wait_recv()
        at = (piece(ci), ALL, lanes_of(ci))
        s.out[at] = s.out[at] + s.r1[ci].astype(F32)
        pltpu.make_async_copy(s.out.at[at], s.sums_out.at[at], s.io.at[4]).start()

    def pack_of(fn):
        return lambda ci: fn(flows(ci))

    stages = (
        (S_K0, k0),
        (S_K1, pack_of(k1)),
        (S_K1B, pack_of(k1b)),
        (S_K2, pack_of(k2)),
        (S_K3, pack_of(k3)),
        (S_K4, pack_of(k4)),
        (S_K5, k5),
        (S_K6, k6),
    )
    def zcopy(k):
        dz = (p.z + k) % 4
        src = s.pb.at[pl.ds(pl.multiple_of(dz * 64, 64), 64), :]
        return rcopy(src, s.zb.at[k], s.zs.at[0, k], s.zr.at[0, k], (p.b, dz))

    def bcopy(k):
        db = (p.b + k) % 8
        src = s.half.at[pl.ds(pl.multiple_of(db * 8, 8), 8), :]
        return rcopy(src, s.bb.at[k], s.bs.at[0, k], s.br.at[0, k], (db, p.z))

    def vectors_out():
        pack_vectors(s)
        for k in range(1, 4):
            zcopy(k).start()

    def vectors_half():
        total = s.pb[pl.ds(pl.multiple_of(p.z * 64, 64), 64), :]
        for k in range(1, 4):
            zcopy(k).wait()
            total = total + s.zb[k]
        s.half[...] = total
        for k in range(1, 8):
            bcopy(k).start()

    def vectors_in():
        total = s.half[pl.ds(pl.multiple_of(p.b * 8, 8), 8), :]
        for k in range(1, 8):
            bcopy(k).wait()
            total = total + s.bb[k]
        s.bias_out[...] = total

    def drain():
        for kind, ref in ((0, s.wa), (1, s.wb)):
            sems = lambda st, kind=kind: s.gs.at[st, kind]
            Scatter(p, ref, kind, sems, sems, (None,) * 6, (ALL,)).drain()
        rcopy(s.st, s.r1, s.g1s.at[0], s.g1r.at[0], p.zdev).wait_send()

    return stages, (vectors_out, vectors_half, vectors_in), early, drain


def done_by(spans, t):
    total = 0
    for first, many, chunks in spans:
        total = total + jnp.minimum(jnp.maximum((t - first + 1) * many, 0), chunks)
    return total


def run_span(spans, t, fn):
    pl.loop(done_by(spans, t - 1), done_by(spans, t))(fn)


def run_stages(stages, t):
    for spans, fn in stages:
        run_span(spans, t, fn)


def run_at(t, table):
    for when, fn in table:

        @pl.when(t == when)
        def _(fn=fn):
            fn()


def layer_kernel(*refs):
    s = Bag()
    names = list(INS) + list(OUTS) + list(SCRATCH) + list(SEMS)
    for name, ref in zip(names, refs):
        setattr(s, name, ref)
    p = Place()
    greet(p)
    me = p.b * 4 + p.z
    vectors = Spread(p, s, s.small, 0, 8)
    scores = Spread(p, s, s.sc, 1, 8)
    firsts = Spread(p, s, s.call, 2, 16)
    copies = {
        name: pltpu.make_async_copy(src, dst, s.io.at[k])
        for k, (name, src, dst) in enumerate(
            (
                ("x", s.x_in, s.x),
                ("up", s.up_in, s.up),
                ("lo", s.lo, s.lo_out),
                ("hg", s.hg, s.hg_out),
            )
        )
    }
    copies["x"].start()
    copies["up"].start()
    stages, query_steps, drain = gather_steps(p, s, me, vectors)

    def passages(fn, lo, many):
        def go():
            pl.loop(lo, lo + many)(lambda i: fn(s, i))

        return go

    def small_done():
        vectors.finish()
        unpack_small(s)

    forward = [
        (1, copies["x"].wait),
        (1, copies["up"].wait),
        (2, vectors.second),
        (6, small_done),
        (7, lambda: queries_keys(s)),
        (9, lambda: values(s)),
        (9, passages(attn_fwd, 0, 1)),
        (10, passages(attn_fwd, 1, 2)),
        (11, passages(attn_fwd, 3, 1)),
        (11, lambda: attn_out(s)),
    ]
    forward += [(5 + 2 * k, fn) for k, fn in enumerate(query_steps)]
    forward += [(14, lambda: unpack_queries(s))]

    @pl.loop(0, G_END)
    def _(t):
        run_stages(stages, t)
        run_at(t, forward)
        run_span(G_FULL, t, lambda j: ffn_fwd(s, j, 0, D))
        run_span(G_HALF, t, lambda h: ffn_fwd(s, 3, h, LW))

    s.sc[pl.ds(pl.multiple_of(me * 8, 8), 8), :] = first_rows(s, me)
    scores.first()
    s.gv[...] = jnp.zeros_like(s.gv)
    norm2(s)
    norm2_back(s)
    scores.second()
    firsts.first()
    copies["lo"].start()
    drain()
    scores.finish()
    loss_part(s, me)
    add_cls(s)

    stages, vector_steps, early, drain = scatter_steps(p, s)
    outer_back(s, 0)
    early(1)
    inner_back(s, 0)
    early(0)
    def hidden():
        qkv_back(s)
        copies["hg"].start()

    def query():
        firsts.finish()
        query_gradient(s, me)

    backward = [
        (1, firsts.second),
        (3, lambda: norm1_back(s)),
        (4, passages(attn_back, 0, 1)),
        (5, passages(attn_back, 1, 1)),
        (6, passages(attn_back, 2, 2)),
        (8, hidden),
        (9, query),
        (10, vector_steps[0]),
        (13, vector_steps[1]),
        (17, vector_steps[2]),
    ]

    @pl.loop(0, S_END)
    def _(t):
        run_stages(stages, t)

        @pl.when(t < 3)
        def _():
            ffn_back(s, t + 1)

        run_at(t, backward)

    drain()
    copies["lo"].wait()
    copies["hg"].wait()
    pltpu.make_async_copy(s.out, s.sums_out, s.io.at[4]).wait()


SMEM = pl.BlockSpec(memory_space=pltpu.SMEM)


def layer(*args):
    return pl.pallas_call(
        layer_kernel,
        out_shape=tuple(jax.ShapeDtypeStruct(*o) for o in OUTS.values()),
        in_specs=[HBM] * 2 + [VM] * (len(INS) - 5) + [SMEM] * 3,
        out_specs=(HBM,) * 3 + (VM,) * 4,
        scratch_shapes=[pltpu.VMEM(*b) for b in SCRATCH.values()] + [DMA(n) for n in SEMS.values()],
        compiler_params=pltpu.CompilerParams(
            collective_id=1, has_side_effects=True, vmem_limit_bytes=VMEM_LIMIT
        ),
    )(*args)


def finish_kernel(
    lo_in, hg_in, out, q_out, bias, loss, cgrad,
    lo, hg, query_grad, query_loss, g_query, g_key, g_value, g_attn,
    g_qb, g_vb, g_ab, g_fg, g_fs, g_inner, g_ib, g_outer, g_ob, g_sg, g_ss, cls_grad, held, sums, sems
):
    me = lax.axis_index("blk") * 4 + lax.axis_index("grp")
    part = TOK // 8
    into, away = [], []
    for k, (src, dst) in enumerate(((lo_in, lo), (hg_in, hg))):
        for h in range(8):
            at = pl.ds(h * part, part)
            into.append(pltpu.make_async_copy(src.at[at], held.at[k, at], sems.at[0, 8 * k + h]))
            away.append(pltpu.make_async_copy(held.at[k, at], dst.at[at], sems.at[1, 8 * k + h]))
    top, low = pl.ds(0, ROWS), pl.ds(ROWS, ROWS)
    pieces = [(0, top, g_query), (0, low, g_key), (1, top, g_value), (1, low, g_attn)]
    for j in range(4):
        at = pl.ds(j * D, D)
        pieces += [(2 + j, top, g_inner.at[:, at]), (2 + j, low, g_outer.at[:, at])]
    for i in range(6):
        into.append(pltpu.make_async_copy(out.at[i], sums.at[i], sems.at[0, 16 + i]))
    for n, (i, rows, dst) in enumerate(pieces):
        away.append(pltpu.make_async_copy(sums.at[i, rows], dst, sems.at[1, 16 + n]))
    for move in into:
        move.start()
    for k in range(16):
        into[k].wait()
        away[k].start()
    for i in range(6):
        into[16 + i].wait()
    for n in range(12):
        away[16 + n].start()
    query_grad[...] = q_out[0:4, :]
    cls_grad[...] = cgrad[0:4, :]
    for t, ref in enumerate((g_qb, g_vb, g_ab, g_fg, g_fs, g_ob, g_sg, g_ss)):
        ref[...] = pltpu.roll(bias[...], 32, 1)[t, :ROWS]
    g_ib[...] = bias[0, :96]
    query_loss[...] = pltpu.roll(loss[...], lax.rem(128 - 4 * me, 128), 1)[0, :4]
    for move in away:
        move.wait()


def finish(*args):
    f32 = lambda *dims: jax.ShapeDtypeStruct(dims, F32)
    square = f32(ROWS, D)
    vec = f32(ROWS)
    tokens = jax.ShapeDtypeStruct((TOK, D), BF)
    outs = [tokens, tokens, f32(4, D), f32(4)] + [square] * 4 + [vec] * 5
    outs += [f32(ROWS, 4 * D), f32(96), f32(ROWS, 4 * D), vec, vec, vec, f32(4, D)]
    return pl.pallas_call(
        finish_kernel,
        out_shape=outs,
        in_specs=[HBM] * 3 + [VM] * 4,
        out_specs=[HBM] * 2 + [VM] * 2 + [HBM] * 4 + [VM] * 5 + [HBM, VM, HBM] + [VM] * 4,
        scratch_shapes=[pltpu.VMEM((2, TOK, D), BF), pltpu.VMEM((6, 48, D), F32), DMA((2, 28))],
        compiler_params=pltpu.CompilerParams(vmem_limit_bytes=VMEM_LIMIT),
    )(*args)


def fast_local(
    hidden_in,
    upstream_grad,
    query_vectors,
    loss_weight,
    positive_ids,
    positive_count,
    query_proj,
    key_proj,
    value_proj,
    attn_proj,
    query_bias,
    value_bias,
    attn_bias,
    first_gain,
    first_shift,
    inner_proj,
    inner_bias,
    outer_proj,
    outer_bias,
    second_gain,
    second_shift,
):
    results = layer(
        hidden_in.reshape(TOK, D),
        upstream_grad.reshape(TOK, D),
        query_proj,
        key_proj,
        value_proj,
        attn_proj.T,
        inner_proj,
        outer_proj.T,
        query_vectors,
        query_bias,
        value_bias,
        attn_bias,
        first_gain,
        first_shift,
        outer_bias,
        second_gain,
        second_shift,
        inner_bias,
        loss_weight,
        positive_ids,
        positive_count,
    )
    layer_output, hidden_grad, *rest = finish(*results)
    rest[5] = rest[5].T
    rest[13] = rest[13].T
    return (layer_output.reshape(hidden_in.shape), hidden_grad.reshape(hidden_in.shape), *rest)


def solution(mesh):
    in_specs = (
        P(("blk", "grp"), None, None),
        P(("blk", "grp"), None, None),
        P(("blk", "grp"), None),
        P(("blk", "grp")),
        P(("blk", "grp"), None),
        P(("blk", "grp")),
        P(("blk", "grp"), None),
        P(("blk", "grp"), None),
        P(("blk", "grp"), None),
        P(None, ("blk", "grp")),
        P(("blk", "grp")),
        P(("blk", "grp")),
        P(("blk", "grp")),
        P(("blk", "grp")),
        P(("blk", "grp")),
        P(("blk", "grp"), None),
        P(("blk", "grp")),
        P(None, ("blk", "grp")),
        P(("blk", "grp")),
        P(("blk", "grp")),
        P(("blk", "grp")),
    )
    out_specs = (
        P(("blk", "grp"), None, None),
        P(("blk", "grp"), None, None),
        P(("blk", "grp"), None),
        P(("blk", "grp")),
        P(("blk", "grp"), None),
        P(("blk", "grp"), None),
        P(("blk", "grp"), None),
        P(None, ("blk", "grp")),
        P(("blk", "grp")),
        P(("blk", "grp")),
        P(("blk", "grp")),
        P(("blk", "grp")),
        P(("blk", "grp")),
        P(("blk", "grp"), None),
        P(("blk", "grp")),
        P(None, ("blk", "grp")),
        P(("blk", "grp")),
        P(("blk", "grp")),
        P(("blk", "grp")),
        P(("blk", "grp"), None),
    )
    tiled = mesh.shape["blk"] == 8 and mesh.shape["grp"] == 4
    local = fast_local if tiled else plain_local
    return jax.shard_map(local, mesh=mesh, in_specs=in_specs, out_specs=out_specs, check_vma=False)
```

```python
import jax
import jax.numpy as jnp
from jax import lax
from jax.experimental import pallas as pl
from jax.experimental.pallas import tpu as pltpu
from jax.sharding import PartitionSpec as P

D = 768
HEADS = 12
HEAD_DIM = 64
LEN = 128


NORM_EPS = 1e-05
NEG_FILL = -1e30


def product(left_side, right_side):
    return jnp.dot(left_side, right_side, preferred_element_type=jnp.float32)


def contract(form_text, first_side, second_side):
    return jnp.einsum(form_text, first_side, second_side, preferred_element_type=jnp.float32)


def norm_forward(resid_sum, gain_vec, shift_vec):
    centered = resid_sum - jnp.mean(resid_sum, axis=-1, keepdims=True)
    inv_dev = lax.rsqrt(jnp.mean(centered * centered, axis=-1, keepdims=True) + NORM_EPS)
    normal_part = centered * inv_dev
    return (normal_part * gain_vec + shift_vec, normal_part, inv_dev)


def norm_backward(out_grad, normal_part, inv_dev, gain_vec):
    scaled_grad = out_grad * gain_vec
    mean_grad = jnp.mean(scaled_grad, axis=-1, keepdims=True)
    mean_cross = jnp.mean(scaled_grad * normal_part, axis=-1, keepdims=True)
    return inv_dev * (scaled_grad - mean_grad - normal_part * mean_cross)


def gelu_exact(pre_act):
    return jax.nn.gelu(pre_act, approximate=False)


def gelu_grad(pre_act, act_grad):
    unused_out, pullback = jax.vjp(gelu_exact, pre_act)
    return pullback(act_grad)[0]


def positive_block(positive_ids, positive_count, span_count):
    slot_live = (
        jnp.arange(positive_ids.shape[1], dtype=jnp.int32)[None, :] < positive_count[:, None]
    )
    passage_index = jnp.arange(span_count, dtype=jnp.int32)
    matches = (positive_ids[:, :, None] == passage_index[None, None, :]) & slot_live[:, :, None]
    return jnp.any(matches, axis=1)


def block_forward(block_in, attn_params, ffn_params):
    (
        query_proj,
        key_proj,
        value_proj,
        attn_proj,
        query_bias,
        value_bias,
        attn_bias,
        first_gain,
        first_shift,
    ) = attn_params
    inner_proj, inner_bias, outer_proj, outer_bias, second_gain, second_shift = ffn_params
    pass_count = block_in.shape[0]
    head_shape = (pass_count, LEN, HEADS, HEAD_DIM)
    tok_rows = block_in.reshape(pass_count * LEN, D)
    queries = ((product(tok_rows, query_proj) + query_bias) * 0.125).astype(jnp.bfloat16)
    keys_low = product(tok_rows, key_proj).astype(jnp.bfloat16)
    values_low = (product(tok_rows, value_proj) + value_bias).astype(jnp.bfloat16)
    scores = contract("bqhd,bkhd->bhqk", queries.reshape(head_shape), keys_low.reshape(head_shape))
    top_score = jnp.max(scores, axis=-1, keepdims=True)
    exp_terms = jnp.exp(scores - top_score)
    totals = jnp.sum(exp_terms, axis=-1, keepdims=True)
    probs_low = (exp_terms / totals).astype(jnp.bfloat16)
    log_norm = top_score + jnp.log(totals)
    context = contract("bhqk,bkhd->bqhd", probs_low, values_low.reshape(head_shape))
    context = context.reshape(pass_count * LEN, D).astype(jnp.bfloat16)
    attn_out = product(context, attn_proj) + attn_bias
    normed, first_normal, first_inv = norm_forward(
        tok_rows.astype(jnp.float32) + attn_out, first_gain, first_shift
    )
    normed_low = normed.astype(jnp.bfloat16)
    inner_pre = product(normed_low, inner_proj) + inner_bias
    activated = gelu_exact(inner_pre).astype(jnp.bfloat16)
    branch = product(activated, outer_proj) + outer_bias
    layer_f32, second_normal, second_inv = norm_forward(normed + branch, second_gain, second_shift)
    kept_state = (
        queries,
        keys_low,
        values_low,
        log_norm,
        context,
        first_normal,
        first_inv,
        normed_low,
        inner_pre,
        activated,
        second_normal,
        second_inv,
    )
    return (layer_f32, kept_state)


def block_backward(block_in, out_grad, kept_state, attn_params, ffn_params):
    (
        query_proj,
        key_proj,
        value_proj,
        attn_proj,
        query_bias,
        value_bias,
        attn_bias,
        first_gain,
        first_shift,
    ) = attn_params
    inner_proj, inner_bias, outer_proj, outer_bias, second_gain, second_shift = ffn_params
    (
        queries,
        keys_low,
        values_low,
        log_norm,
        context,
        first_normal,
        first_inv,
        normed_low,
        inner_pre,
        activated,
        second_normal,
        second_inv,
    ) = kept_state
    pass_count = block_in.shape[0]
    tok_count = pass_count * LEN
    head_shape = (pass_count, LEN, HEADS, HEAD_DIM)
    tok_rows = block_in.reshape(tok_count, D)
    grad_rows = out_grad.reshape(tok_count, D)
    grad_second_gain = jnp.sum(grad_rows * second_normal, axis=0)
    grad_second_shift = jnp.sum(grad_rows, axis=0)
    second_resid = norm_backward(grad_rows, second_normal, second_inv, second_gain)
    branch_grad = second_resid.astype(jnp.bfloat16)
    grad_outer_bias = jnp.sum(branch_grad.astype(jnp.float32), axis=0)
    grad_outer_proj = product(activated.T, branch_grad)
    inner_grad = gelu_grad(inner_pre, product(branch_grad, outer_proj.T)).astype(jnp.bfloat16)
    grad_inner_bias = jnp.sum(inner_grad.astype(jnp.float32), axis=0)
    grad_inner_proj = product(normed_low.T, inner_grad)
    normed_grad = second_resid + product(inner_grad, inner_proj.T)
    grad_first_gain = jnp.sum(normed_grad * first_normal, axis=0)
    grad_first_shift = jnp.sum(normed_grad, axis=0)
    first_resid = norm_backward(normed_grad, first_normal, first_inv, first_gain)
    attn_grad = first_resid.astype(jnp.bfloat16)
    grad_attn_bias = jnp.sum(attn_grad.astype(jnp.float32), axis=0)
    grad_attn_proj = product(context.T, attn_grad)
    context_grad = product(attn_grad, attn_proj.T).astype(jnp.bfloat16).reshape(head_shape)
    query_heads = queries.reshape(head_shape)
    key_heads = keys_low.reshape(head_shape)
    value_heads = values_low.reshape(head_shape)
    scores = contract("bqhd,bkhd->bhqk", query_heads, key_heads)
    prob_full = jnp.exp(scores - log_norm)
    values_grad = contract("bhqk,bqhd->bkhd", prob_full.astype(jnp.bfloat16), context_grad)
    values_grad = values_grad.astype(jnp.bfloat16).reshape(tok_count, D)
    prob_grad = contract("bqhd,bkhd->bhqk", context_grad, value_heads)
    score_grad = (
        prob_full * (prob_grad - jnp.sum(prob_full * prob_grad, axis=-1, keepdims=True))
    ).astype(jnp.bfloat16)
    queries_grad = (
        contract("bhqk,bkhd->bqhd", score_grad, key_heads)
        .astype(jnp.bfloat16)
        .reshape(tok_count, D)
    )
    keys_grad = (
        contract("bhqk,bqhd->bkhd", score_grad, query_heads)
        .astype(jnp.bfloat16)
        .reshape(tok_count, D)
    )
    grad_query_proj = product(tok_rows.T, queries_grad) * 0.125
    grad_query_bias = jnp.sum(queries_grad.astype(jnp.float32), axis=0) * 0.125
    grad_key_proj = product(tok_rows.T, keys_grad)
    grad_value_proj = product(tok_rows.T, values_grad)
    grad_value_bias = jnp.sum(values_grad.astype(jnp.float32), axis=0)
    hidden_grad = (
        first_resid
        + 0.125 * product(queries_grad, query_proj.T)
        + product(keys_grad, key_proj.T)
        + product(values_grad, value_proj.T)
    )
    attn_grads = (
        grad_query_proj,
        grad_key_proj,
        grad_value_proj,
        grad_attn_proj,
        grad_query_bias,
        grad_value_bias,
        grad_attn_bias,
        grad_first_gain,
        grad_first_shift,
    )
    ffn_grads = (
        grad_inner_proj,
        grad_inner_bias,
        grad_outer_proj,
        grad_outer_bias,
        grad_second_gain,
        grad_second_shift,
    )
    return (hidden_grad, attn_grads, ffn_grads)


def plain_local(
    hidden_in,
    upstream_grad,
    query_vectors,
    loss_weight,
    positive_ids,
    positive_count,
    query_proj,
    key_proj,
    value_proj,
    attn_proj,
    query_bias,
    value_bias,
    attn_bias,
    first_gain,
    first_shift,
    inner_proj,
    inner_bias,
    outer_proj,
    outer_bias,
    second_gain,
    second_shift,
):
    attn_params = (
        lax.all_gather(query_proj, ("blk", "grp"), axis=0, tiled=True),
        lax.all_gather(key_proj, ("blk", "grp"), axis=0, tiled=True),
        lax.all_gather(value_proj, ("blk", "grp"), axis=0, tiled=True),
        lax.all_gather(attn_proj, ("blk", "grp"), axis=1, tiled=True),
        lax.all_gather(query_bias, ("blk", "grp"), axis=0, tiled=True),
        lax.all_gather(value_bias, ("blk", "grp"), axis=0, tiled=True),
        lax.all_gather(attn_bias, ("blk", "grp"), axis=0, tiled=True),
        lax.all_gather(first_gain, ("blk", "grp"), axis=0, tiled=True),
        lax.all_gather(first_shift, ("blk", "grp"), axis=0, tiled=True),
    )
    ffn_params = (
        lax.all_gather(inner_proj, ("blk", "grp"), axis=0, tiled=True),
        lax.all_gather(inner_bias, ("blk", "grp"), axis=0, tiled=True),
        lax.all_gather(outer_proj, ("blk", "grp"), axis=1, tiled=True),
        lax.all_gather(outer_bias, ("blk", "grp"), axis=0, tiled=True),
        lax.all_gather(second_gain, ("blk", "grp"), axis=0, tiled=True),
        lax.all_gather(second_shift, ("blk", "grp"), axis=0, tiled=True),
    )
    pass_count = hidden_in.shape[0]
    layer_f32, kept_state = block_forward(hidden_in, attn_params, ffn_params)
    layer_output = layer_f32.astype(jnp.bfloat16).reshape(pass_count, LEN, D)
    cls_local = layer_output[:, 0, :]
    query_count = query_vectors.shape[0]
    lowest = jnp.full((query_count,), NEG_FILL, jnp.float32)
    cls_piece = lax.all_gather(cls_local, ("blk", "grp"), axis=0, tiled=True)
    top_all = lowest
    top_pos = lowest
    scores = contract("qd,pd->qp", query_vectors, cls_piece)
    hit_mask = positive_block(positive_ids, positive_count, cls_piece.shape[0])
    masked = jnp.where(hit_mask, scores, NEG_FILL)
    new_all = jnp.maximum(top_all, jnp.max(scores, axis=1))
    new_pos = jnp.maximum(top_pos, jnp.max(masked, axis=1))
    sum_all = jnp.sum(jnp.exp(scores - new_all[:, None]), axis=1)
    pos_terms = jnp.where(hit_mask, jnp.exp(masked - new_pos[:, None]), 0.0)
    sum_pos = jnp.sum(pos_terms, axis=1)
    top_all, sum_all, top_pos, sum_pos = (new_all, sum_all, new_pos, sum_pos)
    total_all = top_all + jnp.log(sum_all)
    total_pos = top_pos + jnp.log(sum_pos)
    cls_piece = lax.all_gather(cls_local, ("blk", "grp"), axis=0, tiled=True)
    scores = contract("qd,pd->qp", query_vectors, cls_piece)
    hit_mask = positive_block(positive_ids, positive_count, cls_piece.shape[0])
    masked = jnp.where(hit_mask, scores, NEG_FILL)
    weight_rows = loss_weight[:, None] * (
        jnp.exp(scores - total_all[:, None]) - jnp.exp(masked - total_pos[:, None])
    )
    weight_rows = weight_rows.astype(jnp.bfloat16)
    query_acc = product(weight_rows, cls_piece)
    query_loss = total_all - total_pos
    cls_grad = lax.psum_scatter(
        contract("qp,qd->pd", weight_rows, query_vectors),
        ("blk", "grp"),
        scatter_dimension=0,
        tiled=True,
    )
    grad_total = upstream_grad.astype(jnp.float32).at[:, 0, :].add(cls_grad)
    ffn_back = (
        lax.all_gather(inner_proj, ("blk", "grp"), axis=0, tiled=True),
        lax.all_gather(inner_bias, ("blk", "grp"), axis=0, tiled=True),
        lax.all_gather(outer_proj, ("blk", "grp"), axis=1, tiled=True),
        lax.all_gather(outer_bias, ("blk", "grp"), axis=0, tiled=True),
        lax.all_gather(second_gain, ("blk", "grp"), axis=0, tiled=True),
        lax.all_gather(second_shift, ("blk", "grp"), axis=0, tiled=True),
    )
    attn_back = (
        lax.all_gather(query_proj, ("blk", "grp"), axis=0, tiled=True),
        lax.all_gather(key_proj, ("blk", "grp"), axis=0, tiled=True),
        lax.all_gather(value_proj, ("blk", "grp"), axis=0, tiled=True),
        lax.all_gather(attn_proj, ("blk", "grp"), axis=1, tiled=True),
        lax.all_gather(query_bias, ("blk", "grp"), axis=0, tiled=True),
        lax.all_gather(value_bias, ("blk", "grp"), axis=0, tiled=True),
        lax.all_gather(attn_bias, ("blk", "grp"), axis=0, tiled=True),
        lax.all_gather(first_gain, ("blk", "grp"), axis=0, tiled=True),
        lax.all_gather(first_shift, ("blk", "grp"), axis=0, tiled=True),
    )
    hidden_part, attn_grads, ffn_grads = block_backward(
        hidden_in, grad_total, kept_state, attn_back, ffn_back
    )
    attn_shards = (
        lax.psum_scatter(attn_grads[0], ("blk", "grp"), scatter_dimension=0, tiled=True),
        lax.psum_scatter(attn_grads[1], ("blk", "grp"), scatter_dimension=0, tiled=True),
        lax.psum_scatter(attn_grads[2], ("blk", "grp"), scatter_dimension=0, tiled=True),
        lax.psum_scatter(attn_grads[3], ("blk", "grp"), scatter_dimension=1, tiled=True),
        lax.psum_scatter(attn_grads[4], ("blk", "grp"), scatter_dimension=0, tiled=True),
        lax.psum_scatter(attn_grads[5], ("blk", "grp"), scatter_dimension=0, tiled=True),
        lax.psum_scatter(attn_grads[6], ("blk", "grp"), scatter_dimension=0, tiled=True),
        lax.psum_scatter(attn_grads[7], ("blk", "grp"), scatter_dimension=0, tiled=True),
        lax.psum_scatter(attn_grads[8], ("blk", "grp"), scatter_dimension=0, tiled=True),
    )
    ffn_shards = (
        lax.psum_scatter(ffn_grads[0], ("blk", "grp"), scatter_dimension=0, tiled=True),
        lax.psum_scatter(ffn_grads[1], ("blk", "grp"), scatter_dimension=0, tiled=True),
        lax.psum_scatter(ffn_grads[2], ("blk", "grp"), scatter_dimension=1, tiled=True),
        lax.psum_scatter(ffn_grads[3], ("blk", "grp"), scatter_dimension=0, tiled=True),
        lax.psum_scatter(ffn_grads[4], ("blk", "grp"), scatter_dimension=0, tiled=True),
        lax.psum_scatter(ffn_grads[5], ("blk", "grp"), scatter_dimension=0, tiled=True),
    )
    hidden_grad = hidden_part.astype(jnp.bfloat16).reshape(pass_count, LEN, D)
    return (
        layer_output,
        hidden_grad,
        query_acc,
        query_loss,
        attn_shards[0],
        attn_shards[1],
        attn_shards[2],
        attn_shards[3],
        attn_shards[4],
        attn_shards[5],
        attn_shards[6],
        attn_shards[7],
        attn_shards[8],
        ffn_shards[0],
        ffn_shards[1],
        ffn_shards[2],
        ffn_shards[3],
        ffn_shards[4],
        ffn_shards[5],
        cls_grad,
    )


BF = jnp.bfloat16
F32 = jnp.float32
MESH = pl.DeviceIdType.MESH
VM = pl.BlockSpec(memory_space=pltpu.VMEM)
DMA = pltpu.SemaphoreType.DMA
ALL = slice(None)
VMEM_LIMIT = 60 * 2**20
LW = 384
PARTS = 2
NC = 6 * PARTS
ROWS = 24
TOK = 512


class Place:
    def __init__(self):
        self.b = lax.axis_index("blk")
        self.z = lax.axis_index("grp")
        self.y, self.x, self.c = self.b // 4, (self.b // 2) % 2, self.b % 2
        self.zh, self.zl = self.z // 2, self.z % 2
        self.mid = ((self.z + 1) // 2) % 2
        self.xdev = (self.b + 2 - 4 * self.x, self.z)
        self.ydev = (self.b + 4 - 8 * self.y, self.z)
        self.cdev = (self.b + 1 - 2 * self.c, self.z)
        self.zdev = (self.b, self.z + 1 - 2 * self.zl)
        self.fdev = (self.b, 3 - self.z)


def greet(p):
    bar = pltpu.get_barrier_semaphore()
    for k in range(1, 8):
        pl.semaphore_signal(bar, 1, device_id=((p.b + k) % 8, p.z), device_id_type=MESH)
    for k in range(1, 4):
        pl.semaphore_signal(bar, 1, device_id=(p.b, (p.z + k) % 4), device_id_type=MESH)
    pl.semaphore_wait(bar, 10)


def rcopy(src, dst, ss, rs, dev):
    return pltpu.make_async_remote_copy(
        src_ref=src, dst_ref=dst, send_sem=ss, recv_sem=rs, device_id=dev, device_id_type=MESH
    )


class Flow:
    def __init__(self, p, ref, kind, ss, rs, lead=()):
        self.p, self.ref, self.kind, self.ss, self.rs, self.lead = p, ref, kind, ss, rs, lead
        self.f, self.s = (p.x, p.y) if kind == 0 else (p.y, p.x)
        self.fdev, self.sdev = (p.xdev, p.ydev) if kind == 0 else (p.ydev, p.xdev)

    def at(self, f, s, zz, c=None):
        c = self.p.c if c is None else c
        return self.ref.at[self.lead + self.index(f, s, zz, c)]

    def index(self, f, s, zz, c):
        return (s, f, c, zz) if self.kind == 0 else (f, s, c, zz)

    def copy(self, stage, src, dst, dev):
        return rcopy(src, dst, self.ss(stage), self.rs(stage), dev)

    def go(self, stage, view, dev):
        self.copy(stage, view, view, dev).start()

    def got(self, stage, view):
        self.copy(stage, view, view, self.p.cdev).wait_recv()

    def sent(self, stage, view):
        self.copy(stage, view, view, self.p.cdev).wait_send()


class Gather(Flow):
    def s2_send(self):
        self.go(0, self.at(self.f, self.s, self.p.zh), self.fdev)

    def s2_recv(self):
        self.got(0, self.at(1 - self.f, self.s, self.p.zh))

    def s3a_send(self):
        self.go(1, self.at(ALL, self.s, self.p.zh), self.p.fdev)

    def s3a_recv(self):
        self.got(1, self.at(ALL, self.s, 1 - self.p.zh))

    def s3b_send(self):
        self.go(2, self.at(ALL, self.s, 1 - self.p.zh), self.p.zdev)

    def s3b_recv(self):
        self.got(2, self.at(ALL, self.s, 1 - self.p.zh))

    def s4a_send(self):
        self.go(3, self.at(ALL, self.s, self.p.zh), self.sdev)

    def s4b_send(self):
        self.go(4, self.at(ALL, self.s, 1 - self.p.zh), self.sdev)

    def s4_recv(self):
        self.got(3, self.at(ALL, 1 - self.s, self.p.zh))
        self.got(4, self.at(ALL, 1 - self.s, 1 - self.p.zh))

    def core_send(self):
        self.go(5, self.at(ALL, ALL, ALL), self.p.cdev)

    def core_recv(self):
        self.got(5, self.at(ALL, ALL, ALL, 1 - self.p.c))

    def drain(self):
        self.sent(0, self.at(self.f, self.s, self.p.zh))

        @pl.when(self.p.mid == 1)
        def _():
            self.sent(1, self.at(ALL, self.s, self.p.zh))
            self.sent(2, self.at(ALL, self.s, 1 - self.p.zh))

        self.sent(3, self.at(ALL, self.s, self.p.zh))
        self.sent(4, self.at(ALL, self.s, 1 - self.p.zh))
        self.sent(5, self.at(ALL, ALL, ALL))


def lanes_of(ci):
    return pl.ds(pl.multiple_of((ci % PARTS) * LW, 128), LW)


class Scatter(Flow):
    def __init__(self, p, ref, kind, ss, rs, bufs, lead=()):
        super().__init__(p, ref, kind, ss, rs, lead)
        self.rc, self.r4a, self.r4b, self.r3b, self.r3a, self.r2 = bufs

    def add(self, stage, buf, f, s, zz):
        self.copy(stage, buf, buf, self.p.cdev).wait_recv()
        at = self.index(f, s, zz, self.p.c)
        self.ref[at] = self.ref[at] + buf[...]

    def t0_send(self):
        self.copy(0, self.at(ALL, ALL, ALL, 1 - self.p.c), self.rc, self.p.cdev).start()

    def t0_add(self):
        self.add(0, self.rc, ALL, ALL, ALL)

    def t1a_send(self):
        self.copy(1, self.at(ALL, 1 - self.s, 1 - self.p.zh), self.r4a, self.sdev).start()

    def t1a_add(self):
        self.add(1, self.r4a, ALL, self.s, 1 - self.p.zh)

    def t1b_send(self):
        self.copy(5, self.at(ALL, 1 - self.s, self.p.zh), self.r4b, self.sdev).start()

    def t1b_add(self):
        self.add(5, self.r4b, ALL, self.s, self.p.zh)

    def t2a_send(self):
        self.copy(2, self.at(ALL, self.s, 1 - self.p.zh), self.r3b, self.p.zdev).start()

    def t2a_add(self):
        self.add(2, self.r3b, ALL, self.s, 1 - self.p.zh)

    def t2b_send(self):
        self.copy(3, self.at(ALL, self.s, 1 - self.p.zh), self.r3a, self.p.fdev).start()

    def t2b_add(self):
        self.add(3, self.r3a, ALL, self.s, self.p.zh)

    def t3_send(self):
        self.copy(4, self.at(1 - self.f, self.s, self.p.zh), self.r2, self.fdev).start()

    def t3_sum(self):
        self.copy(4, self.r2, self.r2, self.p.cdev).wait_recv()
        at = self.index(self.f, self.s, self.p.zh, self.p.c)
        return self.ref[at].astype(F32) + self.r2[...].astype(F32)

    def drain(self):
        self.sent(0, self.at(ALL, ALL, ALL, 1 - self.p.c))
        self.sent(1, self.at(ALL, 1 - self.s, 1 - self.p.zh))
        self.sent(5, self.at(ALL, 1 - self.s, self.p.zh))

        @pl.when(self.p.mid == 0)
        def _():
            self.sent(2, self.at(ALL, self.s, 1 - self.p.zh))

        @pl.when(self.p.mid == 1)
        def _():
            self.sent(3, self.at(ALL, self.s, 1 - self.p.zh))

        self.sent(4, self.at(1 - self.f, self.s, self.p.zh))


def nn(a, b): return lax.dot_general(a, b, (((1,), (0,)), ((), ())), preferred_element_type=F32)
def nt(a, b): return lax.dot_general(a, b, (((1,), (1,)), ((), ())), preferred_element_type=F32)
def tn(a, b): return lax.dot_general(a, b, (((0,), (0,)), ((), ())), preferred_element_type=F32)

def weight(ref, i): return ref[i].reshape(D, D)
def keep(ref, i, val): ref[i] = val.astype(BF).reshape(2, 2, 2, 2, 48, D)

def tiles(n, body, unroll=None):
    def f(r, c):
        body(pl.ds(pl.multiple_of(r * (TOK // n), TOK // n), TOK // n)); return c
    lax.fori_loop(0, n, f, 0, unroll=unroll)

def masks():
    lane = lax.broadcasted_iota(jnp.int32, (1, 128), 1)
    lo = (lane < 64).astype(F32).astype(BF)
    return lo, (1 - lo.astype(F32)).astype(BF)

def queries_keys(s):
    x = s.x[...]
    s.q[...] = ((nn(x, weight(s.wa, 0)) + s.vec[0:1, :]) * 0.125).astype(BF)
    s.k[...] = nn(x, weight(s.wb, 0)).astype(BF)


def values(s):
    s.v[...] = (nn(s.x[...], weight(s.wa, 1)) + s.vec[1:2, :]).astype(BF)


def split(x, lo, hi): return jnp.concatenate([x * lo, x * hi], 0)

def attn_fwd(s, p):
    lo, hi = masks()
    r = pl.ds(pl.multiple_of(p * 128, 128), 128)
    for h in range(6):
        ln = pl.ds(h * 128, 128)
        sc = nt(s.q[r, ln], split(s.k[r, ln], lo, hi))
        out = []
        for w in (sc[:, :128], sc[:, 128:]):
            e = jnp.exp(w - jnp.max(w, axis=1, keepdims=True))
            out.append((e * (1.0 / jnp.sum(e, axis=1, keepdims=True))).astype(BF))
        pr = jnp.concatenate(out, 1)
        s.p[p, h] = pr
        s.ctx[r, ln] = nn(pr, split(s.v[r, ln], lo, hi)).astype(BF)

def normalize(res):
    c = res - jnp.mean(res, axis=1, keepdims=True)
    inv = lax.rsqrt(jnp.mean(c * c, axis=1, keepdims=True) + NORM_EPS)
    return c * inv, inv

def attn_out(s, n=8):
    s.acc[...] = nt(s.ctx[...], weight(s.wb, 1))
    def body(r):
        n_, inv = normalize(s.x[r, :].astype(F32) + s.acc[r, :] + s.vec[2:3, :])
        s.fn[r, :] = n_
        s.s1[r, :] = inv
        s.nl[r, :] = (n_ * s.vec[3:4, :] + s.vec[4:5, :]).astype(BF)
        s.acc[r, :] = n_ * s.vec[3:4, :] + s.vec[4:5, :] + s.vec[5:6, :]
    tiles(2, body)

def gelu_parts(x):
    ax = jnp.abs(x) * 0.7071067811865476
    t = 1.0 / (1.0 + 0.3275911 * ax)
    e = jnp.exp(x * x * -0.5)
    poly = t * (0.254829592 + t * (-0.284496736 + t * (1.421413741 + t * (-1.453152027 + t * 1.061405429))))
    half = 0.5 * poly * e
    phi = jnp.where(x > 0, 1.0 - half, half)
    return phi, e * 0.3989422804014327

def ffn_fwd(s, j, h, width):
    ln = pl.ds(pl.multiple_of(h * width, 128), width) if width < D else ALL
    w_in = s.wa[2 + j, :, :, :, :, :, ln].reshape(D, width)
    w_out = s.wb[2 + j, :, :, :, :, :, ln].reshape(D, width)
    for r in (slice(0, 256), slice(256, 512)):
        x = nn(s.nl[r, :], w_in) + s.vec[pl.ds(8 + j, 1), ln]
        cdf, pdf = gelu_parts(x)
        act = (x * cdf).astype(BF)
        s.act[j, r, ln] = act
        s.gp[j, r, ln] = (cdf + x * pdf).astype(BF)
        s.acc[r, :] += nt(act, w_out)

def norm2(s):
    def body(r):
        n_, inv = normalize(s.acc[r, :])
        s.acc[r, :] = n_
        s.s2[r, :] = inv
        s.lo[r, :] = (n_ * s.vec[6:7, :] + s.vec[7:8, :]).astype(BF)
    tiles(2, body)

def norm_back(g, n_, inv, gain):
    sg = g * gain
    return inv * (sg - jnp.mean(sg, axis=1, keepdims=True) - n_ * jnp.mean(sg * n_, axis=1, keepdims=True))

def colsum(x): return jnp.sum(x.reshape(-1, 8, x.shape[-1]), axis=0)

def norm2_back(s):
    def body(r):
        g = s.up[r, :].astype(F32)
        n_ = s.acc[r, :]
        s.gv[6] += colsum(g * n_)
        s.gv[7] += colsum(g)
        res = norm_back(g, n_, s.s2[r, :], s.vec[6:7, :])
        s.acc[r, :] = res
        b = res.astype(BF)
        s.bg[r, :] = b
        s.gv[5] += colsum(b.astype(F32))
    tiles(2, body)

def outer_back(s, j):
    s.tmp[...] = nn(s.bg[...], weight(s.wb, 2 + j))
    keep(s.wb, 2 + j, tn(s.bg[...], s.act[j]))


def inner_back(s, j):
    def ew(r):
        ig = (s.tmp[r, :] * s.gp[j, r, :].astype(F32)).astype(BF)
        s.gp[j, r, :] = ig
        s.gv[8 + j] += colsum(ig.astype(F32))

    tiles(2, ew)
    s.acc[...] += nt(s.gp[j], weight(s.wa, 2 + j))
    keep(s.wa, 2 + j, tn(s.nl[...], s.gp[j]))


def ffn_back(s, j):
    outer_back(s, j)
    inner_back(s, j)


def norm1_back(s):
    def body(r):
        g = s.acc[r, :]
        n_ = s.fn[r, :]
        s.gv[3] += colsum(g * n_)
        s.gv[4] += colsum(g)
        res = norm_back(g, n_, s.s1[r, :], s.vec[3:4, :])
        s.acc[r, :] = res
        b = res.astype(BF)
        s.bg[r, :] = b
        s.gv[2] += colsum(b.astype(F32))
    tiles(2, body)
    s.nl[...] = nn(s.bg[...], weight(s.wb, 1)).astype(BF)
    keep(s.wb, 1, tn(s.bg[...], s.ctx[...]))

def attn_back(s, p):
    lo, hi = masks()
    r = pl.ds(pl.multiple_of(p * 128, 128), 128)
    for h in range(6):
        ln = pl.ds(h * 128, 128)
        qp, kp, vp, cg = s.q[r, ln], s.k[r, ln], s.v[r, ln], s.nl[r, ln]
        dp = nt(cg, split(vp, lo, hi))
        pr = s.p[p, h]
        prf = pr.astype(F32)
        t = prf * dp
        ds = []
        for a, b in ((0, 128), (128, 256)):
            ds.append((t[:, a:b] - prf[:, a:b] * jnp.sum(t[:, a:b], axis=1, keepdims=True)).astype(BF))
        dq = nn(jnp.concatenate(ds, 1), split(kp, lo, hi))
        dk = tn(jnp.concatenate(ds, 0), split(qp, lo, hi))
        dv = tn(jnp.concatenate([pr[:, :128], pr[:, 128:]], 0), split(cg, lo, hi))
        s.q[r, ln] = dq.astype(BF)
        s.k[r, ln] = dk.astype(BF)
        s.v[r, ln] = dv.astype(BF)

def qkv_back(s):
    s.acc[...] += 0.125 * nt(s.q[...], weight(s.wa, 0))
    s.acc[...] += nt(s.k[...], weight(s.wb, 0))
    s.hg[...] = (s.acc[...] + nt(s.v[...], weight(s.wa, 1))).astype(BF)
    def sums(r):
        s.gv[0] += colsum(s.q[r, :].astype(F32)) * 0.125
        s.gv[1] += colsum(s.v[r, :].astype(F32))
    tiles(2, sums)
    keep(s.wa, 1, tn(s.x[...], s.v[...]))
    keep(s.wa, 0, tn(s.x[...], s.q[...]) * 0.125)
    keep(s.wb, 0, tn(s.x[...], s.k[...]))


class Bag:
    pass


def column_maps(width, offset, first):
    lane = lax.broadcasted_iota(jnp.int32, (128, D), 0).astype(F32)
    col = lax.broadcasted_iota(jnp.int32, (128, D), 1).astype(F32) + first
    owner = jnp.floor((col + 0.5) * (1.0 / width))
    hot = ((lane - offset) == (col - owner * width)).astype(F32)
    return hot, owner[0:1]


def pack_weights(s, i):
    if i == 0:
        top, low = s.w_query[...].astype(F32), s.w_key[...].astype(F32)
    elif i == 1:
        top, low = s.w_value[...].astype(F32), s.w_attn[...].astype(F32)
    else:
        at = slice((i - 2) * D, (i - 1) * D)
        top, low = s.w_inner[:, at].astype(F32), s.w_outer[:, at].astype(F32)
    s.pack[i] = jnp.concatenate([top, low], 0).astype(BF)


def pack_small(s):
    for t, name in enumerate(VECTORS[:8]):
        s.tile[t : t + 1, 0:ROWS] = getattr(s, name)[...].astype(F32).reshape(1, ROWS)
    row = lax.broadcasted_iota(jnp.int32, (8, 128), 0)
    lane = lax.broadcasted_iota(jnp.int32, (8, 128), 1)
    tile = jnp.where(lane < ROWS, s.tile[...], 0.0)
    inner = s.inner_bias[...].astype(F32).reshape(1, 96)
    inner = pltpu.roll(jnp.concatenate([inner, jnp.zeros((1, 32), F32)], 1), ROWS, 1)
    tile = jnp.where((row == 0) & (lane >= ROWS) & (lane < ROWS + 96), inner, tile)
    for q in range(4):
        values = [s.positive_ids[q, k].astype(F32) for k in range(3)]
        values += [s.positive_count[q].astype(F32), s.loss_weight[q]]
        for t, value in enumerate(values):
            tile = jnp.where((row == t) & (lane == 120 + q), value, tile)
    queries = s.w_queries[...].astype(F32)
    rows = [queries[q : q + 1, k * 128 : (k + 1) * 128] for q in range(4) for k in range(6)]
    s.qpack[...] = jnp.concatenate(rows + [jnp.zeros((8, 128), F32)], 0).astype(BF)
    return tile


def unpack_small(s):
    sm = s.small[...]
    hot, owner = column_maps(24, 0, 0.0)
    dev = jnp.floor((lax.broadcasted_iota(jnp.int32, (256, 1), 0).astype(F32) + 0.5) * 0.125)
    wide = jnp.where(dev == owner, nn(sm.astype(BF), hot.astype(BF)), 0.0)
    s.vec[0:8, :] = jnp.sum(wide.reshape(32, 8, D), axis=0)
    one = s.small[pl.ds(0, 32, stride=8), :].astype(BF)
    dev32 = lax.broadcasted_iota(jnp.int32, (32, 1), 0).astype(F32)
    rows = []
    for j in range(4):
        hot, owner = column_maps(96, 24, float(D * j))
        part = jnp.where(dev32 == owner, nn(one, hot.astype(BF)), 0.0)
        rows.append(jnp.sum(part, axis=0, keepdims=True))
    s.vec[8:16, :] = jnp.concatenate(rows + [jnp.zeros((4, D), F32)], 0)
    hot, owner = column_maps(4, 120, 0.0)
    part = lax.dot_general(
        sm, hot[:, :128], (((1,), (0,)), ((), ())), precision=lax.Precision.HIGHEST, preferred_element_type=F32
    )
    part = jnp.where(dev == owner[:, :128], part, 0.0)
    s.aux[...] = jnp.sum(part.reshape(32, 8, 128), axis=0)


def unpack_queries(s):
    s.qrow[...] = s.qx[...].reshape(D, 128).astype(F32)
    for q in range(4):
        for k in range(6):
            piece = s.qrow[pl.ds(6 * q + k, 32, stride=24), :]
            s.qm[pl.ds(k * 128 + q, 32, stride=4), :] = piece


def all_queries(s):
    return jnp.concatenate([s.qm[k * 128 : (k + 1) * 128, :] for k in range(6)], 1).astype(BF)


def first_rows(s, me):
    rows = [s.acc[p * LEN : p * LEN + 8, :][0:1] for p in range(4)]
    n_, inv = normalize(jnp.concatenate(rows + [jnp.zeros((4, D), F32)], 0))
    s.cn[...] = n_
    s.ci[...] = inv
    cls = (n_ * s.vec[6:7, :] + s.vec[7:8, :]).astype(BF)
    low = cls.astype(F32)
    s.cls[...] = low
    parts = [low[0:4, k * 256 : (k + 1) * 256] for k in range(3)]
    tile = jnp.concatenate(parts + [jnp.zeros((4, 256), F32)], 0).astype(BF)
    s.call[pl.ds(pl.multiple_of(me * 16, 16), 16), :] = tile
    return nt(cls, all_queries(s))


def loss_part(s, me):
    scores = s.sc[...]
    row = lax.broadcasted_iota(jnp.int32, (256, 1), 0).astype(F32)
    dev = jnp.floor((row + 0.5) * 0.125)
    slot = row - 8.0 * dev
    real = slot < 4.0
    passage = 4.0 * dev + slot
    ids, count, weight_q = s.aux[0:3, :], s.aux[3:4, :], s.aux[4:5, :]

    def hits(passage):
        return (
            (ids[0:1] == passage)
            | ((ids[1:2] == passage) & (count > 1.5))
            | ((ids[2:3] == passage) & (count > 2.5))
        )

    everyone = jnp.where(real, scores, NEG_FILL)
    masked = jnp.where(hits(passage) & real, scores, NEG_FILL)
    totals = []
    for part in (everyone, masked):
        top = jnp.max(part, axis=0, keepdims=True)
        totals.append(top + jnp.log(jnp.sum(jnp.exp(part - top), axis=0, keepdims=True)))
    total_all, total_pos = totals
    s.loss[...] = jnp.broadcast_to(total_all - total_pos, (8, 128))
    pull = jnp.where(hits(passage) & real, jnp.exp(scores - total_pos), 0.0)
    grad = jnp.where(real, weight_q * (jnp.exp(jnp.where(real, scores - total_all, 0.0)) - pull), 0.0)
    s.sg[...] = grad
    own = s.sg[pl.ds(pl.multiple_of(me * 8, 8), 8), :].astype(BF)
    s.cgrad[...] = nn(own, all_queries(s))


def query_gradient(s, me):
    own = pltpu.roll(s.sg[...], lax.rem(128 - 4 * me, 128), 1).reshape(32, 8, 128)[:, :4]
    vectors = s.call[...]
    for k in range(3):
        pieces = [jnp.zeros((32, 4, 128), F32)] * k + [own] + [jnp.zeros((32, 4, 128), F32)] * (3 - k)
        grad = jnp.concatenate(pieces, 1).reshape(512, 128).astype(BF)
        s.q_out[:, k * 256 : (k + 1) * 256] = tn(grad, vectors)[0:8]


def pack_vectors(s):
    vec = jnp.sum(s.gv[...], axis=1)
    first = lax.broadcasted_iota(jnp.int32, (8, 96), 0) == 0
    for dev in range(32):
        b, z = dev // 4, dev % 4
        wide = vec[0:8, ROWS * dev : ROWS * (dev + 1)]
        at = 96 * (dev % 8)
        inner = jnp.where(first, vec[8 + dev // 8 : 9 + dev // 8, at : at + 96], 0.0)
        tile = jnp.concatenate([inner, wide, jnp.zeros((8, 8), F32)], 1)
        s.pb[(z * 8 + b) * 8 : (z * 8 + b + 1) * 8, :] = tile


def add_cls(s):
    g = jnp.concatenate([s.up[p * LEN : p * LEN + 16, :][0:1].astype(F32) for p in range(4)] + [jnp.zeros((4, D), F32)], 0)
    extra = s.cgrad[...]
    live = (lax.broadcasted_iota(jnp.int32, (8, 1), 0) < 4).astype(F32)
    n_, inv = s.cn[...] * live, s.ci[...]
    s.gv[6] += extra * n_
    s.gv[7] += extra
    res = norm_back(g + extra, n_, inv, s.vec[6:7, :]) * live
    old = norm_back(g, n_, inv, s.vec[6:7, :]) * live
    low = res.astype(BF).astype(F32)
    s.gv[5] += low - old.astype(BF).astype(F32)
    top = (lax.broadcasted_iota(jnp.int32, (16, 1), 0) == 0)
    for p in range(4):
        at = slice(p * LEN, p * LEN + 16)
        s.acc[at, :] = jnp.where(top, res[p : p + 1], s.acc[at, :])
        s.bg[at, :] = jnp.where(top, low[p : p + 1], s.bg[at, :].astype(F32)).astype(BF)


HBM = pl.BlockSpec(memory_space=pl.ANY)
G_MERGE = ((0, 2, NC),)
G_S23 = ((1, 1, NC),)
G_S4A = ((3, 1, NC),)
G_S34 = ((3, 1, NC),)
G_S45 = ((5, 1, NC),)
G_CORE = ((6, 1, NC),)
G_FULL = ((12, 1, 2), (15, 1, 1))
G_HALF = ((16, 1, 2),)
G_END = 18
S_K0 = ((0, 2, 8), (9, 2, 4))
S_K1 = ((1, 2, 8), (11, 2, 4))
S_K1B = ((2, 1, 8), (13, 2, 4))
S_K2 = ((2, 1, 8), (12, 2, 4))
S_K3 = ((4, 1, NC),)
S_K4 = ((11, 2, NC),)
S_K5 = ((12, 2, NC),)
S_K6 = ((15, 2, NC),)
S_END = 21
OUTS = dict(
    lo_out=((TOK, D), BF),
    hg_out=((TOK, D), BF),
    sums_out=((6, 48, D), F32),
    q_out=((8, D), F32),
    bias_out=((8, 128), F32),
    loss=((8, 128), F32),
    cgrad=((8, D), F32),
)
VECTORS = (
    "query_bias",
    "value_bias",
    "attn_bias",
    "first_gain",
    "first_shift",
    "outer_bias",
    "second_gain",
    "second_shift",
    "inner_bias",
)
INS = ("x_in", "up_in") + ("w_query", "w_key", "w_value", "w_attn", "w_inner", "w_outer", "w_queries") + VECTORS
INS += ("loss_weight", "positive_ids", "positive_count")
SCRATCH = dict(
    wa=((6, 2, 2, 2, 2, 48, D), BF),
    wb=((6, 2, 2, 2, 2, 48, D), BF),
    rb=((6, 48, D), BF),
    pack=((6, 48, D), BF),
    qpack=((32, 128), BF),
    x=((TOK, D), BF),
    up=((TOK, D), BF),
    lo=((TOK, D), BF),
    hg=((TOK, D), BF),
    out=((6, 48, D), F32),
    q=((TOK, D), BF),
    k=((TOK, D), BF),
    v=((TOK, D), BF),
    ctx=((TOK, D), BF),
    p=((4, 6, 128, 256), BF),
    fn=((TOK, D), F32),
    s1=((TOK, 1), F32),
    s2=((TOK, 1), F32),
    nl=((TOK, D), BF),
    acc=((TOK, D), F32),
    act=((4, TOK, D), BF),
    gp=((4, TOK, D), BF),
    bg=((TOK, D), BF),
    tmp=((TOK, D), F32),
    small=((256, 128), F32),
    tile=((8, 128), F32),
    qx=((2, 2, 2, 2, 48, 128), BF),
    qrb=((32, 128), BF),
    sc=((256, 128), F32),
    vec=((16, D), F32),
    gv=((12, 8, D), F32),
    aux=((8, 128), F32),
    qm=((D, 128), F32),
    cn=((8, D), F32),
    ci=((8, 1), F32),
    cls=((8, D), F32),
    qrow=((D, 128), F32),
    rc=((2, NC, 2, 2, 2, 48, LW), BF),
    r4a=((2, NC, 2, 48, LW), BF),
    r4b=((2, NC, 2, 48, LW), BF),
    r3b=((2, NC, 2, 48, LW), BF),
    r3a=((2, NC, 2, 48, LW), BF),
    r2=((2, NC, 48, LW), BF),
    st=((NC, 48, LW), BF),
    r1=((NC, 48, LW), BF),
    call=((512, 256), BF),
    sg=((256, 128), F32),
    pb=((256, 128), F32),
    zb=((4, 64, 128), F32),
    bb=((8, 8, 128), F32),
    half=((64, 128), F32),
)
SEMS = dict(
    gs=(6, 2),
    gr=(6, 2, NC),
    g1s=(1,),
    g1r=(NC,),
    xs=(8,),
    xr=(8,),
    zs=(3, 4),
    zr=(3, 4),
    bs=(3, 8),
    br=(3, 8),
    io=(5,),
)


class Spread:
    def __init__(self, p, s, ref, which, rows):
        self.p, self.s, self.ref, self.which, self.rows = p, s, ref, which, rows

    def zview(self, z):
        r = self.rows
        return self.ref.at[pl.ds(pl.multiple_of((self.p.b * 4 + z) * r, r), r), :]

    def bview(self, b):
        r = self.rows * 4
        return self.ref.at[pl.ds(pl.multiple_of(b * r, r), r), :]

    def zcopy(self, k, view):
        p, s, w = self.p, self.s, self.which
        return rcopy(view, view, s.zs.at[w, k], s.zr.at[w, k], (p.b, (p.z + k) % 4))

    def bcopy(self, k, view):
        p, s, w = self.p, self.s, self.which
        return rcopy(view, view, s.bs.at[w, k], s.br.at[w, k], ((p.b + k) % 8, p.z))

    def first(self):
        for k in range(1, 4):
            self.zcopy(k, self.zview(self.p.z)).start()

    def second(self):
        for k in range(1, 4):
            self.zcopy(k, self.zview((self.p.z + 4 - k) % 4)).wait_recv()
        for k in range(1, 8):
            self.bcopy(k, self.bview(self.p.b)).start()

    def finish(self):
        for k in range(1, 8):
            self.bcopy(k, self.bview((self.p.b + 8 - k) % 8)).wait_recv()
        for k in range(1, 4):
            self.zcopy(k, self.zview(self.p.z)).wait_send()
        for k in range(1, 8):
            self.bcopy(k, self.bview(self.p.b)).wait_send()


def gather_steps(p, s, me, vectors):
    def flows(ci):
        out = []
        for kind, ref in ((0, s.wa), (1, s.wb)):
            view = ref.at[ci // PARTS, :, :, :, :, :, lanes_of(ci)]
            out.append(
                Gather(
                    p,
                    view,
                    kind,
                    lambda st, kind=kind: s.gs.at[st, kind],
                    lambda st, kind=kind: s.gr.at[st, kind, ci],
                )
            )
        return out

    def s1(ci):
        at = (ci // PARTS, ALL, lanes_of(ci))
        return rcopy(s.pack.at[at], s.rb.at[at], s.g1s.at[0], s.g1r.at[ci], p.zdev)

    first = p.zl == 0

    def order(own, oth):
        return jnp.where(first, own, oth), jnp.where(first, oth, own)

    def merge(ci):
        s1(ci).wait_recv()
        i, ln = ci // PARTS, lanes_of(ci)
        lo, hi = order(s.pack[i, :, ln].astype(F32), s.rb[i, :, ln].astype(F32))
        s.wa[i, p.y, p.x, p.c, p.zh, :, ln] = jnp.concatenate([lo[:ROWS], hi[:ROWS]], 0).astype(BF)
        s.wb[i, p.y, p.x, p.c, p.zh, :, ln] = jnp.concatenate([lo[ROWS:], hi[ROWS:]], 0).astype(BF)
        for f in flows(ci):
            f.s2_send()

    def s23(fs):
        for f in fs:
            f.s2_recv()

        @pl.when(p.mid == 1)
        def _():
            for f in fs:
                f.s3a_send()

    def s4a(fs):
        for f in fs:
            f.s4a_send()

    def s34(fs):
        @pl.when(p.mid == 1)
        def _():
            for f in fs:
                f.s3a_recv()
                f.s3b_send()

        @pl.when(p.mid == 0)
        def _():
            for f in fs:
                f.s3b_recv()

        for f in fs:
            f.s4b_send()

    def s45(fs):
        for f in fs:
            f.s4_recv()
            f.core_send()

    def core(fs):
        for f in fs:
            f.core_recv()

    def drain():
        for kind, ref in ((0, s.wa), (1, s.wb)):
            sems = lambda st, kind=kind: s.gs.at[st, kind]
            Gather(p, ref, kind, sems, sems, (ALL,)).drain()
        rcopy(s.pack, s.rb, s.g1s.at[0], s.g1r.at[0], p.zdev).wait_send()
        q.drain()

    q = Gather(p, s.qx, 0, lambda st: s.xs.at[st], lambda st: s.xr.at[st])
    q1 = rcopy(s.qpack, s.qrb, s.xs.at[7], s.xr.at[7], p.zdev)
    for i in range(6):
        pack_weights(s, i)
        for h in range(PARTS):
            s1(PARTS * i + h).start()
        if i == 0:
            s.small[pl.ds(pl.multiple_of(me * 8, 8), 8), :] = pack_small(s)
            vectors.first()
            q1.start()

    def qmerge():
        q1.wait()
        lo, hi = order(s.qpack[...].astype(F32), s.qrb[...].astype(F32))
        s.qx[p.y, p.x, p.c, p.zh] = jnp.concatenate([lo[:ROWS], hi[:ROWS]], 0).astype(BF)
        q.s2_send()

    def q23():
        s23([q])
        s4a([q])

    query_steps = [qmerge, q23, lambda: s34([q]), lambda: s45([q]), lambda: core([q])]

    def pack_of(fn):
        return lambda ci: fn(flows(ci))

    stages = (
        (G_MERGE, merge),
        (G_S23, pack_of(s23)),
        (G_S4A, pack_of(s4a)),
        (G_S34, pack_of(s34)),
        (G_S45, pack_of(s45)),
        (G_CORE, pack_of(core)),
    )
    return stages, query_steps, drain


def scatter_steps(p, s):
    def piece(ci):
        return (ci // PARTS + 2) % 6

    def flows(ci):
        made = []
        for kind, ref in ((0, s.wa), (1, s.wb)):
            bufs = tuple(buf.at[kind, ci] for buf in (s.rc, s.r4a, s.r4b, s.r3b, s.r3a, s.r2))
            made.append(
                Scatter(
                    p,
                    ref.at[piece(ci), :, :, :, :, :, lanes_of(ci)],
                    kind,
                    lambda st, kind=kind: s.gs.at[st, kind],
                    lambda st, kind=kind: s.gr.at[st, kind, ci],
                    bufs,
                )
            )
        return made

    def k0(ci):
        @pl.when(ci >= PARTS)
        def _():
            for f in flows(ci):
                f.t0_send()

    def early(kind):
        for ci in range(PARTS):
            flows(ci)[kind].t0_send()

    def k1(fs):
        for f in fs:
            f.t0_add()
            f.t1a_send()

    def k1b(fs):
        for f in fs:
            f.t1b_send()

    def k2(fs):
        for f in fs:
            f.t1a_add()

            @pl.when(p.mid == 0)
            def _(f=f):
                f.t2a_send()

    def k3(fs):
        @pl.when(p.mid == 1)
        def _():
            for f in fs:
                f.t2a_add()
                f.t2b_send()

    def k4(fs):
        for f in fs:
            f.t1b_add()

            @pl.when(p.mid == 1)
            def _(f=f):
                f.t2b_add()

            f.t3_send()

    first = p.zl == 0

    def halves(total):
        top, low = total[:ROWS], total[ROWS:]
        return jnp.where(first, top, low), jnp.where(first, low, top)

    def s1(ci):
        return rcopy(s.st.at[ci], s.r1.at[ci], s.g1s.at[0], s.g1r.at[ci], p.zdev)

    def k5(ci):
        fa, fb = flows(ci)
        keep_a, give_a = halves(fa.t3_sum())
        keep_b, give_b = halves(fb.t3_sum())
        s.st[ci] = jnp.concatenate([give_a, give_b], 0).astype(BF)
        s1(ci).start()
        s.out[piece(ci), :, lanes_of(ci)] = jnp.concatenate([keep_a, keep_b], 0)

    def k6(ci):
        s1(ci).wait_recv()
        at = (piece(ci), ALL, lanes_of(ci))
        s.out[at] = s.out[at] + s.r1[ci].astype(F32)
        pltpu.make_async_copy(s.out.at[at], s.sums_out.at[at], s.io.at[4]).start()

    def pack_of(fn):
        return lambda ci: fn(flows(ci))

    stages = (
        (S_K0, k0),
        (S_K1, pack_of(k1)),
        (S_K1B, pack_of(k1b)),
        (S_K2, pack_of(k2)),
        (S_K3, pack_of(k3)),
        (S_K4, pack_of(k4)),
        (S_K5, k5),
        (S_K6, k6),
    )
    def zcopy(k):
        dz = (p.z + k) % 4
        src = s.pb.at[pl.ds(pl.multiple_of(dz * 64, 64), 64), :]
        return rcopy(src, s.zb.at[k], s.zs.at[0, k], s.zr.at[0, k], (p.b, dz))

    def bcopy(k):
        db = (p.b + k) % 8
        src = s.half.at[pl.ds(pl.multiple_of(db * 8, 8), 8), :]
        return rcopy(src, s.bb.at[k], s.bs.at[0, k], s.br.at[0, k], (db, p.z))

    def vectors_out():
        pack_vectors(s)
        for k in range(1, 4):
            zcopy(k).start()

    def vectors_half():
        total = s.pb[pl.ds(pl.multiple_of(p.z * 64, 64), 64), :]
        for k in range(1, 4):
            zcopy(k).wait()
            total = total + s.zb[k]
        s.half[...] = total
        for k in range(1, 8):
            bcopy(k).start()

    def vectors_in():
        total = s.half[pl.ds(pl.multiple_of(p.b * 8, 8), 8), :]
        for k in range(1, 8):
            bcopy(k).wait()
            total = total + s.bb[k]
        s.bias_out[...] = total

    def drain():
        for kind, ref in ((0, s.wa), (1, s.wb)):
            sems = lambda st, kind=kind: s.gs.at[st, kind]
            Scatter(p, ref, kind, sems, sems, (None,) * 6, (ALL,)).drain()
        rcopy(s.st, s.r1, s.g1s.at[0], s.g1r.at[0], p.zdev).wait_send()

    return stages, (vectors_out, vectors_half, vectors_in), early, drain


def done_by(spans, t):
    total = 0
    for first, many, chunks in spans:
        total = total + jnp.minimum(jnp.maximum((t - first + 1) * many, 0), chunks)
    return total


def run_span(spans, t, fn):
    pl.loop(done_by(spans, t - 1), done_by(spans, t))(fn)


def run_stages(stages, t):
    for spans, fn in stages:
        run_span(spans, t, fn)


def run_at(t, table):
    for when, fn in table:

        @pl.when(t == when)
        def _(fn=fn):
            fn()


def layer_kernel(*refs):
    s = Bag()
    names = list(INS) + list(OUTS) + list(SCRATCH) + list(SEMS)
    for name, ref in zip(names, refs):
        setattr(s, name, ref)
    p = Place()
    greet(p)
    me = p.b * 4 + p.z
    vectors = Spread(p, s, s.small, 0, 8)
    scores = Spread(p, s, s.sc, 1, 8)
    firsts = Spread(p, s, s.call, 2, 16)
    copies = {
        name: pltpu.make_async_copy(src, dst, s.io.at[k])
        for k, (name, src, dst) in enumerate(
            (
                ("x", s.x_in, s.x),
                ("up", s.up_in, s.up),
                ("lo", s.lo, s.lo_out),
                ("hg", s.hg, s.hg_out),
            )
        )
    }
    copies["x"].start()
    copies["up"].start()
    stages, query_steps, drain = gather_steps(p, s, me, vectors)

    def passages(fn, lo, many):
        def go():
            pl.loop(lo, lo + many)(lambda i: fn(s, i))

        return go

    def small_done():
        vectors.finish()
        unpack_small(s)

    forward = [
        (1, copies["x"].wait),
        (1, copies["up"].wait),
        (2, vectors.second),
        (6, small_done),
        (7, lambda: queries_keys(s)),
        (9, lambda: values(s)),
        (9, passages(attn_fwd, 0, 1)),
        (10, passages(attn_fwd, 1, 2)),
        (11, passages(attn_fwd, 3, 1)),
        (11, lambda: attn_out(s)),
    ]
    forward += [(5 + 2 * k, fn) for k, fn in enumerate(query_steps)]
    forward += [(14, lambda: unpack_queries(s))]

    @pl.loop(0, G_END)
    def _(t):
        run_stages(stages, t)
        run_at(t, forward)
        run_span(G_FULL, t, lambda j: ffn_fwd(s, j, 0, D))
        run_span(G_HALF, t, lambda h: ffn_fwd(s, 3, h, LW))

    s.sc[pl.ds(pl.multiple_of(me * 8, 8), 8), :] = first_rows(s, me)
    scores.first()
    s.gv[...] = jnp.zeros_like(s.gv)
    norm2(s)
    norm2_back(s)
    scores.second()
    firsts.first()
    copies["lo"].start()
    drain()
    scores.finish()
    loss_part(s, me)
    add_cls(s)

    stages, vector_steps, early, drain = scatter_steps(p, s)
    outer_back(s, 0)
    early(1)
    inner_back(s, 0)
    early(0)
    def hidden():
        qkv_back(s)
        copies["hg"].start()

    def query():
        firsts.finish()
        query_gradient(s, me)

    backward = [
        (1, firsts.second),
        (3, lambda: norm1_back(s)),
        (4, passages(attn_back, 0, 1)),
        (5, passages(attn_back, 1, 1)),
        (6, passages(attn_back, 2, 2)),
        (8, hidden),
        (9, query),
        (9, vector_steps[0]),
        (12, vector_steps[1]),
        (18, vector_steps[2]),
    ]

    @pl.loop(0, S_END)
    def _(t):
        run_stages(stages, t)

        @pl.when(t < 3)
        def _():
            ffn_back(s, t + 1)

        run_at(t, backward)

    drain()
    copies["lo"].wait()
    copies["hg"].wait()
    pltpu.make_async_copy(s.out, s.sums_out, s.io.at[4]).wait()


SMEM = pl.BlockSpec(memory_space=pltpu.SMEM)


def layer(*args):
    return pl.pallas_call(
        layer_kernel,
        out_shape=tuple(jax.ShapeDtypeStruct(*o) for o in OUTS.values()),
        in_specs=[HBM] * 2 + [VM] * (len(INS) - 5) + [SMEM] * 3,
        out_specs=(HBM,) * 3 + (VM,) * 4,
        scratch_shapes=[pltpu.VMEM(*b) for b in SCRATCH.values()] + [DMA(n) for n in SEMS.values()],
        compiler_params=pltpu.CompilerParams(
            collective_id=1, has_side_effects=True, vmem_limit_bytes=VMEM_LIMIT
        ),
    )(*args)


def finish_kernel(
    lo_in, hg_in, out, q_out, bias, loss, cgrad,
    lo, hg, query_grad, query_loss, g_query, g_key, g_value, g_attn,
    g_qb, g_vb, g_ab, g_fg, g_fs, g_inner, g_ib, g_outer, g_ob, g_sg, g_ss, cls_grad, held, sums, sems
):
    me = lax.axis_index("blk") * 4 + lax.axis_index("grp")
    part = TOK // 8
    into, away = [], []
    for k, (src, dst) in enumerate(((lo_in, lo), (hg_in, hg))):
        for h in range(8):
            at = pl.ds(h * part, part)
            into.append(pltpu.make_async_copy(src.at[at], held.at[k, at], sems.at[0, 8 * k + h]))
            away.append(pltpu.make_async_copy(held.at[k, at], dst.at[at], sems.at[1, 8 * k + h]))
    top, low = pl.ds(0, ROWS), pl.ds(ROWS, ROWS)
    pieces = [(0, top, g_query), (0, low, g_key), (1, top, g_value), (1, low, g_attn)]
    for j in range(4):
        at = pl.ds(j * D, D)
        pieces += [(2 + j, top, g_inner.at[:, at]), (2 + j, low, g_outer.at[:, at])]
    for i in range(6):
        into.append(pltpu.make_async_copy(out.at[i], sums.at[i], sems.at[0, 16 + i]))
    for n, (i, rows, dst) in enumerate(pieces):
        away.append(pltpu.make_async_copy(sums.at[i, rows], dst, sems.at[1, 16 + n]))
    for move in into:
        move.start()
    for k in range(16):
        into[k].wait()
        away[k].start()
    for i in range(6):
        into[16 + i].wait()
    for n in range(12):
        away[16 + n].start()
    query_grad[...] = q_out[0:4, :]
    cls_grad[...] = cgrad[0:4, :]
    for t, ref in enumerate((g_qb, g_vb, g_ab, g_fg, g_fs, g_ob, g_sg, g_ss)):
        ref[...] = pltpu.roll(bias[...], 32, 1)[t, :ROWS]
    g_ib[...] = bias[0, :96]
    query_loss[...] = pltpu.roll(loss[...], lax.rem(128 - 4 * me, 128), 1)[0, :4]
    for move in away:
        move.wait()


def finish(*args):
    f32 = lambda *dims: jax.ShapeDtypeStruct(dims, F32)
    square = f32(ROWS, D)
    vec = f32(ROWS)
    tokens = jax.ShapeDtypeStruct((TOK, D), BF)
    outs = [tokens, tokens, f32(4, D), f32(4)] + [square] * 4 + [vec] * 5
    outs += [f32(ROWS, 4 * D), f32(96), f32(ROWS, 4 * D), vec, vec, vec, f32(4, D)]
    return pl.pallas_call(
        finish_kernel,
        out_shape=outs,
        in_specs=[HBM] * 3 + [VM] * 4,
        out_specs=[HBM] * 2 + [VM] * 2 + [HBM] * 4 + [VM] * 5 + [HBM, VM, HBM] + [VM] * 4,
        scratch_shapes=[pltpu.VMEM((2, TOK, D), BF), pltpu.VMEM((6, 48, D), F32), DMA((2, 28))],
        compiler_params=pltpu.CompilerParams(vmem_limit_bytes=VMEM_LIMIT),
    )(*args)


def fast_local(
    hidden_in,
    upstream_grad,
    query_vectors,
    loss_weight,
    positive_ids,
    positive_count,
    query_proj,
    key_proj,
    value_proj,
    attn_proj,
    query_bias,
    value_bias,
    attn_bias,
    first_gain,
    first_shift,
    inner_proj,
    inner_bias,
    outer_proj,
    outer_bias,
    second_gain,
    second_shift,
):
    results = layer(
        hidden_in.reshape(TOK, D),
        upstream_grad.reshape(TOK, D),
        query_proj,
        key_proj,
        value_proj,
        attn_proj.T,
        inner_proj,
        outer_proj.T,
        query_vectors,
        query_bias,
        value_bias,
        attn_bias,
        first_gain,
        first_shift,
        outer_bias,
        second_gain,
        second_shift,
        inner_bias,
        loss_weight,
        positive_ids,
        positive_count,
    )
    layer_output, hidden_grad, *rest = finish(*results)
    rest[5] = rest[5].T
    rest[13] = rest[13].T
    return (layer_output.reshape(hidden_in.shape), hidden_grad.reshape(hidden_in.shape), *rest)


def solution(mesh):
    in_specs = (
        P(("blk", "grp"), None, None),
        P(("blk", "grp"), None, None),
        P(("blk", "grp"), None),
        P(("blk", "grp")),
        P(("blk", "grp"), None),
        P(("blk", "grp")),
        P(("blk", "grp"), None),
        P(("blk", "grp"), None),
        P(("blk", "grp"), None),
        P(None, ("blk", "grp")),
        P(("blk", "grp")),
        P(("blk", "grp")),
        P(("blk", "grp")),
        P(("blk", "grp")),
        P(("blk", "grp")),
        P(("blk", "grp"), None),
        P(("blk", "grp")),
        P(None, ("blk", "grp")),
        P(("blk", "grp")),
        P(("blk", "grp")),
        P(("blk", "grp")),
    )
    out_specs = (
        P(("blk", "grp"), None, None),
        P(("blk", "grp"), None, None),
        P(("blk", "grp"), None),
        P(("blk", "grp")),
        P(("blk", "grp"), None),
        P(("blk", "grp"), None),
        P(("blk", "grp"), None),
        P(None, ("blk", "grp")),
        P(("blk", "grp")),
        P(("blk", "grp")),
        P(("blk", "grp")),
        P(("blk", "grp")),
        P(("blk", "grp")),
        P(("blk", "grp"), None),
        P(("blk", "grp")),
        P(None, ("blk", "grp")),
        P(("blk", "grp")),
        P(("blk", "grp")),
        P(("blk", "grp")),
        P(("blk", "grp"), None),
    )
    tiled = mesh.shape["blk"] == 8 and mesh.shape["grp"] == 4
    local = fast_local if tiled else plain_local
    return jax.shard_map(local, mesh=mesh, in_specs=in_specs, out_specs=out_specs, check_vma=False)
```
